32 devices in a mesh: dp: 4 (over y, x), fsdp: 8 (over z, core).
Axes of the slice: x: 2, y: 2, z: 4, core: 2. Of those that a mesh axis runs over, the one named last changes fastest.
Arguments:
- tokens: bfloat16 [8, 1024, 1536], P('fsdp', 'dp'), may hold values from -13 to 13
- cotangent: bfloat16 [4, 8, 1024, 1536], P(None, 'fsdp', 'dp'), may hold values from -6 to 6
- norm1_gain: bfloat16 [1536], P(('dp', 'fsdp')), may hold values from 0.25 to 1.75
- norm1_bias: bfloat16 [1536], P(('dp', 'fsdp')), may hold values from -3 to 3
- query_weight: bfloat16 [1536, 1536], P(('dp', 'fsdp')), may hold values from -0.15625 to 0.15625
- key_weight: bfloat16 [1536, 1536], P(('dp', 'fsdp')), may hold values from -0.15625 to 0.15625
- value_weight: bfloat16 [1536, 1536], P(('dp', 'fsdp')), may hold values from -0.15625 to 0.15625
- out_weight: bfloat16 [1536, 1536], P(('dp', 'fsdp')), may hold values from -3.5 to 3.5
- norm2_gain: bfloat16 [1536], P(('dp', 'fsdp')), may hold values from 0.25 to 1.75
- norm2_bias: bfloat16 [1536], P(('dp', 'fsdp')), may hold values from -3 to 3
- up_weight: bfloat16 [1536, 6144], P(('dp', 'fsdp')), may hold values from -0.15625 to 0.15625
- up_bias: bfloat16 [6144], P(('dp', 'fsdp')), may hold values from -3 to 3
- down_weight: bfloat16 [6144, 1536], P(('dp', 'fsdp')), may hold values from -0.15625 to 0.15625
- down_bias: bfloat16 [1536], P(('dp', 'fsdp')), may hold values from -3 to 3
Outputs:
- activations: bfloat16 [4, 8, 1024, 1536], P(None, 'fsdp', 'dp')
- grad_tokens: bfloat16 [8, 1024, 1536], P('fsdp', 'dp')
- grad_norm1_gain: float32 [1536], P(('dp', 'fsdp'))
- grad_norm1_bias: float32 [1536], P(('dp', 'fsdp'))
- grad_query_weight: float32 [1536, 1536], P(('dp', 'fsdp'))
- grad_key_weight: float32 [1536, 1536], P(('dp', 'fsdp'))
- grad_value_weight: float32 [1536, 1536], P(('dp', 'fsdp'))
- grad_out_weight: float32 [1536, 1536], P(('dp', 'fsdp'))
- grad_norm2_gain: float32 [1536], P(('dp', 'fsdp'))
- grad_norm2_bias: float32 [1536], P(('dp', 'fsdp'))
- grad_up_weight: float32 [1536, 6144], P(('dp', 'fsdp'))
- grad_up_bias: float32 [6144], P(('dp', 'fsdp'))
- grad_down_weight: float32 [6144, 1536], P(('dp', 'fsdp'))
- grad_down_bias: float32 [1536], P(('dp', 'fsdp'))
The draws below stay inside these ranges and needn't reach their ends.
All inputs are finite; a program needn't handle non-finite values.
Results may differ from the reference program's by a relative error of at most 0.019.
Values may be sent and summed in bfloat16 or wider, within the bound.
A program may use at most 320 MiB of HBM per device.

```python
import math
import jax
import jax.numpy as jnp
from jax import lax

D = 1536
HEADS = 12
HEAD_DIM = 128
FF = 6144
GRAN = 4
SEQ = 1024
SEQS = 8


def draw_tokens(key, part):
    key = jax.random.fold_in(key, 7)
    noise_key, row_key, column_key = jax.random.split(key, 3)
    extent = (SEQS, SEQ, D)
    row_scale = jnp.exp(jax.random.uniform(row_key, (SEQS, SEQ, 1), jnp.float32, math.log(0.3), math.log(3.0)))
    column_scale = jnp.exp(jax.random.uniform(column_key, (1, 1, D), jnp.float32, math.log(0.3), math.log(3.0)))
    noise = jax.random.truncated_normal(noise_key, -4.0, 4.0, extent, jnp.float32)
    values = 0.35 * noise * row_scale * column_scale
    return values.astype(jnp.bfloat16)


def shard_levels(key, dims, cuts, low, largest):
    loudness = 1.0
    for position, shards_of in cuts:
        heights = jax.random.uniform(jax.random.fold_in(jax.random.fold_in(key, 6), position), (shards_of,), jnp.float32, low / len(cuts), largest / len(cuts))
        loudness = loudness * jnp.repeat(jnp.exp(heights), dims[position] // shards_of).reshape((-1,) + (1,) * (len(dims) - 1 - position))
    return loudness


def gaussian(rng, dims, scale, reach, cuts=(), kind=jnp.bfloat16):
    drawn = jax.random.normal(rng, dims, jnp.float32) * scale
    if len(cuts) > 0:
        drawn = shard_levels(rng, dims, cuts, -0.22, 0.18) * drawn
    return jnp.clip(drawn, min=-reach, max=reach).astype(kind)


def setup_inputs(seed: int = 0) -> dict:
    key_list = jax.random.split(jax.random.key(seed), 15)
    tokens = draw_tokens(jax.random.fold_in(key_list[14], 71), 0)
    cotangent = gaussian(key_list[1], (GRAN, SEQS, SEQ, D), 1.0, 6.0, ((1, 8), (2, 4)))
    norm1_gain = jnp.clip(1.0 + 0.15 * jax.random.normal(key_list[2], (D,), jnp.float32), 0.25, 1.75).astype(jnp.bfloat16)
    norm1_bias = gaussian(key_list[3], (D,), 0.5, 3.0, ((0, 32),))
    query_weight = gaussian(key_list[4], (D, D), D ** -0.5, 0.15625, ((0, 32),))
    key_weight = gaussian(key_list[5], (D, D), D ** -0.5, 0.15625, ((0, 32),))
    value_weight = gaussian(key_list[6], (D, D), D ** -0.5, 0.15625, ((0, 32),))
    out_weight = gaussian(key_list[7], (D, D), (max(1, 2 * D // SEQ)) ** -0.5, 3.5, ((0, 32),))
    norm2_gain = jnp.clip(1.0 + 0.15 * jax.random.normal(key_list[8], (D,), jnp.float32), 0.25, 1.75).astype(jnp.bfloat16)
    norm2_bias = gaussian(key_list[9], (D,), 0.5, 3.0, ((0, 32),))
    up_weight = gaussian(key_list[10], (D, FF), D ** -0.5, 0.15625, ((0, 32),))
    up_bias = gaussian(key_list[11], (FF,), 0.5, 3.0, ((0, 32),))
    down_weight = gaussian(key_list[12], (FF, D), (FF // 4) ** -0.5, 0.15625, ((0, 32),))
    down_bias = gaussian(key_list[13], (D,), 0.5, 3.0, ((0, 32),))
    return dict(tokens=tokens, cotangent=cotangent, norm1_gain=norm1_gain, norm1_bias=norm1_bias, query_weight=query_weight, key_weight=key_weight, value_weight=value_weight, out_weight=out_weight, norm2_gain=norm2_gain, norm2_bias=norm2_bias, up_weight=up_weight, up_bias=up_bias, down_weight=down_weight, down_bias=down_bias)


highest = lax.Precision.HIGHEST
epsilon = 1e-05
masked_score = -1e+30

@jax.custom_vjp
def low(v):
    return lax.optimization_barrier(v.astype(jnp.bfloat16)).astype(jnp.float32)

@jax.custom_vjp
def low_back(v):
    return v

def low_keep(v):
    return (low(v), None)

def low_pass(kept, grad):
    return (grad,)

def back_keep(v):
    return (v, None)

def back_low(kept, grad):
    return (low(grad),)
low.defvjp(low_keep, low_pass)
low_back.defvjp(back_keep, back_low)

def matmul_high(left, right):
    return jnp.dot(left, right, precision=highest, preferred_element_type=jnp.float32)

def layer_norm(values, gain, shift):
    centred = values - lax.optimization_barrier(jnp.mean(values, axis=-1, keepdims=True))
    spread = lax.optimization_barrier(jnp.mean(centred * centred, axis=-1, keepdims=True))
    return centred * lax.rsqrt(spread + epsilon) * gain + shift

def gelu_tanh(values):
    return 0.5 * values * (1.0 + jnp.tanh(0.7978845608028654 * (values + 0.044715 * values * values * values)))

def rotary_tables(positions, half_size):
    ladder = jnp.arange(half_size).astype(jnp.float32)
    inverse = jnp.exp(ladder * (-math.log(10000.0) / half_size))
    angles = positions[:, None] * inverse[None, :]
    return (jnp.cos(angles)[:, None, :], jnp.sin(angles)[:, None, :])

def rotate(values, cosine, sine):
    half_size = values.shape[-1] // 2
    first = values[..., :half_size]
    second = values[..., half_size:]
    return jnp.concatenate([first * cosine - second * sine, second * cosine + first * sine], axis=-1)

def one_sequence(params, inputs):
    gain_one, bias_one, w_query, w_key, w_value, w_out, gain_two, bias_two, w_up, b_up, w_down, b_down = params
    seq_len = inputs.shape[0]
    attn_in = low(layer_norm(inputs, gain_one, bias_one))
    queries = low_back(matmul_high(attn_in, w_query)).reshape(seq_len, HEADS, HEAD_DIM)
    keys = low_back(matmul_high(attn_in, w_key)).reshape(seq_len, HEADS, HEAD_DIM)
    values = low_back(low(matmul_high(attn_in, w_value))).reshape(seq_len, HEADS, HEAD_DIM)
    positions = jnp.arange(seq_len).astype(jnp.float32)
    cosine, sine = rotary_tables(positions, HEAD_DIM // 2)
    q_rot = low(rotate(queries, cosine, sine) * HEAD_DIM ** (-0.5))
    k_rot = low(rotate(keys, cosine, sine))
    scores = low_back(jnp.einsum('qhd,khd->hqk', q_rot, k_rot, precision=highest))
    causal = jnp.arange(seq_len)[:, None] >= jnp.arange(seq_len)[None, :]
    scores = jnp.where(causal[None], scores, masked_score)
    top_score = lax.optimization_barrier(jnp.max(scores, axis=-1, keepdims=True))
    raised = jnp.exp(scores - top_score)
    probs = low(raised / lax.optimization_barrier(jnp.sum(raised, axis=-1, keepdims=True)))
    mixed = jnp.einsum('hqk,khd->qhd', probs, values, precision=highest)
    mixed = low_back(low(mixed)).reshape(seq_len, HEADS * HEAD_DIM)
    hidden = inputs + low_back(matmul_high(mixed, w_out))
    ffn_in = low(layer_norm(hidden, gain_two, bias_two))
    preact = matmul_high(ffn_in, w_up) + b_up
    results = []
    for level_idx in range(GRAN):
        level_width = FF // 2 ** (GRAN - 1 - level_idx)
        gated = low(gelu_tanh(low_back(preact[:, :level_width])))
        results.append(hidden + matmul_high(gated, w_down[:level_width]) + b_down)
    return jnp.stack(results)

def reference(tokens, cotangent, norm1_gain, norm1_bias, query_weight, key_weight, value_weight, out_weight, norm2_gain, norm2_bias, up_weight, up_bias, down_weight, down_bias):
    params = tuple((weight.astype(jnp.float32) for weight in (norm1_gain, norm1_bias, query_weight, key_weight, value_weight, out_weight, norm2_gain, norm2_bias, up_weight, up_bias, down_weight, down_bias)))

    def stacked(param_tuple, inputs_all):

        def per_sequence(sequence):
            return one_sequence(param_tuple, sequence)
        return lax.map(jax.checkpoint(per_sequence), inputs_all)
    outputs, pullback = jax.vjp(stacked, params, tokens.astype(jnp.float32))
    grads, grad_inputs = pullback(jnp.transpose(cotangent.astype(jnp.float32), (1, 0, 2, 3)))
    activations = jnp.transpose(outputs, (1, 0, 2, 3)).astype(jnp.bfloat16)
    return (activations, grad_inputs.astype(jnp.bfloat16), grads[0], grads[1], grads[2], grads[3], grads[4], grads[5], grads[6], grads[7], grads[8], grads[9], grads[10], grads[11])
```

```python
import functools
import math

import jax
import jax.numpy as jnp
from jax import lax
from jax.sharding import PartitionSpec as P

HEADS = 12
HEAD_DIM = 128
FF = 6144
GRAN = 4


epsilon = 1e-05
masked_score = -1e30


def product(left, right):
    return jnp.dot(left, right, preferred_element_type=jnp.float32)


def gram_product(left, right):
    return lax.dot_general(
        left, right, (((0,), (0,)), ((), ())), preferred_element_type=jnp.float32
    )


def back_product(left, right):
    return lax.dot_general(
        left, right, (((1,), (1,)), ((), ())), preferred_element_type=jnp.float32
    )


def norm_parts(values):
    centred = values - jnp.mean(values, axis=-1, keepdims=True)
    inverse = lax.rsqrt(jnp.mean(centred * centred, axis=-1, keepdims=True) + epsilon)
    return (centred * inverse, inverse)


def norm_backward(grad_normed, normed, inverse, gain):
    scaled = grad_normed * gain
    return inverse * (
        scaled
        - jnp.mean(scaled, axis=-1, keepdims=True)
        - normed * jnp.mean(scaled * normed, axis=-1, keepdims=True)
    )


def gelu_value(values):
    return (
        0.5
        * values
        * (1.0 + jnp.tanh(0.7978845608028654 * (values + 0.044715 * values * values * values)))
    )


def gelu_grad(values):
    tangent = jnp.tanh(0.7978845608028654 * (values + 0.044715 * values * values * values))
    return 0.5 * (1.0 + tangent) + 0.5 * values * (1.0 - tangent * tangent) * 0.7978845608028654 * (
        1.0 + 3.0 * 0.044715 * values * values
    )


def rotary_tables(positions, half_size):
    ladder = jnp.arange(half_size).astype(jnp.float32)
    inverse = jnp.exp(ladder * (-math.log(10000.0) / half_size))
    angles = positions[:, None] * inverse[None, :]
    return (jnp.cos(angles)[:, None, :], jnp.sin(angles)[:, None, :])


def rotate(values, cosine, sine):
    half_size = values.shape[-1] // 2
    first = values[..., :half_size]
    second = values[..., half_size:]
    return jnp.concatenate(
        [first * cosine - second * sine, second * cosine + first * sine], axis=-1
    )


def block_scores(queries, positions, key_block, start_row):
    block_rows = key_block.shape[0]
    scores = jnp.einsum("qhd,khd->hqk", queries, key_block, preferred_element_type=jnp.float32)
    key_positions = start_row + jnp.arange(block_rows, dtype=jnp.int32)
    visible = positions[None, :, None] >= key_positions[None, None, :]
    return (jnp.where(visible, scores, masked_score), visible)


def key_blocking(keys_all, values_all, key_offset):
    seq_len = keys_all.shape[0]
    block_rows = min(512, seq_len)
    block_count = seq_len // block_rows
    key_blocks = keys_all.reshape(block_count, block_rows, HEADS, HEAD_DIM)
    value_blocks = values_all.reshape(block_count, block_rows, HEADS, HEAD_DIM)
    starts = key_offset + jnp.arange(block_count, dtype=jnp.int32) * block_rows
    return (key_blocks, value_blocks, starts)


def attend(queries, keys_all, values_all, positions):
    tok_rows = queries.shape[0]
    key_blocks, value_blocks, starts = key_blocking(keys_all, values_all, jnp.int32(0))

    def measure(state_pair, block_pair):
        top_score, total = state_pair
        key_block, start_row = block_pair
        scores, visible = block_scores(queries, positions, key_block, start_row)
        new_top = jnp.maximum(top_score, jnp.max(scores, axis=-1))
        raised = jnp.where(visible, jnp.exp(scores - new_top[..., None]), 0.0)
        total = total * jnp.exp(top_score - new_top) + jnp.sum(raised, axis=-1)
        return ((new_top, total), None)

    initial = (
        jnp.full((HEADS, tok_rows), masked_score, jnp.float32),
        jnp.zeros((HEADS, tok_rows), jnp.float32),
    )
    (top_score, total), unused = lax.scan(measure, initial, (key_blocks, starts))
    log_total = top_score + jnp.log(total)

    def accumulate(mixed, block_triple):
        key_block, value_block, start_row = block_triple
        scores, visible = block_scores(queries, positions, key_block, start_row)
        probs = jnp.where(visible, jnp.exp(scores - log_total[..., None]), 0.0).astype(jnp.bfloat16)
        return (
            mixed
            + jnp.einsum("hqk,khd->qhd", probs, value_block, preferred_element_type=jnp.float32),
            None,
        )

    mixed, unused = lax.scan(
        accumulate,
        jnp.zeros((tok_rows, HEADS, HEAD_DIM), jnp.float32),
        (key_blocks, value_blocks, starts),
    )
    return (mixed, log_total)


def attend_back(
    queries, positions, keys_all, values_all, key_offset, grad_mixed, log_total, row_delta
):
    tok_rows = queries.shape[0]
    key_blocks, value_blocks, starts = key_blocking(keys_all, values_all, key_offset)

    def backward_block(grad_queries, block_triple):
        key_block, value_block, start_row = block_triple
        scores, visible = block_scores(queries, positions, key_block, start_row)
        probs = jnp.where(visible, jnp.exp(scores - log_total[..., None]), 0.0)
        grad_probs = jnp.einsum(
            "qhd,khd->hqk", grad_mixed, value_block, preferred_element_type=jnp.float32
        )
        grad_scores = (probs * (grad_probs - row_delta[..., None])).astype(jnp.bfloat16)
        grad_queries = grad_queries + jnp.einsum(
            "hqk,khd->qhd", grad_scores, key_block, preferred_element_type=jnp.float32
        )
        grad_key_block = jnp.einsum(
            "hqk,qhd->khd", grad_scores, queries, preferred_element_type=jnp.float32
        )
        grad_value_block = jnp.einsum(
            "hqk,qhd->khd",
            probs.astype(jnp.bfloat16),
            grad_mixed,
            preferred_element_type=jnp.float32,
        )
        return (grad_queries, (grad_key_block, grad_value_block))

    grad_queries, (grad_keys, grad_values) = lax.scan(
        backward_block,
        jnp.zeros((tok_rows, HEADS, HEAD_DIM), jnp.float32),
        (key_blocks, value_blocks, starts),
    )
    key_len = keys_all.shape[0]
    return (
        grad_queries,
        grad_keys.reshape(key_len, HEADS * HEAD_DIM),
        grad_values.reshape(key_len, HEADS * HEAD_DIM),
    )


def local_gathered(
    tokens,
    cotangent,
    norm1_gain,
    norm1_bias,
    query_weight,
    key_weight,
    value_weight,
    out_weight,
    norm2_gain,
    norm2_bias,
    up_weight,
    up_bias,
    down_weight,
    down_bias,
):
    (
        gain_one,
        bias_one,
        w_query,
        w_key,
        w_value,
        w_out,
        gain_two,
        bias_two,
        w_up,
        b_up,
        w_down,
        b_down,
    ) = (
        lax.all_gather(norm1_gain, ("dp", "fsdp"), axis=0, tiled=True),
        lax.all_gather(norm1_bias, ("dp", "fsdp"), axis=0, tiled=True),
        lax.all_gather(query_weight, ("dp", "fsdp"), axis=0, tiled=True),
        lax.all_gather(key_weight, ("dp", "fsdp"), axis=0, tiled=True),
        lax.all_gather(value_weight, ("dp", "fsdp"), axis=0, tiled=True),
        lax.all_gather(out_weight, ("dp", "fsdp"), axis=0, tiled=True),
        lax.all_gather(norm2_gain, ("dp", "fsdp"), axis=0, tiled=True),
        lax.all_gather(norm2_bias, ("dp", "fsdp"), axis=0, tiled=True),
        lax.all_gather(up_weight, ("dp", "fsdp"), axis=0, tiled=True),
        lax.all_gather(up_bias, ("dp", "fsdp"), axis=0, tiled=True),
        lax.all_gather(down_weight, ("dp", "fsdp"), axis=0, tiled=True),
        lax.all_gather(down_bias, ("dp", "fsdp"), axis=0, tiled=True),
    )
    seq_count = tokens.shape[0]
    tok_rows = tokens.shape[1]
    model_width = tokens.shape[2]
    all_rows = seq_count * tok_rows
    scaling = HEAD_DIM ** (-0.5)
    inputs = tokens.reshape(all_rows, model_width).astype(jnp.float32)
    normed_one, inverse_one = norm_parts(inputs)
    attn_in = (normed_one * gain_one.astype(jnp.float32) + bias_one.astype(jnp.float32)).astype(
        jnp.bfloat16
    )
    queries = product(attn_in, w_query).reshape(seq_count, tok_rows, HEADS, HEAD_DIM)
    key_raw = product(attn_in, w_key).reshape(seq_count, tok_rows, HEADS, HEAD_DIM)
    value_low = (
        product(attn_in, w_value).astype(jnp.bfloat16).reshape(seq_count, tok_rows, model_width)
    )
    key_offset = lax.axis_index("dp") * tok_rows
    positions = key_offset + jnp.arange(tok_rows, dtype=jnp.int32)
    cosine, sine = rotary_tables(positions.astype(jnp.float32), HEAD_DIM // 2)
    q_rot = (rotate(queries, cosine, sine) * scaling).astype(jnp.bfloat16)
    k_flat = (
        rotate(key_raw, cosine, sine).astype(jnp.bfloat16).reshape(seq_count, tok_rows, model_width)
    )
    keys_all, values_all = (
        lax.all_gather(k_flat, "dp", axis=1, tiled=True),
        lax.all_gather(value_low, "dp", axis=1, tiled=True),
    )
    seq_len = keys_all.shape[1]
    mixed, log_total = jax.vmap(attend, in_axes=(0, 0, 0, None))(
        q_rot,
        keys_all.reshape(seq_count, seq_len, HEADS, HEAD_DIM),
        values_all.reshape(seq_count, seq_len, HEADS, HEAD_DIM),
        positions,
    )
    mixed_low = mixed.reshape(all_rows, model_width).astype(jnp.bfloat16)
    hidden = inputs + product(mixed_low, w_out)
    normed_two, inverse_two = norm_parts(hidden)
    ffn_in = (normed_two * gain_two.astype(jnp.float32) + bias_two.astype(jnp.float32)).astype(
        jnp.bfloat16
    )
    preact = product(ffn_in, w_up) + b_up.astype(jnp.float32)
    edges = [0] + [FF // 2 ** (GRAN - 1 - level_idx) for level_idx in range(GRAN)]
    gated_list = []
    result_list = []
    for level_idx in range(GRAN):
        level_width = edges[level_idx + 1]
        gated = gelu_value(preact[:, :level_width]).astype(jnp.bfloat16)
        gated_list.append(gated)
        result = hidden + product(gated, w_down[:level_width]) + b_down.astype(jnp.float32)
        result_list.append(result.astype(jnp.bfloat16))
    activations = jnp.stack(result_list).reshape(GRAN, seq_count, tok_rows, model_width)
    back_gain_one, back_query, back_key, back_value, back_out, back_gain_two, back_up, back_down = (
        lax.all_gather(norm1_gain, ("dp", "fsdp"), axis=0, tiled=True),
        lax.all_gather(query_weight, ("dp", "fsdp"), axis=0, tiled=True),
        lax.all_gather(key_weight, ("dp", "fsdp"), axis=0, tiled=True),
        lax.all_gather(value_weight, ("dp", "fsdp"), axis=0, tiled=True),
        lax.all_gather(out_weight, ("dp", "fsdp"), axis=0, tiled=True),
        lax.all_gather(norm2_gain, ("dp", "fsdp"), axis=0, tiled=True),
        lax.all_gather(up_weight, ("dp", "fsdp"), axis=0, tiled=True),
        lax.all_gather(down_weight, ("dp", "fsdp"), axis=0, tiled=True),
    )
    grads_out = cotangent.reshape(GRAN, all_rows, model_width)
    grad_hidden = jnp.sum(grads_out.astype(jnp.float32), axis=0)
    grad_down_bias = jnp.sum(grad_hidden, axis=0)
    grad_ffn_in = jnp.zeros((all_rows, model_width), jnp.float32)
    pre_grads = []
    for level_idx in range(GRAN):
        level_width = edges[level_idx + 1]
        grad_gated = back_product(grads_out[level_idx], back_down[:level_width])
        grad_pre = (grad_gated * gelu_grad(preact[:, :level_width])).astype(jnp.bfloat16)
        pre_grads.append(grad_pre)
        grad_ffn_in = grad_ffn_in + back_product(grad_pre, back_up[:, :level_width])
    up_blocks = []
    bias_blocks = []
    down_blocks = []
    for block_idx in range(GRAN):
        start_col = edges[block_idx]
        stop_col = edges[block_idx + 1]
        stacked_grad = jnp.concatenate(
            [pre_grads[level_idx][:, start_col:stop_col] for level_idx in range(block_idx, GRAN)],
            axis=0,
        )
        stacked_in = jnp.concatenate([ffn_in] * (GRAN - block_idx), axis=0)
        up_blocks.append(gram_product(stacked_in, stacked_grad))
        bias_blocks.append(jnp.sum(stacked_grad.astype(jnp.float32), axis=0))
        stacked_gated = jnp.concatenate(
            [gated_list[level_idx][:, start_col:stop_col] for level_idx in range(block_idx, GRAN)],
            axis=0,
        )
        stacked_out = jnp.concatenate(
            [grads_out[level_idx] for level_idx in range(block_idx, GRAN)], axis=0
        )
        down_blocks.append(gram_product(stacked_gated, stacked_out))
    grad_up_weight = jnp.concatenate(up_blocks, axis=1)
    grad_up_bias = jnp.concatenate(bias_blocks, axis=0)
    grad_down_weight = jnp.concatenate(down_blocks, axis=0)
    grad_gain_two = jnp.sum(grad_ffn_in * normed_two, axis=0)
    grad_bias_two = jnp.sum(grad_ffn_in, axis=0)
    grad_hidden = grad_hidden + norm_backward(
        grad_ffn_in, normed_two, inverse_two, back_gain_two.astype(jnp.float32)
    )
    grad_branch = grad_hidden.astype(jnp.bfloat16)
    grad_out_weight = gram_product(mixed_low, grad_branch)
    grad_mixed = (
        back_product(grad_branch, back_out)
        .astype(jnp.bfloat16)
        .reshape(seq_count, tok_rows, HEADS, HEAD_DIM)
    )
    row_delta = jnp.einsum("sqhd,sqhd->shq", grad_mixed.astype(jnp.float32), mixed)
    keys_again, values_again = (
        lax.all_gather(k_flat, "dp", axis=1, tiled=True),
        lax.all_gather(value_low, "dp", axis=1, tiled=True),
    )
    back_all = jax.vmap(attend_back, in_axes=(0, None, 0, 0, None, 0, 0, 0))
    grad_q_rot, grad_keys_all, grad_values_all = back_all(
        q_rot,
        positions,
        keys_again.reshape(seq_count, seq_len, HEADS, HEAD_DIM),
        values_again.reshape(seq_count, seq_len, HEADS, HEAD_DIM),
        jnp.int32(0),
        grad_mixed,
        log_total,
        row_delta,
    )
    every_query, every_grad = (
        lax.all_gather(q_rot, "dp", axis=1, tiled=True),
        lax.all_gather(grad_mixed, "dp", axis=1, tiled=True),
    )
    every_total, every_delta = (
        lax.all_gather(jnp.transpose(log_total, (0, 2, 1)), "dp", axis=1, tiled=True),
        lax.all_gather(jnp.transpose(row_delta, (0, 2, 1)), "dp", axis=1, tiled=True),
    )
    every_position = jnp.arange(seq_len, dtype=jnp.int32)
    unused_rows, grad_key_mine, grad_value_mine = back_all(
        every_query,
        every_position,
        k_flat.reshape(seq_count, tok_rows, HEADS, HEAD_DIM),
        value_low.reshape(seq_count, tok_rows, HEADS, HEAD_DIM),
        key_offset,
        every_grad,
        jnp.transpose(every_total, (0, 2, 1)),
        jnp.transpose(every_delta, (0, 2, 1)),
    )
    grad_query = (
        rotate(grad_q_rot * scaling, cosine, -sine)
        .reshape(all_rows, model_width)
        .astype(jnp.bfloat16)
    )
    grad_key = (
        rotate(grad_key_mine.reshape(seq_count, tok_rows, HEADS, HEAD_DIM), cosine, -sine)
        .reshape(all_rows, model_width)
        .astype(jnp.bfloat16)
    )
    grad_val = grad_value_mine.reshape(all_rows, model_width).astype(jnp.bfloat16)
    grad_query_weight = gram_product(attn_in, grad_query)
    grad_key_weight = gram_product(attn_in, grad_key)
    grad_value_weight = gram_product(attn_in, grad_val)
    grad_attn_in = (
        back_product(grad_query, back_query)
        + back_product(grad_key, back_key)
        + back_product(grad_val, back_value)
    )
    grad_gain_one = jnp.sum(grad_attn_in * normed_one, axis=0)
    grad_bias_one = jnp.sum(grad_attn_in, axis=0)
    grad_inputs = grad_hidden + norm_backward(
        grad_attn_in, normed_one, inverse_one, back_gain_one.astype(jnp.float32)
    )
    (
        sum_gain_one,
        sum_bias_one,
        sum_query,
        sum_key,
        sum_value,
        sum_out,
        sum_gain_two,
        sum_bias_two,
        sum_up,
        sum_up_bias,
        sum_down,
        sum_down_bias,
    ) = (
        lax.psum_scatter(grad_gain_one, ("dp", "fsdp"), scatter_dimension=0, tiled=True),
        lax.psum_scatter(grad_bias_one, ("dp", "fsdp"), scatter_dimension=0, tiled=True),
        lax.psum_scatter(grad_query_weight, ("dp", "fsdp"), scatter_dimension=0, tiled=True),
        lax.psum_scatter(grad_key_weight, ("dp", "fsdp"), scatter_dimension=0, tiled=True),
        lax.psum_scatter(grad_value_weight, ("dp", "fsdp"), scatter_dimension=0, tiled=True),
        lax.psum_scatter(grad_out_weight, ("dp", "fsdp"), scatter_dimension=0, tiled=True),
        lax.psum_scatter(grad_gain_two, ("dp", "fsdp"), scatter_dimension=0, tiled=True),
        lax.psum_scatter(grad_bias_two, ("dp", "fsdp"), scatter_dimension=0, tiled=True),
        lax.psum_scatter(grad_up_weight, ("dp", "fsdp"), scatter_dimension=0, tiled=True),
        lax.psum_scatter(grad_up_bias, ("dp", "fsdp"), scatter_dimension=0, tiled=True),
        lax.psum_scatter(grad_down_weight, ("dp", "fsdp"), scatter_dimension=0, tiled=True),
        lax.psum_scatter(grad_down_bias, ("dp", "fsdp"), scatter_dimension=0, tiled=True),
    )
    return (
        activations,
        grad_inputs.astype(jnp.bfloat16).reshape(seq_count, tok_rows, model_width),
        sum_gain_one,
        sum_bias_one,
        sum_query,
        sum_key,
        sum_value,
        sum_out,
        sum_gain_two,
        sum_bias_two,
        sum_up,
        sum_up_bias,
        sum_down,
        sum_down_bias,
    )


def piece_blocks(ranks):
    piece_count = max(2 ** (GRAN - 1), ranks)
    width = FF // piece_count
    edges = [FF // 2 ** (GRAN - 1 - level_idx) for level_idx in range(GRAN)]
    blocks = []
    for piece in range(piece_count):
        blocks.append(next(b for b in range(GRAN) if piece * width < edges[b]))
    per_rank = piece_count // ranks
    return [blocks[rank * per_rank : (rank + 1) * per_rank] for rank in range(ranks)], width


def local_split(ranks, shards, *arguments):
    (
        tokens,
        cotangent,
        norm1_gain,
        norm1_bias,
        query_weight,
        key_weight,
        value_weight,
        out_weight,
        norm2_gain,
        norm2_bias,
        up_weight,
        up_bias,
        down_weight,
        down_bias,
    ) = arguments
    model_width = tokens.shape[2]
    tok_rows = tokens.shape[1]
    seq_len = tok_rows * ranks
    own = query_weight.shape[0]
    heads = HEADS // ranks
    head_cols = heads * HEAD_DIM
    ff_cols = FF // ranks
    scaling = HEAD_DIM ** (-0.5)
    rank = lax.axis_index("dp")

    small = jnp.concatenate([norm1_gain, norm1_bias, norm2_gain, norm2_bias, down_bias, up_bias])
    small = lax.all_gather(small, ("dp", "fsdp"), axis=0, tiled=False).astype(jnp.float32)
    gain_one, bias_one, gain_two, bias_two, b_down = (
        small[:, i * own : (i + 1) * own].reshape(model_width) for i in range(5)
    )
    b_up_all = small[:, 5 * own :].reshape(ranks, ff_cols)
    b_up = lax.dynamic_index_in_dim(b_up_all, rank, 0, keepdims=False)

    def to_parts(weight):
        return weight.reshape(own, ranks, -1).transpose(1, 0, 2)

    mixed_weights = jnp.concatenate(
        [to_parts(w) for w in (query_weight, key_weight, value_weight)], axis=2
    )

    def spread(parts):
        parts = lax.all_to_all(parts, "dp", split_axis=0, concat_axis=0)
        parts = lax.all_gather(parts, "fsdp", axis=1, tiled=False)
        return parts.reshape(model_width, -1)

    w_qkv = spread(mixed_weights)
    w_out = lax.all_gather(out_weight, "fsdp", axis=0, tiled=True)
    w_up = spread(to_parts(up_weight))
    w_down = lax.all_gather(down_weight, "fsdp", axis=0, tiled=True)

    own_tokens = tokens.reshape(tok_rows, model_width)
    all_tokens = lax.all_gather(own_tokens, "dp", axis=0, tiled=True).astype(jnp.float32)
    normed_all, unused = norm_parts(all_tokens)
    attn_in = (normed_all * gain_one + bias_one).astype(jnp.bfloat16)
    qkv = product(attn_in, w_qkv)
    queries = qkv[:, :head_cols].reshape(seq_len, heads, HEAD_DIM)
    key_raw = qkv[:, head_cols : 2 * head_cols].reshape(seq_len, heads, HEAD_DIM)
    values = qkv[:, 2 * head_cols :].astype(jnp.bfloat16).reshape(seq_len, heads, HEAD_DIM)
    positions = jnp.arange(seq_len, dtype=jnp.int32)
    cosine, sine = rotary_tables(positions.astype(jnp.float32), HEAD_DIM // 2)
    q_rot = (rotate(queries, cosine, sine) * scaling).astype(jnp.bfloat16)
    k_rot = rotate(key_raw, cosine, sine).astype(jnp.bfloat16)
    visible = (positions[:, None] >= positions[None, :])[None]

    def weigh(log_total=None):
        scores = jnp.einsum("qhd,khd->hqk", q_rot, k_rot, preferred_element_type=jnp.float32)
        scores = jnp.where(visible, scores, masked_score)
        if log_total is None:
            top = jnp.max(scores, axis=-1)
            log_total = top + jnp.log(jnp.sum(jnp.exp(scores - top[..., None]), axis=-1))
        return jnp.exp(scores - log_total[..., None]), log_total

    probs, log_total = weigh()
    mixed = jnp.einsum(
        "hqk,khd->qhd", probs.astype(jnp.bfloat16), values, preferred_element_type=jnp.float32
    )
    mixed_low = mixed.reshape(seq_len, head_cols).astype(jnp.bfloat16)

    def add_up(partial):
        return lax.psum_scatter(
            partial.astype(jnp.bfloat16), "dp", scatter_dimension=0, tiled=True
        ).astype(jnp.float32)

    inputs = own_tokens.astype(jnp.float32)
    hidden = inputs + add_up(product(mixed_low, w_out))
    normed_two, inverse_two = norm_parts(hidden)
    ffn_in_own = (normed_two * gain_two + bias_two).astype(jnp.bfloat16)
    ffn_in = lax.all_gather(ffn_in_own, "dp", axis=0, tiled=True)
    preact = product(ffn_in, w_up) + b_up
    gated = gelu_value(preact).astype(jnp.bfloat16)

    blocks, width = piece_blocks(ranks)
    pieces = len(blocks[0])
    terms = jnp.stack(
        [
            product(gated[:, i * width : (i + 1) * width], w_down[i * width : (i + 1) * width])
            .astype(jnp.bfloat16)
            .reshape(ranks, tok_rows, model_width)
            for i in range(pieces)
        ],
        axis=1,
    )
    terms = lax.all_to_all(terms, "dp", split_axis=0, concat_axis=0)
    total = hidden + b_down
    result_list = []
    for level_idx in range(GRAN):
        for source in range(ranks):
            for i in range(pieces):
                if blocks[source][i] == level_idx:
                    total = total + terms[source, i].astype(jnp.float32)
        result_list.append(total.astype(jnp.bfloat16))
    activations = jnp.stack(result_list).reshape(GRAN, 1, tok_rows, model_width)

    grads_out = cotangent.reshape(GRAN, tok_rows, model_width).astype(jnp.float32)
    suffix = [grads_out[GRAN - 1]]
    for level_idx in range(GRAN - 2, -1, -1):
        suffix.insert(0, suffix[0] + grads_out[level_idx])
    grad_hidden = suffix[0]
    suffix = [s.astype(jnp.bfloat16) for s in suffix]
    outgoing = jnp.stack([jnp.stack([suffix[b] for b in blocks[j]]) for j in range(ranks)])
    incoming = lax.all_to_all(outgoing, "dp", split_axis=0, concat_axis=0)
    incoming = incoming.transpose(1, 0, 2, 3).reshape(pieces, seq_len, model_width)

    grad_gated = jnp.concatenate(
        [back_product(incoming[i], w_down[i * width : (i + 1) * width]) for i in range(pieces)],
        axis=1,
    )
    grad_pre_wide = grad_gated * gelu_grad(preact)
    grad_pre = grad_pre_wide.astype(jnp.bfloat16)
    grad_up_bias = jnp.sum(grad_pre_wide, axis=0)
    grad_ffn_in = add_up(back_product(grad_pre, w_up))

    def collect(grad):
        return lax.psum_scatter(
            grad.astype(jnp.bfloat16), "fsdp", scatter_dimension=0, tiled=True
        )

    def collect_columns(grad):
        columns = grad.shape[1]
        grad = grad.astype(jnp.bfloat16).reshape(ranks, shards, own, columns)
        grad = grad.transpose(1, 0, 2, 3).reshape(model_width, columns)
        grad = lax.psum_scatter(grad, "fsdp", scatter_dimension=0, tiled=True)
        grad = grad.reshape(ranks, own, columns)
        grad = lax.all_to_all(grad, "dp", split_axis=0, concat_axis=0)
        return grad.astype(jnp.float32)

    sum_down = collect(
        jnp.concatenate(
            [gram_product(gated[:, i * width : (i + 1) * width], incoming[i]) for i in range(pieces)],
            axis=0,
        )
    ).astype(jnp.float32)
    sum_up = collect_columns(gram_product(ffn_in, grad_pre))
    sum_up = sum_up.transpose(1, 0, 2).reshape(own, FF)

    grad_down_bias = jnp.sum(grad_hidden, axis=0)
    grad_gain_two = jnp.sum(grad_ffn_in * normed_two, axis=0)
    grad_bias_two = jnp.sum(grad_ffn_in, axis=0)
    grad_hidden = grad_hidden + norm_backward(grad_ffn_in, normed_two, inverse_two, gain_two)
    grad_branch = lax.all_gather(grad_hidden.astype(jnp.bfloat16), "dp", axis=0, tiled=True)
    sum_out = collect(gram_product(mixed_low, grad_branch)).astype(jnp.float32)
    grad_mixed = (
        back_product(grad_branch, w_out).astype(jnp.bfloat16).reshape(seq_len, heads, HEAD_DIM)
    )
    row_delta = jnp.einsum("qhd,qhd->hq", grad_mixed.astype(jnp.float32), mixed)
    probs, unused = weigh(log_total)
    grad_probs = jnp.einsum("qhd,khd->hqk", grad_mixed, values, preferred_element_type=jnp.float32)
    grad_scores = (probs * (grad_probs - row_delta[..., None])).astype(jnp.bfloat16)
    grad_q_rot = jnp.einsum(
        "hqk,khd->qhd", grad_scores, k_rot, preferred_element_type=jnp.float32
    )
    grad_k_rot = jnp.einsum(
        "hqk,qhd->khd", grad_scores, q_rot, preferred_element_type=jnp.float32
    )
    grad_values = jnp.einsum(
        "hqk,qhd->khd", probs.astype(jnp.bfloat16), grad_mixed, preferred_element_type=jnp.float32
    )
    grad_qkv = jnp.concatenate(
        [
            rotate(grad_q_rot * scaling, cosine, -sine).reshape(seq_len, head_cols),
            rotate(grad_k_rot, cosine, -sine).reshape(seq_len, head_cols),
            grad_values.reshape(seq_len, head_cols),
        ],
        axis=1,
    ).astype(jnp.bfloat16)
    sum_qkv = collect_columns(gram_product(attn_in, grad_qkv)).transpose(1, 0, 2)
    sum_query, sum_key, sum_value = (
        sum_qkv[:, :, i * head_cols : (i + 1) * head_cols].reshape(own, model_width)
        for i in range(3)
    )
    grad_attn_in = add_up(back_product(grad_qkv, w_qkv))
    normed_one, inverse_one = norm_parts(inputs)
    grad_gain_one = jnp.sum(grad_attn_in * normed_one, axis=0)
    grad_bias_one = jnp.sum(grad_attn_in, axis=0)
    grad_inputs = grad_hidden + norm_backward(grad_attn_in, normed_one, inverse_one, gain_one)

    sums = jnp.stack([grad_gain_one, grad_bias_one, grad_gain_two, grad_bias_two, grad_down_bias])
    sums = lax.psum_scatter(
        sums.reshape(5, ranks * shards, own).transpose(1, 0, 2).reshape(ranks * shards, 5 * own),
        ("dp", "fsdp"),
        scatter_dimension=0,
        tiled=True,
    ).reshape(5, own)
    sum_up_bias = lax.psum_scatter(grad_up_bias, "fsdp", scatter_dimension=0, tiled=True)
    return (
        activations,
        grad_inputs.astype(jnp.bfloat16).reshape(1, tok_rows, model_width),
        sums[0],
        sums[1],
        sum_query,
        sum_key,
        sum_value,
        sum_out,
        sums[2],
        sums[3],
        sum_up,
        sum_up_bias,
        sum_down,
        sums[4],
    )


def solution(mesh):
    placed = (
        P("fsdp", "dp", None),
        P(None, "fsdp", "dp", None),
        P(("dp", "fsdp")),
        P(("dp", "fsdp")),
        P(("dp", "fsdp"), None),
        P(("dp", "fsdp"), None),
        P(("dp", "fsdp"), None),
        P(("dp", "fsdp"), None),
        P(("dp", "fsdp")),
        P(("dp", "fsdp")),
        P(("dp", "fsdp"), None),
        P(("dp", "fsdp")),
        P(("dp", "fsdp"), None),
        P(("dp", "fsdp")),
    )
    ranks, shards = mesh.shape["dp"], mesh.shape["fsdp"]
    local = local_gathered
    if HEADS % ranks == 0:
        local = functools.partial(local_split, ranks, shards)
    return jax.shard_map(
        local,
        mesh=mesh,
        in_specs=placed,
        out_specs=(
            P(None, "fsdp", "dp", None),
            P("fsdp", "dp", None),
            P(("dp", "fsdp")),
            P(("dp", "fsdp")),
            P(("dp", "fsdp"), None),
            P(("dp", "fsdp"), None),
            P(("dp", "fsdp"), None),
            P(("dp", "fsdp"), None),
            P(("dp", "fsdp")),
            P(("dp", "fsdp")),
            P(("dp", "fsdp"), None),
            P(("dp", "fsdp")),
            P(("dp", "fsdp"), None),
            P(("dp", "fsdp")),
        ),
        check_vma=False,
    )
```

```python
import functools
import math

import jax
import jax.numpy as jnp
from jax import lax
from jax.experimental import pallas as pl
from jax.experimental.pallas import tpu as pltpu
from jax.sharding import PartitionSpec as P

HEADS = 12
HEAD_DIM = 128
FF = 6144
GRAN = 4


epsilon = 1e-05
masked_score = -1e30


def product(left, right):
    return jnp.dot(left, right, preferred_element_type=jnp.float32)


def gram_product(left, right):
    return lax.dot_general(
        left, right, (((0,), (0,)), ((), ())), preferred_element_type=jnp.float32
    )


def back_product(left, right):
    return lax.dot_general(
        left, right, (((1,), (1,)), ((), ())), preferred_element_type=jnp.float32
    )


def norm_parts(values):
    centred = values - jnp.mean(values, axis=-1, keepdims=True)
    inverse = lax.rsqrt(jnp.mean(centred * centred, axis=-1, keepdims=True) + epsilon)
    return (centred * inverse, inverse)


def norm_backward(grad_normed, normed, inverse, gain):
    scaled = grad_normed * gain
    return inverse * (
        scaled
        - jnp.mean(scaled, axis=-1, keepdims=True)
        - normed * jnp.mean(scaled * normed, axis=-1, keepdims=True)
    )


def gelu_value(values):
    return (
        0.5
        * values
        * (1.0 + jnp.tanh(0.7978845608028654 * (values + 0.044715 * values * values * values)))
    )


def gelu_grad(values):
    tangent = jnp.tanh(0.7978845608028654 * (values + 0.044715 * values * values * values))
    return 0.5 * (1.0 + tangent) + 0.5 * values * (1.0 - tangent * tangent) * 0.7978845608028654 * (
        1.0 + 3.0 * 0.044715 * values * values
    )


def rotary_tables(positions, half_size):
    ladder = jnp.arange(half_size).astype(jnp.float32)
    inverse = jnp.exp(ladder * (-math.log(10000.0) / half_size))
    angles = positions[:, None] * inverse[None, :]
    return (jnp.cos(angles)[:, None, :], jnp.sin(angles)[:, None, :])


def rotate(values, cosine, sine):
    half_size = values.shape[-1] // 2
    first = values[..., :half_size]
    second = values[..., half_size:]
    return jnp.concatenate(
        [first * cosine - second * sine, second * cosine + first * sine], axis=-1
    )


def block_scores(queries, positions, key_block, start_row):
    block_rows = key_block.shape[0]
    scores = jnp.einsum("qhd,khd->hqk", queries, key_block, preferred_element_type=jnp.float32)
    key_positions = start_row + jnp.arange(block_rows, dtype=jnp.int32)
    visible = positions[None, :, None] >= key_positions[None, None, :]
    return (jnp.where(visible, scores, masked_score), visible)


def key_blocking(keys_all, values_all, key_offset):
    seq_len = keys_all.shape[0]
    block_rows = min(512, seq_len)
    block_count = seq_len // block_rows
    key_blocks = keys_all.reshape(block_count, block_rows, HEADS, HEAD_DIM)
    value_blocks = values_all.reshape(block_count, block_rows, HEADS, HEAD_DIM)
    starts = key_offset + jnp.arange(block_count, dtype=jnp.int32) * block_rows
    return (key_blocks, value_blocks, starts)


def attend(queries, keys_all, values_all, positions):
    tok_rows = queries.shape[0]
    key_blocks, value_blocks, starts = key_blocking(keys_all, values_all, jnp.int32(0))

    def measure(state_pair, block_pair):
        top_score, total = state_pair
        key_block, start_row = block_pair
        scores, visible = block_scores(queries, positions, key_block, start_row)
        new_top = jnp.maximum(top_score, jnp.max(scores, axis=-1))
        raised = jnp.where(visible, jnp.exp(scores - new_top[..., None]), 0.0)
        total = total * jnp.exp(top_score - new_top) + jnp.sum(raised, axis=-1)
        return ((new_top, total), None)

    initial = (
        jnp.full((HEADS, tok_rows), masked_score, jnp.float32),
        jnp.zeros((HEADS, tok_rows), jnp.float32),
    )
    (top_score, total), unused = lax.scan(measure, initial, (key_blocks, starts))
    log_total = top_score + jnp.log(total)

    def accumulate(mixed, block_triple):
        key_block, value_block, start_row = block_triple
        scores, visible = block_scores(queries, positions, key_block, start_row)
        probs = jnp.where(visible, jnp.exp(scores - log_total[..., None]), 0.0).astype(jnp.bfloat16)
        return (
            mixed
            + jnp.einsum("hqk,khd->qhd", probs, value_block, preferred_element_type=jnp.float32),
            None,
        )

    mixed, unused = lax.scan(
        accumulate,
        jnp.zeros((tok_rows, HEADS, HEAD_DIM), jnp.float32),
        (key_blocks, value_blocks, starts),
    )
    return (mixed, log_total)


def attend_back(
    queries, positions, keys_all, values_all, key_offset, grad_mixed, log_total, row_delta
):
    tok_rows = queries.shape[0]
    key_blocks, value_blocks, starts = key_blocking(keys_all, values_all, key_offset)

    def backward_block(grad_queries, block_triple):
        key_block, value_block, start_row = block_triple
        scores, visible = block_scores(queries, positions, key_block, start_row)
        probs = jnp.where(visible, jnp.exp(scores - log_total[..., None]), 0.0)
        grad_probs = jnp.einsum(
            "qhd,khd->hqk", grad_mixed, value_block, preferred_element_type=jnp.float32
        )
        grad_scores = (probs * (grad_probs - row_delta[..., None])).astype(jnp.bfloat16)
        grad_queries = grad_queries + jnp.einsum(
            "hqk,khd->qhd", grad_scores, key_block, preferred_element_type=jnp.float32
        )
        grad_key_block = jnp.einsum(
            "hqk,qhd->khd", grad_scores, queries, preferred_element_type=jnp.float32
        )
        grad_value_block = jnp.einsum(
            "hqk,qhd->khd",
            probs.astype(jnp.bfloat16),
            grad_mixed,
            preferred_element_type=jnp.float32,
        )
        return (grad_queries, (grad_key_block, grad_value_block))

    grad_queries, (grad_keys, grad_values) = lax.scan(
        backward_block,
        jnp.zeros((tok_rows, HEADS, HEAD_DIM), jnp.float32),
        (key_blocks, value_blocks, starts),
    )
    key_len = keys_all.shape[0]
    return (
        grad_queries,
        grad_keys.reshape(key_len, HEADS * HEAD_DIM),
        grad_values.reshape(key_len, HEADS * HEAD_DIM),
    )


def local_gathered(
    tokens,
    cotangent,
    norm1_gain,
    norm1_bias,
    query_weight,
    key_weight,
    value_weight,
    out_weight,
    norm2_gain,
    norm2_bias,
    up_weight,
    up_bias,
    down_weight,
    down_bias,
):
    (
        gain_one,
        bias_one,
        w_query,
        w_key,
        w_value,
        w_out,
        gain_two,
        bias_two,
        w_up,
        b_up,
        w_down,
        b_down,
    ) = (
        lax.all_gather(norm1_gain, ("dp", "fsdp"), axis=0, tiled=True),
        lax.all_gather(norm1_bias, ("dp", "fsdp"), axis=0, tiled=True),
        lax.all_gather(query_weight, ("dp", "fsdp"), axis=0, tiled=True),
        lax.all_gather(key_weight, ("dp", "fsdp"), axis=0, tiled=True),
        lax.all_gather(value_weight, ("dp", "fsdp"), axis=0, tiled=True),
        lax.all_gather(out_weight, ("dp", "fsdp"), axis=0, tiled=True),
        lax.all_gather(norm2_gain, ("dp", "fsdp"), axis=0, tiled=True),
        lax.all_gather(norm2_bias, ("dp", "fsdp"), axis=0, tiled=True),
        lax.all_gather(up_weight, ("dp", "fsdp"), axis=0, tiled=True),
        lax.all_gather(up_bias, ("dp", "fsdp"), axis=0, tiled=True),
        lax.all_gather(down_weight, ("dp", "fsdp"), axis=0, tiled=True),
        lax.all_gather(down_bias, ("dp", "fsdp"), axis=0, tiled=True),
    )
    seq_count = tokens.shape[0]
    tok_rows = tokens.shape[1]
    model_width = tokens.shape[2]
    all_rows = seq_count * tok_rows
    scaling = HEAD_DIM ** (-0.5)
    inputs = tokens.reshape(all_rows, model_width).astype(jnp.float32)
    normed_one, inverse_one = norm_parts(inputs)
    attn_in = (normed_one * gain_one.astype(jnp.float32) + bias_one.astype(jnp.float32)).astype(
        jnp.bfloat16
    )
    queries = product(attn_in, w_query).reshape(seq_count, tok_rows, HEADS, HEAD_DIM)
    key_raw = product(attn_in, w_key).reshape(seq_count, tok_rows, HEADS, HEAD_DIM)
    value_low = (
        product(attn_in, w_value).astype(jnp.bfloat16).reshape(seq_count, tok_rows, model_width)
    )
    key_offset = lax.axis_index("dp") * tok_rows
    positions = key_offset + jnp.arange(tok_rows, dtype=jnp.int32)
    cosine, sine = rotary_tables(positions.astype(jnp.float32), HEAD_DIM // 2)
    q_rot = (rotate(queries, cosine, sine) * scaling).astype(jnp.bfloat16)
    k_flat = (
        rotate(key_raw, cosine, sine).astype(jnp.bfloat16).reshape(seq_count, tok_rows, model_width)
    )
    keys_all, values_all = (
        lax.all_gather(k_flat, "dp", axis=1, tiled=True),
        lax.all_gather(value_low, "dp", axis=1, tiled=True),
    )
    seq_len = keys_all.shape[1]
    mixed, log_total = jax.vmap(attend, in_axes=(0, 0, 0, None))(
        q_rot,
        keys_all.reshape(seq_count, seq_len, HEADS, HEAD_DIM),
        values_all.reshape(seq_count, seq_len, HEADS, HEAD_DIM),
        positions,
    )
    mixed_low = mixed.reshape(all_rows, model_width).astype(jnp.bfloat16)
    hidden = inputs + product(mixed_low, w_out)
    normed_two, inverse_two = norm_parts(hidden)
    ffn_in = (normed_two * gain_two.astype(jnp.float32) + bias_two.astype(jnp.float32)).astype(
        jnp.bfloat16
    )
    preact = product(ffn_in, w_up) + b_up.astype(jnp.float32)
    edges = [0] + [FF // 2 ** (GRAN - 1 - level_idx) for level_idx in range(GRAN)]
    gated_list = []
    result_list = []
    for level_idx in range(GRAN):
        level_width = edges[level_idx + 1]
        gated = gelu_value(preact[:, :level_width]).astype(jnp.bfloat16)
        gated_list.append(gated)
        result = hidden + product(gated, w_down[:level_width]) + b_down.astype(jnp.float32)
        result_list.append(result.astype(jnp.bfloat16))
    activations = jnp.stack(result_list).reshape(GRAN, seq_count, tok_rows, model_width)
    back_gain_one, back_query, back_key, back_value, back_out, back_gain_two, back_up, back_down = (
        lax.all_gather(norm1_gain, ("dp", "fsdp"), axis=0, tiled=True),
        lax.all_gather(query_weight, ("dp", "fsdp"), axis=0, tiled=True),
        lax.all_gather(key_weight, ("dp", "fsdp"), axis=0, tiled=True),
        lax.all_gather(value_weight, ("dp", "fsdp"), axis=0, tiled=True),
        lax.all_gather(out_weight, ("dp", "fsdp"), axis=0, tiled=True),
        lax.all_gather(norm2_gain, ("dp", "fsdp"), axis=0, tiled=True),
        lax.all_gather(up_weight, ("dp", "fsdp"), axis=0, tiled=True),
        lax.all_gather(down_weight, ("dp", "fsdp"), axis=0, tiled=True),
    )
    grads_out = cotangent.reshape(GRAN, all_rows, model_width)
    grad_hidden = jnp.sum(grads_out.astype(jnp.float32), axis=0)
    grad_down_bias = jnp.sum(grad_hidden, axis=0)
    grad_ffn_in = jnp.zeros((all_rows, model_width), jnp.float32)
    pre_grads = []
    for level_idx in range(GRAN):
        level_width = edges[level_idx + 1]
        grad_gated = back_product(grads_out[level_idx], back_down[:level_width])
        grad_pre = (grad_gated * gelu_grad(preact[:, :level_width])).astype(jnp.bfloat16)
        pre_grads.append(grad_pre)
        grad_ffn_in = grad_ffn_in + back_product(grad_pre, back_up[:, :level_width])
    up_blocks = []
    bias_blocks = []
    down_blocks = []
    for block_idx in range(GRAN):
        start_col = edges[block_idx]
        stop_col = edges[block_idx + 1]
        stacked_grad = jnp.concatenate(
            [pre_grads[level_idx][:, start_col:stop_col] for level_idx in range(block_idx, GRAN)],
            axis=0,
        )
        stacked_in = jnp.concatenate([ffn_in] * (GRAN - block_idx), axis=0)
        up_blocks.append(gram_product(stacked_in, stacked_grad))
        bias_blocks.append(jnp.sum(stacked_grad.astype(jnp.float32), axis=0))
        stacked_gated = jnp.concatenate(
            [gated_list[level_idx][:, start_col:stop_col] for level_idx in range(block_idx, GRAN)],
            axis=0,
        )
        stacked_out = jnp.concatenate(
            [grads_out[level_idx] for level_idx in range(block_idx, GRAN)], axis=0
        )
        down_blocks.append(gram_product(stacked_gated, stacked_out))
    grad_up_weight = jnp.concatenate(up_blocks, axis=1)
    grad_up_bias = jnp.concatenate(bias_blocks, axis=0)
    grad_down_weight = jnp.concatenate(down_blocks, axis=0)
    grad_gain_two = jnp.sum(grad_ffn_in * normed_two, axis=0)
    grad_bias_two = jnp.sum(grad_ffn_in, axis=0)
    grad_hidden = grad_hidden + norm_backward(
        grad_ffn_in, normed_two, inverse_two, back_gain_two.astype(jnp.float32)
    )
    grad_branch = grad_hidden.astype(jnp.bfloat16)
    grad_out_weight = gram_product(mixed_low, grad_branch)
    grad_mixed = (
        back_product(grad_branch, back_out)
        .astype(jnp.bfloat16)
        .reshape(seq_count, tok_rows, HEADS, HEAD_DIM)
    )
    row_delta = jnp.einsum("sqhd,sqhd->shq", grad_mixed.astype(jnp.float32), mixed)
    keys_again, values_again = (
        lax.all_gather(k_flat, "dp", axis=1, tiled=True),
        lax.all_gather(value_low, "dp", axis=1, tiled=True),
    )
    back_all = jax.vmap(attend_back, in_axes=(0, None, 0, 0, None, 0, 0, 0))
    grad_q_rot, grad_keys_all, grad_values_all = back_all(
        q_rot,
        positions,
        keys_again.reshape(seq_count, seq_len, HEADS, HEAD_DIM),
        values_again.reshape(seq_count, seq_len, HEADS, HEAD_DIM),
        jnp.int32(0),
        grad_mixed,
        log_total,
        row_delta,
    )
    every_query, every_grad = (
        lax.all_gather(q_rot, "dp", axis=1, tiled=True),
        lax.all_gather(grad_mixed, "dp", axis=1, tiled=True),
    )
    every_total, every_delta = (
        lax.all_gather(jnp.transpose(log_total, (0, 2, 1)), "dp", axis=1, tiled=True),
        lax.all_gather(jnp.transpose(row_delta, (0, 2, 1)), "dp", axis=1, tiled=True),
    )
    every_position = jnp.arange(seq_len, dtype=jnp.int32)
    unused_rows, grad_key_mine, grad_value_mine = back_all(
        every_query,
        every_position,
        k_flat.reshape(seq_count, tok_rows, HEADS, HEAD_DIM),
        value_low.reshape(seq_count, tok_rows, HEADS, HEAD_DIM),
        key_offset,
        every_grad,
        jnp.transpose(every_total, (0, 2, 1)),
        jnp.transpose(every_delta, (0, 2, 1)),
    )
    grad_query = (
        rotate(grad_q_rot * scaling, cosine, -sine)
        .reshape(all_rows, model_width)
        .astype(jnp.bfloat16)
    )
    grad_key = (
        rotate(grad_key_mine.reshape(seq_count, tok_rows, HEADS, HEAD_DIM), cosine, -sine)
        .reshape(all_rows, model_width)
        .astype(jnp.bfloat16)
    )
    grad_val = grad_value_mine.reshape(all_rows, model_width).astype(jnp.bfloat16)
    grad_query_weight = gram_product(attn_in, grad_query)
    grad_key_weight = gram_product(attn_in, grad_key)
    grad_value_weight = gram_product(attn_in, grad_val)
    grad_attn_in = (
        back_product(grad_query, back_query)
        + back_product(grad_key, back_key)
        + back_product(grad_val, back_value)
    )
    grad_gain_one = jnp.sum(grad_attn_in * normed_one, axis=0)
    grad_bias_one = jnp.sum(grad_attn_in, axis=0)
    grad_inputs = grad_hidden + norm_backward(
        grad_attn_in, normed_one, inverse_one, back_gain_one.astype(jnp.float32)
    )
    (
        sum_gain_one,
        sum_bias_one,
        sum_query,
        sum_key,
        sum_value,
        sum_out,
        sum_gain_two,
        sum_bias_two,
        sum_up,
        sum_up_bias,
        sum_down,
        sum_down_bias,
    ) = (
        lax.psum_scatter(grad_gain_one, ("dp", "fsdp"), scatter_dimension=0, tiled=True),
        lax.psum_scatter(grad_bias_one, ("dp", "fsdp"), scatter_dimension=0, tiled=True),
        lax.psum_scatter(grad_query_weight, ("dp", "fsdp"), scatter_dimension=0, tiled=True),
        lax.psum_scatter(grad_key_weight, ("dp", "fsdp"), scatter_dimension=0, tiled=True),
        lax.psum_scatter(grad_value_weight, ("dp", "fsdp"), scatter_dimension=0, tiled=True),
        lax.psum_scatter(grad_out_weight, ("dp", "fsdp"), scatter_dimension=0, tiled=True),
        lax.psum_scatter(grad_gain_two, ("dp", "fsdp"), scatter_dimension=0, tiled=True),
        lax.psum_scatter(grad_bias_two, ("dp", "fsdp"), scatter_dimension=0, tiled=True),
        lax.psum_scatter(grad_up_weight, ("dp", "fsdp"), scatter_dimension=0, tiled=True),
        lax.psum_scatter(grad_up_bias, ("dp", "fsdp"), scatter_dimension=0, tiled=True),
        lax.psum_scatter(grad_down_weight, ("dp", "fsdp"), scatter_dimension=0, tiled=True),
        lax.psum_scatter(grad_down_bias, ("dp", "fsdp"), scatter_dimension=0, tiled=True),
    )
    return (
        activations,
        grad_inputs.astype(jnp.bfloat16).reshape(seq_count, tok_rows, model_width),
        sum_gain_one,
        sum_bias_one,
        sum_query,
        sum_key,
        sum_value,
        sum_out,
        sum_gain_two,
        sum_bias_two,
        sum_up,
        sum_up_bias,
        sum_down,
        sum_down_bias,
    )


MESH = pl.DeviceIdType.MESH


class Place:
    def __init__(self, chips):
        self.chips = chips
        self.rank = lax.axis_index("dp")
        self.shard = lax.axis_index("fsdp")
        self.z = lax.div(self.shard, 2)
        self.core = lax.rem(self.shard, 2)
        along_x = self.rank + 1 - 2 * lax.rem(self.rank, 2)
        along_y = self.rank + 2 - 4 * lax.div(self.rank, 2)
        self.first = jnp.where(self.core == 0, along_x, along_y)
        self.second = jnp.where(self.core == 0, along_y, along_x)
        self.across = 3 - self.rank
        self.sibling = self.shard + 1 - 2 * self.core

    def at(self, rank=None, shard=None):
        return (self.rank if rank is None else rank, self.shard if shard is None else shard)

    def greet(self, plane=True, sibling=False, chain=False, ring=False):
        barrier = pltpu.get_barrier_semaphore()
        count = 0
        targets = []
        if plane:
            targets += [self.at(rank=r) for r in (self.first, self.second, self.across)]
        if sibling:
            targets.append(self.at(shard=self.sibling))
        if ring:
            targets += [self.at(shard=self.hop(k)) for k in range(1, self.chips)]
        for target in targets:
            pl.semaphore_signal(barrier, inc=1, device_id=target, device_id_type=MESH)
            count += 1
        if chain:
            for step, there in ((2, self.z < self.chips - 1), (-2, self.z > 0)):

                @pl.when(there)
                def greet_neighbour(step=step):
                    pl.semaphore_signal(
                        barrier,
                        inc=1,
                        device_id=self.at(shard=self.shard + step),
                        device_id_type=MESH,
                    )

                count = count + there.astype(jnp.int32)
        pl.semaphore_wait(barrier, count)

    def hop(self, k):
        return 2 * lax.rem(self.z + k, self.chips) + self.core


def under(condition, action):
    if condition is None:
        action()
    else:
        pl.when(condition)(action)


class Message:
    def __init__(self, links, src, dst, target, sent=None, comes=None):
        index = links.take()
        self.copy = pltpu.make_async_remote_copy(
            src_ref=src,
            dst_ref=dst,
            send_sem=links.send.at[index],
            recv_sem=links.recv.at[index],
            device_id=target,
            device_id_type=MESH,
        )
        self.sent, self.comes = sent, comes
        links.open.append(self)
        under(sent, self.copy.start)

    def arrive(self):
        under(self.comes, self.copy.wait_recv)

    def leave(self):
        under(self.sent, self.copy.wait_send)


class Near:
    def __init__(self, links, src, dst, where):
        self.copy = pltpu.make_async_copy(src, dst, links.near.at[links.used_near])
        links.used_near += 1
        self.where = where
        self.waits = True
        under(where, self.copy.start)

    def arrive(self):
        if self.waits:
            under(self.where, self.copy.wait)
        self.waits = False


class Links:
    def __init__(self, send, recv, near):
        self.send, self.recv, self.near = send, recv, near
        self.used = 0
        self.used_near = 0
        self.open = []
        self.open_near = []

    def take(self):
        self.used += 1
        return self.used - 1

    def keep(self, src, dst, where=None):
        copy = Near(self, src, dst, where)
        self.open_near.append(copy)
        return copy

    def drain(self):
        for copy in self.open_near:
            copy.arrive()
        for message in self.open:
            message.leave()


LINK_SCRATCH = [
    pltpu.SemaphoreType.DMA((128,)),
    pltpu.SemaphoreType.DMA((128,)),
    pltpu.SemaphoreType.DMA((32,)),
]


class PlaneGather:
    def __init__(self, place, links, src, dst, parts):
        self.place, self.links, self.dst = place, links, dst
        rows = src.shape[0] // parts
        self.cuts = [pl.ds(k * rows, rows) for k in range(parts)]
        links.keep(src, dst.at[place.rank])
        self.first, self.second = [], []
        for cut in self.cuts:
            for side, target in ((self.first, place.first), (self.second, place.second)):
                block = dst.at[place.rank, cut]
                side.append(Message(links, src.at[cut], block, place.at(rank=target)))
        self.passed = []

    def relay(self, k):
        self.first[k].arrive()
        block = self.dst.at[self.place.first, self.cuts[k]]
        target = self.place.at(rank=self.place.second)
        self.passed.append(Message(self.links, block, block, target))

    def finish(self):
        for message in self.second + self.passed:
            message.arrive()


class PlaneScatter:
    def __init__(self, place, links, partial, landing, turn):
        self.place, self.links, self.partial, self.landing, self.turn = (
            place,
            links,
            partial,
            landing,
            turn,
        )
        target = place.at(rank=place.first)
        self.far = Message(links, partial.at[place.across], landing.at[0], target)
        self.near = Message(links, partial.at[place.first], landing.at[1], target)

    def relay(self):
        self.far.arrive()
        mine = self.partial[self.place.second].astype(jnp.float32)
        self.turn[...] = (mine + self.landing[0].astype(jnp.float32)).astype(jnp.bfloat16)
        self.last = Message(
            self.links, self.turn, self.landing.at[2], self.place.at(rank=self.place.second)
        )

    def total(self):
        self.near.arrive()
        self.last.arrive()
        total = self.partial[self.place.rank].astype(jnp.float32)
        return total + self.landing[1].astype(jnp.float32) + self.landing[2].astype(jnp.float32)


class Chain:
    def __init__(self, place, links, src, slot):
        self.place, self.links, self.slot = place, links, slot
        z, last = place.z, place.chips - 1
        own = slot(place.shard)
        self.up = Message(links, src, own, place.at(shard=place.shard + 2), z < last, z > 0)
        self.down = Message(links, src, own, place.at(shard=place.shard - 2), z > 0, z < last)
        self.beside = [Message(links, src, own, place.at(shard=place.sibling))]

    def step(self, s):
        place, links = self.place, self.links
        z, last = place.z, place.chips - 1
        below = self.slot(jnp.maximum(place.shard - 2 * s, place.core))
        above = self.slot(jnp.minimum(place.shard + 2 * s, 2 * last + place.core))
        self.up.arrive()
        has_below, has_above = z >= s, z <= last - s
        up = down = None
        if s < last:
            target = place.at(shard=place.shard + 2)
            up = Message(links, below, below, target, has_below & (z < last), z >= s + 1)
        self.beside.append(
            Message(links, below, below, place.at(shard=place.sibling), has_below, has_below)
        )
        self.down.arrive()
        if s < last:
            target = place.at(shard=place.shard - 2)
            down = Message(links, above, above, target, has_above & (z > 0), z <= last - s - 1)
        self.beside.append(
            Message(links, above, above, place.at(shard=place.sibling), has_above, has_above)
        )
        self.up, self.down = up, down

    def finish(self):
        for message in self.beside:
            message.arrive()


class Collect:
    def __init__(self, place, links, part, own, other, landing):
        self.place, self.links = place, links
        self.own, self.other, self.landing = own, other, landing
        self.beside = Message(
            links, part.at[:, :, 1 - place.core], other, place.at(shard=place.sibling)
        )
        self.mine = links.keep(part.at[:, :, place.core], own)

    def send(self):
        self.mine.arrive()
        self.beside.arrive()

        def add(k, carry):
            total = self.own[:, k].astype(jnp.float32) + self.other[:, k].astype(jnp.float32)
            self.own[:, k] = total.astype(self.own.dtype)
            return carry

        place = self.place
        lax.fori_loop(0, place.chips, add, 0)
        self.along = []
        for k in range(1, place.chips):
            there = lax.rem(place.z + k, place.chips)
            self.along.append(
                Message(
                    self.links,
                    self.own.at[:, there],
                    self.landing.at[k - 1],
                    place.at(shard=place.hop(k)),
                )
            )

    def total(self):
        total = self.own[:, self.place.z].astype(jnp.float32)
        for k, message in enumerate(self.along):
            message.arrive()
            total = total + self.landing[k].astype(jnp.float32)
        return total


def collect_scratch(lead, chips, rows, columns, dtype):
    return [
        pltpu.VMEM((lead, chips, rows, columns), dtype),
        pltpu.VMEM((lead, chips, rows, columns), dtype),
        pltpu.VMEM((chips - 1, lead, rows, columns), dtype),
    ]


class Deal:
    def __init__(self, place, links, pairs):
        self.messages = []
        for part, dst in pairs:
            self.messages.append(links.keep(part(place.rank), dst))
            for rank in (place.first, place.second, place.across):
                self.messages.append(Message(links, part(rank), dst, place.at(rank=rank)))

    def arrive(self):
        for message in self.messages:
            message.arrive()


def gather_kernel(
    chips,
    tokens,
    suffix,
    small,
    w_query,
    w_key,
    w_value,
    w_out,
    w_up,
    w_down,
    all_tokens,
    incoming,
    all_small,
    all_qkv,
    all_out,
    all_up,
    all_down,
    send,
    recv,
    near,
):
    place = Place(chips)
    links = Links(send, recv, near)
    place.greet(plane=True, sibling=True, chain=True)
    rank, shard = place.rank, place.shard

    def columns(weight, width):
        return lambda r: weight.at[:, pl.ds(pl.multiple_of(r * width, 128), width)]

    head_cols = w_query.shape[1] // 4
    own_qkv = all_qkv.at[rank, shard]
    pairs = [(lambda r: small, all_small.at[rank, shard])]
    for i, weight in enumerate((w_query, w_key, w_value)):
        own = own_qkv.at[:, pl.ds(i * head_cols, head_cols)]
        pairs.append((columns(weight, head_cols), own))
    deal_qkv = Deal(place, links, pairs)
    gather = PlaneGather(place, links, tokens, all_tokens, 2)
    deal_up = Deal(place, links, [(columns(w_up, w_up.shape[1] // 4), all_up.at[rank, shard])])

    links.keep(w_out, all_out.at[shard])
    links.keep(w_down, all_down.at[shard])
    chain_out = Chain(place, links, w_out, lambda f: all_out.at[f])
    deal_qkv.arrive()
    small_slot = lambda f: all_small.at[:, f]
    qkv_slot = lambda f: all_qkv.at[:, f]
    up_slot = lambda f: all_up.at[:, f]
    chain_small = Chain(place, links, small_slot(shard), small_slot)
    chain_qkv = Chain(place, links, qkv_slot(shard), qkv_slot)
    gather.relay(0)
    gather.relay(1)
    deal_up.arrive()
    chain_up = Chain(place, links, up_slot(shard), up_slot)
    chain_down = Chain(place, links, w_down, lambda f: all_down.at[f])

    links.keep(suffix.at[block_of(rank)], incoming.at[0, rank])
    links.keep(suffix.at[1], incoming.at[1, rank], rank == 0)
    dealt = []
    for r in (place.first, place.second, place.across):
        dealt.append(
            Message(links, suffix.at[block_of(r)], incoming.at[0, rank], place.at(rank=r))
        )
        dealt.append(
            Message(links, suffix.at[1], incoming.at[1, rank], place.at(rank=r), r == 0, rank == 0)
        )
    for chain in (chain_out, chain_small, chain_qkv, chain_up, chain_down):
        for s in range(1, chips):
            chain.step(s)
        chain.finish()
    gather.finish()
    for message in dealt:
        message.arrive()
    links.drain()


def block_of(r):
    return jnp.where(r == 0, 0, jnp.minimum(r + 1, GRAN - 1))


def scatter_kernel(chips, partial, total, landing, turn, send, recv, near):
    place = Place(chips)
    links = Links(send, recv, near)
    place.greet(plane=True)
    scatter = PlaneScatter(place, links, partial, landing, turn)
    scatter.relay()
    total[...] = scatter.total()
    links.drain()


def spread_kernel(chips, block, blocks, send, recv, near):
    place = Place(chips)
    links = Links(send, recv, near)
    place.greet(plane=True)
    gather = PlaneGather(place, links, block, blocks, 2)
    gather.relay(0)
    gather.relay(1)
    gather.finish()
    links.drain()


def middle_kernel(
    chips,
    branch,
    terms,
    part_down,
    part_up,
    all_branch,
    term_in,
    extra_in,
    sum_down,
    sum_up,
    *scratch,
):
    own_down, other_down, land_down, own_up, other_up, land_up, turn, send, recv, near = scratch
    place = Place(chips)
    links = Links(send, recv, near)
    place.greet(plane=True, sibling=True, ring=True)
    rank = place.rank
    collect_down = Collect(place, links, part_down, own_down, other_down, land_down)
    collect_up = Collect(place, links, part_up, own_up, other_up, land_up)
    gather = PlaneGather(place, links, branch, all_branch, 2)
    collect_down.send()
    collect_up.send()
    gather.relay(0)
    gather.relay(1)
    links.keep(terms.at[0, rank], term_in.at[rank])
    links.keep(terms.at[1, rank], extra_in, rank == 0)
    dealt = []
    for r in (place.first, place.second, place.across):
        dealt.append(Message(links, terms.at[0, r], term_in.at[rank], place.at(rank=r)))
        dealt.append(
            Message(links, terms.at[1, r], extra_in, place.at(rank=r), rank == 0, r == 0)
        )
    sum_down[...] = collect_down.total()[0]
    turn[...] = collect_up.total().astype(jnp.bfloat16)
    deal_up = Deal(
        place, links, [(lambda r: turn.at[r], sum_up.at[rank])]
    )
    gather.finish()
    for message in dealt:
        message.arrive()
    deal_up.arrive()
    links.drain()


def last_kernel(
    chips,
    partial,
    part_out,
    part_qkv,
    part_small,
    total,
    sum_out,
    sum_qkv,
    sum_small,
    *scratch,
):
    landing, passing = scratch[:2]
    own_out, other_out, land_out, own_qkv, other_qkv, land_qkv = scratch[2:8]
    own_small, other_small, land_small, turn, turn_small, land_sums = scratch[8:14]
    send, recv, near = scratch[14:]
    place = Place(chips)
    links = Links(send, recv, near)
    place.greet(plane=True, sibling=True, ring=True)
    rank = place.rank
    collect_small = Collect(place, links, part_small, own_small, other_small, land_small)
    collect_qkv = Collect(place, links, part_qkv, own_qkv, other_qkv, land_qkv)
    collect_out = Collect(place, links, part_out, own_out, other_out, land_out)
    scatter = PlaneScatter(place, links, partial, landing, passing)
    collect_small.send()
    collect_qkv.send()
    collect_out.send()
    scatter.relay()
    turn_small[...] = collect_small.total()
    deal_small = Deal(place, links, [(lambda r: turn_small.at[r], land_sums.at[rank])])
    turn[...] = collect_qkv.total().astype(jnp.bfloat16)
    deal_qkv = Deal(place, links, [(lambda r: turn.at[r], sum_qkv.at[rank])])
    sum_out[...] = collect_out.total()[0]
    total[...] = scatter.total()
    deal_small.arrive()
    sum_small[...] = land_sums[0] + land_sums[1] + land_sums[2] + land_sums[3]
    deal_qkv.arrive()
    links.drain()


ANY = pl.BlockSpec(memory_space=pl.ANY)
ON_CORE = pl.BlockSpec(memory_space=pltpu.VMEM)


def connected(kernel, number, outs, out_specs, in_specs, scratch, operands):
    return pl.pallas_call(
        kernel,
        out_shape=outs,
        in_specs=in_specs,
        out_specs=out_specs,
        scratch_shapes=scratch + LINK_SCRATCH,
        compiler_params=pltpu.CompilerParams(
            collective_id=number, has_side_effects=True, vmem_limit_bytes=60 * 2**20
        ),
    )(*operands)


def array(shape, dtype=jnp.bfloat16):
    return jax.ShapeDtypeStruct(shape, dtype)


def local_split(ranks, shards, *arguments):
    chips = shards // 2
    (
        tokens,
        cotangent,
        norm1_gain,
        norm1_bias,
        query_weight,
        key_weight,
        value_weight,
        out_weight,
        norm2_gain,
        norm2_bias,
        up_weight,
        up_bias,
        down_weight,
        down_bias,
    ) = arguments
    model_width = tokens.shape[2]
    tok_rows = tokens.shape[1]
    seq_len = tok_rows * ranks
    own = query_weight.shape[0]
    heads = HEADS // ranks
    head_cols = heads * HEAD_DIM
    ff_cols = FF // ranks
    scaling = HEAD_DIM ** (-0.5)
    rank = lax.axis_index("dp")

    grads_out = cotangent.reshape(GRAN, tok_rows, model_width).astype(jnp.float32)
    suffix = [grads_out[GRAN - 1]]
    for level_idx in range(GRAN - 2, -1, -1):
        suffix.insert(0, suffix[0] + grads_out[level_idx])
    grad_hidden = suffix[0]
    suffix = jnp.stack([s.astype(jnp.bfloat16) for s in suffix])

    small = jnp.concatenate([norm1_gain, norm1_bias, norm2_gain, norm2_bias, down_bias, up_bias])
    small = jnp.pad(small, (0, 16 * 128 - small.shape[0])).reshape(16, 128)
    own_tokens = tokens.reshape(tok_rows, model_width)
    all_tokens, incoming, all_small, w_qkv, w_out, w_up, w_down = connected(
        functools.partial(gather_kernel, chips),
        1,
        (
            array((ranks, tok_rows, model_width)),
            array((2, ranks, tok_rows, model_width)),
            array((ranks, shards, 16, 128)),
            array((ranks, shards, own, 3 * head_cols)),
            array((shards, own, model_width)),
            array((ranks, shards, own, ff_cols)),
            array((shards, down_weight.shape[0], model_width)),
        ),
        [ANY] * 7,
        [ANY] * 9,
        [],
        (own_tokens, suffix, small, query_weight, key_weight, value_weight, out_weight, up_weight, down_weight),
    )
    small = all_small.reshape(ranks * shards, 16 * 128)[:, : 5 * own + ff_cols // shards].astype(jnp.float32)
    gain_one, bias_one, gain_two, bias_two, b_down = (
        small[:, i * own : (i + 1) * own].reshape(model_width) for i in range(5)
    )
    b_up_all = small[:, 5 * own :].reshape(ranks, ff_cols)
    b_up = lax.dynamic_index_in_dim(b_up_all, rank, 0, keepdims=False)
    w_qkv = w_qkv.reshape(model_width, 3 * head_cols)
    w_up = w_up.reshape(model_width, ff_cols)
    w_out = w_out.reshape(head_cols, model_width)
    w_down = w_down.reshape(ff_cols, model_width)
    all_tokens = all_tokens.reshape(seq_len, model_width).astype(jnp.float32)
    normed_all, unused = norm_parts(all_tokens)
    attn_in = (normed_all * gain_one + bias_one).astype(jnp.bfloat16)
    qkv = product(attn_in, w_qkv)
    queries = qkv[:, :head_cols].reshape(seq_len, heads, HEAD_DIM)
    key_raw = qkv[:, head_cols : 2 * head_cols].reshape(seq_len, heads, HEAD_DIM)
    values = qkv[:, 2 * head_cols :].astype(jnp.bfloat16).reshape(seq_len, heads, HEAD_DIM)
    positions = jnp.arange(seq_len, dtype=jnp.int32)
    cosine, sine = rotary_tables(positions.astype(jnp.float32), HEAD_DIM // 2)
    q_rot = (rotate(queries, cosine, sine) * scaling).astype(jnp.bfloat16)
    k_rot = rotate(key_raw, cosine, sine).astype(jnp.bfloat16)
    visible = (positions[:, None] >= positions[None, :])[None]

    def weigh(log_total=None):
        scores = jnp.einsum("qhd,khd->hqk", q_rot, k_rot, preferred_element_type=jnp.float32)
        scores = jnp.where(visible, scores, masked_score)
        if log_total is None:
            top = jnp.max(scores, axis=-1)
            log_total = top + jnp.log(jnp.sum(jnp.exp(scores - top[..., None]), axis=-1))
        return jnp.exp(scores - log_total[..., None]), log_total

    probs, log_total = weigh()
    mixed = jnp.einsum(
        "hqk,khd->qhd", probs.astype(jnp.bfloat16), values, preferred_element_type=jnp.float32
    )
    mixed_low = mixed.reshape(seq_len, head_cols).astype(jnp.bfloat16)

    blocks_low = array((ranks, tok_rows, model_width))

    def add_up(number, partial):
        return connected(
            functools.partial(scatter_kernel, chips),
            number,
            array((tok_rows, model_width), jnp.float32),
            ON_CORE,
            [ON_CORE],
            [
                pltpu.VMEM((3, tok_rows, model_width), jnp.bfloat16),
                pltpu.VMEM((tok_rows, model_width), jnp.bfloat16),
            ],
            (partial.astype(jnp.bfloat16).reshape(ranks, tok_rows, model_width),),
        )

    inputs = own_tokens.astype(jnp.float32)
    hidden = inputs + add_up(2, product(mixed_low, w_out))
    normed_two, inverse_two = norm_parts(hidden)
    ffn_in_own = (normed_two * gain_two + bias_two).astype(jnp.bfloat16)
    ffn_in = connected(
        functools.partial(spread_kernel, chips), 3, blocks_low, ANY, [ANY], [], (ffn_in_own,)
    ).reshape(seq_len, model_width)
    preact = product(ffn_in, w_up) + b_up
    gated = gelu_value(preact).astype(jnp.bfloat16)

    half = ff_cols // 2
    low_term = product(gated[:, :half], w_down[:half])
    high_term = product(gated[:, half:], w_down[half:])
    terms = jnp.stack(
        [
            (low_term + jnp.where(rank == 0, 0.0, high_term)).astype(jnp.bfloat16),
            high_term.astype(jnp.bfloat16),
        ]
    ).reshape(2, ranks, tok_rows, model_width)
    split_grads = [
        incoming[0].reshape(seq_len, model_width),
        jnp.where(rank == 0, incoming[1], incoming[0]).reshape(seq_len, model_width),
    ]
    grad_gated = jnp.concatenate(
        [back_product(split_grads[i], w_down[i * half : (i + 1) * half]) for i in range(2)],
        axis=1,
    )
    grad_pre_wide = grad_gated * gelu_grad(preact)
    grad_pre = grad_pre_wide.astype(jnp.bfloat16)
    grad_up_bias = jnp.sum(grad_pre_wide, axis=0)
    grad_ffn_in = add_up(4, back_product(grad_pre, w_up))

    part_down = jnp.concatenate(
        [gram_product(gated[:, i * half : (i + 1) * half], split_grads[i]) for i in range(2)],
        axis=0,
    ).astype(jnp.bfloat16)
    part_up = gram_product(ffn_in, grad_pre).astype(jnp.bfloat16)
    grad_down_bias = jnp.sum(grad_hidden, axis=0)
    grad_gain_two = jnp.sum(grad_ffn_in * normed_two, axis=0)
    grad_bias_two = jnp.sum(grad_ffn_in, axis=0)
    grad_hidden = grad_hidden + norm_backward(grad_ffn_in, normed_two, inverse_two, gain_two)
    down_rows = ff_cols // shards
    grad_branch, term_in, extra_in, sum_down, sum_up = connected(
        functools.partial(middle_kernel, chips),
        5,
        (
            blocks_low,
            blocks_low,
            array((tok_rows, model_width)),
            array((down_rows, model_width), jnp.float32),
            array((ranks, own, ff_cols)),
        ),
        [ANY, ANY, ANY, ON_CORE, ANY],
        [ANY] * 4,
        collect_scratch(1, chips, down_rows, model_width, jnp.bfloat16)
        + collect_scratch(ranks, chips, own, ff_cols, jnp.bfloat16)
        + [pltpu.VMEM((ranks, own, ff_cols), jnp.bfloat16)],
        (
            grad_hidden.astype(jnp.bfloat16),
            terms,
            part_down.reshape(1, chips, 2, down_rows, model_width),
            part_up.reshape(ranks, chips, 2, own, ff_cols),
        ),
    )
    grad_branch = grad_branch.reshape(seq_len, model_width)
    sum_up = sum_up.astype(jnp.float32).transpose(1, 0, 2).reshape(own, FF)
    total = hidden + b_down + term_in[0].astype(jnp.float32)
    result_list = [total.astype(jnp.bfloat16)]
    total = total + extra_in.astype(jnp.float32)
    result_list.append(total.astype(jnp.bfloat16))
    total = total + term_in[1].astype(jnp.float32)
    result_list.append(total.astype(jnp.bfloat16))
    total = total + term_in[2].astype(jnp.float32) + term_in[3].astype(jnp.float32)
    result_list.append(total.astype(jnp.bfloat16))
    activations = jnp.stack(result_list).reshape(GRAN, 1, tok_rows, model_width)
    part_out = gram_product(mixed_low, grad_branch).astype(jnp.bfloat16)
    grad_mixed = (
        back_product(grad_branch, w_out).astype(jnp.bfloat16).reshape(seq_len, heads, HEAD_DIM)
    )
    row_delta = jnp.einsum("qhd,qhd->hq", grad_mixed.astype(jnp.float32), mixed)
    probs, unused = weigh(log_total)
    grad_probs = jnp.einsum("qhd,khd->hqk", grad_mixed, values, preferred_element_type=jnp.float32)
    grad_scores = (probs * (grad_probs - row_delta[..., None])).astype(jnp.bfloat16)
    grad_q_rot = jnp.einsum(
        "hqk,khd->qhd", grad_scores, k_rot, preferred_element_type=jnp.float32
    )
    grad_k_rot = jnp.einsum(
        "hqk,qhd->khd", grad_scores, q_rot, preferred_element_type=jnp.float32
    )
    grad_values = jnp.einsum(
        "hqk,qhd->khd", probs.astype(jnp.bfloat16), grad_mixed, preferred_element_type=jnp.float32
    )
    grad_qkv = jnp.concatenate(
        [
            rotate(grad_q_rot * scaling, cosine, -sine).reshape(seq_len, head_cols),
            rotate(grad_k_rot, cosine, -sine).reshape(seq_len, head_cols),
            grad_values.reshape(seq_len, head_cols),
        ],
        axis=1,
    ).astype(jnp.bfloat16)
    part_qkv = gram_product(attn_in, grad_qkv).astype(jnp.bfloat16)
    partial = back_product(grad_qkv, w_qkv).astype(jnp.bfloat16)
    sums = jnp.stack([grad_gain_two, grad_bias_two, grad_down_bias])
    sums = sums.reshape(3, ranks, shards, own).transpose(1, 2, 0, 3).reshape(ranks, shards, 3 * own)
    here = (jnp.arange(ranks) == rank).astype(jnp.float32)[:, None, None]
    sums = jnp.concatenate([sums, here * grad_up_bias.reshape(1, shards, -1)], axis=2)
    used = sums.shape[2]
    sums = jnp.pad(sums, ((0, 0), (0, 0), (0, 1024 - used)))
    grad_attn_in, sum_out, sum_qkv, sums = connected(
        functools.partial(last_kernel, chips),
        6,
        (
            array((tok_rows, model_width), jnp.float32),
            array((own, model_width), jnp.float32),
            array((ranks, own, 3 * head_cols)),
            array((8, 128), jnp.float32),
        ),
        [ON_CORE, ON_CORE, ANY, ON_CORE],
        [ON_CORE, ANY, ANY, ANY],
        [
            pltpu.VMEM((3, tok_rows, model_width), jnp.bfloat16),
            pltpu.VMEM((tok_rows, model_width), jnp.bfloat16),
        ]
        + collect_scratch(1, chips, own, model_width, jnp.bfloat16)
        + collect_scratch(ranks, chips, own, 3 * head_cols, jnp.bfloat16)
        + collect_scratch(ranks, chips, 8, 128, jnp.float32)
        + [
            pltpu.VMEM((ranks, own, 3 * head_cols), jnp.bfloat16),
            pltpu.VMEM((ranks, 8, 128), jnp.float32),
            pltpu.VMEM((ranks, 8, 128), jnp.float32),
        ],
        (
            partial.reshape(ranks, tok_rows, model_width),
            part_out.reshape(1, chips, 2, own, model_width),
            part_qkv.reshape(ranks, chips, 2, own, 3 * head_cols),
            sums.reshape(ranks, chips, 2, 8, 128),
        ),
    )
    sums = sums.reshape(1024)
    sum_gain_two, sum_bias_two, sum_down_bias = (sums[i * own : (i + 1) * own] for i in range(3))
    sum_up_bias = sums[3 * own : used]
    sum_qkv = sum_qkv.astype(jnp.float32).transpose(1, 0, 2)
    sum_query, sum_key, sum_value = (
        sum_qkv[:, :, i * head_cols : (i + 1) * head_cols].reshape(own, model_width)
        for i in range(3)
    )
    normed_one, inverse_one = norm_parts(inputs)
    grad_gain_one = jnp.sum(grad_attn_in * normed_one, axis=0)
    grad_bias_one = jnp.sum(grad_attn_in, axis=0)
    grad_inputs = grad_hidden + norm_backward(grad_attn_in, normed_one, inverse_one, gain_one)

    sums_one = lax.psum_scatter(
        jnp.concatenate(
            [g.reshape(ranks * shards, own) for g in (grad_gain_one, grad_bias_one)], axis=1
        ),
        ("dp", "fsdp"),
        scatter_dimension=0,
        tiled=True,
    ).reshape(2, own)
    return (
        activations,
        grad_inputs.astype(jnp.bfloat16).reshape(1, tok_rows, model_width),
        sums_one[0],
        sums_one[1],
        sum_query,
        sum_key,
        sum_value,
        sum_out,
        sum_gain_two,
        sum_bias_two,
        sum_up,
        sum_up_bias,
        sum_down,
        sum_down_bias,
    )


def solution(mesh):
    placed = (
        P("fsdp", "dp", None),
        P(None, "fsdp", "dp", None),
        P(("dp", "fsdp")),
        P(("dp", "fsdp")),
        P(("dp", "fsdp"), None),
        P(("dp", "fsdp"), None),
        P(("dp", "fsdp"), None),
        P(("dp", "fsdp"), None),
        P(("dp", "fsdp")),
        P(("dp", "fsdp")),
        P(("dp", "fsdp"), None),
        P(("dp", "fsdp")),
        P(("dp", "fsdp"), None),
        P(("dp", "fsdp")),
    )
    ranks, shards = mesh.shape["dp"], mesh.shape["fsdp"]
    local = local_gathered
    if ranks == 4 and shards % 2 == 0:
        local = functools.partial(local_split, ranks, shards)
    return jax.shard_map(
        local,
        mesh=mesh,
        in_specs=placed,
        out_specs=(
            P(None, "fsdp", "dp", None),
            P("fsdp", "dp", None),
            P(("dp", "fsdp")),
            P(("dp", "fsdp")),
            P(("dp", "fsdp"), None),
            P(("dp", "fsdp"), None),
            P(("dp", "fsdp"), None),
            P(("dp", "fsdp"), None),
            P(("dp", "fsdp")),
            P(("dp", "fsdp")),
            P(("dp", "fsdp"), None),
            P(("dp", "fsdp")),
            P(("dp", "fsdp"), None),
            P(("dp", "fsdp")),
        ),
        check_vma=False,
    )
```

```python
import functools
import math

import jax
import jax.numpy as jnp
from jax import lax
from jax.experimental import pallas as pl
from jax.experimental.pallas import tpu as pltpu
from jax.sharding import PartitionSpec as P

HEADS = 12
HEAD_DIM = 128
FF = 6144
GRAN = 4


epsilon = 1e-05
masked_score = -1e30


def product(left, right):
    return jnp.dot(left, right, preferred_element_type=jnp.float32)


def gram_product(left, right):
    return lax.dot_general(
        left, right, (((0,), (0,)), ((), ())), preferred_element_type=jnp.float32
    )


def back_product(left, right):
    return lax.dot_general(
        left, right, (((1,), (1,)), ((), ())), preferred_element_type=jnp.float32
    )


def norm_parts(values):
    centred = values - jnp.mean(values, axis=-1, keepdims=True)
    inverse = lax.rsqrt(jnp.mean(centred * centred, axis=-1, keepdims=True) + epsilon)
    return (centred * inverse, inverse)


def norm_backward(grad_normed, normed, inverse, gain):
    scaled = grad_normed * gain
    return inverse * (
        scaled
        - jnp.mean(scaled, axis=-1, keepdims=True)
        - normed * jnp.mean(scaled * normed, axis=-1, keepdims=True)
    )


def gelu_value(values):
    return (
        0.5
        * values
        * (1.0 + jnp.tanh(0.7978845608028654 * (values + 0.044715 * values * values * values)))
    )


def gelu_grad(values):
    tangent = jnp.tanh(0.7978845608028654 * (values + 0.044715 * values * values * values))
    return 0.5 * (1.0 + tangent) + 0.5 * values * (1.0 - tangent * tangent) * 0.7978845608028654 * (
        1.0 + 3.0 * 0.044715 * values * values
    )


def rotary_tables(positions, half_size):
    ladder = jnp.arange(half_size).astype(jnp.float32)
    inverse = jnp.exp(ladder * (-math.log(10000.0) / half_size))
    angles = positions[:, None] * inverse[None, :]
    return (jnp.cos(angles)[:, None, :], jnp.sin(angles)[:, None, :])


def rotate(values, cosine, sine):
    half_size = values.shape[-1] // 2
    first = values[..., :half_size]
    second = values[..., half_size:]
    return jnp.concatenate(
        [first * cosine - second * sine, second * cosine + first * sine], axis=-1
    )


def block_scores(queries, positions, key_block, start_row):
    block_rows = key_block.shape[0]
    scores = jnp.einsum("qhd,khd->hqk", queries, key_block, preferred_element_type=jnp.float32)
    key_positions = start_row + jnp.arange(block_rows, dtype=jnp.int32)
    visible = positions[None, :, None] >= key_positions[None, None, :]
    return (jnp.where(visible, scores, masked_score), visible)


def key_blocking(keys_all, values_all, key_offset):
    seq_len = keys_all.shape[0]
    block_rows = min(512, seq_len)
    block_count = seq_len // block_rows
    key_blocks = keys_all.reshape(block_count, block_rows, HEADS, HEAD_DIM)
    value_blocks = values_all.reshape(block_count, block_rows, HEADS, HEAD_DIM)
    starts = key_offset + jnp.arange(block_count, dtype=jnp.int32) * block_rows
    return (key_blocks, value_blocks, starts)


def attend(queries, keys_all, values_all, positions):
    tok_rows = queries.shape[0]
    key_blocks, value_blocks, starts = key_blocking(keys_all, values_all, jnp.int32(0))

    def measure(state_pair, block_pair):
        top_score, total = state_pair
        key_block, start_row = block_pair
        scores, visible = block_scores(queries, positions, key_block, start_row)
        new_top = jnp.maximum(top_score, jnp.max(scores, axis=-1))
        raised = jnp.where(visible, jnp.exp(scores - new_top[..., None]), 0.0)
        total = total * jnp.exp(top_score - new_top) + jnp.sum(raised, axis=-1)
        return ((new_top, total), None)

    initial = (
        jnp.full((HEADS, tok_rows), masked_score, jnp.float32),
        jnp.zeros((HEADS, tok_rows), jnp.float32),
    )
    (top_score, total), unused = lax.scan(measure, initial, (key_blocks, starts))
    log_total = top_score + jnp.log(total)

    def accumulate(mixed, block_triple):
        key_block, value_block, start_row = block_triple
        scores, visible = block_scores(queries, positions, key_block, start_row)
        probs = jnp.where(visible, jnp.exp(scores - log_total[..., None]), 0.0).astype(jnp.bfloat16)
        return (
            mixed
            + jnp.einsum("hqk,khd->qhd", probs, value_block, preferred_element_type=jnp.float32),
            None,
        )

    mixed, unused = lax.scan(
        accumulate,
        jnp.zeros((tok_rows, HEADS, HEAD_DIM), jnp.float32),
        (key_blocks, value_blocks, starts),
    )
    return (mixed, log_total)


def attend_back(
    queries, positions, keys_all, values_all, key_offset, grad_mixed, log_total, row_delta
):
    tok_rows = queries.shape[0]
    key_blocks, value_blocks, starts = key_blocking(keys_all, values_all, key_offset)

    def backward_block(grad_queries, block_triple):
        key_block, value_block, start_row = block_triple
        scores, visible = block_scores(queries, positions, key_block, start_row)
        probs = jnp.where(visible, jnp.exp(scores - log_total[..., None]), 0.0)
        grad_probs = jnp.einsum(
            "qhd,khd->hqk", grad_mixed, value_block, preferred_element_type=jnp.float32
        )
        grad_scores = (probs * (grad_probs - row_delta[..., None])).astype(jnp.bfloat16)
        grad_queries = grad_queries + jnp.einsum(
            "hqk,khd->qhd", grad_scores, key_block, preferred_element_type=jnp.float32
        )
        grad_key_block = jnp.einsum(
            "hqk,qhd->khd", grad_scores, queries, preferred_element_type=jnp.float32
        )
        grad_value_block = jnp.einsum(
            "hqk,qhd->khd",
            probs.astype(jnp.bfloat16),
            grad_mixed,
            preferred_element_type=jnp.float32,
        )
        return (grad_queries, (grad_key_block, grad_value_block))

    grad_queries, (grad_keys, grad_values) = lax.scan(
        backward_block,
        jnp.zeros((tok_rows, HEADS, HEAD_DIM), jnp.float32),
        (key_blocks, value_blocks, starts),
    )
    key_len = keys_all.shape[0]
    return (
        grad_queries,
        grad_keys.reshape(key_len, HEADS * HEAD_DIM),
        grad_values.reshape(key_len, HEADS * HEAD_DIM),
    )


def local_gathered(
    tokens,
    cotangent,
    norm1_gain,
    norm1_bias,
    query_weight,
    key_weight,
    value_weight,
    out_weight,
    norm2_gain,
    norm2_bias,
    up_weight,
    up_bias,
    down_weight,
    down_bias,
):
    (
        gain_one,
        bias_one,
        w_query,
        w_key,
        w_value,
        w_out,
        gain_two,
        bias_two,
        w_up,
        b_up,
        w_down,
        b_down,
    ) = (
        lax.all_gather(norm1_gain, ("dp", "fsdp"), axis=0, tiled=True),
        lax.all_gather(norm1_bias, ("dp", "fsdp"), axis=0, tiled=True),
        lax.all_gather(query_weight, ("dp", "fsdp"), axis=0, tiled=True),
        lax.all_gather(key_weight, ("dp", "fsdp"), axis=0, tiled=True),
        lax.all_gather(value_weight, ("dp", "fsdp"), axis=0, tiled=True),
        lax.all_gather(out_weight, ("dp", "fsdp"), axis=0, tiled=True),
        lax.all_gather(norm2_gain, ("dp", "fsdp"), axis=0, tiled=True),
        lax.all_gather(norm2_bias, ("dp", "fsdp"), axis=0, tiled=True),
        lax.all_gather(up_weight, ("dp", "fsdp"), axis=0, tiled=True),
        lax.all_gather(up_bias, ("dp", "fsdp"), axis=0, tiled=True),
        lax.all_gather(down_weight, ("dp", "fsdp"), axis=0, tiled=True),
        lax.all_gather(down_bias, ("dp", "fsdp"), axis=0, tiled=True),
    )
    seq_count = tokens.shape[0]
    tok_rows = tokens.shape[1]
    model_width = tokens.shape[2]
    all_rows = seq_count * tok_rows
    scaling = HEAD_DIM ** (-0.5)
    inputs = tokens.reshape(all_rows, model_width).astype(jnp.float32)
    normed_one, inverse_one = norm_parts(inputs)
    attn_in = (normed_one * gain_one.astype(jnp.float32) + bias_one.astype(jnp.float32)).astype(
        jnp.bfloat16
    )
    queries = product(attn_in, w_query).reshape(seq_count, tok_rows, HEADS, HEAD_DIM)
    key_raw = product(attn_in, w_key).reshape(seq_count, tok_rows, HEADS, HEAD_DIM)
    value_low = (
        product(attn_in, w_value).astype(jnp.bfloat16).reshape(seq_count, tok_rows, model_width)
    )
    key_offset = lax.axis_index("dp") * tok_rows
    positions = key_offset + jnp.arange(tok_rows, dtype=jnp.int32)
    cosine, sine = rotary_tables(positions.astype(jnp.float32), HEAD_DIM // 2)
    q_rot = (rotate(queries, cosine, sine) * scaling).astype(jnp.bfloat16)
    k_flat = (
        rotate(key_raw, cosine, sine).astype(jnp.bfloat16).reshape(seq_count, tok_rows, model_width)
    )
    keys_all, values_all = (
        lax.all_gather(k_flat, "dp", axis=1, tiled=True),
        lax.all_gather(value_low, "dp", axis=1, tiled=True),
    )
    seq_len = keys_all.shape[1]
    mixed, log_total = jax.vmap(attend, in_axes=(0, 0, 0, None))(
        q_rot,
        keys_all.reshape(seq_count, seq_len, HEADS, HEAD_DIM),
        values_all.reshape(seq_count, seq_len, HEADS, HEAD_DIM),
        positions,
    )
    mixed_low = mixed.reshape(all_rows, model_width).astype(jnp.bfloat16)
    hidden = inputs + product(mixed_low, w_out)
    normed_two, inverse_two = norm_parts(hidden)
    ffn_in = (normed_two * gain_two.astype(jnp.float32) + bias_two.astype(jnp.float32)).astype(
        jnp.bfloat16
    )
    preact = product(ffn_in, w_up) + b_up.astype(jnp.float32)
    edges = [0] + [FF // 2 ** (GRAN - 1 - level_idx) for level_idx in range(GRAN)]
    gated_list = []
    result_list = []
    for level_idx in range(GRAN):
        level_width = edges[level_idx + 1]
        gated = gelu_value(preact[:, :level_width]).astype(jnp.bfloat16)
        gated_list.append(gated)
        result = hidden + product(gated, w_down[:level_width]) + b_down.astype(jnp.float32)
        result_list.append(result.astype(jnp.bfloat16))
    activations = jnp.stack(result_list).reshape(GRAN, seq_count, tok_rows, model_width)
    back_gain_one, back_query, back_key, back_value, back_out, back_gain_two, back_up, back_down = (
        lax.all_gather(norm1_gain, ("dp", "fsdp"), axis=0, tiled=True),
        lax.all_gather(query_weight, ("dp", "fsdp"), axis=0, tiled=True),
        lax.all_gather(key_weight, ("dp", "fsdp"), axis=0, tiled=True),
        lax.all_gather(value_weight, ("dp", "fsdp"), axis=0, tiled=True),
        lax.all_gather(out_weight, ("dp", "fsdp"), axis=0, tiled=True),
        lax.all_gather(norm2_gain, ("dp", "fsdp"), axis=0, tiled=True),
        lax.all_gather(up_weight, ("dp", "fsdp"), axis=0, tiled=True),
        lax.all_gather(down_weight, ("dp", "fsdp"), axis=0, tiled=True),
    )
    grads_out = cotangent.reshape(GRAN, all_rows, model_width)
    grad_hidden = jnp.sum(grads_out.astype(jnp.float32), axis=0)
    grad_down_bias = jnp.sum(grad_hidden, axis=0)
    grad_ffn_in = jnp.zeros((all_rows, model_width), jnp.float32)
    pre_grads = []
    for level_idx in range(GRAN):
        level_width = edges[level_idx + 1]
        grad_gated = back_product(grads_out[level_idx], back_down[:level_width])
        grad_pre = (grad_gated * gelu_grad(preact[:, :level_width])).astype(jnp.bfloat16)
        pre_grads.append(grad_pre)
        grad_ffn_in = grad_ffn_in + back_product(grad_pre, back_up[:, :level_width])
    up_blocks = []
    bias_blocks = []
    down_blocks = []
    for block_idx in range(GRAN):
        start_col = edges[block_idx]
        stop_col = edges[block_idx + 1]
        stacked_grad = jnp.concatenate(
            [pre_grads[level_idx][:, start_col:stop_col] for level_idx in range(block_idx, GRAN)],
            axis=0,
        )
        stacked_in = jnp.concatenate([ffn_in] * (GRAN - block_idx), axis=0)
        up_blocks.append(gram_product(stacked_in, stacked_grad))
        bias_blocks.append(jnp.sum(stacked_grad.astype(jnp.float32), axis=0))
        stacked_gated = jnp.concatenate(
            [gated_list[level_idx][:, start_col:stop_col] for level_idx in range(block_idx, GRAN)],
            axis=0,
        )
        stacked_out = jnp.concatenate(
            [grads_out[level_idx] for level_idx in range(block_idx, GRAN)], axis=0
        )
        down_blocks.append(gram_product(stacked_gated, stacked_out))
    grad_up_weight = jnp.concatenate(up_blocks, axis=1)
    grad_up_bias = jnp.concatenate(bias_blocks, axis=0)
    grad_down_weight = jnp.concatenate(down_blocks, axis=0)
    grad_gain_two = jnp.sum(grad_ffn_in * normed_two, axis=0)
    grad_bias_two = jnp.sum(grad_ffn_in, axis=0)
    grad_hidden = grad_hidden + norm_backward(
        grad_ffn_in, normed_two, inverse_two, back_gain_two.astype(jnp.float32)
    )
    grad_branch = grad_hidden.astype(jnp.bfloat16)
    grad_out_weight = gram_product(mixed_low, grad_branch)
    grad_mixed = (
        back_product(grad_branch, back_out)
        .astype(jnp.bfloat16)
        .reshape(seq_count, tok_rows, HEADS, HEAD_DIM)
    )
    row_delta = jnp.einsum("sqhd,sqhd->shq", grad_mixed.astype(jnp.float32), mixed)
    keys_again, values_again = (
        lax.all_gather(k_flat, "dp", axis=1, tiled=True),
        lax.all_gather(value_low, "dp", axis=1, tiled=True),
    )
    back_all = jax.vmap(attend_back, in_axes=(0, None, 0, 0, None, 0, 0, 0))
    grad_q_rot, grad_keys_all, grad_values_all = back_all(
        q_rot,
        positions,
        keys_again.reshape(seq_count, seq_len, HEADS, HEAD_DIM),
        values_again.reshape(seq_count, seq_len, HEADS, HEAD_DIM),
        jnp.int32(0),
        grad_mixed,
        log_total,
        row_delta,
    )
    every_query, every_grad = (
        lax.all_gather(q_rot, "dp", axis=1, tiled=True),
        lax.all_gather(grad_mixed, "dp", axis=1, tiled=True),
    )
    every_total, every_delta = (
        lax.all_gather(jnp.transpose(log_total, (0, 2, 1)), "dp", axis=1, tiled=True),
        lax.all_gather(jnp.transpose(row_delta, (0, 2, 1)), "dp", axis=1, tiled=True),
    )
    every_position = jnp.arange(seq_len, dtype=jnp.int32)
    unused_rows, grad_key_mine, grad_value_mine = back_all(
        every_query,
        every_position,
        k_flat.reshape(seq_count, tok_rows, HEADS, HEAD_DIM),
        value_low.reshape(seq_count, tok_rows, HEADS, HEAD_DIM),
        key_offset,
        every_grad,
        jnp.transpose(every_total, (0, 2, 1)),
        jnp.transpose(every_delta, (0, 2, 1)),
    )
    grad_query = (
        rotate(grad_q_rot * scaling, cosine, -sine)
        .reshape(all_rows, model_width)
        .astype(jnp.bfloat16)
    )
    grad_key = (
        rotate(grad_key_mine.reshape(seq_count, tok_rows, HEADS, HEAD_DIM), cosine, -sine)
        .reshape(all_rows, model_width)
        .astype(jnp.bfloat16)
    )
    grad_val = grad_value_mine.reshape(all_rows, model_width).astype(jnp.bfloat16)
    grad_query_weight = gram_product(attn_in, grad_query)
    grad_key_weight = gram_product(attn_in, grad_key)
    grad_value_weight = gram_product(attn_in, grad_val)
    grad_attn_in = (
        back_product(grad_query, back_query)
        + back_product(grad_key, back_key)
        + back_product(grad_val, back_value)
    )
    grad_gain_one = jnp.sum(grad_attn_in * normed_one, axis=0)
    grad_bias_one = jnp.sum(grad_attn_in, axis=0)
    grad_inputs = grad_hidden + norm_backward(
        grad_attn_in, normed_one, inverse_one, back_gain_one.astype(jnp.float32)
    )
    (
        sum_gain_one,
        sum_bias_one,
        sum_query,
        sum_key,
        sum_value,
        sum_out,
        sum_gain_two,
        sum_bias_two,
        sum_up,
        sum_up_bias,
        sum_down,
        sum_down_bias,
    ) = (
        lax.psum_scatter(grad_gain_one, ("dp", "fsdp"), scatter_dimension=0, tiled=True),
        lax.psum_scatter(grad_bias_one, ("dp", "fsdp"), scatter_dimension=0, tiled=True),
        lax.psum_scatter(grad_query_weight, ("dp", "fsdp"), scatter_dimension=0, tiled=True),
        lax.psum_scatter(grad_key_weight, ("dp", "fsdp"), scatter_dimension=0, tiled=True),
        lax.psum_scatter(grad_value_weight, ("dp", "fsdp"), scatter_dimension=0, tiled=True),
        lax.psum_scatter(grad_out_weight, ("dp", "fsdp"), scatter_dimension=0, tiled=True),
        lax.psum_scatter(grad_gain_two, ("dp", "fsdp"), scatter_dimension=0, tiled=True),
        lax.psum_scatter(grad_bias_two, ("dp", "fsdp"), scatter_dimension=0, tiled=True),
        lax.psum_scatter(grad_up_weight, ("dp", "fsdp"), scatter_dimension=0, tiled=True),
        lax.psum_scatter(grad_up_bias, ("dp", "fsdp"), scatter_dimension=0, tiled=True),
        lax.psum_scatter(grad_down_weight, ("dp", "fsdp"), scatter_dimension=0, tiled=True),
        lax.psum_scatter(grad_down_bias, ("dp", "fsdp"), scatter_dimension=0, tiled=True),
    )
    return (
        activations,
        grad_inputs.astype(jnp.bfloat16).reshape(seq_count, tok_rows, model_width),
        sum_gain_one,
        sum_bias_one,
        sum_query,
        sum_key,
        sum_value,
        sum_out,
        sum_gain_two,
        sum_bias_two,
        sum_up,
        sum_up_bias,
        sum_down,
        sum_down_bias,
    )


MESH = pl.DeviceIdType.MESH


class Place:
    def __init__(self, chips):
        self.chips = chips
        self.rank = lax.axis_index("dp")
        self.shard = lax.axis_index("fsdp")
        self.z = lax.div(self.shard, 2)
        self.core = lax.rem(self.shard, 2)
        along_x = self.rank + 1 - 2 * lax.rem(self.rank, 2)
        along_y = self.rank + 2 - 4 * lax.div(self.rank, 2)
        self.first = jnp.where(self.core == 0, along_x, along_y)
        self.second = jnp.where(self.core == 0, along_y, along_x)
        self.across = 3 - self.rank
        self.sibling = self.shard + 1 - 2 * self.core

    def at(self, rank=None, shard=None):
        return (self.rank if rank is None else rank, self.shard if shard is None else shard)

    def greet(self, plane=True, sibling=False, chain=False, ring=False):
        barrier = pltpu.get_barrier_semaphore()
        count = 0
        targets = []
        if plane:
            targets += [self.at(rank=r) for r in (self.first, self.second, self.across)]
        if sibling:
            targets.append(self.at(shard=self.sibling))
        if ring:
            targets += [self.at(shard=self.hop(k)) for k in range(1, self.chips)]
        for target in targets:
            pl.semaphore_signal(barrier, inc=1, device_id=target, device_id_type=MESH)
            count += 1
        if chain:
            for step, there in ((2, self.z < self.chips - 1), (-2, self.z > 0)):

                @pl.when(there)
                def greet_neighbour(step=step):
                    pl.semaphore_signal(
                        barrier,
                        inc=1,
                        device_id=self.at(shard=self.shard + step),
                        device_id_type=MESH,
                    )

                count = count + there.astype(jnp.int32)
        pl.semaphore_wait(barrier, count)

    def hop(self, k):
        return 2 * lax.rem(self.z + k, self.chips) + self.core


def under(condition, action):
    if condition is None:
        action()
    else:
        pl.when(condition)(action)


class Message:
    def __init__(self, links, src, dst, target, sent=None, comes=None):
        index = links.take()
        self.copy = pltpu.make_async_remote_copy(
            src_ref=src,
            dst_ref=dst,
            send_sem=links.send.at[index],
            recv_sem=links.recv.at[index],
            device_id=target,
            device_id_type=MESH,
        )
        self.sent, self.comes = sent, comes
        links.open.append(self)
        under(sent, self.copy.start)

    def arrive(self):
        under(self.comes, self.copy.wait_recv)

    def leave(self):
        under(self.sent, self.copy.wait_send)


class Near:
    def __init__(self, links, src, dst, where):
        self.copy = pltpu.make_async_copy(src, dst, links.near.at[links.used_near])
        links.used_near += 1
        self.where = where
        self.waits = True
        under(where, self.copy.start)

    def arrive(self):
        if self.waits:
            under(self.where, self.copy.wait)
        self.waits = False


class Links:
    def __init__(self, send, recv, near):
        self.send, self.recv, self.near = send, recv, near
        self.used = 0
        self.used_near = 0
        self.open = []
        self.open_near = []

    def take(self):
        self.used += 1
        return self.used - 1

    def keep(self, src, dst, where=None):
        copy = Near(self, src, dst, where)
        self.open_near.append(copy)
        return copy

    def drain(self):
        for copy in self.open_near:
            copy.arrive()
        for message in self.open:
            message.leave()


LINK_SCRATCH = [
    pltpu.SemaphoreType.DMA((128,)),
    pltpu.SemaphoreType.DMA((128,)),
    pltpu.SemaphoreType.DMA((32,)),
]


def normed(values):
    centred = values - jnp.mean(values, axis=-1, keepdims=True)
    inverse = lax.rsqrt(jnp.mean(centred * centred, axis=-1, keepdims=True) + epsilon)
    return centred * inverse, inverse


def in_rows(count, step, body):
    def one(i, carry):
        body(pl.ds(pl.multiple_of(i * step, step), step))
        return carry

    lax.fori_loop(0, count // step, one, 0)


def turn_half(values, cosine, sine):
    return values * cosine + pltpu.roll(values, HEAD_DIM // 2, 1) * sine


class PlaneGather:
    def __init__(self, place, links, src, dst, parts):
        self.place, self.links, self.dst = place, links, dst
        rows = src.shape[0] // parts
        self.cuts = [pl.ds(k * rows, rows) for k in range(parts)]
        links.keep(src, dst.at[place.rank])
        self.first, self.second = [], []
        for cut in self.cuts:
            for side, target in ((self.first, place.first), (self.second, place.second)):
                block = dst.at[place.rank, cut]
                side.append(Message(links, src.at[cut], block, place.at(rank=target)))
        self.passed = []

    def relay(self, k):
        self.first[k].arrive()
        block = self.dst.at[self.place.first, self.cuts[k]]
        target = self.place.at(rank=self.place.second)
        self.passed.append(Message(self.links, block, block, target))

    def finish(self):
        for message in self.second + self.passed:
            message.arrive()


class PlaneScatter:
    def __init__(self, place, links, partial, landing, turn):
        self.place, self.links, self.partial, self.landing, self.turn = (
            place,
            links,
            partial,
            landing,
            turn,
        )
        self.target = place.at(rank=place.first)

    def send_far(self):
        self.far = Message(
            self.links, self.partial.at[self.place.across], self.landing.at[0], self.target
        )

    def send_near(self):
        self.near = Message(
            self.links, self.partial.at[self.place.first], self.landing.at[1], self.target
        )

    def relay(self):
        self.far.arrive()

        def add(cut):
            mine = self.partial[self.place.second, cut].astype(jnp.float32)
            mine = mine + self.landing[0, cut].astype(jnp.float32)
            self.turn[cut] = mine.astype(jnp.bfloat16)

        in_rows(self.turn.shape[0], 64, add)
        self.last = Message(
            self.links, self.turn, self.landing.at[2], self.place.at(rank=self.place.second)
        )

    def settle(self):
        self.near.arrive()
        self.last.arrive()

    def total(self, cut):
        total = self.partial[self.place.rank, cut].astype(jnp.float32)
        total = total + self.landing[1, cut].astype(jnp.float32)
        return total + self.landing[2, cut].astype(jnp.float32)


class Chain:
    def __init__(self, place, links, src, slot):
        self.place, self.links, self.slot = place, links, slot
        z, last = place.z, place.chips - 1
        own = slot(place.shard)
        self.up = Message(links, src, own, place.at(shard=place.shard + 2), z < last, z > 0)
        self.down = Message(links, src, own, place.at(shard=place.shard - 2), z > 0, z < last)
        self.beside = [Message(links, src, own, place.at(shard=place.sibling))]

    def step(self, s):
        place, links = self.place, self.links
        z, last = place.z, place.chips - 1
        below = self.slot(jnp.maximum(place.shard - 2 * s, place.core))
        above = self.slot(jnp.minimum(place.shard + 2 * s, 2 * last + place.core))
        self.up.arrive()
        has_below, has_above = z >= s, z <= last - s
        up = down = None
        if s < last:
            target = place.at(shard=place.shard + 2)
            up = Message(links, below, below, target, has_below & (z < last), z >= s + 1)
        self.beside.append(
            Message(links, below, below, place.at(shard=place.sibling), has_below, has_below)
        )
        self.down.arrive()
        if s < last:
            target = place.at(shard=place.shard - 2)
            down = Message(links, above, above, target, has_above & (z > 0), z <= last - s - 1)
        self.beside.append(
            Message(links, above, above, place.at(shard=place.sibling), has_above, has_above)
        )
        self.up, self.down = up, down

    def finish(self):
        for message in self.beside:
            message.arrive()


class Beside:
    def __init__(self, place, links, part, other):
        self.place, self.part, self.other = place, part, other
        self.message = Message(
            links, part.at[:, :, 1 - place.core], other, place.at(shard=place.sibling)
        )

    def add(self):
        self.message.arrive()
        core = self.place.core

        def one(k, carry):
            total = self.part[:, k, core].astype(jnp.float32) + self.other[:, k].astype(jnp.float32)
            self.part[:, k, core] = total.astype(self.part.dtype)
            return carry

        lax.fori_loop(0, self.place.chips, one, 0)


class Along:
    def __init__(self, place, links, share, landing):
        self.landing = landing
        self.messages = []
        for k in range(1, place.chips):
            there = lax.rem(place.z + k, place.chips)
            self.messages.append(
                Message(links, share(there), landing.at[k - 1], place.at(shard=place.hop(k)))
            )

    def total(self, mine):
        total = mine.astype(jnp.float32)
        for k, message in enumerate(self.messages):
            message.arrive()
            total = total + self.landing[k].astype(jnp.float32)
        return total


class Deal:
    def __init__(self, place, links, pairs):
        self.messages = []
        for part, dst in pairs:
            self.messages.append(links.keep(part(place.rank), dst))
            for rank in (place.first, place.second, place.across):
                self.messages.append(Message(links, part(rank), dst, place.at(rank=rank)))

    def arrive(self):
        for message in self.messages:
            message.arrive()


def block_of(r):
    return jnp.where(r == 0, 0, jnp.minimum(r + 1, GRAN - 1))


def forward_kernel(
    chips,
    tokens,
    suffix,
    small,
    w_query,
    w_key,
    w_value,
    w_out,
    w_up,
    w_down,
    comb,
    mask,
    cosine,
    sine,
    all_tokens,
    attn_in,
    qkv_rot,
    mixed_low,
    hidden,
    all_ffn_in,
    gains,
    incoming,
    all_qkv,
    all_out,
    all_up,
    all_down,
    tokens_v,
    attn_v,
    rot_v,
    mixed_v,
    qkv_v,
    out_v,
    partial,
    landing,
    passing,
    ffn_v,
    all_small,
    send,
    recv,
    near,
):
    place = Place(chips)
    links = Links(send, recv, near)
    place.greet(plane=True, sibling=True, chain=True)
    rank, shard = place.rank, place.shard
    ranks, tok_rows, model_width = tokens_v.shape
    head_cols = w_query.shape[1] // ranks
    heads = head_cols // HEAD_DIM

    def columns(weight, width):
        return lambda r: weight.at[:, pl.ds(pl.multiple_of(r * width, 128), width)]

    own_qkv = all_qkv.at[rank, shard]
    pairs = [(lambda r: small, all_small.at[rank, shard])]
    for i, weight in enumerate((w_query, w_key, w_value)):
        pairs.append(
            (columns(weight, head_cols), own_qkv.at[:, pl.ds(i * head_cols, head_cols)])
        )
    deal_qkv = Deal(place, links, pairs)
    gather = PlaneGather(place, links, tokens, tokens_v, 2)
    deal_up = Deal(place, links, [(columns(w_up, w_up.shape[1] // ranks), all_up.at[rank, shard])])
    links.keep(w_out, all_out.at[shard])
    links.keep(w_down, all_down.at[shard])
    out_slot = lambda f: all_out.at[f]
    down_slot = lambda f: all_down.at[f]
    small_slot = lambda f: all_small.at[:, f]
    qkv_slot = lambda f: all_qkv.at[:, f]
    up_slot = lambda f: all_up.at[:, f]
    chain_out = Chain(place, links, w_out, out_slot)
    deal_qkv.arrive()
    chain_small = Chain(place, links, small_slot(shard), small_slot)
    chain_qkv = Chain(place, links, qkv_slot(shard), qkv_slot)
    chain_small.step(1)
    gather.relay(0)
    chain_small.step(2)
    chain_out.step(1)
    chain_small.step(3)
    gather.relay(1)
    chain_qkv.step(1)
    chain_small.finish()
    chain_out.step(2)

    def wide(rows):
        spread = jnp.dot(rows, comb[...], preferred_element_type=jnp.float32)
        return jnp.sum(spread * mask[...], axis=0, keepdims=True)

    devices = ranks * 2 * chips
    for i in range(5):
        gains[i : i + 1] = wide(all_small[:, :, i].reshape(devices, 128))
    up_rows = all_small[rank, :, 5:9].astype(jnp.float32).reshape(devices, 128)
    gains[5:6] = wide(up_rows.astype(jnp.bfloat16))
    gains[6:8] = jnp.zeros((2, model_width), jnp.float32)

    def norm_block(r):
        def rows_of(cut):
            value, unused = normed(tokens_v[r, cut].astype(jnp.float32))
            attn_v[r, cut] = (value * gains[0:1] + gains[1:2]).astype(jnp.bfloat16)

        in_rows(tok_rows, 64, rows_of)

    for copy in links.open_near:
        copy.arrive()
    norm_block(rank)
    norm_block(place.first)
    chain_qkv.step(2)
    deal_up.arrive()
    chain_up = Chain(place, links, up_slot(shard), up_slot)
    gather.finish()
    norm_block(place.second)
    norm_block(place.across)
    links.keep(tokens_v, all_tokens)
    links.keep(attn_v, attn_in)
    chain_out.step(3)
    chain_out.finish()
    load_out = links.keep(all_out, out_v)
    chain_qkv.step(3)
    chain_qkv.finish()
    load_qkv = links.keep(all_qkv, qkv_v)
    links.keep(suffix.at[block_of(rank)], incoming.at[0, rank])
    links.keep(suffix.at[1], incoming.at[1, rank], rank == 0)
    dealt = []
    for r in (place.first, place.second, place.across):
        dealt.append(
            Message(links, suffix.at[block_of(r)], incoming.at[0, rank], place.at(rank=r))
        )
    load_qkv.arrive()

    def project(r, carry):
        rows = pl.ds(pl.multiple_of(r * tok_rows, tok_rows), tok_rows)
        for part in range(3):
            cut = slice(part * head_cols, (part + 1) * head_cols)
            weight = qkv_v[:, :, :, cut].reshape(model_width, head_cols)
            value = jnp.dot(attn_v[r], weight, preferred_element_type=jnp.float32)
            if part < 2:
                turned = []
                for h in range(heads):
                    head = value[:, h * HEAD_DIM : (h + 1) * HEAD_DIM]
                    turned.append(turn_half(head, cosine[rows], sine[rows]))
                value = jnp.concatenate(turned, axis=1)
                if part == 0:
                    value = value * HEAD_DIM ** (-0.5)
            rot_v[r, :, cut] = value.astype(jnp.bfloat16)
        return carry

    lax.fori_loop(0, ranks, project, 0)
    links.keep(rot_v, qkv_rot)
    chain_up.step(1)
    load_out.arrive()

    def attend_block(r):
        def head(h, carry):
            def part(i):
                return pl.ds(pl.multiple_of(i * head_cols + h * HEAD_DIM, HEAD_DIM), HEAD_DIM)

            scores = back_product(rot_v[r, :, part(0)], rot_v[:, :, part(1)].reshape(-1, HEAD_DIM))
            row = lax.broadcasted_iota(jnp.int32, scores.shape, 0) + r * tok_rows
            column = lax.broadcasted_iota(jnp.int32, scores.shape, 1)
            scores = jnp.where(row >= column, scores, masked_score)
            raised = jnp.exp(scores - jnp.max(scores, axis=-1, keepdims=True))
            scale = 1.0 / jnp.sum(raised, axis=-1, keepdims=True)
            probs = (raised * scale).astype(jnp.bfloat16)
            mixed = product(probs, rot_v[:, :, part(2)].reshape(-1, HEAD_DIM))
            mixed_v[r, :, part(0)] = mixed.astype(jnp.bfloat16)
            return carry

        lax.fori_loop(0, heads, head, 0)
        weight = out_v[...].reshape(head_cols, model_width)
        partial[r] = product(mixed_v[r], weight).astype(jnp.bfloat16)

    scatter = PlaneScatter(place, links, partial, landing, passing)
    attend_block(place.across)
    scatter.send_far()
    attend_block(place.first)
    scatter.send_near()
    chain_up.step(2)
    chain_down = Chain(place, links, w_down, down_slot)
    attend_block(place.second)
    scatter.relay()
    attend_block(rank)
    links.keep(mixed_v, mixed_low)
    chain_up.step(3)
    chain_down.step(1)
    scatter.settle()

    def second_norm(cut):
        value = scatter.total(cut) + tokens_v[rank, cut].astype(jnp.float32)
        hidden[cut] = value
        value, unused = normed(value)
        ffn_v[cut] = (value * gains[2:3] + gains[3:4]).astype(jnp.bfloat16)

    in_rows(tok_rows, 64, second_norm)
    gather = PlaneGather(place, links, ffn_v, all_ffn_in, 2)
    dealt_more = []
    for r in (place.first, place.second, place.across):
        dealt_more.append(
            Message(links, suffix.at[1], incoming.at[1, rank], place.at(rank=r), r == 0, rank == 0)
        )
    chain_down.step(2)
    gather.relay(0)
    gather.relay(1)
    chain_up.finish()
    chain_down.step(3)
    gather.finish()
    chain_down.finish()
    for message in dealt + dealt_more:
        message.arrive()
    links.drain()


def middle_kernel(
    chips,
    all_ffn_in,
    incoming,
    w_up,
    w_down,
    hidden,
    cotangent_sum,
    gains,
    grad_hidden,
    sums,
    share_down,
    share_up,
    terms,
    ffn_v,
    csum_v,
    up_v,
    down_v,
    gated_v,
    grad_v,
    part_down,
    other_down,
    other_up,
    terms_v,
    partial,
    landing,
    passing,
    send,
    recv,
    near,
):
    place = Place(chips)
    links = Links(send, recv, near)
    rank = place.rank
    ranks, tok_rows, model_width = ffn_v.shape
    ff_cols = up_v.shape[-1]
    half = ff_cols // 2
    load_up = links.keep(w_up, up_v)
    order = (place.across, place.first, place.second, rank)
    load_ffn = [links.keep(all_ffn_in.at[t], ffn_v.at[t]) for t in order]
    load_down = links.keep(w_down, down_v)
    load_csum = [links.keep(incoming.at[0, t], csum_v.at[0, t]) for t in order]
    load_more = links.keep(incoming.at[1], csum_v.at[1], rank == 0)
    place.greet(plane=True, sibling=True)
    slots = (0, jnp.where(rank == 0, 1, 0))
    sums[...] = jnp.zeros_like(sums)
    load_up.arrive()
    scatter = PlaneScatter(place, links, partial, landing, passing)

    def block(k):
        t = order[k]
        load_ffn[k].arrive()
        for i in range(2):
            cut = slice(i * half, (i + 1) * half)
            weight = up_v[:, :, :, :, cut].reshape(model_width, half)
            pre = product(ffn_v[t], weight) + gains[5:6, cut]
            square = pre * pre
            tangent = jnp.tanh(0.7978845608028654 * pre * (1.0 + 0.044715 * square))
            gated_v[t, :, cut] = (0.5 * pre * (1.0 + tangent)).astype(jnp.bfloat16)
            slope = 0.5 * (1.0 + tangent) + 0.5 * pre * (1.0 - tangent * tangent) * (
                0.7978845608028654 * (1.0 + 3.0 * 0.044715 * square)
            )
            if k == 0 and i == 0:
                load_down.arrive()
                load_more.arrive()
            if i == 0:
                load_csum[k].arrive()
            weight = down_v[4 * i : 4 * i + 4].reshape(half, model_width)
            grad = back_product(csum_v[slots[i], t], weight) * slope
            grad_v[t, :, cut] = grad.astype(jnp.bfloat16)
            sums[3:4, cut] += jnp.sum(grad, axis=0, keepdims=True)

        def back(i, carry):
            own = model_width // ranks
            value = back_product(grad_v[t], up_v[i].reshape(own, ff_cols))
            partial[t, :, pl.ds(pl.multiple_of(i * own, 128), own)] = value.astype(jnp.bfloat16)
            return carry

        lax.fori_loop(0, ranks, back, 0)

    block(0)
    scatter.send_far()
    block(1)
    scatter.send_near()
    block(2)
    scatter.relay()
    block(3)

    def down_tile(i, carry):
        rows = ff_cols // ranks
        left = gated_v[:, :, pl.ds(pl.multiple_of(i * rows, 128), rows)].reshape(-1, rows)
        slot = jnp.where(i < 2, slots[0], slots[1])
        value = gram_product(left, csum_v[slot].reshape(-1, model_width))
        part_down[0, i] = value.astype(jnp.bfloat16).reshape(part_down.shape[2:])
        return carry

    lax.fori_loop(0, ranks, down_tile, 0)
    beside_down = Beside(place, links, part_down, other_down)

    def up_tile(i, carry):
        rows = model_width // ranks
        left = ffn_v[:, :, pl.ds(pl.multiple_of(i * rows, 128), rows)].reshape(-1, rows)
        value = gram_product(left, grad_v[...].reshape(-1, ff_cols))
        up_v[i] = value.astype(jnp.bfloat16).reshape(up_v.shape[1:])
        return carry

    lax.fori_loop(0, ranks, up_tile, 0)
    beside_up = Beside(place, links, up_v, other_up)
    beside_down.add()
    links.keep(part_down.at[:, :, place.core], share_down)

    def term_tile(t, carry):
        low_term = product(gated_v[t, :, :half], down_v[:4].reshape(half, model_width))
        high_term = product(gated_v[t, :, half:], down_v[4:].reshape(half, model_width))
        terms_v[1, t] = high_term.astype(jnp.bfloat16)
        low_term = low_term + high_term * jnp.where(rank == 0, 0.0, 1.0)
        terms_v[0, t] = low_term.astype(jnp.bfloat16)
        return carry

    lax.fori_loop(0, ranks, term_tile, 0)
    links.keep(terms_v, terms)
    beside_up.add()
    links.keep(up_v.at[:, :, place.core], share_up)
    scatter.settle()

    def norm_back(cut):
        value, inverse = normed(hidden[cut])
        grad = scatter.total(cut)
        sums[0:1] += jnp.sum(grad * value, axis=0, keepdims=True)
        sums[1:2] += jnp.sum(grad, axis=0, keepdims=True)
        sums[2:3] += jnp.sum(cotangent_sum[cut], axis=0, keepdims=True)
        grad_hidden[cut] = cotangent_sum[cut] + norm_backward(grad, value, inverse, gains[2:3])

    in_rows(tok_rows, 64, norm_back)
    links.drain()


def last_kernel(
    chips,
    branch,
    share_down,
    share_up,
    terms,
    qkv_rot,
    mixed_low,
    w_out,
    w_qkv,
    attn_in,
    all_tokens,
    grad_hidden,
    hidden,
    gains,
    sums,
    comb,
    mask,
    cosine,
    sine,
    activations,
    grad_tokens,
    sum_down,
    sum_out,
    sum_up,
    sum_qkv,
    sum_small,
    branch_v,
    rot_v,
    mixed_v,
    grad_mixed_v,
    out_v,
    qkv_v,
    attn_v,
    tokens_v,
    grad_v,
    key_sum,
    value_sum,
    partial,
    landing,
    passing,
    term_in,
    extra_in,
    mine_down,
    land_down,
    mine_up,
    land_up,
    turn_up,
    part_out,
    other_out,
    land_out,
    part_qkv,
    other_qkv,
    land_qkv,
    turn_qkv,
    part_small,
    other_small,
    land_small,
    turn_small,
    land_sums,
    more_sums,
    send,
    recv,
    near,
):
    place = Place(chips)
    links = Links(send, recv, near)
    rank, z = place.rank, place.z
    ranks, tok_rows, model_width = branch_v.shape
    head_cols = mixed_v.shape[2]
    heads = head_cols // HEAD_DIM
    load_out = links.keep(w_out, out_v)
    load_mixed = links.keep(mixed_low, mixed_v)
    load_rot = links.keep(qkv_rot, rot_v)
    load_qkv = links.keep(w_qkv, qkv_v)
    load_attn = links.keep(attn_in, attn_v)
    load_tokens = links.keep(all_tokens, tokens_v)
    load_down = links.keep(share_down.at[:, z], mine_down)
    load_up = links.keep(share_up.at[:, z], mine_up)
    place.greet(plane=True, sibling=True, ring=True)
    gather = PlaneGather(place, links, branch, branch_v, 2)
    along_down = Along(place, links, lambda there: share_down.at[:, there], land_down)
    along_up = Along(place, links, lambda there: share_up.at[:, there], land_up)
    load_out.arrive()

    def mix_back(t):
        weight = out_v[...].reshape(head_cols, model_width)
        grad_mixed_v[t] = back_product(branch_v[t], weight).astype(jnp.bfloat16)

    links.open_near[8].arrive()
    mix_back(rank)
    gather.relay(0)
    gather.relay(1)
    mix_back(place.first)
    gather.finish()
    mix_back(place.second)
    mix_back(place.across)
    links.keep(terms.at[0, rank], term_in.at[rank])
    links.keep(terms.at[1, rank], extra_in, rank == 0)
    dealt = []
    for r in (place.first, place.second, place.across):
        dealt.append(Message(links, terms.at[0, r], term_in.at[rank], place.at(rank=r)))
    load_mixed.arrive()
    value = gram_product(
        mixed_v[...].reshape(-1, head_cols), branch_v[...].reshape(-1, model_width)
    )
    part_out[0] = value.astype(jnp.bfloat16).reshape(part_out.shape[1:])
    beside_out = Beside(place, links, part_out, other_out)
    load_rot.arrive()

    def head(h, carry):
        def part(i):
            return pl.ds(pl.multiple_of(i * head_cols + h * HEAD_DIM, HEAD_DIM), HEAD_DIM)

        for t in range(ranks - 1, -1, -1):
            count = t + 1
            keys = rot_v[:count, :, part(1)].reshape(-1, HEAD_DIM)
            values = rot_v[:count, :, part(2)].reshape(-1, HEAD_DIM)
            queries = rot_v[t, :, part(0)]
            grad_mixed = grad_mixed_v[t, :, part(0)]
            scores = back_product(queries, keys)
            row = lax.broadcasted_iota(jnp.int32, scores.shape, 0) + t * tok_rows
            column = lax.broadcasted_iota(jnp.int32, scores.shape, 1)
            scores = jnp.where(row >= column, scores, masked_score)
            raised = jnp.exp(scores - jnp.max(scores, axis=-1, keepdims=True))
            probs = raised * (1.0 / jnp.sum(raised, axis=-1, keepdims=True))
            delta = jnp.sum(
                grad_mixed.astype(jnp.float32) * mixed_v[t, :, part(0)].astype(jnp.float32),
                axis=-1,
                keepdims=True,
            )
            grad_scores = (probs * (back_product(grad_mixed, values) - delta)).astype(jnp.bfloat16)
            rows = pl.ds(t * tok_rows, tok_rows)
            grad_query = product(grad_scores, keys)
            grad_query = turn_half(grad_query, cosine[rows], -sine[rows]) * HEAD_DIM ** (-0.5)
            grad_v[t, :, part(0)] = grad_query.astype(jnp.bfloat16)
            grad_key = gram_product(grad_scores, queries)
            grad_value = gram_product(probs.astype(jnp.bfloat16), grad_mixed)
            seen = count * tok_rows
            if t == ranks - 1:
                key_sum[...] = grad_key
                value_sum[...] = grad_value
            else:
                key_sum[:seen] += grad_key
                value_sum[:seen] += grad_value
        grad_key = turn_half(key_sum[...], cosine[...], -sine[...]).astype(jnp.bfloat16)
        grad_v[:, :, part(1)] = grad_key.reshape(ranks, tok_rows, HEAD_DIM)
        grad_value = value_sum[...].astype(jnp.bfloat16)
        grad_v[:, :, part(2)] = grad_value.reshape(ranks, tok_rows, HEAD_DIM)
        return carry

    lax.fori_loop(0, heads, head, 0)
    beside_out.add()
    along_out = Along(place, links, lambda there: part_out.at[:, there, place.core], land_out)
    load_qkv.arrive()
    load_attn.arrive()
    load_tokens.arrive()

    def qkv_tile(i, carry):
        rows = model_width // ranks
        left = attn_v[:, :, pl.ds(pl.multiple_of(i * rows, 128), rows)].reshape(-1, rows)
        value = gram_product(left, grad_v[...].reshape(-1, 3 * head_cols))
        part_qkv[i] = value.astype(jnp.bfloat16).reshape(part_qkv.shape[1:])
        return carry

    lax.fori_loop(0, ranks, qkv_tile, 0)
    beside_qkv = Beside(place, links, part_qkv, other_qkv)
    scatter = PlaneScatter(place, links, partial, landing, passing)
    more_sums[...] = jnp.zeros_like(more_sums)

    def attn_back(t):
        def tile(i, carry):
            own = model_width // ranks
            value = back_product(grad_v[t], qkv_v[i].reshape(own, 3 * head_cols))
            partial[t, :, pl.ds(pl.multiple_of(i * own, 128), own)] = value.astype(jnp.bfloat16)
            return carry

        lax.fori_loop(0, ranks, tile, 0)

        def count(cut):
            value, unused = normed(tokens_v[t, cut].astype(jnp.float32))
            grad = partial[t, cut].astype(jnp.float32)
            more_sums[0:1] += jnp.sum(grad * value, axis=0, keepdims=True)
            more_sums[1:2] += jnp.sum(grad, axis=0, keepdims=True)

        return count

    count_across = attn_back(place.across)
    scatter.send_far()
    count_first = attn_back(place.first)
    scatter.send_near()
    beside_qkv.add()
    along_qkv = Along(place, links, lambda there: part_qkv.at[:, there, place.core], land_qkv)
    count_second = attn_back(place.second)
    scatter.relay()
    count_own = attn_back(rank)
    for count in (count_across, count_first, count_second, count_own):
        in_rows(tok_rows, 64, count)

    def pieces(row):
        spread = (row * mask[...]).astype(jnp.float32)
        return lax.dot_general(
            spread,
            comb[...].astype(jnp.float32),
            (((1,), (1,)), ((), ())),
            precision=lax.Precision.HIGHEST,
            preferred_element_type=jnp.float32,
        )

    part_small[...] = jnp.zeros_like(part_small)
    rows = (more_sums[0:1], more_sums[1:2], sums[0:1], sums[1:2], sums[2:3])
    for k, row in enumerate(rows):
        part_small[:, :, :, k] = pieces(row).reshape(ranks, chips, 2, 128)
    part_small[rank, :, :, 5:9] = pieces(sums[3:4]).reshape(chips, 2, 4, 128)
    beside_small = Beside(place, links, part_small, other_small)
    dealt_more = []
    for r in (place.first, place.second, place.across):
        dealt_more.append(
            Message(links, terms.at[1, r], extra_in, place.at(rank=r), rank == 0, r == 0)
        )
    load_down.arrive()
    sum_down[...] = along_down.total(mine_down[...])[0]
    load_up.arrive()
    turn_up[...] = along_up.total(mine_up[...]).astype(jnp.bfloat16)
    deal_up = Deal(place, links, [(lambda r: turn_up.at[r], sum_up.at[rank])])
    beside_small.add()
    along_small = Along(place, links, lambda there: part_small.at[:, there, place.core], land_small)
    sum_out[...] = along_out.total(part_out[:, z, place.core])[0]
    scatter.settle()

    def norm_back(cut):
        value, inverse = normed(tokens_v[rank, cut].astype(jnp.float32))
        grad = norm_backward(scatter.total(cut), value, inverse, gains[0:1])
        grad_tokens[cut] = (grad_hidden[cut] + grad).astype(jnp.bfloat16)

    in_rows(tok_rows, 64, norm_back)
    turn_small[...] = along_small.total(part_small[:, z, place.core])
    deal_small = Deal(place, links, [(lambda r: turn_small.at[r], land_sums.at[rank])])
    turn_qkv[...] = along_qkv.total(part_qkv[:, z, place.core]).astype(jnp.bfloat16)
    deal_qkv = Deal(place, links, [(lambda r: turn_qkv.at[r], sum_qkv.at[rank])])
    for copy in links.open_near:
        copy.arrive()
    for message in dealt + dealt_more:
        message.arrive()

    def add_terms(cut):
        total = hidden[cut] + gains[4:5] + term_in[0, cut].astype(jnp.float32)
        activations[0, cut] = total.astype(jnp.bfloat16)
        total = total + extra_in[cut].astype(jnp.float32)
        activations[1, cut] = total.astype(jnp.bfloat16)
        total = total + term_in[1, cut].astype(jnp.float32)
        activations[2, cut] = total.astype(jnp.bfloat16)
        total = total + term_in[2, cut].astype(jnp.float32) + term_in[3, cut].astype(jnp.float32)
        activations[3, cut] = total.astype(jnp.bfloat16)

    in_rows(tok_rows, 64, add_terms)
    deal_up.arrive()
    deal_small.arrive()
    sum_small[...] = land_sums[0] + land_sums[1] + land_sums[2] + land_sums[3]
    deal_qkv.arrive()
    links.drain()


ANY = pl.BlockSpec(memory_space=pl.ANY)
ON_CORE = pl.BlockSpec(memory_space=pltpu.VMEM)


def connected(kernel, number, outs, out_specs, in_specs, scratch, operands):
    return pl.pallas_call(
        kernel,
        out_shape=outs,
        in_specs=in_specs,
        out_specs=out_specs,
        scratch_shapes=scratch + LINK_SCRATCH,
        compiler_params=pltpu.CompilerParams(
            collective_id=number, has_side_effects=True, vmem_limit_bytes=63 * 2**20
        ),
    )(*operands)


def array(shape, dtype=jnp.bfloat16):
    return jax.ShapeDtypeStruct(shape, dtype)


def local_split(ranks, shards, *arguments):
    chips = shards // 2
    (
        tokens,
        cotangent,
        norm1_gain,
        norm1_bias,
        query_weight,
        key_weight,
        value_weight,
        out_weight,
        norm2_gain,
        norm2_bias,
        up_weight,
        up_bias,
        down_weight,
        down_bias,
    ) = arguments
    model_width = tokens.shape[2]
    tok_rows = tokens.shape[1]
    seq_len = tok_rows * ranks
    own = query_weight.shape[0]
    heads = HEADS // ranks
    head_cols = heads * HEAD_DIM
    ff_cols = FF // ranks
    scaling = HEAD_DIM ** (-0.5)
    rank = lax.axis_index("dp")

    grads_out = cotangent.reshape(GRAN, tok_rows, model_width).astype(jnp.float32)
    suffix = [grads_out[GRAN - 1]]
    for level_idx in range(GRAN - 2, -1, -1):
        suffix.insert(0, suffix[0] + grads_out[level_idx])
    cotangent_sum = suffix[0]
    suffix = jnp.stack([s.astype(jnp.bfloat16) for s in suffix])

    rows = [
        jnp.pad(v.reshape(-1, own), ((0, 0), (0, 128 - own)))
        for v in (norm1_gain, norm1_bias, norm2_gain, norm2_bias, down_bias, up_bias)
    ]
    small = jnp.pad(jnp.concatenate(rows), ((0, 16 - 5 - up_bias.shape[0] // own), (0, 0)))
    column = jnp.arange(model_width, dtype=jnp.int32)
    comb = (column[None, :] % own == jnp.arange(128, dtype=jnp.int32)[:, None]).astype(jnp.bfloat16)
    mask = column[None, :] // own == jnp.arange(ranks * shards, dtype=jnp.int32)[:, None]
    mask = mask.astype(jnp.float32)
    cosine, sine = rotary_tables(jnp.arange(seq_len).astype(jnp.float32), HEAD_DIM // 2)
    cosine, sine = cosine[:, 0], sine[:, 0]
    cosine = jnp.concatenate([cosine, cosine], axis=1)
    sine = jnp.concatenate([-sine, sine], axis=1)
    own_tokens = tokens.reshape(tok_rows, model_width)
    blocks_low = array((ranks, tok_rows, model_width))
    down_rows = down_weight.shape[0]
    vmem = pltpu.VMEM
    (
        all_tokens,
        attn_in,
        qkv_rot,
        mixed_low,
        hidden,
        ffn_in,
        gains,
        incoming,
        w_qkv,
        w_out,
        w_up,
        w_down,
    ) = connected(
        functools.partial(forward_kernel, chips),
        1,
        (
            blocks_low,
            blocks_low,
            array((ranks, tok_rows, 3 * head_cols)),
            array((ranks, tok_rows, head_cols)),
            array((tok_rows, model_width), jnp.float32),
            blocks_low,
            array((8, model_width), jnp.float32),
            array((2, ranks, tok_rows, model_width)),
            array((ranks, shards, own, 3 * head_cols)),
            array((shards, own, model_width)),
            array((ranks, shards, own, ff_cols)),
            array((shards, down_rows, model_width)),
        ),
        [ANY] * 4 + [ON_CORE, ANY, ON_CORE] + [ANY] * 5,
        [ANY] * 9 + [ON_CORE] * 4,
        [
            vmem((ranks, tok_rows, model_width), jnp.bfloat16),
            vmem((ranks, tok_rows, model_width), jnp.bfloat16),
            vmem((ranks, tok_rows, 3 * head_cols), jnp.bfloat16),
            vmem((ranks, tok_rows, head_cols), jnp.bfloat16),
            vmem((ranks, shards, own, 3 * head_cols), jnp.bfloat16),
            vmem((shards, own, model_width), jnp.bfloat16),
            vmem((ranks, tok_rows, model_width), jnp.bfloat16),
            vmem((3, tok_rows, model_width), jnp.bfloat16),
            vmem((tok_rows, model_width), jnp.bfloat16),
            vmem((tok_rows, model_width), jnp.bfloat16),
            vmem((ranks, shards, 16, 128), jnp.bfloat16),
        ],
        (
            own_tokens,
            suffix,
            small,
            query_weight,
            key_weight,
            value_weight,
            out_weight,
            up_weight,
            down_weight,
            comb,
            mask,
            cosine,
            sine,
        ),
    )
    low = jnp.bfloat16
    f32 = jnp.float32
    grad_hidden, sums, share_down, share_up, terms = connected(
        functools.partial(middle_kernel, chips),
        2,
        (
            array((tok_rows, model_width), f32),
            array((8, model_width), f32),
            array((1, chips, down_rows, model_width)),
            array((ranks, chips, own, ff_cols)),
            array((2, ranks, tok_rows, model_width)),
        ),
        [ON_CORE] * 2 + [ANY] * 3,
        [ANY] * 4 + [ON_CORE] * 3,
        [
            vmem((ranks, tok_rows, model_width), low),
            vmem((2, ranks, tok_rows, model_width), low),
            vmem((ranks, chips, 2, own, ff_cols), low),
            vmem((shards, down_rows, model_width), low),
            vmem((ranks, tok_rows, ff_cols), low),
            vmem((ranks, tok_rows, ff_cols), low),
            vmem((1, chips, 2, down_rows, model_width), low),
            vmem((1, chips, down_rows, model_width), low),
            vmem((ranks, chips, own, ff_cols), low),
            vmem((2, ranks, tok_rows, model_width), low),
            vmem((ranks, tok_rows, model_width), low),
            vmem((3, tok_rows, model_width), low),
            vmem((tok_rows, model_width), low),
        ],
        (
            ffn_in,
            incoming,
            w_up.reshape(ranks, chips, 2, own, ff_cols),
            w_down,
            hidden,
            cotangent_sum,
            gains,
        ),
    )
    (
        activations,
        grad_inputs,
        sum_down,
        sum_out,
        sum_up,
        sum_qkv,
        small_sums,
    ) = connected(
        functools.partial(last_kernel, chips),
        3,
        (
            array((GRAN, tok_rows, model_width)),
            array((tok_rows, model_width)),
            array((down_rows, model_width), f32),
            array((own, model_width), f32),
            array((ranks, own, ff_cols)),
            array((ranks, own, 3 * head_cols)),
            array((16, 128), f32),
        ),
        [ON_CORE] * 4 + [ANY, ANY, ON_CORE],
        [ANY] * 10 + [ON_CORE] * 8,
        [
            vmem((ranks, tok_rows, model_width), low),
            vmem((ranks, tok_rows, 3 * head_cols), low),
            vmem((ranks, tok_rows, head_cols), low),
            vmem((ranks, tok_rows, head_cols), low),
            vmem((shards, own, model_width), low),
            vmem((ranks, shards, own, 3 * head_cols), low),
            vmem((ranks, tok_rows, model_width), low),
            vmem((ranks, tok_rows, model_width), low),
            vmem((ranks, tok_rows, 3 * head_cols), low),
            vmem((seq_len, HEAD_DIM), f32),
            vmem((seq_len, HEAD_DIM), f32),
            vmem((ranks, tok_rows, model_width), low),
            vmem((3, tok_rows, model_width), low),
            vmem((tok_rows, model_width), low),
            vmem((ranks, tok_rows, model_width), low),
            vmem((tok_rows, model_width), low),
            vmem((1, down_rows, model_width), low),
            vmem((chips - 1, 1, down_rows, model_width), low),
            vmem((ranks, own, ff_cols), low),
            vmem((chips - 1, ranks, own, ff_cols), low),
            vmem((ranks, own, ff_cols), low),
            vmem((1, chips, 2, own, model_width), low),
            vmem((1, chips, own, model_width), low),
            vmem((chips - 1, 1, own, model_width), low),
            vmem((ranks, chips, 2, own, 3 * head_cols), low),
            vmem((ranks, chips, own, 3 * head_cols), low),
            vmem((chips - 1, ranks, own, 3 * head_cols), low),
            vmem((ranks, own, 3 * head_cols), low),
            vmem((ranks, chips, 2, 16, 128), f32),
            vmem((ranks, chips, 16, 128), f32),
            vmem((chips - 1, ranks, 16, 128), f32),
            vmem((ranks, 16, 128), f32),
            vmem((ranks, 16, 128), f32),
            vmem((8, model_width), f32),
        ],
        (
            grad_hidden.astype(low),
            share_down,
            share_up,
            terms,
            qkv_rot,
            mixed_low,
            w_out,
            w_qkv,
            attn_in,
            all_tokens,
            grad_hidden,
            hidden,
            gains,
            sums,
            comb,
            mask,
            cosine,
            sine,
        ),
    )
    activations = activations.reshape(GRAN, 1, tok_rows, model_width)
    sum_up = sum_up.astype(f32).transpose(1, 0, 2).reshape(own, FF)
    sum_qkv = sum_qkv.astype(f32).transpose(1, 0, 2)
    sum_query, sum_key, sum_value = (
        sum_qkv[:, :, i * head_cols : (i + 1) * head_cols].reshape(own, model_width)
        for i in range(3)
    )
    gain_sums = [small_sums[i, :own] for i in range(5)]
    sum_up_bias = small_sums[5:9, :own].reshape(-1)
    return (
        activations,
        grad_inputs.reshape(1, tok_rows, model_width),
        gain_sums[0],
        gain_sums[1],
        sum_query,
        sum_key,
        sum_value,
        sum_out,
        gain_sums[2],
        gain_sums[3],
        sum_up,
        sum_up_bias,
        sum_down,
        gain_sums[4],
    )


def solution(mesh):
    placed = (
        P("fsdp", "dp", None),
        P(None, "fsdp", "dp", None),
        P(("dp", "fsdp")),
        P(("dp", "fsdp")),
        P(("dp", "fsdp"), None),
        P(("dp", "fsdp"), None),
        P(("dp", "fsdp"), None),
        P(("dp", "fsdp"), None),
        P(("dp", "fsdp")),
        P(("dp", "fsdp")),
        P(("dp", "fsdp"), None),
        P(("dp", "fsdp")),
        P(("dp", "fsdp"), None),
        P(("dp", "fsdp")),
    )
    ranks, shards = mesh.shape["dp"], mesh.shape["fsdp"]
    local = local_gathered
    if ranks == 4 and shards % 2 == 0:
        local = functools.partial(local_split, ranks, shards)
    return jax.shard_map(
        local,
        mesh=mesh,
        in_specs=placed,
        out_specs=(
            P(None, "fsdp", "dp", None),
            P("fsdp", "dp", None),
            P(("dp", "fsdp")),
            P(("dp", "fsdp")),
            P(("dp", "fsdp"), None),
            P(("dp", "fsdp"), None),
            P(("dp", "fsdp"), None),
            P(("dp", "fsdp"), None),
            P(("dp", "fsdp")),
            P(("dp", "fsdp")),
            P(("dp", "fsdp"), None),
            P(("dp", "fsdp")),
            P(("dp", "fsdp"), None),
            P(("dp", "fsdp")),
        ),
        check_vma=False,
    )
```

```python
import functools
import math

import jax
import jax.numpy as jnp
import numpy as np
from jax import lax
from jax.experimental import pallas as pl
from jax.experimental.pallas import tpu as pltpu
from jax.sharding import PartitionSpec as P

HEADS = 12
HEAD_DIM = 128
FF = 6144
GRAN = 4


epsilon = 1e-05
masked_score = -1e30


def product(left, right):
    return jnp.dot(left, right, preferred_element_type=jnp.float32)


def gram_product(left, right):
    return lax.dot_general(
        left, right, (((0,), (0,)), ((), ())), preferred_element_type=jnp.float32
    )


def back_product(left, right):
    return lax.dot_general(
        left, right, (((1,), (1,)), ((), ())), preferred_element_type=jnp.float32
    )


def norm_parts(values):
    centred = values - jnp.mean(values, axis=-1, keepdims=True)
    inverse = lax.rsqrt(jnp.mean(centred * centred, axis=-1, keepdims=True) + epsilon)
    return (centred * inverse, inverse)


def norm_backward(grad_normed, normed, inverse, gain):
    scaled = grad_normed * gain
    return inverse * (
        scaled
        - jnp.mean(scaled, axis=-1, keepdims=True)
        - normed * jnp.mean(scaled * normed, axis=-1, keepdims=True)
    )


def gelu_value(values):
    return (
        0.5
        * values
        * (1.0 + jnp.tanh(0.7978845608028654 * (values + 0.044715 * values * values * values)))
    )


def gelu_grad(values):
    tangent = jnp.tanh(0.7978845608028654 * (values + 0.044715 * values * values * values))
    return 0.5 * (1.0 + tangent) + 0.5 * values * (1.0 - tangent * tangent) * 0.7978845608028654 * (
        1.0 + 3.0 * 0.044715 * values * values
    )


def rotary_tables(positions, half_size):
    ladder = jnp.arange(half_size).astype(jnp.float32)
    inverse = jnp.exp(ladder * (-math.log(10000.0) / half_size))
    angles = positions[:, None] * inverse[None, :]
    return (jnp.cos(angles)[:, None, :], jnp.sin(angles)[:, None, :])


def rotate(values, cosine, sine):
    half_size = values.shape[-1] // 2
    first = values[..., :half_size]
    second = values[..., half_size:]
    return jnp.concatenate(
        [first * cosine - second * sine, second * cosine + first * sine], axis=-1
    )


def block_scores(queries, positions, key_block, start_row):
    block_rows = key_block.shape[0]
    scores = jnp.einsum("qhd,khd->hqk", queries, key_block, preferred_element_type=jnp.float32)
    key_positions = start_row + jnp.arange(block_rows, dtype=jnp.int32)
    visible = positions[None, :, None] >= key_positions[None, None, :]
    return (jnp.where(visible, scores, masked_score), visible)


def key_blocking(keys_all, values_all, key_offset):
    seq_len = keys_all.shape[0]
    block_rows = min(512, seq_len)
    block_count = seq_len // block_rows
    key_blocks = keys_all.reshape(block_count, block_rows, HEADS, HEAD_DIM)
    value_blocks = values_all.reshape(block_count, block_rows, HEADS, HEAD_DIM)
    starts = key_offset + jnp.arange(block_count, dtype=jnp.int32) * block_rows
    return (key_blocks, value_blocks, starts)


def attend(queries, keys_all, values_all, positions):
    tok_rows = queries.shape[0]
    key_blocks, value_blocks, starts = key_blocking(keys_all, values_all, jnp.int32(0))

    def measure(state_pair, block_pair):
        top_score, total = state_pair
        key_block, start_row = block_pair
        scores, visible = block_scores(queries, positions, key_block, start_row)
        new_top = jnp.maximum(top_score, jnp.max(scores, axis=-1))
        raised = jnp.where(visible, jnp.exp(scores - new_top[..., None]), 0.0)
        total = total * jnp.exp(top_score - new_top) + jnp.sum(raised, axis=-1)
        return ((new_top, total), None)

    initial = (
        jnp.full((HEADS, tok_rows), masked_score, jnp.float32),
        jnp.zeros((HEADS, tok_rows), jnp.float32),
    )
    (top_score, total), unused = lax.scan(measure, initial, (key_blocks, starts))
    log_total = top_score + jnp.log(total)

    def accumulate(mixed, block_triple):
        key_block, value_block, start_row = block_triple
        scores, visible = block_scores(queries, positions, key_block, start_row)
        probs = jnp.where(visible, jnp.exp(scores - log_total[..., None]), 0.0).astype(jnp.bfloat16)
        return (
            mixed
            + jnp.einsum("hqk,khd->qhd", probs, value_block, preferred_element_type=jnp.float32),
            None,
        )

    mixed, unused = lax.scan(
        accumulate,
        jnp.zeros((tok_rows, HEADS, HEAD_DIM), jnp.float32),
        (key_blocks, value_blocks, starts),
    )
    return (mixed, log_total)


def attend_back(
    queries, positions, keys_all, values_all, key_offset, grad_mixed, log_total, row_delta
):
    tok_rows = queries.shape[0]
    key_blocks, value_blocks, starts = key_blocking(keys_all, values_all, key_offset)

    def backward_block(grad_queries, block_triple):
        key_block, value_block, start_row = block_triple
        scores, visible = block_scores(queries, positions, key_block, start_row)
        probs = jnp.where(visible, jnp.exp(scores - log_total[..., None]), 0.0)
        grad_probs = jnp.einsum(
            "qhd,khd->hqk", grad_mixed, value_block, preferred_element_type=jnp.float32
        )
        grad_scores = (probs * (grad_probs - row_delta[..., None])).astype(jnp.bfloat16)
        grad_queries = grad_queries + jnp.einsum(
            "hqk,khd->qhd", grad_scores, key_block, preferred_element_type=jnp.float32
        )
        grad_key_block = jnp.einsum(
            "hqk,qhd->khd", grad_scores, queries, preferred_element_type=jnp.float32
        )
        grad_value_block = jnp.einsum(
            "hqk,qhd->khd",
            probs.astype(jnp.bfloat16),
            grad_mixed,
            preferred_element_type=jnp.float32,
        )
        return (grad_queries, (grad_key_block, grad_value_block))

    grad_queries, (grad_keys, grad_values) = lax.scan(
        backward_block,
        jnp.zeros((tok_rows, HEADS, HEAD_DIM), jnp.float32),
        (key_blocks, value_blocks, starts),
    )
    key_len = keys_all.shape[0]
    return (
        grad_queries,
        grad_keys.reshape(key_len, HEADS * HEAD_DIM),
        grad_values.reshape(key_len, HEADS * HEAD_DIM),
    )


def local_gathered(
    tokens,
    cotangent,
    norm1_gain,
    norm1_bias,
    query_weight,
    key_weight,
    value_weight,
    out_weight,
    norm2_gain,
    norm2_bias,
    up_weight,
    up_bias,
    down_weight,
    down_bias,
):
    (
        gain_one,
        bias_one,
        w_query,
        w_key,
        w_value,
        w_out,
        gain_two,
        bias_two,
        w_up,
        b_up,
        w_down,
        b_down,
    ) = (
        lax.all_gather(norm1_gain, ("dp", "fsdp"), axis=0, tiled=True),
        lax.all_gather(norm1_bias, ("dp", "fsdp"), axis=0, tiled=True),
        lax.all_gather(query_weight, ("dp", "fsdp"), axis=0, tiled=True),
        lax.all_gather(key_weight, ("dp", "fsdp"), axis=0, tiled=True),
        lax.all_gather(value_weight, ("dp", "fsdp"), axis=0, tiled=True),
        lax.all_gather(out_weight, ("dp", "fsdp"), axis=0, tiled=True),
        lax.all_gather(norm2_gain, ("dp", "fsdp"), axis=0, tiled=True),
        lax.all_gather(norm2_bias, ("dp", "fsdp"), axis=0, tiled=True),
        lax.all_gather(up_weight, ("dp", "fsdp"), axis=0, tiled=True),
        lax.all_gather(up_bias, ("dp", "fsdp"), axis=0, tiled=True),
        lax.all_gather(down_weight, ("dp", "fsdp"), axis=0, tiled=True),
        lax.all_gather(down_bias, ("dp", "fsdp"), axis=0, tiled=True),
    )
    seq_count = tokens.shape[0]
    tok_rows = tokens.shape[1]
    model_width = tokens.shape[2]
    all_rows = seq_count * tok_rows
    scaling = HEAD_DIM ** (-0.5)
    inputs = tokens.reshape(all_rows, model_width).astype(jnp.float32)
    normed_one, inverse_one = norm_parts(inputs)
    attn_in = (normed_one * gain_one.astype(jnp.float32) + bias_one.astype(jnp.float32)).astype(
        jnp.bfloat16
    )
    queries = product(attn_in, w_query).reshape(seq_count, tok_rows, HEADS, HEAD_DIM)
    key_raw = product(attn_in, w_key).reshape(seq_count, tok_rows, HEADS, HEAD_DIM)
    value_low = (
        product(attn_in, w_value).astype(jnp.bfloat16).reshape(seq_count, tok_rows, model_width)
    )
    key_offset = lax.axis_index("dp") * tok_rows
    positions = key_offset + jnp.arange(tok_rows, dtype=jnp.int32)
    cosine, sine = rotary_tables(positions.astype(jnp.float32), HEAD_DIM // 2)
    q_rot = (rotate(queries, cosine, sine) * scaling).astype(jnp.bfloat16)
    k_flat = (
        rotate(key_raw, cosine, sine).astype(jnp.bfloat16).reshape(seq_count, tok_rows, model_width)
    )
    keys_all, values_all = (
        lax.all_gather(k_flat, "dp", axis=1, tiled=True),
        lax.all_gather(value_low, "dp", axis=1, tiled=True),
    )
    seq_len = keys_all.shape[1]
    mixed, log_total = jax.vmap(attend, in_axes=(0, 0, 0, None))(
        q_rot,
        keys_all.reshape(seq_count, seq_len, HEADS, HEAD_DIM),
        values_all.reshape(seq_count, seq_len, HEADS, HEAD_DIM),
        positions,
    )
    mixed_low = mixed.reshape(all_rows, model_width).astype(jnp.bfloat16)
    hidden = inputs + product(mixed_low, w_out)
    normed_two, inverse_two = norm_parts(hidden)
    ffn_in = (normed_two * gain_two.astype(jnp.float32) + bias_two.astype(jnp.float32)).astype(
        jnp.bfloat16
    )
    preact = product(ffn_in, w_up) + b_up.astype(jnp.float32)
    edges = [0] + [FF // 2 ** (GRAN - 1 - level_idx) for level_idx in range(GRAN)]
    gated_list = []
    result_list = []
    for level_idx in range(GRAN):
        level_width = edges[level_idx + 1]
        gated = gelu_value(preact[:, :level_width]).astype(jnp.bfloat16)
        gated_list.append(gated)
        result = hidden + product(gated, w_down[:level_width]) + b_down.astype(jnp.float32)
        result_list.append(result.astype(jnp.bfloat16))
    activations = jnp.stack(result_list).reshape(GRAN, seq_count, tok_rows, model_width)
    back_gain_one, back_query, back_key, back_value, back_out, back_gain_two, back_up, back_down = (
        lax.all_gather(norm1_gain, ("dp", "fsdp"), axis=0, tiled=True),
        lax.all_gather(query_weight, ("dp", "fsdp"), axis=0, tiled=True),
        lax.all_gather(key_weight, ("dp", "fsdp"), axis=0, tiled=True),
        lax.all_gather(value_weight, ("dp", "fsdp"), axis=0, tiled=True),
        lax.all_gather(out_weight, ("dp", "fsdp"), axis=0, tiled=True),
        lax.all_gather(norm2_gain, ("dp", "fsdp"), axis=0, tiled=True),
        lax.all_gather(up_weight, ("dp", "fsdp"), axis=0, tiled=True),
        lax.all_gather(down_weight, ("dp", "fsdp"), axis=0, tiled=True),
    )
    grads_out = cotangent.reshape(GRAN, all_rows, model_width)
    grad_hidden = jnp.sum(grads_out.astype(jnp.float32), axis=0)
    grad_down_bias = jnp.sum(grad_hidden, axis=0)
    grad_ffn_in = jnp.zeros((all_rows, model_width), jnp.float32)
    pre_grads = []
    for level_idx in range(GRAN):
        level_width = edges[level_idx + 1]
        grad_gated = back_product(grads_out[level_idx], back_down[:level_width])
        grad_pre = (grad_gated * gelu_grad(preact[:, :level_width])).astype(jnp.bfloat16)
        pre_grads.append(grad_pre)
        grad_ffn_in = grad_ffn_in + back_product(grad_pre, back_up[:, :level_width])
    up_blocks = []
    bias_blocks = []
    down_blocks = []
    for block_idx in range(GRAN):
        start_col = edges[block_idx]
        stop_col = edges[block_idx + 1]
        stacked_grad = jnp.concatenate(
            [pre_grads[level_idx][:, start_col:stop_col] for level_idx in range(block_idx, GRAN)],
            axis=0,
        )
        stacked_in = jnp.concatenate([ffn_in] * (GRAN - block_idx), axis=0)
        up_blocks.append(gram_product(stacked_in, stacked_grad))
        bias_blocks.append(jnp.sum(stacked_grad.astype(jnp.float32), axis=0))
        stacked_gated = jnp.concatenate(
            [gated_list[level_idx][:, start_col:stop_col] for level_idx in range(block_idx, GRAN)],
            axis=0,
        )
        stacked_out = jnp.concatenate(
            [grads_out[level_idx] for level_idx in range(block_idx, GRAN)], axis=0
        )
        down_blocks.append(gram_product(stacked_gated, stacked_out))
    grad_up_weight = jnp.concatenate(up_blocks, axis=1)
    grad_up_bias = jnp.concatenate(bias_blocks, axis=0)
    grad_down_weight = jnp.concatenate(down_blocks, axis=0)
    grad_gain_two = jnp.sum(grad_ffn_in * normed_two, axis=0)
    grad_bias_two = jnp.sum(grad_ffn_in, axis=0)
    grad_hidden = grad_hidden + norm_backward(
        grad_ffn_in, normed_two, inverse_two, back_gain_two.astype(jnp.float32)
    )
    grad_branch = grad_hidden.astype(jnp.bfloat16)
    grad_out_weight = gram_product(mixed_low, grad_branch)
    grad_mixed = (
        back_product(grad_branch, back_out)
        .astype(jnp.bfloat16)
        .reshape(seq_count, tok_rows, HEADS, HEAD_DIM)
    )
    row_delta = jnp.einsum("sqhd,sqhd->shq", grad_mixed.astype(jnp.float32), mixed)
    keys_again, values_again = (
        lax.all_gather(k_flat, "dp", axis=1, tiled=True),
        lax.all_gather(value_low, "dp", axis=1, tiled=True),
    )
    back_all = jax.vmap(attend_back, in_axes=(0, None, 0, 0, None, 0, 0, 0))
    grad_q_rot, grad_keys_all, grad_values_all = back_all(
        q_rot,
        positions,
        keys_again.reshape(seq_count, seq_len, HEADS, HEAD_DIM),
        values_again.reshape(seq_count, seq_len, HEADS, HEAD_DIM),
        jnp.int32(0),
        grad_mixed,
        log_total,
        row_delta,
    )
    every_query, every_grad = (
        lax.all_gather(q_rot, "dp", axis=1, tiled=True),
        lax.all_gather(grad_mixed, "dp", axis=1, tiled=True),
    )
    every_total, every_delta = (
        lax.all_gather(jnp.transpose(log_total, (0, 2, 1)), "dp", axis=1, tiled=True),
        lax.all_gather(jnp.transpose(row_delta, (0, 2, 1)), "dp", axis=1, tiled=True),
    )
    every_position = jnp.arange(seq_len, dtype=jnp.int32)
    unused_rows, grad_key_mine, grad_value_mine = back_all(
        every_query,
        every_position,
        k_flat.reshape(seq_count, tok_rows, HEADS, HEAD_DIM),
        value_low.reshape(seq_count, tok_rows, HEADS, HEAD_DIM),
        key_offset,
        every_grad,
        jnp.transpose(every_total, (0, 2, 1)),
        jnp.transpose(every_delta, (0, 2, 1)),
    )
    grad_query = (
        rotate(grad_q_rot * scaling, cosine, -sine)
        .reshape(all_rows, model_width)
        .astype(jnp.bfloat16)
    )
    grad_key = (
        rotate(grad_key_mine.reshape(seq_count, tok_rows, HEADS, HEAD_DIM), cosine, -sine)
        .reshape(all_rows, model_width)
        .astype(jnp.bfloat16)
    )
    grad_val = grad_value_mine.reshape(all_rows, model_width).astype(jnp.bfloat16)
    grad_query_weight = gram_product(attn_in, grad_query)
    grad_key_weight = gram_product(attn_in, grad_key)
    grad_value_weight = gram_product(attn_in, grad_val)
    grad_attn_in = (
        back_product(grad_query, back_query)
        + back_product(grad_key, back_key)
        + back_product(grad_val, back_value)
    )
    grad_gain_one = jnp.sum(grad_attn_in * normed_one, axis=0)
    grad_bias_one = jnp.sum(grad_attn_in, axis=0)
    grad_inputs = grad_hidden + norm_backward(
        grad_attn_in, normed_one, inverse_one, back_gain_one.astype(jnp.float32)
    )
    (
        sum_gain_one,
        sum_bias_one,
        sum_query,
        sum_key,
        sum_value,
        sum_out,
        sum_gain_two,
        sum_bias_two,
        sum_up,
        sum_up_bias,
        sum_down,
        sum_down_bias,
    ) = (
        lax.psum_scatter(grad_gain_one, ("dp", "fsdp"), scatter_dimension=0, tiled=True),
        lax.psum_scatter(grad_bias_one, ("dp", "fsdp"), scatter_dimension=0, tiled=True),
        lax.psum_scatter(grad_query_weight, ("dp", "fsdp"), scatter_dimension=0, tiled=True),
        lax.psum_scatter(grad_key_weight, ("dp", "fsdp"), scatter_dimension=0, tiled=True),
        lax.psum_scatter(grad_value_weight, ("dp", "fsdp"), scatter_dimension=0, tiled=True),
        lax.psum_scatter(grad_out_weight, ("dp", "fsdp"), scatter_dimension=0, tiled=True),
        lax.psum_scatter(grad_gain_two, ("dp", "fsdp"), scatter_dimension=0, tiled=True),
        lax.psum_scatter(grad_bias_two, ("dp", "fsdp"), scatter_dimension=0, tiled=True),
        lax.psum_scatter(grad_up_weight, ("dp", "fsdp"), scatter_dimension=0, tiled=True),
        lax.psum_scatter(grad_up_bias, ("dp", "fsdp"), scatter_dimension=0, tiled=True),
        lax.psum_scatter(grad_down_weight, ("dp", "fsdp"), scatter_dimension=0, tiled=True),
        lax.psum_scatter(grad_down_bias, ("dp", "fsdp"), scatter_dimension=0, tiled=True),
    )
    return (
        activations,
        grad_inputs.astype(jnp.bfloat16).reshape(seq_count, tok_rows, model_width),
        sum_gain_one,
        sum_bias_one,
        sum_query,
        sum_key,
        sum_value,
        sum_out,
        sum_gain_two,
        sum_bias_two,
        sum_up,
        sum_up_bias,
        sum_down,
        sum_down_bias,
    )


MESH = pl.DeviceIdType.MESH


class Place:
    def __init__(self, chips):
        self.chips = chips
        self.rank = lax.axis_index("dp")
        self.shard = lax.axis_index("fsdp")
        self.z = lax.div(self.shard, 2)
        self.core = lax.rem(self.shard, 2)
        along_x = self.rank + 1 - 2 * lax.rem(self.rank, 2)
        along_y = self.rank + 2 - 4 * lax.div(self.rank, 2)
        self.first = jnp.where(self.core == 0, along_x, along_y)
        self.second = jnp.where(self.core == 0, along_y, along_x)
        self.across = 3 - self.rank
        self.sibling = self.shard + 1 - 2 * self.core

    def at(self, rank=None, shard=None):
        return (self.rank if rank is None else rank, self.shard if shard is None else shard)

    def others(self):
        return [lax.rem(self.shard + k, 2 * self.chips) for k in range(1, 2 * self.chips)]

    def greet(self, plane=True, sibling=False, ring=False, group=False):
        barrier = pltpu.get_barrier_semaphore()
        count = 0
        targets = []
        if plane:
            targets += [self.at(rank=r) for r in (self.first, self.second, self.across)]
        if sibling:
            targets.append(self.at(shard=self.sibling))
        if ring:
            targets += [self.at(shard=self.hop(k)) for k in range(1, self.chips)]
        if group:
            targets += [self.at(shard=f) for f in self.others()]
        for target in targets:
            pl.semaphore_signal(barrier, inc=1, device_id=target, device_id_type=MESH)
            count += 1
        pl.semaphore_wait(barrier, count)

    def hop(self, k):
        return 2 * lax.rem(self.z + k, self.chips) + self.core


def under(condition, action):
    if condition is None:
        action()
    else:
        pl.when(condition)(action)


class Message:
    def __init__(self, links, src, dst, target, sent=None, comes=None):
        index = links.take()
        self.copy = pltpu.make_async_remote_copy(
            src_ref=src,
            dst_ref=dst,
            send_sem=links.send.at[index],
            recv_sem=links.recv.at[index],
            device_id=target,
            device_id_type=MESH,
        )
        self.sent, self.comes = sent, comes
        links.open.append(self)
        under(sent, self.copy.start)

    def arrive(self):
        under(self.comes, self.copy.wait_recv)

    def leave(self):
        under(self.sent, self.copy.wait_send)


class Near:
    def __init__(self, links, src, dst, where):
        self.copy = pltpu.make_async_copy(src, dst, links.near.at[links.used_near])
        links.used_near += 1
        self.where = where
        self.waits = True
        under(where, self.copy.start)

    def arrive(self):
        if self.waits:
            under(self.where, self.copy.wait)
        self.waits = False


class Links:
    def __init__(self, send, recv, near):
        self.send, self.recv, self.near = send, recv, near
        self.used = 0
        self.used_near = 0
        self.open = []
        self.open_near = []

    def take(self):
        self.used += 1
        return self.used - 1

    def keep(self, src, dst, where=None):
        copy = Near(self, src, dst, where)
        self.open_near.append(copy)
        return copy

    def drain(self):
        for copy in self.open_near:
            copy.arrive()
        for message in self.open:
            message.leave()


LINK_SCRATCH = [
    pltpu.SemaphoreType.DMA((128,)),
    pltpu.SemaphoreType.DMA((128,)),
    pltpu.SemaphoreType.DMA((32,)),
]


def normed(values):
    centred = values - jnp.mean(values, axis=-1, keepdims=True)
    inverse = lax.rsqrt(jnp.mean(centred * centred, axis=-1, keepdims=True) + epsilon)
    return centred * inverse, inverse


def in_rows(count, step, body):
    def one(i, carry):
        body(pl.ds(pl.multiple_of(i * step, step), step))
        return carry

    lax.fori_loop(0, count // step, one, 0)


def turn_half(values, cosine, sine):
    return values * cosine + pltpu.roll(values, HEAD_DIM // 2, 1) * sine


class PlaneGather:
    def __init__(self, place, links, src, dst, parts):
        self.place, self.links, self.dst = place, links, dst
        rows = src.shape[0] // parts
        self.cuts = [pl.ds(k * rows, rows) for k in range(parts)]
        links.keep(src, dst.at[place.rank])
        self.first, self.second = [], []
        for cut in self.cuts:
            for side, target in ((self.first, place.first), (self.second, place.second)):
                block = dst.at[place.rank, cut]
                side.append(Message(links, src.at[cut], block, place.at(rank=target)))
        self.passed = []

    def relay(self, k):
        self.first[k].arrive()
        block = self.dst.at[self.place.first, self.cuts[k]]
        target = self.place.at(rank=self.place.second)
        self.passed.append(Message(self.links, block, block, target))

    def finish(self):
        for message in self.second + self.passed:
            message.arrive()


class PlaneScatter:
    def __init__(self, place, links, partial, landing, turn):
        self.place, self.links, self.partial, self.landing, self.turn = (
            place,
            links,
            partial,
            landing,
            turn,
        )
        self.target = place.at(rank=place.first)

    def send_far(self):
        self.far = Message(
            self.links, self.partial.at[self.place.across], self.landing.at[0], self.target
        )

    def send_near(self):
        self.near = Message(
            self.links, self.partial.at[self.place.first], self.landing.at[1], self.target
        )

    def relay(self):
        self.far.arrive()

        def add(cut):
            mine = self.partial[self.place.second, cut].astype(jnp.float32)
            mine = mine + self.landing[0, cut].astype(jnp.float32)
            self.turn[cut] = mine.astype(jnp.bfloat16)

        in_rows(self.turn.shape[0], 64, add)
        self.last = Message(
            self.links, self.turn, self.landing.at[2], self.place.at(rank=self.place.second)
        )

    def settle(self):
        self.near.arrive()
        self.last.arrive()

    def total(self, cut):
        total = self.partial[self.place.rank, cut].astype(jnp.float32)
        total = total + self.landing[1, cut].astype(jnp.float32)
        return total + self.landing[2, cut].astype(jnp.float32)


class Chain:
    def __init__(self, place, links, src, slot):
        self.place, self.links, self.slot = place, links, slot
        z, last = place.z, place.chips - 1
        own = slot(place.shard)
        self.up = Message(links, src, own, place.at(shard=place.shard + 2), z < last, z > 0)
        self.down = Message(links, src, own, place.at(shard=place.shard - 2), z > 0, z < last)
        self.beside = [Message(links, src, own, place.at(shard=place.sibling))]

    def step(self, s):
        place, links = self.place, self.links
        z, last = place.z, place.chips - 1
        below = self.slot(jnp.maximum(place.shard - 2 * s, place.core))
        above = self.slot(jnp.minimum(place.shard + 2 * s, 2 * last + place.core))
        self.up.arrive()
        has_below, has_above = z >= s, z <= last - s
        up = down = None
        if s < last:
            target = place.at(shard=place.shard + 2)
            up = Message(links, below, below, target, has_below & (z < last), z >= s + 1)
        self.beside.append(
            Message(links, below, below, place.at(shard=place.sibling), has_below, has_below)
        )
        self.down.arrive()
        if s < last:
            target = place.at(shard=place.shard - 2)
            down = Message(links, above, above, target, has_above & (z > 0), z <= last - s - 1)
        self.beside.append(
            Message(links, above, above, place.at(shard=place.sibling), has_above, has_above)
        )
        self.up, self.down = up, down

    def finish(self):
        for message in self.beside:
            message.arrive()


class Beside:
    def __init__(self, place, links, part, other):
        self.place, self.part, self.other = place, part, other
        self.message = Message(
            links, part.at[:, :, 1 - place.core], other, place.at(shard=place.sibling)
        )

    def add(self):
        self.message.arrive()
        core = self.place.core

        def one(k, carry):
            total = self.part[:, k, core].astype(jnp.float32) + self.other[:, k].astype(jnp.float32)
            self.part[:, k, core] = total.astype(self.part.dtype)
            return carry

        lax.fori_loop(0, self.place.chips, one, 0)


class Along:
    def __init__(self, place, links, share, landing, far=None):
        self.place, self.links, self.landing = place, links, landing
        z = place.z
        self.middle = (z == 1) | (z == 2)
        end = jnp.logical_not(self.middle)
        partner = z + 1 - 2 * lax.rem(z, 2)
        over = jnp.where(z < 2, 2, 1)
        self.other_end = jnp.where(z < 2, 3, 0)
        self.far = share(self.other_end) if far is None else far

        def to(chip):
            return place.at(shard=2 * chip + place.core)

        self.to = to

        @pl.when(end)
        def nothing_comes():
            landing[2] = jnp.zeros_like(landing[2])

        self.merge = Message(
            links, share(self.other_end), landing.at[3], to(partner), end, self.middle
        )
        self.messages = [
            Message(links, share(partner), landing.at[0], to(partner)),
            Message(links, share(over), landing.at[1], to(over), end, self.middle),
            Message(links, share(over), landing.at[2], to(over), self.middle, self.middle),
        ]

    def relay(self):
        self.merge.arrive()
        landing = self.landing

        @pl.when(self.middle)
        def add():
            total = landing[3].astype(jnp.float32) + self.far[...].astype(jnp.float32)
            landing[3] = total.astype(landing.dtype)

        end = jnp.logical_not(self.middle)
        self.messages.append(
            Message(
                self.links, landing.at[3], landing.at[1], self.to(self.other_end), self.middle, end
            )
        )

    def total(self, mine):
        total = mine.astype(jnp.float32)
        for message in self.messages:
            message.arrive()
        for k in range(3):
            total = total + self.landing[k].astype(jnp.float32)
        return total


class Detour:
    def __init__(self, place, links, src, dst, stop, source, turn, goal):
        self.place, self.links, self.dst, self.stop = place, links, dst, stop
        straight = place.core == 0
        around = place.core == 1
        across = place.at(rank=place.across)
        self.goal = around & (place.rank == goal)
        self.turn = around & (place.rank == turn)
        here = place.rank == source
        self.straight = Message(
            links, src, dst, across, straight & here, straight & (place.rank == goal)
        )
        self.leg = Message(
            links, src, stop, place.at(rank=place.first), around & here, self.turn
        )

    def relay(self):
        self.leg.arrive()
        target = self.place.at(rank=self.place.second)
        self.last = Message(self.links, self.stop, self.dst, target, self.turn, self.goal)

    def arrive(self):
        self.straight.arrive()
        self.last.arrive()


class Deal:
    def __init__(self, place, links, pairs):
        self.messages = []
        for part, dst in pairs:
            self.messages.append(links.keep(part(place.rank), dst))
            for rank in (place.first, place.second, place.across):
                self.messages.append(Message(links, part(rank), dst, place.at(rank=rank)))

    def arrive(self):
        for message in self.messages:
            message.arrive()


def block_of(r):
    return jnp.where(r == 0, 0, jnp.minimum(r + 1, GRAN - 1))


def forward_kernel(
    chips,
    tokens,
    cotangent,
    gain_one,
    bias_one,
    gain_two,
    bias_two,
    b_down,
    b_up,
    w_query,
    w_key,
    w_value,
    w_out,
    w_up,
    w_down,
    comb,
    mask,
    cosine,
    sine,
    all_tokens,
    attn_in,
    qkv_rot,
    mixed_low,
    hidden,
    all_ffn_in,
    gains,
    incoming,
    cotangent_sum,
    next_sum,
    all_qkv,
    all_out,
    all_up,
    all_down,
    cotangent_v,
    suffix,
    small,
    tokens_v,
    attn_v,
    rot_v,
    mixed_v,
    qkv_v,
    out_v,
    partial,
    landing,
    passing,
    ffn_v,
    all_small,
    send,
    recv,
    near,
):
    place = Place(chips)
    links = Links(send, recv, near)
    load_cotangent = links.keep(cotangent, cotangent_v)
    own = gain_one.shape[1]
    packed = [v[...].astype(jnp.float32) for v in (gain_one, bias_one, gain_two, bias_two, b_down)]
    wide_bias = b_up[...].astype(jnp.float32)
    packed += [wide_bias[:, q * own : (q + 1) * own] for q in range(4)]
    packed = jnp.concatenate(packed + [jnp.zeros((7, own), jnp.float32)], axis=0)
    packed = jnp.concatenate([packed, jnp.zeros((16, 128 - own), jnp.float32)], axis=1)
    small[...] = packed.astype(jnp.bfloat16)
    place.greet(plane=True, group=True)
    rank, shard = place.rank, place.shard
    ranks, tok_rows, model_width = tokens_v.shape
    head_cols = w_query.shape[1] // ranks
    heads = head_cols // HEAD_DIM

    def columns(weight, width):
        return lambda r: weight.at[:, pl.ds(pl.multiple_of(r * width, 128), width)]

    own_qkv = all_qkv.at[rank, shard]
    deal_small = Deal(place, links, [(lambda r: small, all_small.at[rank, shard])])
    pairs = []
    for i, weight in enumerate((w_query, w_key, w_value)):
        pairs.append(
            (columns(weight, head_cols), own_qkv.at[:, pl.ds(i * head_cols, head_cols)])
        )
    deal_qkv = Deal(place, links, pairs)
    gather = PlaneGather(place, links, tokens, tokens_v, 2)
    deal_up = Deal(place, links, [(columns(w_up, w_up.shape[1] // ranks), all_up.at[rank, shard])])
    links.keep(w_out, all_out.at[shard])
    links.keep(w_down, all_down.at[shard])
    out_slot = lambda f: all_out.at[f]
    down_slot = lambda f: all_down.at[f]
    small_slot = lambda f: all_small.at[:, f]
    qkv_slot = lambda f: all_qkv.at[:, f]
    up_slot = lambda f: all_up.at[:, f]
    chain_out = Chain(place, links, w_out, out_slot)
    load_cotangent.arrive()

    def add_cotangents(cut):
        total = jnp.zeros((64, model_width), jnp.float32)
        for g in range(GRAN - 1, -1, -1):
            total = total + cotangent_v[g, cut].astype(jnp.float32)
            suffix[g, cut] = total.astype(jnp.bfloat16)
        cotangent_sum[cut] = total

    in_rows(tok_rows, 64, add_cotangents)
    links.keep(suffix.at[1], next_sum)
    deal_small.arrive()
    own_small = small_slot(shard)
    told = [Message(links, own_small, own_small, place.at(shard=f)) for f in place.others()]
    deal_qkv.arrive()
    chain_qkv = Chain(place, links, qkv_slot(shard), qkv_slot)
    gather.relay(0)
    for message in told:
        message.arrive()
    gather.relay(1)
    chain_qkv.step(1)

    def wide(rows):
        spread = jnp.dot(rows, comb[...], preferred_element_type=jnp.float32)
        return jnp.sum(spread * mask[...], axis=0, keepdims=True)

    devices = ranks * 2 * chips
    for i in range(5):
        gains[i : i + 1] = wide(all_small[:, :, i].reshape(devices, 128))
    up_rows = all_small[rank, :, 5:9].astype(jnp.float32).reshape(devices, 128)
    gains[5:6] = wide(up_rows.astype(jnp.bfloat16))
    gains[6:8] = jnp.zeros((2, model_width), jnp.float32)

    def norm_block(r):
        def rows_of(cut):
            value, unused = normed(tokens_v[r, cut].astype(jnp.float32))
            attn_v[r, cut] = (value * gains[0:1] + gains[1:2]).astype(jnp.bfloat16)

        in_rows(tok_rows, 64, rows_of)

    for copy in links.open_near:
        copy.arrive()
    norm_block(rank)
    norm_block(place.first)
    chain_qkv.step(2)
    deal_up.arrive()
    chain_up = Chain(place, links, up_slot(shard), up_slot)
    gather.finish()
    links.keep(suffix.at[block_of(rank)], incoming.at[rank])
    dealt = []
    for r in (place.first, place.second, place.across):
        dealt.append(Message(links, suffix.at[block_of(r)], incoming.at[rank], place.at(rank=r)))
    norm_block(place.second)
    norm_block(place.across)
    links.keep(tokens_v, all_tokens)
    links.keep(attn_v, attn_in)
    chain_out.step(1)
    chain_qkv.step(3)
    chain_out.step(2)
    chain_down = Chain(place, links, w_down, down_slot)
    chain_qkv.finish()
    load_qkv = links.keep(all_qkv, qkv_v)
    load_qkv.arrive()

    def project(r, carry):
        rows = pl.ds(pl.multiple_of(r * tok_rows, tok_rows), tok_rows)
        for part in range(3):
            cut = slice(part * head_cols, (part + 1) * head_cols)
            weight = qkv_v[:, :, :, cut].reshape(model_width, head_cols)
            value = jnp.dot(attn_v[r], weight, preferred_element_type=jnp.float32)
            if part < 2:
                turned = []
                for h in range(heads):
                    head = value[:, h * HEAD_DIM : (h + 1) * HEAD_DIM]
                    turned.append(turn_half(head, cosine[rows], sine[rows]))
                value = jnp.concatenate(turned, axis=1)
                if part == 0:
                    value = value * HEAD_DIM ** (-0.5)
            rot_v[r, :, cut] = value.astype(jnp.bfloat16)
        return carry

    lax.fori_loop(0, ranks, project, 0)
    links.keep(rot_v, qkv_rot)
    chain_out.step(3)
    chain_out.finish()
    load_out = links.keep(all_out, out_v)

    def attend_block(r):
        def head(h, carry):
            def part(i):
                return pl.ds(pl.multiple_of(i * head_cols + h * HEAD_DIM, HEAD_DIM), HEAD_DIM)

            for t in range(ranks):

                @pl.when(r == t)
                def with_keys(seen=t + 1):
                    keys = rot_v[:seen, :, part(1)].reshape(-1, HEAD_DIM)
                    scores = back_product(rot_v[r, :, part(0)], keys)
                    row = lax.broadcasted_iota(jnp.int32, scores.shape, 0) + r * tok_rows
                    column = lax.broadcasted_iota(jnp.int32, scores.shape, 1)
                    scores = jnp.where(row >= column, scores, masked_score)
                    raised = jnp.exp(scores - jnp.max(scores, axis=-1, keepdims=True))
                    scale = 1.0 / jnp.sum(raised, axis=-1, keepdims=True)
                    probs = (raised * scale).astype(jnp.bfloat16)
                    mixed = product(probs, rot_v[:seen, :, part(2)].reshape(-1, HEAD_DIM))
                    mixed_v[r, :, part(0)] = mixed.astype(jnp.bfloat16)

            return carry

        lax.fori_loop(0, heads, head, 0)

    def project_block(r):
        weight = out_v[...].reshape(head_cols, model_width)
        partial[r] = product(mixed_v[r], weight).astype(jnp.bfloat16)

    scatter = PlaneScatter(place, links, partial, landing, passing)
    attend_block(place.across)
    load_out.arrive()
    project_block(place.across)
    scatter.send_far()
    attend_block(place.first)
    project_block(place.first)
    scatter.send_near()
    chain_up.step(1)
    attend_block(place.second)
    project_block(place.second)
    scatter.relay()
    chain_down.step(1)
    attend_block(rank)
    project_block(rank)
    chain_up.step(2)
    links.keep(mixed_v, mixed_low)
    scatter.settle()

    def second_norm(cut):
        value = scatter.total(cut) + tokens_v[rank, cut].astype(jnp.float32)
        hidden[cut] = value
        value, unused = normed(value)
        ffn_v[cut] = (value * gains[2:3] + gains[3:4]).astype(jnp.bfloat16)

    in_rows(tok_rows, 64, second_norm)
    gather = PlaneGather(place, links, ffn_v, all_ffn_in, 2)
    chain_down.step(2)
    gather.relay(0)
    chain_up.step(3)
    gather.relay(1)
    chain_down.step(3)
    chain_up.finish()
    gather.finish()
    chain_down.finish()
    for message in dealt:
        message.arrive()
    links.drain()


def middle_kernel(
    chips,
    all_ffn_in,
    incoming,
    next_sum,
    w_up,
    w_down,
    hidden,
    cotangent_sum,
    gains,
    grad_hidden,
    branch,
    sums,
    sum_down,
    share_down,
    share_up,
    terms,
    extra_in,
    ffn_v,
    csum_v,
    up_v,
    down_v,
    gated_v,
    grad_v,
    part_down,
    other_down,
    land_down,
    other_up,
    terms_v,
    stop,
    stop_more,
    partial,
    landing,
    passing,
    send,
    recv,
    near,
):
    place = Place(chips)
    links = Links(send, recv, near)
    rank = place.rank
    ranks, tok_rows, model_width = ffn_v.shape
    ff_cols = up_v.shape[-1]
    half = ff_cols // 2
    load_up = links.keep(w_up, up_v)
    order = (place.across, place.first, place.second, rank)
    load_ffn = [links.keep(all_ffn_in.at[t], ffn_v.at[t]) for t in order]
    load_down = links.keep(w_down, down_v)
    load_csum = links.keep(incoming, csum_v.at[0])
    load_more = links.keep(next_sum, csum_v.at[1, rank], rank == 0)
    place.greet(plane=True, sibling=True, ring=True)
    detour = Detour(place, links, next_sum, csum_v.at[1, 3], stop, 3, 1, 0)
    dealt = []
    for r in (place.first, place.second):
        dealt.append(
            Message(links, next_sum, csum_v.at[1, rank], place.at(rank=r), r == 0, rank == 0)
        )
    slots = (0, jnp.where(rank == 0, 1, 0))
    sums[...] = jnp.zeros_like(sums)
    load_up.arrive()
    scatter = PlaneScatter(place, links, partial, landing, passing)

    def widen(k):
        t = order[k]
        load_ffn[k].arrive()
        for i in range(2):
            cut = slice(i * half, (i + 1) * half)
            weight = up_v[:, :, :, :, cut].reshape(model_width, half)
            pre = product(ffn_v[t], weight) + gains[5:6, cut]
            square = pre * pre
            tangent = jnp.tanh(0.7978845608028654 * pre * (1.0 + 0.044715 * square))
            gated_v[t, :, cut] = (0.5 * pre * (1.0 + tangent)).astype(jnp.bfloat16)
            slope = 0.5 * (1.0 + tangent) + 0.5 * pre * (1.0 - tangent * tangent) * (
                0.7978845608028654 * (1.0 + 3.0 * 0.044715 * square)
            )
            grad_v[t, :, cut] = slope.astype(jnp.bfloat16)

    def high_tile(t, carry):
        high_term = product(gated_v[t, :, half:], down_v[4:].reshape(half, model_width))
        terms_v[1, t] = high_term.astype(jnp.bfloat16)
        return carry

    def low_tile(t, carry):
        low_term = product(gated_v[t, :, :half], down_v[:4].reshape(half, model_width))
        high_term = terms_v[1, t].astype(jnp.float32) * jnp.where(rank == 0, 0.0, 1.0)
        terms_v[0, t] = (low_term + high_term).astype(jnp.bfloat16)
        return carry

    def block(k):
        t = order[k]
        for i in range(2):
            cut = slice(i * half, (i + 1) * half)
            weight = down_v[4 * i : 4 * i + 4].reshape(half, model_width)
            grad = back_product(csum_v[slots[i], t], weight) * grad_v[t, :, cut].astype(jnp.float32)
            grad_v[t, :, cut] = grad.astype(jnp.bfloat16)
            sums[3:4, cut] += jnp.sum(grad, axis=0, keepdims=True)

        def back(i, carry):
            own = model_width // ranks
            value = back_product(grad_v[t], up_v[i].reshape(own, ff_cols))
            partial[t, :, pl.ds(pl.multiple_of(i * own, 128), own)] = value.astype(jnp.bfloat16)
            return carry

        lax.fori_loop(0, ranks, back, 0)

    widen(0)
    widen(1)
    widen(2)
    widen(3)
    load_down.arrive()
    lax.fori_loop(0, ranks, high_tile, 0)
    detour.relay()
    detour_more = Detour(
        place, links, terms_v.at[1, place.across], extra_in, stop_more, 0, 2, 3
    )
    links.keep(terms_v.at[1, rank], extra_in, rank == 0)
    dealt_more = [detour_more]
    for r in (place.first, place.second):
        dealt_more.append(
            Message(links, terms_v.at[1, r], extra_in, place.at(rank=r), rank == 0, r == 0)
        )
    lax.fori_loop(0, ranks, low_tile, 0)
    links.keep(terms_v.at[0], terms)
    load_csum.arrive()
    load_more.arrive()
    for message in dealt + [detour]:
        message.arrive()

    def down_tiles(h):
        width = model_width // 2
        right = slice(h * width, (h + 1) * width)

        def down_tile(i, carry):
            rows = ff_cols // ranks
            left = gated_v[:, :, pl.ds(pl.multiple_of(i * rows, 128), rows)].reshape(-1, rows)
            slot = jnp.where(i < 2, slots[0], slots[1])
            value = gram_product(left, csum_v[slot, :, :, right].reshape(-1, width))
            part_down[h, i] = value.astype(jnp.bfloat16).reshape(part_down.shape[2:])
            return carry

        lax.fori_loop(0, ranks, down_tile, 0)
        here = pl.ds(h, 1)
        return Beside(place, links, part_down.at[here], other_down.at[here])

    block(0)
    scatter.send_far()
    block(1)
    scatter.send_near()
    beside_low = down_tiles(0)
    block(2)
    scatter.relay()
    detour_more.relay()
    block(3)
    beside_low.add()
    share_low = part_down.at[pl.ds(0, 1)]
    along_down = Along(place, links, lambda there: share_low.at[:, there, place.core], land_down)

    def up_tile(i, carry):
        rows = model_width // ranks
        left = ffn_v[:, :, pl.ds(pl.multiple_of(i * rows, 128), rows)].reshape(-1, rows)
        value = gram_product(left, grad_v[...].reshape(-1, ff_cols))
        up_v[i] = value.astype(jnp.bfloat16).reshape(up_v.shape[1:])
        return carry

    lax.fori_loop(0, ranks, up_tile, 0)
    beside_up = Beside(place, links, up_v, other_up)
    beside_high = down_tiles(1)
    along_down.relay()

    beside_up.add()
    links.keep(up_v.at[:, :, place.core], share_up)
    scatter.settle()

    def norm_back(cut):
        value, inverse = normed(hidden[cut])
        grad = scatter.total(cut)
        sums[0:1] += jnp.sum(grad * value, axis=0, keepdims=True)
        sums[1:2] += jnp.sum(grad, axis=0, keepdims=True)
        sums[2:3] += jnp.sum(cotangent_sum[cut], axis=0, keepdims=True)
        total = cotangent_sum[cut] + norm_backward(grad, value, inverse, gains[2:3])
        grad_hidden[cut] = total
        branch[cut] = total.astype(jnp.bfloat16)

    in_rows(tok_rows, 64, norm_back)
    beside_high.add()
    links.keep(part_down.at[pl.ds(1, 1), :, place.core], share_down)
    sum_down[...] = along_down.total(part_down[0:1, place.z, place.core])[0]
    for message in dealt_more:
        message.arrive()
    links.drain()


def last_kernel(
    chips,
    branch,
    share_down,
    share_up,
    terms,
    qkv_rot,
    mixed_low,
    w_out,
    w_qkv,
    attn_in,
    all_tokens,
    grad_hidden,
    gains,
    sums,
    comb,
    mask,
    cosine,
    sine,
    term_in,
    grad_tokens,
    sum_out,
    sum_down,
    land_sum_up,
    land_sum_qkv,
    sum_small,
    branch_v,
    rot_v,
    mixed_v,
    grad_mixed_v,
    out_v,
    qkv_v,
    attn_v,
    tokens_v,
    grad_v,
    key_sum,
    value_sum,
    partial,
    landing,
    passing,
    mine_down,
    far_down,
    land_down,
    mine_up,
    far_up,
    land_up,
    part_out,
    other_out,
    land_out,
    part_qkv,
    other_qkv,
    land_qkv,
    turn_qkv,
    part_small,
    other_small,
    land_small,
    turn_small,
    land_sums,
    more_sums,
    send,
    recv,
    near,
):
    place = Place(chips)
    links = Links(send, recv, near)
    rank, z = place.rank, place.z
    ranks, tok_rows, model_width = branch_v.shape
    head_cols = mixed_v.shape[2]
    heads = head_cols // HEAD_DIM
    load_out = links.keep(w_out, out_v)
    load_mixed = links.keep(mixed_low, mixed_v)
    load_rot = links.keep(qkv_rot, rot_v)
    load_qkv = links.keep(w_qkv, qkv_v)
    load_attn = links.keep(attn_in, attn_v)
    load_tokens = links.keep(all_tokens, tokens_v)
    load_up = links.keep(share_up.at[:, z], mine_up)
    other_end = jnp.where(z < 2, chips - 1, 0)
    load_far = [
        links.keep(share_up.at[:, other_end], far_up),
        links.keep(share_down.at[:, other_end], far_down),
    ]
    load_down = links.keep(share_down.at[:, z], mine_down)
    place.greet(plane=True, sibling=True, ring=True)
    gather = PlaneGather(place, links, branch, branch_v, 2)
    along_up = Along(place, links, lambda there: share_up.at[:, there], land_up, far_up)
    along_down = Along(place, links, lambda there: share_down.at[:, there], land_down, far_down)
    load_out.arrive()

    def mix_back(t):
        weight = out_v[...].reshape(head_cols, model_width)
        grad_mixed_v[t] = back_product(branch_v[t], weight).astype(jnp.bfloat16)

    links.open_near[10].arrive()
    mix_back(rank)
    gather.relay(0)
    gather.relay(1)
    mix_back(place.first)
    gather.finish()
    mix_back(place.second)
    mix_back(place.across)
    links.keep(terms.at[rank], term_in.at[rank])
    dealt = []
    for r in (place.first, place.second, place.across):
        dealt.append(Message(links, terms.at[r], term_in.at[rank], place.at(rank=r)))
    for copy in load_far:
        copy.arrive()
    along_up.relay()
    along_down.relay()
    load_mixed.arrive()
    value = gram_product(
        mixed_v[...].reshape(-1, head_cols), branch_v[...].reshape(-1, model_width)
    )
    part_out[0] = value.astype(jnp.bfloat16).reshape(part_out.shape[1:])
    beside_out = Beside(place, links, part_out, other_out)
    load_rot.arrive()

    def head(h, carry):
        def part(i):
            return pl.ds(pl.multiple_of(i * head_cols + h * HEAD_DIM, HEAD_DIM), HEAD_DIM)

        for t in range(ranks - 1, -1, -1):
            count = t + 1
            keys = rot_v[:count, :, part(1)].reshape(-1, HEAD_DIM)
            values = rot_v[:count, :, part(2)].reshape(-1, HEAD_DIM)
            queries = rot_v[t, :, part(0)]
            grad_mixed = grad_mixed_v[t, :, part(0)]
            scores = back_product(queries, keys)
            row = lax.broadcasted_iota(jnp.int32, scores.shape, 0) + t * tok_rows
            column = lax.broadcasted_iota(jnp.int32, scores.shape, 1)
            scores = jnp.where(row >= column, scores, masked_score)
            raised = jnp.exp(scores - jnp.max(scores, axis=-1, keepdims=True))
            probs = raised * (1.0 / jnp.sum(raised, axis=-1, keepdims=True))
            delta = jnp.sum(
                grad_mixed.astype(jnp.float32) * mixed_v[t, :, part(0)].astype(jnp.float32),
                axis=-1,
                keepdims=True,
            )
            grad_scores = (probs * (back_product(grad_mixed, values) - delta)).astype(jnp.bfloat16)
            rows = pl.ds(t * tok_rows, tok_rows)
            grad_query = product(grad_scores, keys)
            grad_query = turn_half(grad_query, cosine[rows], -sine[rows]) * HEAD_DIM ** (-0.5)
            grad_v[t, :, part(0)] = grad_query.astype(jnp.bfloat16)
            grad_key = gram_product(grad_scores, queries)
            grad_value = gram_product(probs.astype(jnp.bfloat16), grad_mixed)
            seen = count * tok_rows
            if t == ranks - 1:
                key_sum[...] = grad_key
                value_sum[...] = grad_value
            else:
                key_sum[:seen] += grad_key
                value_sum[:seen] += grad_value
        grad_key = turn_half(key_sum[...], cosine[...], -sine[...]).astype(jnp.bfloat16)
        grad_v[:, :, part(1)] = grad_key.reshape(ranks, tok_rows, HEAD_DIM)
        grad_value = value_sum[...].astype(jnp.bfloat16)
        grad_v[:, :, part(2)] = grad_value.reshape(ranks, tok_rows, HEAD_DIM)
        return carry

    lax.fori_loop(0, heads, head, 0)
    beside_out.add()
    along_out = Along(place, links, lambda there: part_out.at[:, there, place.core], land_out)
    load_qkv.arrive()
    load_attn.arrive()
    load_tokens.arrive()

    def qkv_tile(i, carry):
        rows = model_width // ranks
        left = attn_v[:, :, pl.ds(pl.multiple_of(i * rows, 128), rows)].reshape(-1, rows)
        value = gram_product(left, grad_v[...].reshape(-1, 3 * head_cols))
        part_qkv[i] = value.astype(jnp.bfloat16).reshape(part_qkv.shape[1:])
        return carry

    lax.fori_loop(0, ranks, qkv_tile, 0)
    beside_qkv = Beside(place, links, part_qkv, other_qkv)
    scatter = PlaneScatter(place, links, partial, landing, passing)
    more_sums[...] = jnp.zeros_like(more_sums)

    def attn_back(t):
        def tile(i, carry):
            own = model_width // ranks
            value = back_product(grad_v[t], qkv_v[i].reshape(own, 3 * head_cols))
            partial[t, :, pl.ds(pl.multiple_of(i * own, 128), own)] = value.astype(jnp.bfloat16)
            return carry

        lax.fori_loop(0, ranks, tile, 0)

        def count(cut):
            value, unused = normed(tokens_v[t, cut].astype(jnp.float32))
            grad = partial[t, cut].astype(jnp.float32)
            more_sums[0:1] += jnp.sum(grad * value, axis=0, keepdims=True)
            more_sums[1:2] += jnp.sum(grad, axis=0, keepdims=True)

        return count

    count_across = attn_back(place.across)
    scatter.send_far()
    count_first = attn_back(place.first)
    scatter.send_near()
    beside_qkv.add()
    along_qkv = Along(place, links, lambda there: part_qkv.at[:, there, place.core], land_qkv)
    count_second = attn_back(place.second)
    scatter.relay()
    count_own = attn_back(rank)
    for count in (count_across, count_first, count_second, count_own):
        in_rows(tok_rows, 64, count)

    def pieces(row):
        spread = (row * mask[...]).astype(jnp.float32)
        return lax.dot_general(
            spread,
            comb[...].astype(jnp.float32),
            (((1,), (1,)), ((), ())),
            precision=lax.Precision.HIGHEST,
            preferred_element_type=jnp.float32,
        )

    part_small[...] = jnp.zeros_like(part_small)
    rows = (more_sums[0:1], more_sums[1:2], sums[0:1], sums[1:2], sums[2:3])
    for k, row in enumerate(rows):
        part_small[:, :, :, k] = pieces(row).reshape(ranks, chips, 2, 128)
    part_small[rank, :, :, 5:9] = pieces(sums[3:4]).reshape(chips, 2, 4, 128)
    beside_small = Beside(place, links, part_small, other_small)
    along_out.relay()
    load_down.arrive()
    sum_down[...] = along_down.total(mine_down[...])[0]
    load_up.arrive()
    mine_up[...] = along_up.total(mine_up[...]).astype(jnp.bfloat16)
    deal_up = Deal(place, links, [(lambda r: mine_up.at[r], land_sum_up.at[rank])])
    along_qkv.relay()
    beside_small.add()
    along_small = Along(place, links, lambda there: part_small.at[:, there, place.core], land_small)
    sum_out[...] = along_out.total(part_out[:, z, place.core])[0]
    along_small.relay()
    scatter.settle()

    def norm_back(cut):
        value, inverse = normed(tokens_v[rank, cut].astype(jnp.float32))
        grad = norm_backward(scatter.total(cut), value, inverse, gains[0:1])
        grad_tokens[cut] = (grad_hidden[cut] + grad).astype(jnp.bfloat16)

    in_rows(tok_rows, 64, norm_back)
    turn_small[...] = along_small.total(part_small[:, z, place.core])
    deal_small = Deal(place, links, [(lambda r: turn_small.at[r], land_sums.at[rank])])
    turn_qkv[...] = along_qkv.total(part_qkv[:, z, place.core]).astype(jnp.bfloat16)
    deal_qkv = Deal(place, links, [(lambda r: turn_qkv.at[r], land_sum_qkv.at[rank])])
    for message in dealt:
        message.arrive()
    deal_up.arrive()
    deal_small.arrive()
    sum_small[...] = land_sums[0] + land_sums[1] + land_sums[2] + land_sums[3]
    deal_qkv.arrive()
    links.drain()


def closing_kernel(
    hidden,
    gains,
    term_in,
    extra_in,
    grad_in,
    out_in,
    down_low,
    down_high,
    up_in,
    qkv_in,
    small_in,
    activations,
    grad_tokens,
    sum_query,
    sum_key,
    sum_value,
    sum_out,
    sum_up,
    sum_down,
    *small_sums,
):
    def add_terms(cut):
        total = hidden[cut] + gains[4:5] + term_in[0, cut].astype(jnp.float32)
        activations[0, cut] = total.astype(jnp.bfloat16)
        total = total + extra_in[cut].astype(jnp.float32)
        activations[1, cut] = total.astype(jnp.bfloat16)
        total = total + term_in[1, cut].astype(jnp.float32)
        activations[2, cut] = total.astype(jnp.bfloat16)
        total = total + term_in[2, cut].astype(jnp.float32) + term_in[3, cut].astype(jnp.float32)
        activations[3, cut] = total.astype(jnp.bfloat16)
        grad_tokens[cut] = grad_in[cut]

    in_rows(hidden.shape[0], 64, add_terms)
    sum_out[...] = out_in[...]
    half = down_low.shape[1]
    sum_down[:, :half] = down_low[...]
    sum_down[:, half:] = down_high[...]
    ranks, own, ff_cols = up_in.shape
    head_cols = qkv_in.shape[2] // 3
    for r in range(ranks):
        sum_up[:, r * ff_cols : (r + 1) * ff_cols] = up_in[r].astype(jnp.float32)
        for i, total in enumerate((sum_query, sum_key, sum_value)):
            value = qkv_in[r, :, i * head_cols : (i + 1) * head_cols]
            total[:, r * head_cols : (r + 1) * head_cols] = value.astype(jnp.float32)
    for i in range(5):
        small_sums[i][...] = small_in[i : i + 1, :own]
    small_sums[5][...] = jnp.concatenate([small_in[5 + q : 6 + q, :own] for q in range(4)], axis=1)


ANY = pl.BlockSpec(memory_space=pl.ANY)
ON_CORE = pl.BlockSpec(memory_space=pltpu.VMEM)


def connected(kernel, number, outs, out_specs, in_specs, scratch, operands):
    return pl.pallas_call(
        kernel,
        out_shape=outs,
        in_specs=in_specs,
        out_specs=out_specs,
        scratch_shapes=scratch + LINK_SCRATCH,
        compiler_params=pltpu.CompilerParams(
            collective_id=number, has_side_effects=True, vmem_limit_bytes=63 * 2**20
        ),
    )(*operands)


def array(shape, dtype=jnp.bfloat16):
    return jax.ShapeDtypeStruct(shape, dtype)


def turning(count):
    half_size = HEAD_DIM // 2
    inverse = np.exp(np.arange(half_size, dtype=np.float32) * np.float32(-math.log(10000.0) / half_size))
    angles = np.arange(count, dtype=np.float32)[:, None] * inverse.astype(np.float32)[None, :]
    cosine, sine = np.cos(angles), np.sin(angles)
    cosine = np.concatenate([cosine, cosine], axis=1)
    return jnp.asarray(cosine), jnp.asarray(np.concatenate([-sine, sine], axis=1))


def local_split(ranks, shards, *arguments):
    chips = shards // 2
    (
        tokens,
        cotangent,
        norm1_gain,
        norm1_bias,
        query_weight,
        key_weight,
        value_weight,
        out_weight,
        norm2_gain,
        norm2_bias,
        up_weight,
        up_bias,
        down_weight,
        down_bias,
    ) = arguments
    model_width = tokens.shape[2]
    tok_rows = tokens.shape[1]
    seq_len = tok_rows * ranks
    own = query_weight.shape[0]
    heads = HEADS // ranks
    head_cols = heads * HEAD_DIM
    ff_cols = FF // ranks
    scaling = HEAD_DIM ** (-0.5)
    rank = lax.axis_index("dp")

    column = np.arange(model_width)
    comb = jnp.asarray(column[None, :] % own == np.arange(128)[:, None], jnp.bfloat16)
    mask = jnp.asarray(column[None, :] // own == np.arange(ranks * shards)[:, None], jnp.float32)
    cosine, sine = turning(seq_len)
    own_tokens = tokens.reshape(tok_rows, model_width)
    blocks_low = array((ranks, tok_rows, model_width))
    down_rows = down_weight.shape[0]
    vmem = pltpu.VMEM
    low = jnp.bfloat16
    f32 = jnp.float32
    (
        all_tokens,
        attn_in,
        qkv_rot,
        mixed_low,
        hidden,
        ffn_in,
        gains,
        incoming,
        cotangent_sum,
        next_sum,
        w_qkv,
        w_out,
        w_up,
        w_down,
    ) = connected(
        functools.partial(forward_kernel, chips),
        1,
        (
            blocks_low,
            blocks_low,
            array((ranks, tok_rows, 3 * head_cols)),
            array((ranks, tok_rows, head_cols)),
            array((tok_rows, model_width), jnp.float32),
            blocks_low,
            array((8, model_width), jnp.float32),
            blocks_low,
            array((tok_rows, model_width), f32),
            array((tok_rows, model_width)),
            array((ranks, shards, own, 3 * head_cols)),
            array((shards, own, model_width)),
            array((ranks, shards, own, ff_cols)),
            array((shards, down_rows, model_width)),
        ),
        [ANY] * 4 + [ON_CORE, ANY, ON_CORE, ANY, ON_CORE] + [ANY] * 5,
        [ANY] * 2 + [ON_CORE] * 6 + [ANY] * 6 + [ON_CORE] * 4,
        [
            vmem((GRAN, tok_rows, model_width), low),
            vmem((GRAN, tok_rows, model_width), low),
            vmem((16, 128), low),
            vmem((ranks, tok_rows, model_width), jnp.bfloat16),
            vmem((ranks, tok_rows, model_width), jnp.bfloat16),
            vmem((ranks, tok_rows, 3 * head_cols), jnp.bfloat16),
            vmem((ranks, tok_rows, head_cols), jnp.bfloat16),
            vmem((ranks, shards, own, 3 * head_cols), jnp.bfloat16),
            vmem((shards, own, model_width), jnp.bfloat16),
            vmem((ranks, tok_rows, model_width), jnp.bfloat16),
            vmem((3, tok_rows, model_width), jnp.bfloat16),
            vmem((tok_rows, model_width), jnp.bfloat16),
            vmem((tok_rows, model_width), jnp.bfloat16),
            vmem((ranks, shards, 16, 128), jnp.bfloat16),
        ],
        (
            own_tokens,
            cotangent.reshape(GRAN, tok_rows, model_width),
            norm1_gain.reshape(1, own),
            norm1_bias.reshape(1, own),
            norm2_gain.reshape(1, own),
            norm2_bias.reshape(1, own),
            down_bias.reshape(1, own),
            up_bias.reshape(1, -1),
            query_weight,
            key_weight,
            value_weight,
            out_weight,
            up_weight,
            down_weight,
            comb,
            mask,
            cosine,
            sine,
        ),
    )
    grad_hidden, branch, sums, down_low, share_down, share_up, terms, extra_in = connected(
        functools.partial(middle_kernel, chips),
        2,
        (
            array((tok_rows, model_width), f32),
            array((tok_rows, model_width)),
            array((8, model_width), f32),
            array((down_rows, model_width // 2), f32),
            array((1, chips, down_rows, model_width // 2)),
            array((ranks, chips, own, ff_cols)),
            blocks_low,
            array((tok_rows, model_width)),
        ),
        [ON_CORE] * 4 + [ANY] * 4,
        [ANY] * 5 + [ON_CORE] * 3,
        [
            vmem((ranks, tok_rows, model_width), low),
            vmem((2, ranks, tok_rows, model_width), low),
            vmem((ranks, chips, 2, own, ff_cols), low),
            vmem((shards, down_rows, model_width), low),
            vmem((ranks, tok_rows, ff_cols), low),
            vmem((ranks, tok_rows, ff_cols), low),
            vmem((2, chips, 2, down_rows, model_width // 2), low),
            vmem((2, chips, down_rows, model_width // 2), low),
            vmem((4, 1, down_rows, model_width // 2), low),
            vmem((ranks, chips, own, ff_cols), low),
            vmem((2, ranks, tok_rows, model_width), low),
            vmem((tok_rows, model_width), low),
            vmem((tok_rows, model_width), low),
            vmem((ranks, tok_rows, model_width), low),
            vmem((3, tok_rows, model_width), low),
            vmem((tok_rows, model_width), low),
        ],
        (
            ffn_in,
            incoming,
            next_sum,
            w_up.reshape(ranks, chips, 2, own, ff_cols),
            w_down,
            hidden,
            cotangent_sum,
            gains,
        ),
    )
    term_in, grad_inputs, sum_out, down_high, sum_up, sum_qkv, small_sums = connected(
        functools.partial(last_kernel, chips),
        3,
        (
            blocks_low,
            array((tok_rows, model_width)),
            array((own, model_width), f32),
            array((down_rows, model_width // 2), f32),
            array((ranks, own, ff_cols)),
            array((ranks, own, 3 * head_cols)),
            array((16, 128), f32),
        ),
        [ANY] + [ON_CORE] * 3 + [ANY] * 2 + [ON_CORE],
        [ANY] * 10 + [ON_CORE] * 7,
        [
            vmem((ranks, tok_rows, model_width), low),
            vmem((ranks, tok_rows, 3 * head_cols), low),
            vmem((ranks, tok_rows, head_cols), low),
            vmem((ranks, tok_rows, head_cols), low),
            vmem((shards, own, model_width), low),
            vmem((ranks, shards, own, 3 * head_cols), low),
            vmem((ranks, tok_rows, model_width), low),
            vmem((ranks, tok_rows, model_width), low),
            vmem((ranks, tok_rows, 3 * head_cols), low),
            vmem((seq_len, HEAD_DIM), f32),
            vmem((seq_len, HEAD_DIM), f32),
            vmem((ranks, tok_rows, model_width), low),
            vmem((3, tok_rows, model_width), low),
            vmem((tok_rows, model_width), low),
            vmem((1, down_rows, model_width // 2), low),
            vmem((1, down_rows, model_width // 2), low),
            vmem((4, 1, down_rows, model_width // 2), low),
            vmem((ranks, own, ff_cols), low),
            vmem((ranks, own, ff_cols), low),
            vmem((4, ranks, own, ff_cols), low),
            vmem((1, chips, 2, own, model_width), low),
            vmem((1, chips, own, model_width), low),
            vmem((4, 1, own, model_width), low),
            vmem((ranks, chips, 2, own, 3 * head_cols), low),
            vmem((ranks, chips, own, 3 * head_cols), low),
            vmem((4, ranks, own, 3 * head_cols), low),
            vmem((ranks, own, 3 * head_cols), low),
            vmem((ranks, chips, 2, 16, 128), f32),
            vmem((ranks, chips, 16, 128), f32),
            vmem((4, ranks, 16, 128), f32),
            vmem((ranks, 16, 128), f32),
            vmem((ranks, 16, 128), f32),
            vmem((8, model_width), f32),
        ],
        (
            branch,
            share_down,
            share_up,
            terms,
            qkv_rot,
            mixed_low,
            w_out,
            w_qkv,
            attn_in,
            all_tokens,
            grad_hidden,
            gains,
            sums,
            comb,
            mask,
            cosine,
            sine,
        ),
    )
    (
        activations,
        grad_tokens,
        sum_query,
        sum_key,
        sum_value,
        sum_out,
        sum_up,
        sum_down,
        *gain_sums,
    ) = pl.pallas_call(
        closing_kernel,
        out_shape=(
            array((GRAN, tok_rows, model_width)),
            array((tok_rows, model_width)),
            *[array((own, model_width), f32) for i in range(4)],
            array((own, FF), f32),
            array((down_rows, model_width), f32),
            *[array((1, own), f32) for i in range(5)],
            array((1, down_rows), f32),
        ),
        in_specs=[ON_CORE] * 11,
        out_specs=[ON_CORE] * 14,
        compiler_params=pltpu.CompilerParams(vmem_limit_bytes=48 * 2**20),
    )(
        hidden,
        gains,
        term_in,
        extra_in,
        grad_inputs,
        sum_out,
        down_low,
        down_high,
        sum_up,
        sum_qkv,
        small_sums,
    )
    gain_sums = [v.reshape(-1) for v in gain_sums]
    return (
        activations.reshape(GRAN, 1, tok_rows, model_width),
        grad_tokens.reshape(1, tok_rows, model_width),
        gain_sums[0],
        gain_sums[1],
        sum_query,
        sum_key,
        sum_value,
        sum_out,
        gain_sums[2],
        gain_sums[3],
        sum_up,
        gain_sums[5],
        sum_down,
        gain_sums[4],
    )


def solution(mesh):
    placed = (
        P("fsdp", "dp", None),
        P(None, "fsdp", "dp", None),
        P(("dp", "fsdp")),
        P(("dp", "fsdp")),
        P(("dp", "fsdp"), None),
        P(("dp", "fsdp"), None),
        P(("dp", "fsdp"), None),
        P(("dp", "fsdp"), None),
        P(("dp", "fsdp")),
        P(("dp", "fsdp")),
        P(("dp", "fsdp"), None),
        P(("dp", "fsdp")),
        P(("dp", "fsdp"), None),
        P(("dp", "fsdp")),
    )
    ranks, shards = mesh.shape["dp"], mesh.shape["fsdp"]
    local = local_gathered
    if ranks == 4 and shards == 8:
        local = functools.partial(local_split, ranks, shards)
    return jax.shard_map(
        local,
        mesh=mesh,
        in_specs=placed,
        out_specs=(
            P(None, "fsdp", "dp", None),
            P("fsdp", "dp", None),
            P(("dp", "fsdp")),
            P(("dp", "fsdp")),
            P(("dp", "fsdp"), None),
            P(("dp", "fsdp"), None),
            P(("dp", "fsdp"), None),
            P(("dp", "fsdp"), None),
            P(("dp", "fsdp")),
            P(("dp", "fsdp")),
            P(("dp", "fsdp"), None),
            P(("dp", "fsdp")),
            P(("dp", "fsdp"), None),
            P(("dp", "fsdp")),
        ),
        check_vma=False,
    )
```

```python
import functools
import math

import jax
import jax.numpy as jnp
import numpy as np
from jax import lax
from jax.experimental import pallas as pl
from jax.experimental.pallas import tpu as pltpu
from jax.sharding import PartitionSpec as P

HEADS = 12
HEAD_DIM = 128
FF = 6144
GRAN = 4


epsilon = 1e-05
masked_score = -1e30


def product(left, right):
    return jnp.dot(left, right, preferred_element_type=jnp.float32)


def gram_product(left, right):
    return lax.dot_general(
        left, right, (((0,), (0,)), ((), ())), preferred_element_type=jnp.float32
    )


def back_product(left, right):
    return lax.dot_general(
        left, right, (((1,), (1,)), ((), ())), preferred_element_type=jnp.float32
    )


def norm_parts(values):
    centred = values - jnp.mean(values, axis=-1, keepdims=True)
    inverse = lax.rsqrt(jnp.mean(centred * centred, axis=-1, keepdims=True) + epsilon)
    return (centred * inverse, inverse)


def norm_backward(grad_normed, normed, inverse, gain):
    scaled = grad_normed * gain
    return inverse * (
        scaled
        - jnp.mean(scaled, axis=-1, keepdims=True)
        - normed * jnp.mean(scaled * normed, axis=-1, keepdims=True)
    )


def gelu_value(values):
    return (
        0.5
        * values
        * (1.0 + jnp.tanh(0.7978845608028654 * (values + 0.044715 * values * values * values)))
    )


def gelu_grad(values):
    tangent = jnp.tanh(0.7978845608028654 * (values + 0.044715 * values * values * values))
    return 0.5 * (1.0 + tangent) + 0.5 * values * (1.0 - tangent * tangent) * 0.7978845608028654 * (
        1.0 + 3.0 * 0.044715 * values * values
    )


def rotary_tables(positions, half_size):
    ladder = jnp.arange(half_size).astype(jnp.float32)
    inverse = jnp.exp(ladder * (-math.log(10000.0) / half_size))
    angles = positions[:, None] * inverse[None, :]
    return (jnp.cos(angles)[:, None, :], jnp.sin(angles)[:, None, :])


def rotate(values, cosine, sine):
    half_size = values.shape[-1] // 2
    first = values[..., :half_size]
    second = values[..., half_size:]
    return jnp.concatenate(
        [first * cosine - second * sine, second * cosine + first * sine], axis=-1
    )


def block_scores(queries, positions, key_block, start_row):
    block_rows = key_block.shape[0]
    scores = jnp.einsum("qhd,khd->hqk", queries, key_block, preferred_element_type=jnp.float32)
    key_positions = start_row + jnp.arange(block_rows, dtype=jnp.int32)
    visible = positions[None, :, None] >= key_positions[None, None, :]
    return (jnp.where(visible, scores, masked_score), visible)


def key_blocking(keys_all, values_all, key_offset):
    seq_len = keys_all.shape[0]
    block_rows = min(512, seq_len)
    block_count = seq_len // block_rows
    key_blocks = keys_all.reshape(block_count, block_rows, HEADS, HEAD_DIM)
    value_blocks = values_all.reshape(block_count, block_rows, HEADS, HEAD_DIM)
    starts = key_offset + jnp.arange(block_count, dtype=jnp.int32) * block_rows
    return (key_blocks, value_blocks, starts)


def attend(queries, keys_all, values_all, positions):
    tok_rows = queries.shape[0]
    key_blocks, value_blocks, starts = key_blocking(keys_all, values_all, jnp.int32(0))

    def measure(state_pair, block_pair):
        top_score, total = state_pair
        key_block, start_row = block_pair
        scores, visible = block_scores(queries, positions, key_block, start_row)
        new_top = jnp.maximum(top_score, jnp.max(scores, axis=-1))
        raised = jnp.where(visible, jnp.exp(scores - new_top[..., None]), 0.0)
        total = total * jnp.exp(top_score - new_top) + jnp.sum(raised, axis=-1)
        return ((new_top, total), None)

    initial = (
        jnp.full((HEADS, tok_rows), masked_score, jnp.float32),
        jnp.zeros((HEADS, tok_rows), jnp.float32),
    )
    (top_score, total), unused = lax.scan(measure, initial, (key_blocks, starts))
    log_total = top_score + jnp.log(total)

    def accumulate(mixed, block_triple):
        key_block, value_block, start_row = block_triple
        scores, visible = block_scores(queries, positions, key_block, start_row)
        probs = jnp.where(visible, jnp.exp(scores - log_total[..., None]), 0.0).astype(jnp.bfloat16)
        return (
            mixed
            + jnp.einsum("hqk,khd->qhd", probs, value_block, preferred_element_type=jnp.float32),
            None,
        )

    mixed, unused = lax.scan(
        accumulate,
        jnp.zeros((tok_rows, HEADS, HEAD_DIM), jnp.float32),
        (key_blocks, value_blocks, starts),
    )
    return (mixed, log_total)


def attend_back(
    queries, positions, keys_all, values_all, key_offset, grad_mixed, log_total, row_delta
):
    tok_rows = queries.shape[0]
    key_blocks, value_blocks, starts = key_blocking(keys_all, values_all, key_offset)

    def backward_block(grad_queries, block_triple):
        key_block, value_block, start_row = block_triple
        scores, visible = block_scores(queries, positions, key_block, start_row)
        probs = jnp.where(visible, jnp.exp(scores - log_total[..., None]), 0.0)
        grad_probs = jnp.einsum(
            "qhd,khd->hqk", grad_mixed, value_block, preferred_element_type=jnp.float32
        )
        grad_scores = (probs * (grad_probs - row_delta[..., None])).astype(jnp.bfloat16)
        grad_queries = grad_queries + jnp.einsum(
            "hqk,khd->qhd", grad_scores, key_block, preferred_element_type=jnp.float32
        )
        grad_key_block = jnp.einsum(
            "hqk,qhd->khd", grad_scores, queries, preferred_element_type=jnp.float32
        )
        grad_value_block = jnp.einsum(
            "hqk,qhd->khd",
            probs.astype(jnp.bfloat16),
            grad_mixed,
            preferred_element_type=jnp.float32,
        )
        return (grad_queries, (grad_key_block, grad_value_block))

    grad_queries, (grad_keys, grad_values) = lax.scan(
        backward_block,
        jnp.zeros((tok_rows, HEADS, HEAD_DIM), jnp.float32),
        (key_blocks, value_blocks, starts),
    )
    key_len = keys_all.shape[0]
    return (
        grad_queries,
        grad_keys.reshape(key_len, HEADS * HEAD_DIM),
        grad_values.reshape(key_len, HEADS * HEAD_DIM),
    )


def local_gathered(
    tokens,
    cotangent,
    norm1_gain,
    norm1_bias,
    query_weight,
    key_weight,
    value_weight,
    out_weight,
    norm2_gain,
    norm2_bias,
    up_weight,
    up_bias,
    down_weight,
    down_bias,
):
    (
        gain_one,
        bias_one,
        w_query,
        w_key,
        w_value,
        w_out,
        gain_two,
        bias_two,
        w_up,
        b_up,
        w_down,
        b_down,
    ) = (
        lax.all_gather(norm1_gain, ("dp", "fsdp"), axis=0, tiled=True),
        lax.all_gather(norm1_bias, ("dp", "fsdp"), axis=0, tiled=True),
        lax.all_gather(query_weight, ("dp", "fsdp"), axis=0, tiled=True),
        lax.all_gather(key_weight, ("dp", "fsdp"), axis=0, tiled=True),
        lax.all_gather(value_weight, ("dp", "fsdp"), axis=0, tiled=True),
        lax.all_gather(out_weight, ("dp", "fsdp"), axis=0, tiled=True),
        lax.all_gather(norm2_gain, ("dp", "fsdp"), axis=0, tiled=True),
        lax.all_gather(norm2_bias, ("dp", "fsdp"), axis=0, tiled=True),
        lax.all_gather(up_weight, ("dp", "fsdp"), axis=0, tiled=True),
        lax.all_gather(up_bias, ("dp", "fsdp"), axis=0, tiled=True),
        lax.all_gather(down_weight, ("dp", "fsdp"), axis=0, tiled=True),
        lax.all_gather(down_bias, ("dp", "fsdp"), axis=0, tiled=True),
    )
    seq_count = tokens.shape[0]
    tok_rows = tokens.shape[1]
    model_width = tokens.shape[2]
    all_rows = seq_count * tok_rows
    scaling = HEAD_DIM ** (-0.5)
    inputs = tokens.reshape(all_rows, model_width).astype(jnp.float32)
    normed_one, inverse_one = norm_parts(inputs)
    attn_in = (normed_one * gain_one.astype(jnp.float32) + bias_one.astype(jnp.float32)).astype(
        jnp.bfloat16
    )
    queries = product(attn_in, w_query).reshape(seq_count, tok_rows, HEADS, HEAD_DIM)
    key_raw = product(attn_in, w_key).reshape(seq_count, tok_rows, HEADS, HEAD_DIM)
    value_low = (
        product(attn_in, w_value).astype(jnp.bfloat16).reshape(seq_count, tok_rows, model_width)
    )
    key_offset = lax.axis_index("dp") * tok_rows
    positions = key_offset + jnp.arange(tok_rows, dtype=jnp.int32)
    cosine, sine = rotary_tables(positions.astype(jnp.float32), HEAD_DIM // 2)
    q_rot = (rotate(queries, cosine, sine) * scaling).astype(jnp.bfloat16)
    k_flat = (
        rotate(key_raw, cosine, sine).astype(jnp.bfloat16).reshape(seq_count, tok_rows, model_width)
    )
    keys_all, values_all = (
        lax.all_gather(k_flat, "dp", axis=1, tiled=True),
        lax.all_gather(value_low, "dp", axis=1, tiled=True),
    )
    seq_len = keys_all.shape[1]
    mixed, log_total = jax.vmap(attend, in_axes=(0, 0, 0, None))(
        q_rot,
        keys_all.reshape(seq_count, seq_len, HEADS, HEAD_DIM),
        values_all.reshape(seq_count, seq_len, HEADS, HEAD_DIM),
        positions,
    )
    mixed_low = mixed.reshape(all_rows, model_width).astype(jnp.bfloat16)
    hidden = inputs + product(mixed_low, w_out)
    normed_two, inverse_two = norm_parts(hidden)
    ffn_in = (normed_two * gain_two.astype(jnp.float32) + bias_two.astype(jnp.float32)).astype(
        jnp.bfloat16
    )
    preact = product(ffn_in, w_up) + b_up.astype(jnp.float32)
    edges = [0] + [FF // 2 ** (GRAN - 1 - level_idx) for level_idx in range(GRAN)]
    gated_list = []
    result_list = []
    for level_idx in range(GRAN):
        level_width = edges[level_idx + 1]
        gated = gelu_value(preact[:, :level_width]).astype(jnp.bfloat16)
        gated_list.append(gated)
        result = hidden + product(gated, w_down[:level_width]) + b_down.astype(jnp.float32)
        result_list.append(result.astype(jnp.bfloat16))
    activations = jnp.stack(result_list).reshape(GRAN, seq_count, tok_rows, model_width)
    back_gain_one, back_query, back_key, back_value, back_out, back_gain_two, back_up, back_down = (
        lax.all_gather(norm1_gain, ("dp", "fsdp"), axis=0, tiled=True),
        lax.all_gather(query_weight, ("dp", "fsdp"), axis=0, tiled=True),
        lax.all_gather(key_weight, ("dp", "fsdp"), axis=0, tiled=True),
        lax.all_gather(value_weight, ("dp", "fsdp"), axis=0, tiled=True),
        lax.all_gather(out_weight, ("dp", "fsdp"), axis=0, tiled=True),
        lax.all_gather(norm2_gain, ("dp", "fsdp"), axis=0, tiled=True),
        lax.all_gather(up_weight, ("dp", "fsdp"), axis=0, tiled=True),
        lax.all_gather(down_weight, ("dp", "fsdp"), axis=0, tiled=True),
    )
    grads_out = cotangent.reshape(GRAN, all_rows, model_width)
    grad_hidden = jnp.sum(grads_out.astype(jnp.float32), axis=0)
    grad_down_bias = jnp.sum(grad_hidden, axis=0)
    grad_ffn_in = jnp.zeros((all_rows, model_width), jnp.float32)
    pre_grads = []
    for level_idx in range(GRAN):
        level_width = edges[level_idx + 1]
        grad_gated = back_product(grads_out[level_idx], back_down[:level_width])
        grad_pre = (grad_gated * gelu_grad(preact[:, :level_width])).astype(jnp.bfloat16)
        pre_grads.append(grad_pre)
        grad_ffn_in = grad_ffn_in + back_product(grad_pre, back_up[:, :level_width])
    up_blocks = []
    bias_blocks = []
    down_blocks = []
    for block_idx in range(GRAN):
        start_col = edges[block_idx]
        stop_col = edges[block_idx + 1]
        stacked_grad = jnp.concatenate(
            [pre_grads[level_idx][:, start_col:stop_col] for level_idx in range(block_idx, GRAN)],
            axis=0,
        )
        stacked_in = jnp.concatenate([ffn_in] * (GRAN - block_idx), axis=0)
        up_blocks.append(gram_product(stacked_in, stacked_grad))
        bias_blocks.append(jnp.sum(stacked_grad.astype(jnp.float32), axis=0))
        stacked_gated = jnp.concatenate(
            [gated_list[level_idx][:, start_col:stop_col] for level_idx in range(block_idx, GRAN)],
            axis=0,
        )
        stacked_out = jnp.concatenate(
            [grads_out[level_idx] for level_idx in range(block_idx, GRAN)], axis=0
        )
        down_blocks.append(gram_product(stacked_gated, stacked_out))
    grad_up_weight = jnp.concatenate(up_blocks, axis=1)
    grad_up_bias = jnp.concatenate(bias_blocks, axis=0)
    grad_down_weight = jnp.concatenate(down_blocks, axis=0)
    grad_gain_two = jnp.sum(grad_ffn_in * normed_two, axis=0)
    grad_bias_two = jnp.sum(grad_ffn_in, axis=0)
    grad_hidden = grad_hidden + norm_backward(
        grad_ffn_in, normed_two, inverse_two, back_gain_two.astype(jnp.float32)
    )
    grad_branch = grad_hidden.astype(jnp.bfloat16)
    grad_out_weight = gram_product(mixed_low, grad_branch)
    grad_mixed = (
        back_product(grad_branch, back_out)
        .astype(jnp.bfloat16)
        .reshape(seq_count, tok_rows, HEADS, HEAD_DIM)
    )
    row_delta = jnp.einsum("sqhd,sqhd->shq", grad_mixed.astype(jnp.float32), mixed)
    keys_again, values_again = (
        lax.all_gather(k_flat, "dp", axis=1, tiled=True),
        lax.all_gather(value_low, "dp", axis=1, tiled=True),
    )
    back_all = jax.vmap(attend_back, in_axes=(0, None, 0, 0, None, 0, 0, 0))
    grad_q_rot, grad_keys_all, grad_values_all = back_all(
        q_rot,
        positions,
        keys_again.reshape(seq_count, seq_len, HEADS, HEAD_DIM),
        values_again.reshape(seq_count, seq_len, HEADS, HEAD_DIM),
        jnp.int32(0),
        grad_mixed,
        log_total,
        row_delta,
    )
    every_query, every_grad = (
        lax.all_gather(q_rot, "dp", axis=1, tiled=True),
        lax.all_gather(grad_mixed, "dp", axis=1, tiled=True),
    )
    every_total, every_delta = (
        lax.all_gather(jnp.transpose(log_total, (0, 2, 1)), "dp", axis=1, tiled=True),
        lax.all_gather(jnp.transpose(row_delta, (0, 2, 1)), "dp", axis=1, tiled=True),
    )
    every_position = jnp.arange(seq_len, dtype=jnp.int32)
    unused_rows, grad_key_mine, grad_value_mine = back_all(
        every_query,
        every_position,
        k_flat.reshape(seq_count, tok_rows, HEADS, HEAD_DIM),
        value_low.reshape(seq_count, tok_rows, HEADS, HEAD_DIM),
        key_offset,
        every_grad,
        jnp.transpose(every_total, (0, 2, 1)),
        jnp.transpose(every_delta, (0, 2, 1)),
    )
    grad_query = (
        rotate(grad_q_rot * scaling, cosine, -sine)
        .reshape(all_rows, model_width)
        .astype(jnp.bfloat16)
    )
    grad_key = (
        rotate(grad_key_mine.reshape(seq_count, tok_rows, HEADS, HEAD_DIM), cosine, -sine)
        .reshape(all_rows, model_width)
        .astype(jnp.bfloat16)
    )
    grad_val = grad_value_mine.reshape(all_rows, model_width).astype(jnp.bfloat16)
    grad_query_weight = gram_product(attn_in, grad_query)
    grad_key_weight = gram_product(attn_in, grad_key)
    grad_value_weight = gram_product(attn_in, grad_val)
    grad_attn_in = (
        back_product(grad_query, back_query)
        + back_product(grad_key, back_key)
        + back_product(grad_val, back_value)
    )
    grad_gain_one = jnp.sum(grad_attn_in * normed_one, axis=0)
    grad_bias_one = jnp.sum(grad_attn_in, axis=0)
    grad_inputs = grad_hidden + norm_backward(
        grad_attn_in, normed_one, inverse_one, back_gain_one.astype(jnp.float32)
    )
    (
        sum_gain_one,
        sum_bias_one,
        sum_query,
        sum_key,
        sum_value,
        sum_out,
        sum_gain_two,
        sum_bias_two,
        sum_up,
        sum_up_bias,
        sum_down,
        sum_down_bias,
    ) = (
        lax.psum_scatter(grad_gain_one, ("dp", "fsdp"), scatter_dimension=0, tiled=True),
        lax.psum_scatter(grad_bias_one, ("dp", "fsdp"), scatter_dimension=0, tiled=True),
        lax.psum_scatter(grad_query_weight, ("dp", "fsdp"), scatter_dimension=0, tiled=True),
        lax.psum_scatter(grad_key_weight, ("dp", "fsdp"), scatter_dimension=0, tiled=True),
        lax.psum_scatter(grad_value_weight, ("dp", "fsdp"), scatter_dimension=0, tiled=True),
        lax.psum_scatter(grad_out_weight, ("dp", "fsdp"), scatter_dimension=0, tiled=True),
        lax.psum_scatter(grad_gain_two, ("dp", "fsdp"), scatter_dimension=0, tiled=True),
        lax.psum_scatter(grad_bias_two, ("dp", "fsdp"), scatter_dimension=0, tiled=True),
        lax.psum_scatter(grad_up_weight, ("dp", "fsdp"), scatter_dimension=0, tiled=True),
        lax.psum_scatter(grad_up_bias, ("dp", "fsdp"), scatter_dimension=0, tiled=True),
        lax.psum_scatter(grad_down_weight, ("dp", "fsdp"), scatter_dimension=0, tiled=True),
        lax.psum_scatter(grad_down_bias, ("dp", "fsdp"), scatter_dimension=0, tiled=True),
    )
    return (
        activations,
        grad_inputs.astype(jnp.bfloat16).reshape(seq_count, tok_rows, model_width),
        sum_gain_one,
        sum_bias_one,
        sum_query,
        sum_key,
        sum_value,
        sum_out,
        sum_gain_two,
        sum_bias_two,
        sum_up,
        sum_up_bias,
        sum_down,
        sum_down_bias,
    )


MESH = pl.DeviceIdType.MESH


class Place:
    def __init__(self, chips):
        self.chips = chips
        self.rank = lax.axis_index("dp")
        self.shard = lax.axis_index("fsdp")
        self.z = lax.div(self.shard, 2)
        self.core = lax.rem(self.shard, 2)
        along_x = self.rank + 1 - 2 * lax.rem(self.rank, 2)
        along_y = self.rank + 2 - 4 * lax.div(self.rank, 2)
        self.first = jnp.where(self.core == 0, along_x, along_y)
        self.second = jnp.where(self.core == 0, along_y, along_x)
        self.across = 3 - self.rank
        self.sibling = self.shard + 1 - 2 * self.core

    def at(self, rank=None, shard=None):
        return (self.rank if rank is None else rank, self.shard if shard is None else shard)

    def others(self):
        return [lax.rem(self.shard + k, 2 * self.chips) for k in range(1, 2 * self.chips)]

    def greet(self, plane=True, sibling=False, ring=False, group=False):
        barrier = pltpu.get_barrier_semaphore()
        count = 0
        targets = []
        if plane:
            targets += [self.at(rank=r) for r in (self.first, self.second, self.across)]
        if sibling:
            targets.append(self.at(shard=self.sibling))
        if ring:
            targets += [self.at(shard=self.hop(k)) for k in range(1, self.chips)]
        if group:
            targets += [self.at(shard=f) for f in self.others()]
        for target in targets:
            pl.semaphore_signal(barrier, inc=1, device_id=target, device_id_type=MESH)
            count += 1
        pl.semaphore_wait(barrier, count)

    def hop(self, k):
        return 2 * lax.rem(self.z + k, self.chips) + self.core


def under(condition, action):
    if condition is None:
        action()
    else:
        pl.when(condition)(action)


class Message:
    def __init__(self, links, src, dst, target, sent=None, comes=None):
        index = links.take()
        self.copy = pltpu.make_async_remote_copy(
            src_ref=src,
            dst_ref=dst,
            send_sem=links.send.at[index],
            recv_sem=links.recv.at[index],
            device_id=target,
            device_id_type=MESH,
        )
        self.sent, self.comes = sent, comes
        links.open.append(self)
        under(sent, self.copy.start)

    def arrive(self):
        under(self.comes, self.copy.wait_recv)

    def leave(self):
        under(self.sent, self.copy.wait_send)


class Near:
    def __init__(self, links, src, dst, where):
        self.copy = pltpu.make_async_copy(src, dst, links.near.at[links.used_near])
        links.used_near += 1
        self.where = where
        self.waits = True
        under(where, self.copy.start)

    def arrive(self):
        if self.waits:
            under(self.where, self.copy.wait)
        self.waits = False


class Links:
    def __init__(self, send, recv, near):
        self.send, self.recv, self.near = send, recv, near
        self.used = 0
        self.used_near = 0
        self.open = []
        self.open_near = []

    def take(self):
        self.used += 1
        return self.used - 1

    def keep(self, src, dst, where=None):
        copy = Near(self, src, dst, where)
        self.open_near.append(copy)
        return copy

    def drain(self):
        for copy in self.open_near:
            copy.arrive()
        for message in self.open:
            message.leave()


LINK_SCRATCH = [
    pltpu.SemaphoreType.DMA((128,)),
    pltpu.SemaphoreType.DMA((128,)),
    pltpu.SemaphoreType.DMA((32,)),
]


def normed(values):
    centred = values - jnp.mean(values, axis=-1, keepdims=True)
    inverse = lax.rsqrt(jnp.mean(centred * centred, axis=-1, keepdims=True) + epsilon)
    return centred * inverse, inverse


def in_rows(count, step, body):
    def one(i, carry):
        body(pl.ds(pl.multiple_of(i * step, step), step))
        return carry

    lax.fori_loop(0, count // step, one, 0)


def turn_half(values, cosine, sine):
    return values * cosine + pltpu.roll(values, HEAD_DIM // 2, 1) * sine


class PlaneGather:
    def __init__(self, place, links, src, dst, parts):
        self.place, self.links, self.dst = place, links, dst
        rows = src.shape[0] // parts
        self.cuts = [pl.ds(k * rows, rows) for k in range(parts)]
        self.own = links.keep(src, dst.at[place.rank])
        self.first, self.second = [], []
        for cut in self.cuts:
            for side, target in ((self.first, place.first), (self.second, place.second)):
                block = dst.at[place.rank, cut]
                side.append(Message(links, src.at[cut], block, place.at(rank=target)))
        self.passed = []

    def relay(self, k):
        self.first[k].arrive()
        block = self.dst.at[self.place.first, self.cuts[k]]
        target = self.place.at(rank=self.place.second)
        self.passed.append(Message(self.links, block, block, target))

    def finish(self):
        for message in self.second + self.passed:
            message.arrive()


class PlaneScatter:
    def __init__(self, place, links, partial, landing, turn):
        self.place, self.links, self.partial, self.landing, self.turn = (
            place,
            links,
            partial,
            landing,
            turn,
        )
        self.target = place.at(rank=place.first)

    def send_far(self):
        self.far = Message(
            self.links, self.partial.at[self.place.across], self.landing.at[0], self.target
        )

    def send_near(self):
        self.near = Message(
            self.links, self.partial.at[self.place.first], self.landing.at[1], self.target
        )

    def relay(self):
        self.far.arrive()

        def add(cut):
            mine = self.partial[self.place.second, cut].astype(jnp.float32)
            mine = mine + self.landing[0, cut].astype(jnp.float32)
            self.turn[cut] = mine.astype(jnp.bfloat16)

        in_rows(self.turn.shape[0], 64, add)
        self.last = Message(
            self.links, self.turn, self.landing.at[2], self.place.at(rank=self.place.second)
        )

    def settle(self):
        self.near.arrive()
        self.last.arrive()

    def total(self, cut):
        total = self.partial[self.place.rank, cut].astype(jnp.float32)
        total = total + self.landing[1, cut].astype(jnp.float32)
        return total + self.landing[2, cut].astype(jnp.float32)


class Chain:
    def __init__(self, place, links, src, slot):
        self.place, self.links, self.slot = place, links, slot
        z, last = place.z, place.chips - 1
        own = slot(place.shard)
        self.up = Message(links, src, own, place.at(shard=place.shard + 2), z < last, z > 0)
        self.down = Message(links, src, own, place.at(shard=place.shard - 2), z > 0, z < last)
        self.beside = [Message(links, src, own, place.at(shard=place.sibling))]

    def step(self, s):
        place, links = self.place, self.links
        z, last = place.z, place.chips - 1
        below = self.slot(jnp.maximum(place.shard - 2 * s, place.core))
        above = self.slot(jnp.minimum(place.shard + 2 * s, 2 * last + place.core))
        self.up.arrive()
        has_below, has_above = z >= s, z <= last - s
        up = down = None
        if s < last:
            target = place.at(shard=place.shard + 2)
            up = Message(links, below, below, target, has_below & (z < last), z >= s + 1)
        self.beside.append(
            Message(links, below, below, place.at(shard=place.sibling), has_below, has_below)
        )
        self.down.arrive()
        if s < last:
            target = place.at(shard=place.shard - 2)
            down = Message(links, above, above, target, has_above & (z > 0), z <= last - s - 1)
        self.beside.append(
            Message(links, above, above, place.at(shard=place.sibling), has_above, has_above)
        )
        self.up, self.down = up, down

    def finish(self):
        for message in self.beside:
            message.arrive()


class Beside:
    def __init__(self, place, links, part, other):
        self.place, self.part, self.other = place, part, other
        self.message = Message(
            links, part.at[:, :, 1 - place.core], other, place.at(shard=place.sibling)
        )

    def add(self):
        self.message.arrive()
        core = self.place.core

        def one(k, carry):
            total = self.part[:, k, core].astype(jnp.float32) + self.other[:, k].astype(jnp.float32)
            self.part[:, k, core] = total.astype(self.part.dtype)
            return carry

        lax.fori_loop(0, self.place.chips, one, 0)


class Along:
    def __init__(self, place, links, share, landing, far=None):
        self.place, self.links, self.landing = place, links, landing
        z = place.z
        self.middle = (z == 1) | (z == 2)
        end = jnp.logical_not(self.middle)
        partner = z + 1 - 2 * lax.rem(z, 2)
        over = jnp.where(z < 2, 2, 1)
        self.other_end = jnp.where(z < 2, 3, 0)
        self.far = share(self.other_end) if far is None else far

        def to(chip):
            return place.at(shard=2 * chip + place.core)

        self.to = to

        @pl.when(end)
        def nothing_comes():
            landing[2] = jnp.zeros_like(landing[2])

        self.merge = Message(
            links, share(self.other_end), landing.at[3], to(partner), end, self.middle
        )
        self.messages = [
            Message(links, share(partner), landing.at[0], to(partner)),
            Message(links, share(over), landing.at[1], to(over), end, self.middle),
            Message(links, share(over), landing.at[2], to(over), self.middle, self.middle),
        ]

    def relay(self):
        self.merge.arrive()
        landing = self.landing

        @pl.when(self.middle)
        def add():
            total = landing[3].astype(jnp.float32) + self.far[...].astype(jnp.float32)
            landing[3] = total.astype(landing.dtype)

        end = jnp.logical_not(self.middle)
        self.messages.append(
            Message(
                self.links, landing.at[3], landing.at[1], self.to(self.other_end), self.middle, end
            )
        )

    def total(self, mine):
        total = mine.astype(jnp.float32)
        for message in self.messages:
            message.arrive()
        for k in range(3):
            total = total + self.landing[k].astype(jnp.float32)
        return total


class Detour:
    def __init__(self, place, links, src, dst, stop, source, turn, goal):
        self.place, self.links, self.dst, self.stop = place, links, dst, stop
        straight = place.core == 0
        around = place.core == 1
        across = place.at(rank=place.across)
        self.goal = around & (place.rank == goal)
        self.turn = around & (place.rank == turn)
        here = place.rank == source
        self.straight = Message(
            links, src, dst, across, straight & here, straight & (place.rank == goal)
        )
        self.leg = Message(
            links, src, stop, place.at(rank=place.first), around & here, self.turn
        )

    def relay(self):
        self.leg.arrive()
        target = self.place.at(rank=self.place.second)
        self.last = Message(self.links, self.stop, self.dst, target, self.turn, self.goal)

    def arrive(self):
        self.straight.arrive()
        self.last.arrive()


class Deal:
    def __init__(self, place, links, pairs):
        self.messages = []
        for part, dst in pairs:
            self.messages.append(links.keep(part(place.rank), dst))
            for rank in (place.first, place.second, place.across):
                self.messages.append(Message(links, part(rank), dst, place.at(rank=rank)))

    def arrive(self):
        for message in self.messages:
            message.arrive()


def block_of(r):
    return jnp.where(r == 0, 0, jnp.minimum(r + 1, GRAN - 1))


def forward_kernel(
    chips,
    tokens,
    cotangent,
    gain_one,
    bias_one,
    gain_two,
    bias_two,
    b_down,
    b_up,
    w_query,
    w_key,
    w_value,
    w_out,
    w_up,
    w_down,
    comb,
    mask,
    cosine,
    sine,
    all_tokens,
    attn_in,
    qkv_rot,
    mixed_low,
    hidden,
    all_ffn_in,
    gains,
    incoming,
    cotangent_sum,
    next_sum,
    all_qkv,
    all_out,
    all_up,
    all_down,
    hidden_v,
    sum_v,
    cotangent_v,
    suffix,
    small,
    tokens_v,
    attn_v,
    rot_v,
    mixed_v,
    qkv_v,
    out_v,
    partial,
    landing,
    passing,
    ffn_v,
    all_small,
    send,
    recv,
    near,
):
    place = Place(chips)
    links = Links(send, recv, near)
    load_cotangent = links.keep(cotangent, cotangent_v)
    own = gain_one.shape[1]
    packed = [v[...].astype(jnp.float32) for v in (gain_one, bias_one, gain_two, bias_two, b_down)]
    wide_bias = b_up[...].astype(jnp.float32)
    packed += [wide_bias[:, q * own : (q + 1) * own] for q in range(4)]
    packed = jnp.concatenate(packed + [jnp.zeros((7, own), jnp.float32)], axis=0)
    packed = jnp.concatenate([packed, jnp.zeros((16, 128 - own), jnp.float32)], axis=1)
    small[...] = packed.astype(jnp.bfloat16)
    place.greet(plane=True, group=True)
    rank, shard = place.rank, place.shard
    ranks, tok_rows, model_width = tokens_v.shape
    head_cols = w_query.shape[1] // ranks
    heads = head_cols // HEAD_DIM

    def columns(weight, width):
        return lambda r: weight.at[:, pl.ds(pl.multiple_of(r * width, 128), width)]

    own_qkv = all_qkv.at[rank, shard]
    deal_small = Deal(place, links, [(lambda r: small, all_small.at[rank, shard])])
    pairs = []
    for i, weight in enumerate((w_query, w_key, w_value)):
        pairs.append(
            (columns(weight, head_cols), own_qkv.at[:, pl.ds(i * head_cols, head_cols)])
        )
    deal_qkv = Deal(place, links, pairs)
    gather = PlaneGather(place, links, tokens, tokens_v, 2)
    deal_up = Deal(place, links, [(columns(w_up, w_up.shape[1] // ranks), all_up.at[rank, shard])])
    links.keep(w_out, all_out.at[shard])
    low_half = pl.ds(0, model_width // 2)
    links.keep(w_down.at[:, low_half], all_down.at[shard])
    out_slot = lambda f: all_out.at[f]
    down_slot = lambda f: all_down.at[f]
    small_slot = lambda f: all_small.at[:, f]
    qkv_slot = lambda f: all_qkv.at[:, f]
    up_slot = lambda f: all_up.at[:, f]
    chain_out = Chain(place, links, w_out, out_slot)
    deal_small.arrive()
    own_small = small_slot(shard)
    told = [Message(links, own_small, own_small, place.at(shard=f)) for f in place.others()]
    deal_qkv.arrive()
    chain_qkv = Chain(place, links, qkv_slot(shard), qkv_slot)
    load_cotangent.arrive()

    def add_cotangents(cut):
        total = jnp.zeros((64, model_width), jnp.float32)
        for g in range(GRAN - 1, -1, -1):
            total = total + cotangent_v[g, cut].astype(jnp.float32)
            suffix[g, cut] = total.astype(jnp.bfloat16)
        sum_v[cut] = total

    in_rows(tok_rows, 64, add_cotangents)
    links.keep(sum_v, cotangent_sum)
    links.keep(suffix.at[1], next_sum)
    for message in told:
        message.arrive()
    chain_qkv.step(1)
    gather.relay(0)
    gather.relay(1)

    def wide(rows):
        spread = jnp.dot(rows, comb[...], preferred_element_type=jnp.float32)
        return jnp.sum(spread * mask[...], axis=0, keepdims=True)

    devices = ranks * 2 * chips
    for i in range(5):
        gains[i : i + 1] = wide(all_small[:, :, i].reshape(devices, 128))
    up_rows = all_small[rank, :, 5:9].astype(jnp.float32).reshape(devices, 128)
    gains[5:6] = wide(up_rows.astype(jnp.bfloat16))
    gains[6:8] = jnp.zeros((2, model_width), jnp.float32)

    def norm_block(r):
        def rows_of(cut):
            value, unused = normed(tokens_v[r, cut].astype(jnp.float32))
            attn_v[r, cut] = (value * gains[0:1] + gains[1:2]).astype(jnp.bfloat16)

        in_rows(tok_rows, 64, rows_of)

    for copy in links.open_near:
        copy.arrive()
    norm_block(rank)
    norm_block(place.first)
    chain_qkv.step(2)
    deal_up.arrive()
    chain_up = Chain(place, links, up_slot(shard), up_slot)
    gather.finish()
    links.keep(suffix.at[block_of(rank)], incoming.at[rank])
    dealt = []
    for r in (place.first, place.second, place.across):
        dealt.append(Message(links, suffix.at[block_of(r)], incoming.at[rank], place.at(rank=r)))
    norm_block(place.second)
    norm_block(place.across)
    links.keep(tokens_v, all_tokens)
    links.keep(attn_v, attn_in)
    chain_out.step(1)
    chain_qkv.step(3)
    chain_out.step(2)
    chain_down = Chain(place, links, w_down.at[:, low_half], down_slot)
    chain_qkv.finish()
    load_qkv = links.keep(all_qkv, qkv_v)
    load_qkv.arrive()

    def project(r, carry):
        rows = pl.ds(pl.multiple_of(r * tok_rows, tok_rows), tok_rows)
        for part in range(3):
            cut = slice(part * head_cols, (part + 1) * head_cols)
            weight = qkv_v[:, :, :, cut].reshape(model_width, head_cols)
            value = jnp.dot(attn_v[r], weight, preferred_element_type=jnp.float32)
            if part < 2:
                turned = []
                for h in range(heads):
                    head = value[:, h * HEAD_DIM : (h + 1) * HEAD_DIM]
                    turned.append(turn_half(head, cosine[rows], sine[rows]))
                value = jnp.concatenate(turned, axis=1)
                if part == 0:
                    value = value * HEAD_DIM ** (-0.5)
            rot_v[r, :, cut] = value.astype(jnp.bfloat16)
        return carry

    lax.fori_loop(0, ranks, project, 0)
    links.keep(rot_v, qkv_rot)
    chain_out.step(3)
    chain_out.finish()
    load_out = links.keep(all_out, out_v)

    def attend_block(r):
        def head(h, carry):
            def part(i):
                return pl.ds(pl.multiple_of(i * head_cols + h * HEAD_DIM, HEAD_DIM), HEAD_DIM)

            for t in range(ranks):

                @pl.when(r == t)
                def with_keys(seen=t + 1):
                    keys = rot_v[:seen, :, part(1)].reshape(-1, HEAD_DIM)
                    scores = back_product(rot_v[r, :, part(0)], keys)
                    row = lax.broadcasted_iota(jnp.int32, scores.shape, 0) + r * tok_rows
                    column = lax.broadcasted_iota(jnp.int32, scores.shape, 1)
                    scores = jnp.where(row >= column, scores, masked_score)
                    raised = jnp.exp(scores - jnp.max(scores, axis=-1, keepdims=True))
                    scale = 1.0 / jnp.sum(raised, axis=-1, keepdims=True)
                    probs = (raised * scale).astype(jnp.bfloat16)
                    mixed = product(probs, rot_v[:seen, :, part(2)].reshape(-1, HEAD_DIM))
                    mixed_v[r, :, part(0)] = mixed.astype(jnp.bfloat16)

            return carry

        lax.fori_loop(0, heads, head, 0)

    def project_block(r):
        weight = out_v[...].reshape(head_cols, model_width)
        partial[r] = product(mixed_v[r], weight).astype(jnp.bfloat16)

    scatter = PlaneScatter(place, links, partial, landing, passing)
    attend_block(place.across)
    load_out.arrive()
    project_block(place.across)
    scatter.send_far()
    attend_block(place.first)
    project_block(place.first)
    scatter.send_near()
    chain_up.step(1)
    attend_block(place.second)
    project_block(place.second)
    scatter.relay()
    chain_down.step(1)
    attend_block(rank)
    project_block(rank)
    chain_up.step(2)
    links.keep(mixed_v, mixed_low)
    scatter.settle()

    def second_norm(cut):
        value = scatter.total(cut) + tokens_v[rank, cut].astype(jnp.float32)
        hidden_v[cut] = value
        value, unused = normed(value)
        ffn_v[cut] = (value * gains[2:3] + gains[3:4]).astype(jnp.bfloat16)

    in_rows(tok_rows, 64, second_norm)
    gather = PlaneGather(place, links, ffn_v, all_ffn_in, 2)
    links.keep(hidden_v, hidden)
    chain_down.step(2)
    gather.relay(0)
    chain_up.step(3)
    gather.relay(1)
    chain_down.step(3)
    chain_up.finish()
    gather.finish()
    chain_down.finish()
    for message in dealt:
        message.arrive()
    links.drain()


def middle_kernel(
    chips,
    all_ffn_in,
    incoming,
    next_sum,
    w_up,
    down_low,
    w_down,
    hidden,
    cotangent_sum,
    gains,
    grad_hidden,
    sums,
    sum_down,
    sum_up_low,
    share_up,
    all_branch,
    terms,
    own_term,
    extra_in,
    ffn_v,
    csum_v,
    up_v,
    down_v,
    gated_v,
    grad_v,
    part_down,
    other_down,
    land_down,
    other_up,
    land_up,
    terms_v,
    stop,
    stop_more,
    branch,
    grad_hidden_v,
    sum_down_v,
    partial,
    landing,
    passing,
    send,
    recv,
    near,
):
    place = Place(chips)
    links = Links(send, recv, near)
    rank = place.rank
    ranks, tok_rows, model_width = ffn_v.shape
    ff_cols = up_v.shape[-1]
    half = ff_cols // 2
    load_up = links.keep(w_up, up_v)
    order = (place.across, place.first, place.second, rank)
    load_ffn = [links.keep(all_ffn_in.at[t], ffn_v.at[t]) for t in order]
    wide = model_width // 2
    columns = (pl.ds(0, wide), pl.ds(wide, wide))
    load_down = links.keep(down_low, down_v.at[:, :, columns[0]])
    own_down = w_down.at[:, columns[1]]
    load_own = links.keep(own_down, down_v.at[place.shard, :, columns[1]])
    load_csum = links.keep(incoming, csum_v.at[0])
    load_more = links.keep(next_sum, csum_v.at[1, rank], rank == 0)
    place.greet(plane=True, sibling=True, ring=True)
    chain_down = Chain(place, links, own_down, lambda f: down_v.at[f, :, columns[1]])
    detour = Detour(place, links, next_sum, csum_v.at[1, 3], stop, 3, 1, 0)
    dealt = []
    for r in (place.first, place.second):
        dealt.append(
            Message(links, next_sum, csum_v.at[1, rank], place.at(rank=r), r == 0, rank == 0)
        )
    slots = (0, jnp.where(rank == 0, 1, 0))
    sums[...] = jnp.zeros_like(sums)
    load_up.arrive()
    scatter = PlaneScatter(place, links, partial, landing, passing)

    def widen(k):
        t = order[k]
        load_ffn[k].arrive()
        for i in range(2):
            cut = slice(i * half, (i + 1) * half)
            weight = up_v[:, :, :, :, cut].reshape(model_width, half)
            pre = product(ffn_v[t], weight) + gains[5:6, cut]
            square = pre * pre
            tangent = jnp.tanh(0.7978845608028654 * pre * (1.0 + 0.044715 * square))
            gated_v[t, :, cut] = (0.5 * pre * (1.0 + tangent)).astype(jnp.bfloat16)
            slope = 0.5 * (1.0 + tangent) + 0.5 * pre * (1.0 - tangent * tangent) * (
                0.7978845608028654 * (1.0 + 3.0 * 0.044715 * square)
            )
            grad_v[t, :, cut] = slope.astype(jnp.bfloat16)

    def high_tile(h):
        right = slice(h * wide, (h + 1) * wide)

        def one(t, carry):
            weight = down_v[4:, :, right].reshape(half, wide)
            value = product(gated_v[t, :, half:], weight)
            terms_v[1, t, :, right] = value.astype(jnp.bfloat16)
            return carry

        lax.fori_loop(0, ranks, one, 0)
        cut = columns[h]
        links.keep(terms_v.at[1, rank, :, cut], extra_in.at[:, cut], rank == 0)
        detour = Detour(
            place,
            links,
            terms_v.at[1, place.across, :, cut],
            extra_in.at[:, cut],
            stop_more.at[:, cut],
            0,
            2,
            3,
        )
        for r in (place.first, place.second):
            dealt_more.append(
                Message(
                    links,
                    terms_v.at[1, r, :, cut],
                    extra_in.at[:, cut],
                    place.at(rank=r),
                    rank == 0,
                    r == 0,
                )
            )
        return detour

    def low_tile(t, carry):
        low_term = product(gated_v[t, :, :half], down_v[:4].reshape(half, model_width))
        high_term = terms_v[1, t].astype(jnp.float32) * jnp.where(rank == 0, 0.0, 1.0)
        terms_v[0, t] = (low_term + high_term).astype(jnp.bfloat16)
        return carry

    def block(k):
        t = order[k]
        for i in range(2):
            cut = slice(i * half, (i + 1) * half)
            weight = down_v[4 * i : 4 * i + 4].reshape(half, model_width)
            grad = back_product(csum_v[slots[i], t], weight) * grad_v[t, :, cut].astype(jnp.float32)
            grad_v[t, :, cut] = grad.astype(jnp.bfloat16)
            sums[3:4, cut] += jnp.sum(grad, axis=0, keepdims=True)

        def back(i, carry):
            own = model_width // ranks
            value = back_product(grad_v[t], up_v[i].reshape(own, ff_cols))
            partial[t, :, pl.ds(pl.multiple_of(i * own, 128), own)] = value.astype(jnp.bfloat16)
            return carry

        lax.fori_loop(0, ranks, back, 0)

    dealt_more = []
    widen(0)
    widen(1)
    chain_down.step(1)
    widen(2)
    widen(3)
    load_down.arrive()
    detour_low = high_tile(0)
    chain_down.step(2)
    detour.relay()
    chain_down.step(3)
    chain_down.finish()
    load_own.arrive()
    detour_high = high_tile(1)
    detour_low.relay()
    lax.fori_loop(0, ranks, low_tile, 0)
    links.keep(terms_v.at[0], terms)
    links.keep(terms_v.at[0, rank], own_term)
    load_csum.arrive()
    load_more.arrive()
    for message in dealt + [detour]:
        message.arrive()

    def down_tiles(h):
        width = model_width // 2
        right = slice(h * width, (h + 1) * width)

        def down_tile(i, carry):
            rows = ff_cols // ranks
            left = gated_v[:, :, pl.ds(pl.multiple_of(i * rows, 128), rows)].reshape(-1, rows)
            slot = jnp.where(i < 2, slots[0], slots[1])
            value = gram_product(left, csum_v[slot, :, :, right].reshape(-1, width))
            part_down[h, i] = value.astype(jnp.bfloat16).reshape(part_down.shape[2:])
            return carry

        lax.fori_loop(0, ranks, down_tile, 0)
        here = pl.ds(h, 1)
        return Beside(place, links, part_down.at[here], other_down.at[here])

    def along_half(beside, h):
        beside.add()
        share = part_down.at[pl.ds(h, 1)]
        return Along(
            place, links, lambda there: share.at[:, there, place.core], land_down.at[h]
        )

    beside_low = down_tiles(0)
    block(0)
    scatter.send_far()
    along_low = along_half(beside_low, 0)
    block(1)
    scatter.send_near()
    beside_high = down_tiles(1)
    block(2)
    scatter.relay()
    along_high = along_half(beside_high, 1)
    detour_high.relay()
    along_low.relay()
    block(3)

    def up_tile(i, carry):
        rows = model_width // ranks
        left = ffn_v[:, :, pl.ds(pl.multiple_of(i * rows, 128), rows)].reshape(-1, rows)
        value = gram_product(left, grad_v[...].reshape(-1, ff_cols))
        up_v[i] = value.astype(jnp.bfloat16).reshape(up_v.shape[1:])
        return carry

    lax.fori_loop(0, ranks, up_tile, 0)
    beside_up = Beside(place, links, up_v, other_up)
    along_high.relay()

    beside_up.add()
    share_low = up_v.at[:, :, :, :, columns[0]]
    along_up = Along(place, links, lambda there: share_low.at[:, there, place.core], land_up)
    links.keep(up_v.at[:, :, place.core, :, columns[1]], share_up)
    scatter.settle()

    def norm_back(cut):
        value, inverse = normed(hidden[cut])
        grad = scatter.total(cut)
        sums[0:1] += jnp.sum(grad * value, axis=0, keepdims=True)
        sums[1:2] += jnp.sum(grad, axis=0, keepdims=True)
        sums[2:3] += jnp.sum(cotangent_sum[cut], axis=0, keepdims=True)
        total = cotangent_sum[cut] + norm_backward(grad, value, inverse, gains[2:3])
        grad_hidden_v[cut] = total
        branch[cut] = total.astype(jnp.bfloat16)

    in_rows(tok_rows, 64, norm_back)
    gather = PlaneGather(place, links, branch, all_branch, 2)
    links.keep(grad_hidden_v, grad_hidden)
    gather.relay(0)
    along_up.relay()
    gather.relay(1)
    for h, along in enumerate((along_low, along_high)):
        mine = part_down[h : h + 1, place.z, place.core]
        sum_down_v[:, h * wide : (h + 1) * wide] = along.total(mine)[0]
    links.keep(sum_down_v, sum_down)
    mine = up_v[:, place.z, place.core, :, :wide]
    sum_up_low[...] = along_up.total(mine).astype(jnp.bfloat16)
    gather.finish()
    for message in dealt_more + [detour_low, detour_high]:
        message.arrive()
    links.drain()


def last_kernel(
    chips,
    all_branch,
    sum_up_low,
    share_up,
    terms,
    qkv_rot,
    mixed_low,
    w_out,
    w_qkv,
    attn_in,
    all_tokens,
    grad_hidden,
    gains,
    sums,
    comb,
    mask,
    cosine,
    sine,
    term_in,
    grad_tokens,
    sum_out,
    land_sum_up,
    land_sum_qkv,
    sum_small,
    branch_v,
    rot_v,
    mixed_v,
    grad_mixed_v,
    out_v,
    qkv_v,
    attn_v,
    tokens_v,
    grad_v,
    key_sum,
    value_sum,
    partial,
    landing,
    passing,
    turn_up,
    mine_up,
    far_up,
    land_up,
    part_out,
    other_out,
    land_out,
    part_qkv,
    other_qkv,
    land_qkv,
    turn_qkv,
    part_small,
    other_small,
    land_small,
    turn_small,
    land_sums,
    more_sums,
    send,
    recv,
    near,
):
    place = Place(chips)
    links = Links(send, recv, near)
    rank, z = place.rank, place.z
    ranks, tok_rows, model_width = branch_v.shape
    head_cols = mixed_v.shape[2]
    heads = head_cols // HEAD_DIM
    load_branch = links.keep(all_branch, branch_v)
    load_out = links.keep(w_out, out_v)
    load_mixed = links.keep(mixed_low, mixed_v)
    load_rot = links.keep(qkv_rot, rot_v)
    piece = 3 * HEAD_DIM
    load_qkv = [
        links.keep(
            w_qkv.at[:, :, :, pl.ds(i * head_cols + h * HEAD_DIM, HEAD_DIM)],
            qkv_v.at[:, :, :, pl.ds(h * piece + i * HEAD_DIM, HEAD_DIM)],
        )
        for h in range(heads)
        for i in range(3)
    ]
    load_attn = links.keep(attn_in, attn_v)
    load_tokens = links.keep(all_tokens, tokens_v)
    load_up = links.keep(share_up.at[:, z], mine_up)
    other_end = jnp.where(z < 2, chips - 1, 0)
    load_far = links.keep(share_up.at[:, other_end], far_up)
    wide = model_width // 2
    load_low = links.keep(sum_up_low, turn_up.at[:, :, pl.ds(0, wide)])
    place.greet(plane=True, sibling=True, ring=True)
    along_up = Along(place, links, lambda there: share_up.at[:, there], land_up, far_up)
    dealt = []
    for r in (place.first, place.second, place.across):
        dealt.append(Message(links, terms.at[r], term_in.at[rank], place.at(rank=r)))
    load_out.arrive()

    def mix_back(t):
        weight = out_v[...].reshape(head_cols, model_width)
        grad_mixed_v[t] = back_product(branch_v[t], weight).astype(jnp.bfloat16)

    load_branch.arrive()
    for r in range(ranks):
        mix_back(r)
    load_mixed.arrive()
    value = gram_product(
        mixed_v[...].reshape(-1, head_cols), branch_v[...].reshape(-1, model_width)
    )
    part_out[0] = value.astype(jnp.bfloat16).reshape(part_out.shape[1:])
    beside_out = Beside(place, links, part_out, other_out)
    load_rot.arrive()

    def head(h):
        def part(i):
            return slice(i * head_cols + h * HEAD_DIM, i * head_cols + (h + 1) * HEAD_DIM)

        def place_of(i):
            return slice(h * piece + i * HEAD_DIM, h * piece + (i + 1) * HEAD_DIM)

        for t in range(ranks - 1, -1, -1):
            count = t + 1
            keys = rot_v[:count, :, part(1)].reshape(-1, HEAD_DIM)
            values = rot_v[:count, :, part(2)].reshape(-1, HEAD_DIM)
            queries = rot_v[t, :, part(0)]
            grad_mixed = grad_mixed_v[t, :, part(0)]
            scores = back_product(queries, keys)
            row = lax.broadcasted_iota(jnp.int32, scores.shape, 0) + t * tok_rows
            column = lax.broadcasted_iota(jnp.int32, scores.shape, 1)
            scores = jnp.where(row >= column, scores, masked_score)
            raised = jnp.exp(scores - jnp.max(scores, axis=-1, keepdims=True))
            probs = raised * (1.0 / jnp.sum(raised, axis=-1, keepdims=True))
            delta = jnp.sum(
                grad_mixed.astype(jnp.float32) * mixed_v[t, :, part(0)].astype(jnp.float32),
                axis=-1,
                keepdims=True,
            )
            grad_scores = (probs * (back_product(grad_mixed, values) - delta)).astype(jnp.bfloat16)
            rows = pl.ds(t * tok_rows, tok_rows)
            grad_query = product(grad_scores, keys)
            grad_query = turn_half(grad_query, cosine[rows], -sine[rows]) * HEAD_DIM ** (-0.5)
            grad_v[t, :, place_of(0)] = grad_query.astype(jnp.bfloat16)
            grad_key = gram_product(grad_scores, queries)
            grad_value = gram_product(probs.astype(jnp.bfloat16), grad_mixed)
            seen = count * tok_rows
            if t == ranks - 1:
                key_sum[...] = grad_key
                value_sum[...] = grad_value
            else:
                key_sum[:seen] += grad_key
                value_sum[:seen] += grad_value
        grad_key = turn_half(key_sum[...], cosine[...], -sine[...]).astype(jnp.bfloat16)
        grad_v[:, :, place_of(1)] = grad_key.reshape(ranks, tok_rows, HEAD_DIM)
        grad_value = value_sum[...].astype(jnp.bfloat16)
        grad_v[:, :, place_of(2)] = grad_value.reshape(ranks, tok_rows, HEAD_DIM)

        def qkv_tile(i, carry):
            rows = model_width // ranks
            left = attn_v[:, :, pl.ds(pl.multiple_of(i * rows, 128), rows)].reshape(-1, rows)
            right = grad_v[:, :, h * piece : (h + 1) * piece].reshape(-1, piece)
            value = gram_product(left, right)
            part_qkv[h, i] = value.astype(jnp.bfloat16).reshape(part_qkv.shape[2:])
            return carry

        if h == 0:
            load_attn.arrive()
        lax.fori_loop(0, ranks, qkv_tile, 0)
        return Beside(place, links, part_qkv.at[h], other_qkv.at[h])

    def along_head(h):
        return Along(
            place, links, lambda there: part_qkv.at[h, :, there, place.core], land_qkv.at[h]
        )

    beside_qkv = [head(0)]
    load_far.arrive()
    along_up.relay()
    beside_out.add()
    along_out = Along(place, links, lambda there: part_out.at[:, there, place.core], land_out)
    along_qkv = []
    for h in range(1, heads):
        beside_qkv.append(head(h))
        beside_qkv[h - 1].add()
        along_qkv.append(along_head(h - 1))
    along_out.relay()
    for copy in load_qkv:
        copy.arrive()
    load_tokens.arrive()
    scatter = PlaneScatter(place, links, partial, landing, passing)
    more_sums[...] = jnp.zeros_like(more_sums)

    def attn_back(t):
        def tile(i, carry):
            own = model_width // ranks
            value = back_product(grad_v[t], qkv_v[i].reshape(own, 3 * head_cols))
            partial[t, :, pl.ds(pl.multiple_of(i * own, 128), own)] = value.astype(jnp.bfloat16)
            return carry

        lax.fori_loop(0, ranks, tile, 0)

        def count(cut):
            value, unused = normed(tokens_v[t, cut].astype(jnp.float32))
            grad = partial[t, cut].astype(jnp.float32)
            more_sums[0:1] += jnp.sum(grad * value, axis=0, keepdims=True)
            more_sums[1:2] += jnp.sum(grad, axis=0, keepdims=True)

        return count

    count_across = attn_back(place.across)
    scatter.send_far()
    count_first = attn_back(place.first)
    scatter.send_near()
    beside_qkv[heads - 1].add()
    along_qkv.append(along_head(heads - 1))
    along_qkv[0].relay()
    count_second = attn_back(place.second)
    scatter.relay()
    for h in range(1, heads - 1):
        along_qkv[h].relay()
    count_own = attn_back(rank)
    for count in (count_across, count_first, count_second, count_own):
        in_rows(tok_rows, 64, count)

    def pieces(row):
        spread = (row * mask[...]).astype(jnp.float32)
        return lax.dot_general(
            spread,
            comb[...].astype(jnp.float32),
            (((1,), (1,)), ((), ())),
            precision=lax.Precision.HIGHEST,
            preferred_element_type=jnp.float32,
        )

    part_small[...] = jnp.zeros_like(part_small)
    rows = (more_sums[0:1], more_sums[1:2], sums[0:1], sums[1:2], sums[2:3])
    for k, row in enumerate(rows):
        part_small[:, :, :, k] = pieces(row).reshape(ranks, chips, 2, 128)
    part_small[rank, :, :, 5:9] = pieces(sums[3:4]).reshape(chips, 2, 4, 128)
    beside_small = Beside(place, links, part_small, other_small)
    along_qkv[heads - 1].relay()
    load_up.arrive()
    load_low.arrive()
    turn_up[:, :, wide:] = along_up.total(mine_up[...]).astype(jnp.bfloat16)
    deal_up = Deal(place, links, [(lambda r: turn_up.at[r], land_sum_up.at[rank])])
    beside_small.add()
    along_small = Along(place, links, lambda there: part_small.at[:, there, place.core], land_small)
    sum_out[...] = along_out.total(part_out[:, z, place.core])[0]
    along_small.relay()
    deal_qkv = []

    def settle_head(h):
        total = along_qkv[h].total(part_qkv[h, :, z, place.core])
        turn_qkv[h] = total.astype(jnp.bfloat16)
        deal_qkv.append(
            Deal(place, links, [(lambda r: turn_qkv.at[h, r], land_sum_qkv.at[h, rank])])
        )

    for h in range(heads - 1):
        settle_head(h)
    scatter.settle()

    def norm_back(cut):
        value, inverse = normed(tokens_v[rank, cut].astype(jnp.float32))
        grad = norm_backward(scatter.total(cut), value, inverse, gains[0:1])
        grad_tokens[cut] = (grad_hidden[cut] + grad).astype(jnp.bfloat16)

    in_rows(tok_rows, 64, norm_back)
    turn_small[...] = along_small.total(part_small[:, z, place.core])
    deal_small = Deal(place, links, [(lambda r: turn_small.at[r], land_sums.at[rank])])
    settle_head(heads - 1)
    for message in dealt:
        message.arrive()
    deal_up.arrive()
    deal_small.arrive()
    sum_small[...] = land_sums[0] + land_sums[1] + land_sums[2] + land_sums[3]
    for deal in deal_qkv:
        deal.arrive()
    links.drain()


def closing_kernel(*refs):
    own_term, ins, outs = refs[0], refs[1:10], refs[10:23]
    held, act_v, near, leaving = refs[23:32], refs[32], refs[33], refs[34]
    rank = lax.axis_index("dp")
    hidden, gains, term_in, extra_in, grad_in, out_in = held[:6]
    up_in, qkv_in, small_in = held[6:]
    activations, grad_tokens, sum_query, sum_key, sum_value, sum_out, sum_up = outs[:7]
    steps = near.shape[0] - 1
    rows = hidden.shape[0] // steps
    cuts = [pl.ds(k * rows, rows) for k in range(steps)]
    copies = []
    for k, cut in enumerate(cuts):
        batch = []
        for i in (0, 3, 4):
            copy = pltpu.make_async_copy(ins[i].at[cut], held[i].at[cut], near.at[k, i])
            copy.start()
            batch.append(copy)
        for r in range(term_in.shape[0]):
            here, sem = term_in.at[r, cut], near.at[k, 9 + r]
            there = pltpu.make_async_copy(ins[2].at[r, cut], here, sem)
            own = pltpu.make_async_copy(own_term.at[cut], here, sem)
            pl.when(rank != r)(there.start)
            pl.when(rank == r)(own.start)
            batch.append(there)
        copies.append(batch)
    rest = []
    for i in (1, 5, 6, 7, 8):
        rest.append(pltpu.make_async_copy(ins[i], held[i], near.at[steps, i]))
        rest[-1].start()
    rest[0].wait()
    left = []
    for k, cut in enumerate(cuts):
        for copy in copies[k]:
            copy.wait()
        total = hidden[cut] + gains[4:5] + term_in[0, cut].astype(jnp.float32)
        act_v[0, cut] = total.astype(jnp.bfloat16)
        total = total + extra_in[cut].astype(jnp.float32)
        act_v[1, cut] = total.astype(jnp.bfloat16)
        total = total + term_in[1, cut].astype(jnp.float32)
        act_v[2, cut] = total.astype(jnp.bfloat16)
        total = total + term_in[2, cut].astype(jnp.float32) + term_in[3, cut].astype(jnp.float32)
        act_v[3, cut] = total.astype(jnp.bfloat16)
        left.append(
            pltpu.make_async_copy(act_v.at[:, cut], activations.at[:, cut], leaving.at[k, 0])
        )
        left[-1].start()
        left.append(pltpu.make_async_copy(grad_in.at[cut], grad_tokens.at[cut], leaving.at[k, 1]))
        left[-1].start()
    for copy in rest[1:]:
        copy.wait()
    sum_out[...] = out_in[...]
    ranks, own, ff_cols = up_in.shape
    heads, head_cols = qkv_in.shape[0], qkv_in.shape[0] * HEAD_DIM
    for r in range(ranks):
        sum_up[:, r * ff_cols : (r + 1) * ff_cols] = up_in[r].astype(jnp.float32)
        for i, total in enumerate((sum_query, sum_key, sum_value)):
            for h in range(heads):
                start = r * head_cols + h * HEAD_DIM
                value = qkv_in[h, r, :, i * HEAD_DIM : (i + 1) * HEAD_DIM]
                total[:, start : start + HEAD_DIM] = value.astype(jnp.float32)
    small_sums = outs[7:]
    for i in range(5):
        small_sums[i][...] = small_in[i : i + 1, :own]
    small_sums[5][...] = jnp.concatenate([small_in[5 + q : 6 + q, :own] for q in range(4)], axis=1)
    for copy in left:
        copy.wait()


ANY = pl.BlockSpec(memory_space=pl.ANY)
ON_CORE = pl.BlockSpec(memory_space=pltpu.VMEM)


def connected(kernel, number, outs, out_specs, in_specs, scratch, operands):
    return pl.pallas_call(
        kernel,
        out_shape=outs,
        in_specs=in_specs,
        out_specs=out_specs,
        scratch_shapes=scratch + LINK_SCRATCH,
        compiler_params=pltpu.CompilerParams(
            collective_id=number, has_side_effects=True, vmem_limit_bytes=63 * 2**20
        ),
    )(*operands)


def array(shape, dtype=jnp.bfloat16):
    return jax.ShapeDtypeStruct(shape, dtype)


def turning(count):
    half_size = HEAD_DIM // 2
    inverse = np.exp(np.arange(half_size, dtype=np.float32) * np.float32(-math.log(10000.0) / half_size))
    angles = np.arange(count, dtype=np.float32)[:, None] * inverse.astype(np.float32)[None, :]
    cosine, sine = np.cos(angles), np.sin(angles)
    cosine = np.concatenate([cosine, cosine], axis=1)
    return jnp.asarray(cosine), jnp.asarray(np.concatenate([-sine, sine], axis=1))


def local_split(ranks, shards, *arguments):
    chips = shards // 2
    (
        tokens,
        cotangent,
        norm1_gain,
        norm1_bias,
        query_weight,
        key_weight,
        value_weight,
        out_weight,
        norm2_gain,
        norm2_bias,
        up_weight,
        up_bias,
        down_weight,
        down_bias,
    ) = arguments
    model_width = tokens.shape[2]
    tok_rows = tokens.shape[1]
    seq_len = tok_rows * ranks
    own = query_weight.shape[0]
    heads = HEADS // ranks
    head_cols = heads * HEAD_DIM
    ff_cols = FF // ranks
    scaling = HEAD_DIM ** (-0.5)
    rank = lax.axis_index("dp")

    column = np.arange(model_width)
    comb = jnp.asarray(column[None, :] % own == np.arange(128)[:, None], jnp.bfloat16)
    mask = jnp.asarray(column[None, :] // own == np.arange(ranks * shards)[:, None], jnp.float32)
    cosine, sine = turning(seq_len)
    own_tokens = tokens.reshape(tok_rows, model_width)
    blocks_low = array((ranks, tok_rows, model_width))
    down_rows = down_weight.shape[0]
    vmem = pltpu.VMEM
    low = jnp.bfloat16
    f32 = jnp.float32
    (
        all_tokens,
        attn_in,
        qkv_rot,
        mixed_low,
        hidden,
        ffn_in,
        gains,
        incoming,
        cotangent_sum,
        next_sum,
        w_qkv,
        w_out,
        w_up,
        w_down,
    ) = connected(
        functools.partial(forward_kernel, chips),
        1,
        (
            blocks_low,
            blocks_low,
            array((ranks, tok_rows, 3 * head_cols)),
            array((ranks, tok_rows, head_cols)),
            array((tok_rows, model_width), jnp.float32),
            blocks_low,
            array((8, model_width), jnp.float32),
            blocks_low,
            array((tok_rows, model_width), f32),
            array((tok_rows, model_width)),
            array((ranks, shards, own, 3 * head_cols)),
            array((shards, own, model_width)),
            array((ranks, shards, own, ff_cols)),
            array((shards, down_rows, model_width // 2)),
        ),
        [ANY] * 6 + [ON_CORE] + [ANY] * 7,
        [ANY] * 2 + [ON_CORE] * 16,
        [
            vmem((tok_rows, model_width), f32),
            vmem((tok_rows, model_width), f32),
            vmem((GRAN, tok_rows, model_width), low),
            vmem((GRAN, tok_rows, model_width), low),
            vmem((16, 128), low),
            vmem((ranks, tok_rows, model_width), jnp.bfloat16),
            vmem((ranks, tok_rows, model_width), jnp.bfloat16),
            vmem((ranks, tok_rows, 3 * head_cols), jnp.bfloat16),
            vmem((ranks, tok_rows, head_cols), jnp.bfloat16),
            vmem((ranks, shards, own, 3 * head_cols), jnp.bfloat16),
            vmem((shards, own, model_width), jnp.bfloat16),
            vmem((ranks, tok_rows, model_width), jnp.bfloat16),
            vmem((3, tok_rows, model_width), jnp.bfloat16),
            vmem((tok_rows, model_width), jnp.bfloat16),
            vmem((tok_rows, model_width), jnp.bfloat16),
            vmem((ranks, shards, 16, 128), jnp.bfloat16),
        ],
        (
            own_tokens,
            cotangent.reshape(GRAN, tok_rows, model_width),
            norm1_gain.reshape(1, own),
            norm1_bias.reshape(1, own),
            norm2_gain.reshape(1, own),
            norm2_bias.reshape(1, own),
            down_bias.reshape(1, own),
            up_bias.reshape(1, -1),
            query_weight,
            key_weight,
            value_weight,
            out_weight,
            up_weight,
            down_weight,
            comb,
            mask,
            cosine,
            sine,
        ),
    )
    (
        grad_hidden,
        sums,
        sum_down,
        sum_up_low,
        share_up,
        all_branch,
        terms,
        own_term,
        extra_in,
    ) = connected(
        functools.partial(middle_kernel, chips),
        2,
        (
            array((tok_rows, model_width), f32),
            array((8, model_width), f32),
            array((down_rows, model_width), f32),
            array((ranks, own, ff_cols // 2)),
            array((ranks, chips, own, ff_cols // 2)),
            blocks_low,
            blocks_low,
            array((tok_rows, model_width)),
            array((tok_rows, model_width)),
        ),
        [ANY, ON_CORE, ANY, ON_CORE] + [ANY] * 5,
        [ANY] * 6 + [ON_CORE] * 3,
        [
            vmem((ranks, tok_rows, model_width), low),
            vmem((2, ranks, tok_rows, model_width), low),
            vmem((ranks, chips, 2, own, ff_cols), low),
            vmem((shards, down_rows, model_width), low),
            vmem((ranks, tok_rows, ff_cols), low),
            vmem((ranks, tok_rows, ff_cols), low),
            vmem((2, chips, 2, down_rows, model_width // 2), low),
            vmem((2, chips, down_rows, model_width // 2), low),
            vmem((2, 4, 1, down_rows, model_width // 2), low),
            vmem((ranks, chips, own, ff_cols), low),
            vmem((4, ranks, own, ff_cols // 2), low),
            vmem((2, ranks, tok_rows, model_width), low),
            vmem((tok_rows, model_width), low),
            vmem((tok_rows, model_width), low),
            vmem((tok_rows, model_width), low),
            vmem((tok_rows, model_width), f32),
            vmem((down_rows, model_width), f32),
            vmem((ranks, tok_rows, model_width), low),
            vmem((3, tok_rows, model_width), low),
            vmem((tok_rows, model_width), low),
        ],
        (
            ffn_in,
            incoming,
            next_sum,
            w_up.reshape(ranks, chips, 2, own, ff_cols),
            w_down,
            down_weight,
            hidden,
            cotangent_sum,
            gains,
        ),
    )
    term_in, grad_inputs, sum_out, sum_up, sum_qkv, small_sums = connected(
        functools.partial(last_kernel, chips),
        3,
        (
            blocks_low,
            array((tok_rows, model_width)),
            array((own, model_width), f32),
            array((ranks, own, ff_cols)),
            array((heads, ranks, own, 3 * HEAD_DIM)),
            array((16, 128), f32),
        ),
        [ANY] + [ON_CORE] * 2 + [ANY] * 2 + [ON_CORE],
        [ANY] * 10 + [ON_CORE] * 7,
        [
            vmem((ranks, tok_rows, model_width), low),
            vmem((ranks, tok_rows, 3 * head_cols), low),
            vmem((ranks, tok_rows, head_cols), low),
            vmem((ranks, tok_rows, head_cols), low),
            vmem((shards, own, model_width), low),
            vmem((ranks, shards, own, 3 * head_cols), low),
            vmem((ranks, tok_rows, model_width), low),
            vmem((ranks, tok_rows, model_width), low),
            vmem((ranks, tok_rows, 3 * head_cols), low),
            vmem((seq_len, HEAD_DIM), f32),
            vmem((seq_len, HEAD_DIM), f32),
            vmem((ranks, tok_rows, model_width), low),
            vmem((3, tok_rows, model_width), low),
            vmem((tok_rows, model_width), low),
            vmem((ranks, own, ff_cols), low),
            vmem((ranks, own, ff_cols // 2), low),
            vmem((ranks, own, ff_cols // 2), low),
            vmem((4, ranks, own, ff_cols // 2), low),
            vmem((1, chips, 2, own, model_width), low),
            vmem((1, chips, own, model_width), low),
            vmem((4, 1, own, model_width), low),
            vmem((heads, ranks, chips, 2, own, 3 * HEAD_DIM), low),
            vmem((heads, ranks, chips, own, 3 * HEAD_DIM), low),
            vmem((heads, 4, ranks, own, 3 * HEAD_DIM), low),
            vmem((heads, ranks, own, 3 * HEAD_DIM), low),
            vmem((ranks, chips, 2, 16, 128), f32),
            vmem((ranks, chips, 16, 128), f32),
            vmem((4, ranks, 16, 128), f32),
            vmem((ranks, 16, 128), f32),
            vmem((ranks, 16, 128), f32),
            vmem((8, model_width), f32),
        ],
        (
            all_branch,
            sum_up_low,
            share_up,
            terms,
            qkv_rot,
            mixed_low,
            w_out,
            w_qkv,
            attn_in,
            all_tokens,
            grad_hidden,
            gains,
            sums,
            comb,
            mask,
            cosine,
            sine,
        ),
    )
    (
        activations,
        grad_tokens,
        sum_query,
        sum_key,
        sum_value,
        sum_out,
        sum_up,
        *gain_sums,
    ) = pl.pallas_call(
        closing_kernel,
        out_shape=(
            array((GRAN, tok_rows, model_width)),
            array((tok_rows, model_width)),
            *[array((own, model_width), f32) for i in range(4)],
            array((own, FF), f32),
            *[array((1, own), f32) for i in range(5)],
            array((1, down_rows), f32),
        ),
        in_specs=[ANY] * 10,
        out_specs=[ANY] * 2 + [ON_CORE] * 11,
        scratch_shapes=[
            vmem((tok_rows, model_width), f32),
            vmem((8, model_width), f32),
            vmem((ranks, tok_rows, model_width), low),
            vmem((tok_rows, model_width), low),
            vmem((tok_rows, model_width), low),
            vmem((own, model_width), f32),
            vmem((ranks, own, ff_cols), low),
            vmem((heads, ranks, own, 3 * HEAD_DIM), low),
            vmem((16, 128), f32),
            vmem((GRAN, tok_rows, model_width), low),
            pltpu.SemaphoreType.DMA((5, 13)),
            pltpu.SemaphoreType.DMA((4, 2)),
        ],
        compiler_params=pltpu.CompilerParams(vmem_limit_bytes=60 * 2**20),
    )(
        own_term,
        hidden,
        gains,
        term_in,
        extra_in,
        grad_inputs,
        sum_out,
        sum_up,
        sum_qkv,
        small_sums,
    )
    gain_sums = [v.reshape(-1) for v in gain_sums]
    return (
        activations.reshape(GRAN, 1, tok_rows, model_width),
        grad_tokens.reshape(1, tok_rows, model_width),
        gain_sums[0],
        gain_sums[1],
        sum_query,
        sum_key,
        sum_value,
        sum_out,
        gain_sums[2],
        gain_sums[3],
        sum_up,
        gain_sums[5],
        sum_down,
        gain_sums[4],
    )


def solution(mesh):
    placed = (
        P("fsdp", "dp", None),
        P(None, "fsdp", "dp", None),
        P(("dp", "fsdp")),
        P(("dp", "fsdp")),
        P(("dp", "fsdp"), None),
        P(("dp", "fsdp"), None),
        P(("dp", "fsdp"), None),
        P(("dp", "fsdp"), None),
        P(("dp", "fsdp")),
        P(("dp", "fsdp")),
        P(("dp", "fsdp"), None),
        P(("dp", "fsdp")),
        P(("dp", "fsdp"), None),
        P(("dp", "fsdp")),
    )
    ranks, shards = mesh.shape["dp"], mesh.shape["fsdp"]
    local = local_gathered
    if ranks == 4 and shards == 8:
        local = functools.partial(local_split, ranks, shards)
    return jax.shard_map(
        local,
        mesh=mesh,
        in_specs=placed,
        out_specs=(
            P(None, "fsdp", "dp", None),
            P("fsdp", "dp", None),
            P(("dp", "fsdp")),
            P(("dp", "fsdp")),
            P(("dp", "fsdp"), None),
            P(("dp", "fsdp"), None),
            P(("dp", "fsdp"), None),
            P(("dp", "fsdp"), None),
            P(("dp", "fsdp")),
            P(("dp", "fsdp")),
            P(("dp", "fsdp"), None),
            P(("dp", "fsdp")),
            P(("dp", "fsdp"), None),
            P(("dp", "fsdp")),
        ),
        check_vma=False,
    )
```

```python
import functools
import math

import jax
import jax.numpy as jnp
import numpy as np
from jax import lax
from jax.experimental import pallas as pl
from jax.experimental.pallas import tpu as pltpu
from jax.sharding import PartitionSpec as P

HEADS = 12
HEAD_DIM = 128
FF = 6144
GRAN = 4


epsilon = 1e-05
masked_score = -1e30


def product(left, right):
    return jnp.dot(left, right, preferred_element_type=jnp.float32)


def gram_product(left, right):
    return lax.dot_general(
        left, right, (((0,), (0,)), ((), ())), preferred_element_type=jnp.float32
    )


def back_product(left, right):
    return lax.dot_general(
        left, right, (((1,), (1,)), ((), ())), preferred_element_type=jnp.float32
    )


def norm_parts(values):
    centred = values - jnp.mean(values, axis=-1, keepdims=True)
    inverse = lax.rsqrt(jnp.mean(centred * centred, axis=-1, keepdims=True) + epsilon)
    return (centred * inverse, inverse)


def norm_backward(grad_normed, normed, inverse, gain):
    scaled = grad_normed * gain
    return inverse * (
        scaled
        - jnp.mean(scaled, axis=-1, keepdims=True)
        - normed * jnp.mean(scaled * normed, axis=-1, keepdims=True)
    )


def gelu_value(values):
    return (
        0.5
        * values
        * (1.0 + jnp.tanh(0.7978845608028654 * (values + 0.044715 * values * values * values)))
    )


def gelu_grad(values):
    tangent = jnp.tanh(0.7978845608028654 * (values + 0.044715 * values * values * values))
    return 0.5 * (1.0 + tangent) + 0.5 * values * (1.0 - tangent * tangent) * 0.7978845608028654 * (
        1.0 + 3.0 * 0.044715 * values * values
    )


def rotary_tables(positions, half_size):
    ladder = jnp.arange(half_size).astype(jnp.float32)
    inverse = jnp.exp(ladder * (-math.log(10000.0) / half_size))
    angles = positions[:, None] * inverse[None, :]
    return (jnp.cos(angles)[:, None, :], jnp.sin(angles)[:, None, :])


def rotate(values, cosine, sine):
    half_size = values.shape[-1] // 2
    first = values[..., :half_size]
    second = values[..., half_size:]
    return jnp.concatenate(
        [first * cosine - second * sine, second * cosine + first * sine], axis=-1
    )


def block_scores(queries, positions, key_block, start_row):
    block_rows = key_block.shape[0]
    scores = jnp.einsum("qhd,khd->hqk", queries, key_block, preferred_element_type=jnp.float32)
    key_positions = start_row + jnp.arange(block_rows, dtype=jnp.int32)
    visible = positions[None, :, None] >= key_positions[None, None, :]
    return (jnp.where(visible, scores, masked_score), visible)


def key_blocking(keys_all, values_all, key_offset):
    seq_len = keys_all.shape[0]
    block_rows = min(512, seq_len)
    block_count = seq_len // block_rows
    key_blocks = keys_all.reshape(block_count, block_rows, HEADS, HEAD_DIM)
    value_blocks = values_all.reshape(block_count, block_rows, HEADS, HEAD_DIM)
    starts = key_offset + jnp.arange(block_count, dtype=jnp.int32) * block_rows
    return (key_blocks, value_blocks, starts)


def attend(queries, keys_all, values_all, positions):
    tok_rows = queries.shape[0]
    key_blocks, value_blocks, starts = key_blocking(keys_all, values_all, jnp.int32(0))

    def measure(state_pair, block_pair):
        top_score, total = state_pair
        key_block, start_row = block_pair
        scores, visible = block_scores(queries, positions, key_block, start_row)
        new_top = jnp.maximum(top_score, jnp.max(scores, axis=-1))
        raised = jnp.where(visible, jnp.exp(scores - new_top[..., None]), 0.0)
        total = total * jnp.exp(top_score - new_top) + jnp.sum(raised, axis=-1)
        return ((new_top, total), None)

    initial = (
        jnp.full((HEADS, tok_rows), masked_score, jnp.float32),
        jnp.zeros((HEADS, tok_rows), jnp.float32),
    )
    (top_score, total), unused = lax.scan(measure, initial, (key_blocks, starts))
    log_total = top_score + jnp.log(total)

    def accumulate(mixed, block_triple):
        key_block, value_block, start_row = block_triple
        scores, visible = block_scores(queries, positions, key_block, start_row)
        probs = jnp.where(visible, jnp.exp(scores - log_total[..., None]), 0.0).astype(jnp.bfloat16)
        return (
            mixed
            + jnp.einsum("hqk,khd->qhd", probs, value_block, preferred_element_type=jnp.float32),
            None,
        )

    mixed, unused = lax.scan(
        accumulate,
        jnp.zeros((tok_rows, HEADS, HEAD_DIM), jnp.float32),
        (key_blocks, value_blocks, starts),
    )
    return (mixed, log_total)


def attend_back(
    queries, positions, keys_all, values_all, key_offset, grad_mixed, log_total, row_delta
):
    tok_rows = queries.shape[0]
    key_blocks, value_blocks, starts = key_blocking(keys_all, values_all, key_offset)

    def backward_block(grad_queries, block_triple):
        key_block, value_block, start_row = block_triple
        scores, visible = block_scores(queries, positions, key_block, start_row)
        probs = jnp.where(visible, jnp.exp(scores - log_total[..., None]), 0.0)
        grad_probs = jnp.einsum(
            "qhd,khd->hqk", grad_mixed, value_block, preferred_element_type=jnp.float32
        )
        grad_scores = (probs * (grad_probs - row_delta[..., None])).astype(jnp.bfloat16)
        grad_queries = grad_queries + jnp.einsum(
            "hqk,khd->qhd", grad_scores, key_block, preferred_element_type=jnp.float32
        )
        grad_key_block = jnp.einsum(
            "hqk,qhd->khd", grad_scores, queries, preferred_element_type=jnp.float32
        )
        grad_value_block = jnp.einsum(
            "hqk,qhd->khd",
            probs.astype(jnp.bfloat16),
            grad_mixed,
            preferred_element_type=jnp.float32,
        )
        return (grad_queries, (grad_key_block, grad_value_block))

    grad_queries, (grad_keys, grad_values) = lax.scan(
        backward_block,
        jnp.zeros((tok_rows, HEADS, HEAD_DIM), jnp.float32),
        (key_blocks, value_blocks, starts),
    )
    key_len = keys_all.shape[0]
    return (
        grad_queries,
        grad_keys.reshape(key_len, HEADS * HEAD_DIM),
        grad_values.reshape(key_len, HEADS * HEAD_DIM),
    )


def local_gathered(
    tokens,
    cotangent,
    norm1_gain,
    norm1_bias,
    query_weight,
    key_weight,
    value_weight,
    out_weight,
    norm2_gain,
    norm2_bias,
    up_weight,
    up_bias,
    down_weight,
    down_bias,
):
    (
        gain_one,
        bias_one,
        w_query,
        w_key,
        w_value,
        w_out,
        gain_two,
        bias_two,
        w_up,
        b_up,
        w_down,
        b_down,
    ) = (
        lax.all_gather(norm1_gain, ("dp", "fsdp"), axis=0, tiled=True),
        lax.all_gather(norm1_bias, ("dp", "fsdp"), axis=0, tiled=True),
        lax.all_gather(query_weight, ("dp", "fsdp"), axis=0, tiled=True),
        lax.all_gather(key_weight, ("dp", "fsdp"), axis=0, tiled=True),
        lax.all_gather(value_weight, ("dp", "fsdp"), axis=0, tiled=True),
        lax.all_gather(out_weight, ("dp", "fsdp"), axis=0, tiled=True),
        lax.all_gather(norm2_gain, ("dp", "fsdp"), axis=0, tiled=True),
        lax.all_gather(norm2_bias, ("dp", "fsdp"), axis=0, tiled=True),
        lax.all_gather(up_weight, ("dp", "fsdp"), axis=0, tiled=True),
        lax.all_gather(up_bias, ("dp", "fsdp"), axis=0, tiled=True),
        lax.all_gather(down_weight, ("dp", "fsdp"), axis=0, tiled=True),
        lax.all_gather(down_bias, ("dp", "fsdp"), axis=0, tiled=True),
    )
    seq_count = tokens.shape[0]
    tok_rows = tokens.shape[1]
    model_width = tokens.shape[2]
    all_rows = seq_count * tok_rows
    scaling = HEAD_DIM ** (-0.5)
    inputs = tokens.reshape(all_rows, model_width).astype(jnp.float32)
    normed_one, inverse_one = norm_parts(inputs)
    attn_in = (normed_one * gain_one.astype(jnp.float32) + bias_one.astype(jnp.float32)).astype(
        jnp.bfloat16
    )
    queries = product(attn_in, w_query).reshape(seq_count, tok_rows, HEADS, HEAD_DIM)
    key_raw = product(attn_in, w_key).reshape(seq_count, tok_rows, HEADS, HEAD_DIM)
    value_low = (
        product(attn_in, w_value).astype(jnp.bfloat16).reshape(seq_count, tok_rows, model_width)
    )
    key_offset = lax.axis_index("dp") * tok_rows
    positions = key_offset + jnp.arange(tok_rows, dtype=jnp.int32)
    cosine, sine = rotary_tables(positions.astype(jnp.float32), HEAD_DIM // 2)
    q_rot = (rotate(queries, cosine, sine) * scaling).astype(jnp.bfloat16)
    k_flat = (
        rotate(key_raw, cosine, sine).astype(jnp.bfloat16).reshape(seq_count, tok_rows, model_width)
    )
    keys_all, values_all = (
        lax.all_gather(k_flat, "dp", axis=1, tiled=True),
        lax.all_gather(value_low, "dp", axis=1, tiled=True),
    )
    seq_len = keys_all.shape[1]
    mixed, log_total = jax.vmap(attend, in_axes=(0, 0, 0, None))(
        q_rot,
        keys_all.reshape(seq_count, seq_len, HEADS, HEAD_DIM),
        values_all.reshape(seq_count, seq_len, HEADS, HEAD_DIM),
        positions,
    )
    mixed_low = mixed.reshape(all_rows, model_width).astype(jnp.bfloat16)
    hidden = inputs + product(mixed_low, w_out)
    normed_two, inverse_two = norm_parts(hidden)
    ffn_in = (normed_two * gain_two.astype(jnp.float32) + bias_two.astype(jnp.float32)).astype(
        jnp.bfloat16
    )
    preact = product(ffn_in, w_up) + b_up.astype(jnp.float32)
    edges = [0] + [FF // 2 ** (GRAN - 1 - level_idx) for level_idx in range(GRAN)]
    gated_list = []
    result_list = []
    for level_idx in range(GRAN):
        level_width = edges[level_idx + 1]
        gated = gelu_value(preact[:, :level_width]).astype(jnp.bfloat16)
        gated_list.append(gated)
        result = hidden + product(gated, w_down[:level_width]) + b_down.astype(jnp.float32)
        result_list.append(result.astype(jnp.bfloat16))
    activations = jnp.stack(result_list).reshape(GRAN, seq_count, tok_rows, model_width)
    back_gain_one, back_query, back_key, back_value, back_out, back_gain_two, back_up, back_down = (
        lax.all_gather(norm1_gain, ("dp", "fsdp"), axis=0, tiled=True),
        lax.all_gather(query_weight, ("dp", "fsdp"), axis=0, tiled=True),
        lax.all_gather(key_weight, ("dp", "fsdp"), axis=0, tiled=True),
        lax.all_gather(value_weight, ("dp", "fsdp"), axis=0, tiled=True),
        lax.all_gather(out_weight, ("dp", "fsdp"), axis=0, tiled=True),
        lax.all_gather(norm2_gain, ("dp", "fsdp"), axis=0, tiled=True),
        lax.all_gather(up_weight, ("dp", "fsdp"), axis=0, tiled=True),
        lax.all_gather(down_weight, ("dp", "fsdp"), axis=0, tiled=True),
    )
    grads_out = cotangent.reshape(GRAN, all_rows, model_width)
    grad_hidden = jnp.sum(grads_out.astype(jnp.float32), axis=0)
    grad_down_bias = jnp.sum(grad_hidden, axis=0)
    grad_ffn_in = jnp.zeros((all_rows, model_width), jnp.float32)
    pre_grads = []
    for level_idx in range(GRAN):
        level_width = edges[level_idx + 1]
        grad_gated = back_product(grads_out[level_idx], back_down[:level_width])
        grad_pre = (grad_gated * gelu_grad(preact[:, :level_width])).astype(jnp.bfloat16)
        pre_grads.append(grad_pre)
        grad_ffn_in = grad_ffn_in + back_product(grad_pre, back_up[:, :level_width])
    up_blocks = []
    bias_blocks = []
    down_blocks = []
    for block_idx in range(GRAN):
        start_col = edges[block_idx]
        stop_col = edges[block_idx + 1]
        stacked_grad = jnp.concatenate(
            [pre_grads[level_idx][:, start_col:stop_col] for level_idx in range(block_idx, GRAN)],
            axis=0,
        )
        stacked_in = jnp.concatenate([ffn_in] * (GRAN - block_idx), axis=0)
        up_blocks.append(gram_product(stacked_in, stacked_grad))
        bias_blocks.append(jnp.sum(stacked_grad.astype(jnp.float32), axis=0))
        stacked_gated = jnp.concatenate(
            [gated_list[level_idx][:, start_col:stop_col] for level_idx in range(block_idx, GRAN)],
            axis=0,
        )
        stacked_out = jnp.concatenate(
            [grads_out[level_idx] for level_idx in range(block_idx, GRAN)], axis=0
        )
        down_blocks.append(gram_product(stacked_gated, stacked_out))
    grad_up_weight = jnp.concatenate(up_blocks, axis=1)
    grad_up_bias = jnp.concatenate(bias_blocks, axis=0)
    grad_down_weight = jnp.concatenate(down_blocks, axis=0)
    grad_gain_two = jnp.sum(grad_ffn_in * normed_two, axis=0)
    grad_bias_two = jnp.sum(grad_ffn_in, axis=0)
    grad_hidden = grad_hidden + norm_backward(
        grad_ffn_in, normed_two, inverse_two, back_gain_two.astype(jnp.float32)
    )
    grad_branch = grad_hidden.astype(jnp.bfloat16)
    grad_out_weight = gram_product(mixed_low, grad_branch)
    grad_mixed = (
        back_product(grad_branch, back_out)
        .astype(jnp.bfloat16)
        .reshape(seq_count, tok_rows, HEADS, HEAD_DIM)
    )
    row_delta = jnp.einsum("sqhd,sqhd->shq", grad_mixed.astype(jnp.float32), mixed)
    keys_again, values_again = (
        lax.all_gather(k_flat, "dp", axis=1, tiled=True),
        lax.all_gather(value_low, "dp", axis=1, tiled=True),
    )
    back_all = jax.vmap(attend_back, in_axes=(0, None, 0, 0, None, 0, 0, 0))
    grad_q_rot, grad_keys_all, grad_values_all = back_all(
        q_rot,
        positions,
        keys_again.reshape(seq_count, seq_len, HEADS, HEAD_DIM),
        values_again.reshape(seq_count, seq_len, HEADS, HEAD_DIM),
        jnp.int32(0),
        grad_mixed,
        log_total,
        row_delta,
    )
    every_query, every_grad = (
        lax.all_gather(q_rot, "dp", axis=1, tiled=True),
        lax.all_gather(grad_mixed, "dp", axis=1, tiled=True),
    )
    every_total, every_delta = (
        lax.all_gather(jnp.transpose(log_total, (0, 2, 1)), "dp", axis=1, tiled=True),
        lax.all_gather(jnp.transpose(row_delta, (0, 2, 1)), "dp", axis=1, tiled=True),
    )
    every_position = jnp.arange(seq_len, dtype=jnp.int32)
    unused_rows, grad_key_mine, grad_value_mine = back_all(
        every_query,
        every_position,
        k_flat.reshape(seq_count, tok_rows, HEADS, HEAD_DIM),
        value_low.reshape(seq_count, tok_rows, HEADS, HEAD_DIM),
        key_offset,
        every_grad,
        jnp.transpose(every_total, (0, 2, 1)),
        jnp.transpose(every_delta, (0, 2, 1)),
    )
    grad_query = (
        rotate(grad_q_rot * scaling, cosine, -sine)
        .reshape(all_rows, model_width)
        .astype(jnp.bfloat16)
    )
    grad_key = (
        rotate(grad_key_mine.reshape(seq_count, tok_rows, HEADS, HEAD_DIM), cosine, -sine)
        .reshape(all_rows, model_width)
        .astype(jnp.bfloat16)
    )
    grad_val = grad_value_mine.reshape(all_rows, model_width).astype(jnp.bfloat16)
    grad_query_weight = gram_product(attn_in, grad_query)
    grad_key_weight = gram_product(attn_in, grad_key)
    grad_value_weight = gram_product(attn_in, grad_val)
    grad_attn_in = (
        back_product(grad_query, back_query)
        + back_product(grad_key, back_key)
        + back_product(grad_val, back_value)
    )
    grad_gain_one = jnp.sum(grad_attn_in * normed_one, axis=0)
    grad_bias_one = jnp.sum(grad_attn_in, axis=0)
    grad_inputs = grad_hidden + norm_backward(
        grad_attn_in, normed_one, inverse_one, back_gain_one.astype(jnp.float32)
    )
    (
        sum_gain_one,
        sum_bias_one,
        sum_query,
        sum_key,
        sum_value,
        sum_out,
        sum_gain_two,
        sum_bias_two,
        sum_up,
        sum_up_bias,
        sum_down,
        sum_down_bias,
    ) = (
        lax.psum_scatter(grad_gain_one, ("dp", "fsdp"), scatter_dimension=0, tiled=True),
        lax.psum_scatter(grad_bias_one, ("dp", "fsdp"), scatter_dimension=0, tiled=True),
        lax.psum_scatter(grad_query_weight, ("dp", "fsdp"), scatter_dimension=0, tiled=True),
        lax.psum_scatter(grad_key_weight, ("dp", "fsdp"), scatter_dimension=0, tiled=True),
        lax.psum_scatter(grad_value_weight, ("dp", "fsdp"), scatter_dimension=0, tiled=True),
        lax.psum_scatter(grad_out_weight, ("dp", "fsdp"), scatter_dimension=0, tiled=True),
        lax.psum_scatter(grad_gain_two, ("dp", "fsdp"), scatter_dimension=0, tiled=True),
        lax.psum_scatter(grad_bias_two, ("dp", "fsdp"), scatter_dimension=0, tiled=True),
        lax.psum_scatter(grad_up_weight, ("dp", "fsdp"), scatter_dimension=0, tiled=True),
        lax.psum_scatter(grad_up_bias, ("dp", "fsdp"), scatter_dimension=0, tiled=True),
        lax.psum_scatter(grad_down_weight, ("dp", "fsdp"), scatter_dimension=0, tiled=True),
        lax.psum_scatter(grad_down_bias, ("dp", "fsdp"), scatter_dimension=0, tiled=True),
    )
    return (
        activations,
        grad_inputs.astype(jnp.bfloat16).reshape(seq_count, tok_rows, model_width),
        sum_gain_one,
        sum_bias_one,
        sum_query,
        sum_key,
        sum_value,
        sum_out,
        sum_gain_two,
        sum_bias_two,
        sum_up,
        sum_up_bias,
        sum_down,
        sum_down_bias,
    )


MESH = pl.DeviceIdType.MESH


class Place:
    def __init__(self, chips):
        self.chips = chips
        self.rank = lax.axis_index("dp")
        self.shard = lax.axis_index("fsdp")
        self.z = lax.div(self.shard, 2)
        self.core = lax.rem(self.shard, 2)
        along_x = self.rank + 1 - 2 * lax.rem(self.rank, 2)
        along_y = self.rank + 2 - 4 * lax.div(self.rank, 2)
        self.first = jnp.where(self.core == 0, along_x, along_y)
        self.second = jnp.where(self.core == 0, along_y, along_x)
        self.across = 3 - self.rank
        self.sibling = self.shard + 1 - 2 * self.core

    def at(self, rank=None, shard=None):
        return (self.rank if rank is None else rank, self.shard if shard is None else shard)

    def others(self):
        return [lax.rem(self.shard + k, 2 * self.chips) for k in range(1, 2 * self.chips)]

    def greet(self, plane=True, sibling=False, ring=False, group=False):
        barrier = pltpu.get_barrier_semaphore()
        count = 0
        targets = []
        if plane:
            targets += [self.at(rank=r) for r in (self.first, self.second, self.across)]
        if sibling:
            targets.append(self.at(shard=self.sibling))
        if ring:
            targets += [self.at(shard=self.hop(k)) for k in range(1, self.chips)]
        if group:
            targets += [self.at(shard=f) for f in self.others()]
        for target in targets:
            pl.semaphore_signal(barrier, inc=1, device_id=target, device_id_type=MESH)
            count += 1
        pl.semaphore_wait(barrier, count)

    def hop(self, k):
        return 2 * lax.rem(self.z + k, self.chips) + self.core


def under(condition, action):
    if condition is None:
        action()
    else:
        pl.when(condition)(action)


class Message:
    def __init__(self, links, src, dst, target, sent=None, comes=None):
        index = links.take()
        self.copy = pltpu.make_async_remote_copy(
            src_ref=src,
            dst_ref=dst,
            send_sem=links.send.at[index],
            recv_sem=links.recv.at[index],
            device_id=target,
            device_id_type=MESH,
        )
        self.sent, self.comes = sent, comes
        self.left = False
        links.open.append(self)
        under(sent, self.copy.start)

    def arrive(self):
        under(self.comes, self.copy.wait_recv)

    def leave(self):
        if not self.left:
            under(self.sent, self.copy.wait_send)
        self.left = True


class Near:
    def __init__(self, links, src, dst, where):
        self.copy = pltpu.make_async_copy(src, dst, links.near.at[links.used_near])
        links.used_near += 1
        self.where = where
        self.waits = True
        under(where, self.copy.start)

    def arrive(self):
        if self.waits:
            under(self.where, self.copy.wait)
        self.waits = False


class Links:
    def __init__(self, send, recv, near):
        self.send, self.recv, self.near = send, recv, near
        self.used = 0
        self.used_near = 0
        self.open = []
        self.open_near = []

    def take(self):
        self.used += 1
        return self.used - 1

    def keep(self, src, dst, where=None):
        copy = Near(self, src, dst, where)
        self.open_near.append(copy)
        return copy

    def drain(self):
        for copy in self.open_near:
            copy.arrive()
        for message in self.open:
            message.leave()


LINK_SCRATCH = [
    pltpu.SemaphoreType.DMA((128,)),
    pltpu.SemaphoreType.DMA((128,)),
    pltpu.SemaphoreType.DMA((32,)),
]


def normed(values):
    centred = values - jnp.mean(values, axis=-1, keepdims=True)
    inverse = lax.rsqrt(jnp.mean(centred * centred, axis=-1, keepdims=True) + epsilon)
    return centred * inverse, inverse


def in_rows(count, step, body):
    def one(i, carry):
        body(pl.ds(pl.multiple_of(i * step, step), step))
        return carry

    lax.fori_loop(0, count // step, one, 0)


def turn_half(values, cosine, sine):
    return values * cosine + pltpu.roll(values, HEAD_DIM // 2, 1) * sine


class PlaneGather:
    def __init__(self, place, links, src, dst, parts):
        self.place, self.links, self.dst = place, links, dst
        rows = src.shape[0] // parts
        self.cuts = [pl.ds(k * rows, rows) for k in range(parts)]
        self.own = links.keep(src, dst.at[place.rank])
        self.first, self.second = [], []
        for cut in self.cuts:
            for side, target in ((self.first, place.first), (self.second, place.second)):
                block = dst.at[place.rank, cut]
                side.append(Message(links, src.at[cut], block, place.at(rank=target)))
        self.passed = []

    def relay(self, k):
        self.first[k].arrive()
        block = self.dst.at[self.place.first, self.cuts[k]]
        target = self.place.at(rank=self.place.second)
        self.passed.append(Message(self.links, block, block, target))

    def finish(self):
        for message in self.second + self.passed:
            message.arrive()


class PlaneScatter:
    def __init__(self, place, links, partial, landing, turn):
        self.place, self.links, self.partial, self.landing, self.turn = (
            place,
            links,
            partial,
            landing,
            turn,
        )
        self.target = place.at(rank=place.first)

    def send_far(self):
        self.far = Message(
            self.links, self.partial.at[self.place.across], self.landing.at[0], self.target
        )

    def send_near(self):
        self.near = Message(
            self.links, self.partial.at[self.place.first], self.landing.at[1], self.target
        )

    def relay(self):
        self.far.arrive()

        def add(cut):
            mine = self.partial[self.place.second, cut].astype(jnp.float32)
            mine = mine + self.landing[0, cut].astype(jnp.float32)
            self.turn[cut] = mine.astype(jnp.bfloat16)

        in_rows(self.turn.shape[0], 64, add)
        self.last = Message(
            self.links, self.turn, self.landing.at[2], self.place.at(rank=self.place.second)
        )

    def settle(self):
        self.near.arrive()
        self.last.arrive()

    def total(self, cut):
        total = self.partial[self.place.rank, cut].astype(jnp.float32)
        total = total + self.landing[1, cut].astype(jnp.float32)
        return total + self.landing[2, cut].astype(jnp.float32)


class Chain:
    def __init__(self, place, links, src, slot):
        self.place, self.links, self.slot = place, links, slot
        z, last = place.z, place.chips - 1
        own = slot(place.shard)
        self.up = Message(links, src, own, place.at(shard=place.shard + 2), z < last, z > 0)
        self.down = Message(links, src, own, place.at(shard=place.shard - 2), z > 0, z < last)
        self.beside = [Message(links, src, own, place.at(shard=place.sibling))]

    def step(self, s):
        place, links = self.place, self.links
        z, last = place.z, place.chips - 1
        below = self.slot(jnp.maximum(place.shard - 2 * s, place.core))
        above = self.slot(jnp.minimum(place.shard + 2 * s, 2 * last + place.core))
        self.up.arrive()
        has_below, has_above = z >= s, z <= last - s
        up = down = None
        if s < last:
            target = place.at(shard=place.shard + 2)
            up = Message(links, below, below, target, has_below & (z < last), z >= s + 1)
        self.beside.append(
            Message(links, below, below, place.at(shard=place.sibling), has_below, has_below)
        )
        self.down.arrive()
        if s < last:
            target = place.at(shard=place.shard - 2)
            down = Message(links, above, above, target, has_above & (z > 0), z <= last - s - 1)
        self.beside.append(
            Message(links, above, above, place.at(shard=place.sibling), has_above, has_above)
        )
        self.up, self.down = up, down

    def finish(self):
        for message in self.beside:
            message.arrive()


class Beside:
    def __init__(self, place, links, part, other):
        self.place, self.part, self.other = place, part, other
        self.message = Message(
            links, part.at[:, :, 1 - place.core], other, place.at(shard=place.sibling)
        )

    def add(self):
        self.message.arrive()
        core = self.place.core

        def one(k, carry):
            total = self.part[:, k, core].astype(jnp.float32) + self.other[:, k].astype(jnp.float32)
            self.part[:, k, core] = total.astype(self.part.dtype)
            return carry

        lax.fori_loop(0, self.place.chips, one, 0)


class Along:
    def __init__(self, place, links, share, landing, far=None):
        self.place, self.links, self.landing = place, links, landing
        z = place.z
        self.middle = (z == 1) | (z == 2)
        end = jnp.logical_not(self.middle)
        partner = z + 1 - 2 * lax.rem(z, 2)
        over = jnp.where(z < 2, 2, 1)
        self.other_end = jnp.where(z < 2, 3, 0)
        self.far = share(self.other_end) if far is None else far

        def to(chip):
            return place.at(shard=2 * chip + place.core)

        self.to = to

        @pl.when(end)
        def nothing_comes():
            landing[2] = jnp.zeros_like(landing[2])

        self.merge = Message(
            links, share(self.other_end), landing.at[3], to(partner), end, self.middle
        )
        self.messages = [
            Message(links, share(partner), landing.at[0], to(partner)),
            Message(links, share(over), landing.at[1], to(over), end, self.middle),
            Message(links, share(over), landing.at[2], to(over), self.middle, self.middle),
        ]

    def relay(self):
        self.merge.arrive()
        landing = self.landing

        @pl.when(self.middle)
        def add():
            total = landing[3].astype(jnp.float32) + self.far[...].astype(jnp.float32)
            landing[3] = total.astype(landing.dtype)

        end = jnp.logical_not(self.middle)
        self.messages.append(
            Message(
                self.links, landing.at[3], landing.at[1], self.to(self.other_end), self.middle, end
            )
        )

    def total(self, mine):
        total = mine.astype(jnp.float32)
        for message in self.messages:
            message.arrive()
        for k in range(3):
            total = total + self.landing[k].astype(jnp.float32)
        return total


class Detour:
    def __init__(self, place, links, src, dst, stop, source, turn, goal):
        self.place, self.links, self.dst, self.stop = place, links, dst, stop
        straight = place.core == 0
        around = place.core == 1
        across = place.at(rank=place.across)
        self.goal = around & (place.rank == goal)
        self.turn = around & (place.rank == turn)
        here = place.rank == source
        self.straight = Message(
            links, src, dst, across, straight & here, straight & (place.rank == goal)
        )
        self.leg = Message(
            links, src, stop, place.at(rank=place.first), around & here, self.turn
        )

    def relay(self):
        self.leg.arrive()
        target = self.place.at(rank=self.place.second)
        self.last = Message(self.links, self.stop, self.dst, target, self.turn, self.goal)

    def arrive(self):
        self.straight.arrive()
        self.last.arrive()


class Deal:
    def __init__(self, place, links, pairs):
        self.messages = []
        for part, dst in pairs:
            self.messages.append(links.keep(part(place.rank), dst))
            for rank in (place.first, place.second, place.across):
                self.messages.append(Message(links, part(rank), dst, place.at(rank=rank)))

    def arrive(self):
        for message in self.messages:
            message.arrive()


def block_of(r):
    return jnp.where(r == 0, 0, jnp.minimum(r + 1, GRAN - 1))


def forward_kernel(
    chips,
    tokens,
    cotangent,
    gain_one,
    bias_one,
    gain_two,
    bias_two,
    b_down,
    b_up,
    w_query,
    w_key,
    w_value,
    w_out,
    w_up,
    w_down,
    comb,
    mask,
    cosine,
    sine,
    all_tokens,
    attn_in,
    qkv_rot,
    mixed_low,
    hidden,
    all_ffn_in,
    gains,
    incoming,
    cotangent_sum,
    next_sum,
    all_qkv,
    all_out,
    all_up,
    all_down,
    hidden_v,
    sum_v,
    cotangent_v,
    suffix,
    small,
    tokens_v,
    attn_v,
    rot_v,
    mixed_v,
    qkv_v,
    out_v,
    partial,
    landing,
    passing,
    ffn_v,
    all_small,
    send,
    recv,
    near,
):
    place = Place(chips)
    links = Links(send, recv, near)
    load_cotangent = links.keep(cotangent, cotangent_v)
    own = gain_one.shape[1]
    packed = [v[...].astype(jnp.float32) for v in (gain_one, bias_one, gain_two, bias_two, b_down)]
    wide_bias = b_up[...].astype(jnp.float32)
    packed += [wide_bias[:, q * own : (q + 1) * own] for q in range(4)]
    packed = jnp.concatenate(packed + [jnp.zeros((7, own), jnp.float32)], axis=0)
    packed = jnp.concatenate([packed, jnp.zeros((16, 128 - own), jnp.float32)], axis=1)
    small[...] = packed.astype(jnp.bfloat16)
    place.greet(plane=True, group=True)
    rank, shard = place.rank, place.shard
    ranks, tok_rows, model_width = tokens_v.shape
    head_cols = w_query.shape[1] // ranks
    heads = head_cols // HEAD_DIM

    def columns(weight, width):
        return lambda r: weight.at[:, pl.ds(pl.multiple_of(r * width, 128), width)]

    own_qkv = all_qkv.at[rank, shard]
    deal_small = Deal(place, links, [(lambda r: small, all_small.at[rank, shard])])
    pairs = []
    for i, weight in enumerate((w_query, w_key, w_value)):
        pairs.append(
            (columns(weight, head_cols), own_qkv.at[:, pl.ds(i * head_cols, head_cols)])
        )
    deal_qkv = Deal(place, links, pairs)
    gather = PlaneGather(place, links, tokens, tokens_v, 2)
    deal_up = Deal(place, links, [(columns(w_up, w_up.shape[1] // ranks), all_up.at[rank, shard])])
    links.keep(w_out, all_out.at[shard])
    low_half = pl.ds(0, model_width // 2)
    links.keep(w_down.at[:, low_half], all_down.at[shard])
    out_slot = lambda f: all_out.at[f]
    down_slot = lambda f: all_down.at[f]
    small_slot = lambda f: all_small.at[:, f]
    qkv_slot = lambda f: all_qkv.at[:, f]
    up_slot = lambda f: all_up.at[:, f]
    chain_out = Chain(place, links, w_out, out_slot)
    deal_small.arrive()
    own_small = small_slot(shard)
    told = [Message(links, own_small, own_small, place.at(shard=f)) for f in place.others()]
    deal_qkv.arrive()
    chain_qkv = Chain(place, links, qkv_slot(shard), qkv_slot)
    load_cotangent.arrive()

    def add_cotangents(cut):
        total = jnp.zeros((64, model_width), jnp.float32)
        for g in range(GRAN - 1, -1, -1):
            total = total + cotangent_v[g, cut].astype(jnp.float32)
            suffix[g, cut] = total.astype(jnp.bfloat16)
        sum_v[cut] = total

    in_rows(tok_rows, 64, add_cotangents)
    links.keep(sum_v, cotangent_sum)
    links.keep(suffix.at[1], next_sum)
    for message in told:
        message.arrive()
    chain_qkv.step(1)
    gather.relay(0)
    gather.relay(1)

    def wide(rows):
        spread = jnp.dot(rows, comb[...], preferred_element_type=jnp.float32)
        return jnp.sum(spread * mask[...], axis=0, keepdims=True)

    devices = ranks * 2 * chips
    for i in range(5):
        gains[i : i + 1] = wide(all_small[:, :, i].reshape(devices, 128))
    up_rows = all_small[rank, :, 5:9].astype(jnp.float32).reshape(devices, 128)
    gains[5:6] = wide(up_rows.astype(jnp.bfloat16))
    gains[6:8] = jnp.zeros((2, model_width), jnp.float32)

    def norm_block(r):
        def rows_of(cut):
            value, unused = normed(tokens_v[r, cut].astype(jnp.float32))
            attn_v[r, cut] = (value * gains[0:1] + gains[1:2]).astype(jnp.bfloat16)

        in_rows(tok_rows, 64, rows_of)

    for copy in links.open_near:
        copy.arrive()
    norm_block(rank)
    norm_block(place.first)
    chain_qkv.step(2)
    gather.finish()
    links.keep(suffix.at[block_of(rank)], incoming.at[rank])
    dealt = []
    for r in (place.first, place.second, place.across):
        dealt.append(Message(links, suffix.at[block_of(r)], incoming.at[rank], place.at(rank=r)))
    norm_block(place.second)
    norm_block(place.across)
    links.keep(tokens_v, all_tokens)
    links.keep(attn_v, attn_in)
    deal_up.arrive()
    chain_qkv.up.leave()
    chain_qkv.down.leave()
    chain_out.step(1)
    chain_up = Chain(place, links, up_slot(shard), up_slot)
    chain_qkv.step(3)
    chain_out.step(2)
    chain_down = Chain(place, links, w_down.at[:, low_half], down_slot)
    chain_qkv.finish()
    load_qkv = links.keep(all_qkv, qkv_v)
    load_qkv.arrive()

    def project(r, carry):
        rows = pl.ds(pl.multiple_of(r * tok_rows, tok_rows), tok_rows)
        for part in range(3):
            cut = slice(part * head_cols, (part + 1) * head_cols)
            weight = qkv_v[:, :, :, cut].reshape(model_width, head_cols)
            value = jnp.dot(attn_v[r], weight, preferred_element_type=jnp.float32)
            if part < 2:
                turned = []
                for h in range(heads):
                    head = value[:, h * HEAD_DIM : (h + 1) * HEAD_DIM]
                    turned.append(turn_half(head, cosine[rows], sine[rows]))
                value = jnp.concatenate(turned, axis=1)
                if part == 0:
                    value = value * HEAD_DIM ** (-0.5)
            rot_v[r, :, cut] = value.astype(jnp.bfloat16)
        return carry

    lax.fori_loop(0, ranks, project, 0)
    links.keep(rot_v, qkv_rot)
    chain_out.step(3)
    chain_up.step(1)
    chain_out.finish()
    load_out = links.keep(all_out, out_v)

    def attend_block(r):
        def head(h, carry):
            def part(i):
                return pl.ds(pl.multiple_of(i * head_cols + h * HEAD_DIM, HEAD_DIM), HEAD_DIM)

            for t in range(ranks):

                @pl.when(r == t)
                def with_keys(seen=t + 1):
                    keys = rot_v[:seen, :, part(1)].reshape(-1, HEAD_DIM)
                    scores = back_product(rot_v[r, :, part(0)], keys)
                    row = lax.broadcasted_iota(jnp.int32, scores.shape, 0) + r * tok_rows
                    column = lax.broadcasted_iota(jnp.int32, scores.shape, 1)
                    scores = jnp.where(row >= column, scores, masked_score)
                    raised = jnp.exp(scores - jnp.max(scores, axis=-1, keepdims=True))
                    scale = 1.0 / jnp.sum(raised, axis=-1, keepdims=True)
                    probs = (raised * scale).astype(jnp.bfloat16)
                    mixed = product(probs, rot_v[:seen, :, part(2)].reshape(-1, HEAD_DIM))
                    mixed_v[r, :, part(0)] = mixed.astype(jnp.bfloat16)

            return carry

        lax.fori_loop(0, heads, head, 0)

    def project_block(r):
        weight = out_v[...].reshape(head_cols, model_width)
        partial[r] = product(mixed_v[r], weight).astype(jnp.bfloat16)

    scatter = PlaneScatter(place, links, partial, landing, passing)
    attend_block(place.across)
    load_out.arrive()
    project_block(place.across)
    scatter.send_far()
    attend_block(place.first)
    project_block(place.first)
    scatter.send_near()
    chain_down.step(1)
    attend_block(place.second)
    project_block(place.second)
    scatter.relay()
    chain_up.step(2)
    attend_block(rank)
    project_block(rank)
    chain_down.step(2)
    links.keep(mixed_v, mixed_low)
    scatter.settle()

    def second_norm(cut):
        value = scatter.total(cut) + tokens_v[rank, cut].astype(jnp.float32)
        hidden_v[cut] = value
        value, unused = normed(value)
        ffn_v[cut] = (value * gains[2:3] + gains[3:4]).astype(jnp.bfloat16)

    in_rows(tok_rows, 64, second_norm)
    gather = PlaneGather(place, links, ffn_v, all_ffn_in, 4)
    links.keep(hidden_v, hidden)
    chain_up.step(3)
    gather.relay(0)
    gather.relay(1)
    chain_down.step(3)
    gather.relay(2)
    gather.relay(3)
    chain_up.finish()
    gather.finish()
    chain_down.finish()
    for message in dealt:
        message.arrive()
    links.drain()


def middle_kernel(
    chips,
    all_ffn_in,
    incoming,
    next_sum,
    w_up,
    down_low,
    w_down,
    hidden,
    cotangent_sum,
    gains,
    grad_hidden,
    sums,
    sum_down,
    sum_up_low,
    share_up,
    all_branch,
    terms,
    own_term,
    extra_in,
    ffn_v,
    csum_v,
    up_v,
    down_v,
    gated_v,
    grad_v,
    part_down,
    other_down,
    land_down,
    other_up,
    land_up,
    terms_v,
    stop,
    stop_more,
    branch,
    grad_hidden_v,
    sum_down_v,
    partial,
    landing,
    passing,
    send,
    recv,
    near,
):
    place = Place(chips)
    links = Links(send, recv, near)
    rank = place.rank
    ranks, tok_rows, model_width = ffn_v.shape
    ff_cols = up_v.shape[-1]
    half = ff_cols // 2
    load_up = links.keep(w_up, up_v)
    order = (place.across, place.first, place.second, rank)
    load_ffn = [links.keep(all_ffn_in.at[t], ffn_v.at[t]) for t in order]
    wide = model_width // 2
    columns = (pl.ds(0, wide), pl.ds(wide, wide))
    own_down = w_down.at[:, columns[1]]
    load_own = links.keep(own_down, down_v.at[place.shard, :, columns[1]])
    load_more = links.keep(next_sum, csum_v.at[1, rank], rank == 0)
    place.greet(plane=True, sibling=True, ring=True)
    chain_down = Chain(place, links, own_down, lambda f: down_v.at[f, :, columns[1]])
    detour = Detour(place, links, next_sum, csum_v.at[1, 3], stop, 3, 1, 0)
    dealt = []
    for r in (place.first, place.second):
        dealt.append(
            Message(links, next_sum, csum_v.at[1, rank], place.at(rank=r), r == 0, rank == 0)
        )
    slots = (0, jnp.where(rank == 0, 1, 0))
    sums[...] = jnp.zeros_like(sums)
    load_up.arrive()
    for copy in load_ffn:
        copy.arrive()
    load_down = links.keep(down_low, down_v.at[:, :, columns[0]])
    load_csum = links.keep(incoming, csum_v.at[0])
    scatter = PlaneScatter(place, links, partial, landing, passing)

    def widen(i):
        def one(t, carry):
            cut = slice(i * half, (i + 1) * half)
            weight = up_v[:, :, :, :, cut].reshape(model_width, half)
            pre = product(ffn_v[t], weight) + gains[5:6, cut]
            square = pre * pre
            tangent = jnp.tanh(0.7978845608028654 * pre * (1.0 + 0.044715 * square))
            gated_v[t, :, cut] = (0.5 * pre * (1.0 + tangent)).astype(jnp.bfloat16)
            slope = 0.5 * (1.0 + tangent) + 0.5 * pre * (1.0 - tangent * tangent) * (
                0.7978845608028654 * (1.0 + 3.0 * 0.044715 * square)
            )
            grad_v[t, :, cut] = slope.astype(jnp.bfloat16)
            return carry

        return one

    def high_tile(h):
        right = slice(h * wide, (h + 1) * wide)

        def one(t, carry):
            weight = down_v[4:, :, right].reshape(half, wide)
            value = product(gated_v[t, :, half:], weight)
            terms_v[1, t, :, right] = value.astype(jnp.bfloat16)
            return carry

        lax.fori_loop(0, ranks, one, 0)
        cut = columns[h]
        links.keep(terms_v.at[1, rank, :, cut], extra_in.at[:, cut], rank == 0)
        detour = Detour(
            place,
            links,
            terms_v.at[1, place.across, :, cut],
            extra_in.at[:, cut],
            stop_more.at[:, cut],
            0,
            2,
            3,
        )
        for r in (place.first, place.second):
            dealt_more.append(
                Message(
                    links,
                    terms_v.at[1, r, :, cut],
                    extra_in.at[:, cut],
                    place.at(rank=r),
                    rank == 0,
                    r == 0,
                )
            )
        return detour

    def low_tile(t, carry):
        low_term = product(gated_v[t, :, :half], down_v[:4].reshape(half, model_width))
        high_term = terms_v[1, t].astype(jnp.float32) * jnp.where(rank == 0, 0.0, 1.0)
        terms_v[0, t] = (low_term + high_term).astype(jnp.bfloat16)
        return carry

    def block(k):
        t = order[k]
        for i in range(2):
            cut = slice(i * half, (i + 1) * half)
            weight = down_v[4 * i : 4 * i + 4].reshape(half, model_width)
            grad = back_product(csum_v[slots[i], t], weight) * grad_v[t, :, cut].astype(jnp.float32)
            grad_v[t, :, cut] = grad.astype(jnp.bfloat16)
            sums[3:4, cut] += jnp.sum(grad, axis=0, keepdims=True)

        def back(i, carry):
            own = model_width // ranks
            value = back_product(grad_v[t], up_v[i].reshape(own, ff_cols))
            partial[t, :, pl.ds(pl.multiple_of(i * own, 128), own)] = value.astype(jnp.bfloat16)
            return carry

        lax.fori_loop(0, ranks, back, 0)

    dealt_more = []
    lax.fori_loop(0, ranks, widen(1), 0)
    detour.relay()
    chain_down.step(1)
    load_down.arrive()
    detour_low = high_tile(0)
    chain_down.step(2)
    lax.fori_loop(0, ranks // 2, widen(0), 0)
    chain_down.step(3)
    lax.fori_loop(ranks // 2, ranks, widen(0), 0)
    chain_down.finish()
    load_own.arrive()
    detour_high = high_tile(1)
    detour_low.relay()
    load_csum.arrive()
    load_more.arrive()
    for message in dealt + [detour]:
        message.arrive()

    def down_tiles(h):
        width = model_width // 2
        right = slice(h * width, (h + 1) * width)

        def down_tile(i, carry):
            rows = ff_cols // ranks
            left = gated_v[:, :, pl.ds(pl.multiple_of(i * rows, 128), rows)].reshape(-1, rows)
            slot = jnp.where(i < 2, slots[0], slots[1])
            value = gram_product(left, csum_v[slot, :, :, right].reshape(-1, width))
            part_down[h, i] = value.astype(jnp.bfloat16).reshape(part_down.shape[2:])
            return carry

        lax.fori_loop(0, ranks, down_tile, 0)
        here = pl.ds(h, 1)
        return Beside(place, links, part_down.at[here], other_down.at[here])

    def along_half(beside, h):
        beside.add()
        share = part_down.at[pl.ds(h, 1)]
        return Along(
            place, links, lambda there: share.at[:, there, place.core], land_down.at[h]
        )

    beside_low = down_tiles(0)
    block(0)
    scatter.send_far()
    along_low = along_half(beside_low, 0)
    block(1)
    scatter.send_near()
    beside_high = down_tiles(1)
    block(2)
    scatter.relay()
    along_high = along_half(beside_high, 1)
    detour_high.relay()
    along_low.relay()
    block(3)

    def up_tile(i, carry):
        rows = model_width // ranks
        left = ffn_v[:, :, pl.ds(pl.multiple_of(i * rows, 128), rows)].reshape(-1, rows)
        value = gram_product(left, grad_v[...].reshape(-1, ff_cols))
        up_v[i] = value.astype(jnp.bfloat16).reshape(up_v.shape[1:])
        return carry

    lax.fori_loop(0, ranks, up_tile, 0)
    beside_up = Beside(place, links, up_v, other_up)
    along_high.relay()

    beside_up.add()
    first_cols = sum_up_low.shape[2]
    share_low = up_v.at[:, :, :, :, pl.ds(0, first_cols)]
    along_up = Along(place, links, lambda there: share_low.at[:, there, place.core], land_up)
    rest = pl.ds(first_cols, ff_cols - first_cols)
    links.keep(up_v.at[:, :, place.core, :, rest], share_up)
    scatter.settle()

    def norm_back(cut):
        value, inverse = normed(hidden[cut])
        grad = scatter.total(cut)
        sums[0:1] += jnp.sum(grad * value, axis=0, keepdims=True)
        sums[1:2] += jnp.sum(grad, axis=0, keepdims=True)
        sums[2:3] += jnp.sum(cotangent_sum[cut], axis=0, keepdims=True)
        total = cotangent_sum[cut] + norm_backward(grad, value, inverse, gains[2:3])
        grad_hidden_v[cut] = total
        branch[cut] = total.astype(jnp.bfloat16)

    in_rows(tok_rows, 64, norm_back)
    gather = PlaneGather(place, links, branch, all_branch, 4)
    links.keep(grad_hidden_v, grad_hidden)
    lax.fori_loop(0, ranks, low_tile, 0)
    links.keep(terms_v.at[0], terms)
    links.keep(terms_v.at[0, rank], own_term)
    gather.relay(0)
    gather.relay(1)
    along_up.relay()
    gather.relay(2)
    gather.relay(3)
    for h, along in enumerate((along_low, along_high)):
        mine = part_down[h : h + 1, place.z, place.core]
        sum_down_v[:, h * wide : (h + 1) * wide] = along.total(mine)[0]
    links.keep(sum_down_v, sum_down)
    mine = up_v[:, place.z, place.core, :, :first_cols]
    sum_up_low[...] = along_up.total(mine).astype(jnp.bfloat16)
    gather.finish()
    for message in dealt_more + [detour_low, detour_high]:
        message.arrive()
    links.drain()


def last_kernel(
    chips,
    all_branch,
    sum_up_low,
    share_up,
    terms,
    qkv_rot,
    mixed_low,
    w_out,
    w_qkv,
    attn_in,
    all_tokens,
    grad_hidden,
    gains,
    sums,
    comb,
    mask,
    cosine,
    sine,
    term_in,
    grad_tokens,
    sum_out,
    land_sum_up,
    land_sum_qkv,
    sum_small,
    branch_v,
    rot_v,
    mixed_v,
    grad_mixed_v,
    out_v,
    qkv_v,
    attn_v,
    tokens_v,
    grad_v,
    key_sum,
    value_sum,
    partial,
    landing,
    passing,
    turn_up,
    mine_up,
    far_up,
    land_up,
    part_out,
    other_out,
    land_out,
    part_qkv,
    other_qkv,
    land_qkv,
    turn_qkv,
    part_small,
    other_small,
    land_small,
    turn_small,
    land_sums,
    more_sums,
    send,
    recv,
    near,
):
    place = Place(chips)
    links = Links(send, recv, near)
    rank, z = place.rank, place.z
    ranks, tok_rows, model_width = branch_v.shape
    head_cols = mixed_v.shape[2]
    heads = head_cols // HEAD_DIM
    load_branch = links.keep(all_branch, branch_v)
    load_out = links.keep(w_out, out_v)
    load_mixed = links.keep(mixed_low, mixed_v)
    load_rot = links.keep(qkv_rot, rot_v)
    other_end = jnp.where(z < 2, chips - 1, 0)
    piece = 3 * HEAD_DIM
    load_far = links.keep(share_up.at[:, other_end], far_up)
    first_cols = sum_up_low.shape[2]
    load_low = links.keep(sum_up_low, turn_up.at[:, :, pl.ds(0, first_cols)])
    place.greet(plane=True, sibling=True, ring=True)
    along_up = Along(place, links, lambda there: share_up.at[:, there], land_up, far_up)
    dealt = []
    for r in (place.first, place.second, place.across):
        dealt.append(Message(links, terms.at[r], term_in.at[rank], place.at(rank=r)))
    load_out.arrive()

    def mix_back(t):
        weight = out_v[...].reshape(head_cols, model_width)
        grad_mixed_v[t] = back_product(branch_v[t], weight).astype(jnp.bfloat16)

    load_branch.arrive()
    load_attn = links.keep(attn_in, attn_v)
    load_qkv = [
        links.keep(
            w_qkv.at[:, :, :, pl.ds(i * head_cols + h * HEAD_DIM, HEAD_DIM)],
            qkv_v.at[:, :, :, pl.ds(h * piece + i * HEAD_DIM, HEAD_DIM)],
        )
        for h in range(heads)
        for i in range(3)
    ]
    load_tokens = links.keep(all_tokens, tokens_v)
    load_up = links.keep(share_up.at[:, z], mine_up)
    for r in range(ranks):
        mix_back(r)
    load_mixed.arrive()
    value = gram_product(
        mixed_v[...].reshape(-1, head_cols), branch_v[...].reshape(-1, model_width)
    )
    part_out[0] = value.astype(jnp.bfloat16).reshape(part_out.shape[1:])
    beside_out = Beside(place, links, part_out, other_out)
    load_rot.arrive()

    def head(h):
        def part(i):
            return slice(i * head_cols + h * HEAD_DIM, i * head_cols + (h + 1) * HEAD_DIM)

        def place_of(i):
            return slice(h * piece + i * HEAD_DIM, h * piece + (i + 1) * HEAD_DIM)

        for t in range(ranks - 1, -1, -1):
            count = t + 1
            keys = rot_v[:count, :, part(1)].reshape(-1, HEAD_DIM)
            values = rot_v[:count, :, part(2)].reshape(-1, HEAD_DIM)
            queries = rot_v[t, :, part(0)]
            grad_mixed = grad_mixed_v[t, :, part(0)]
            scores = back_product(queries, keys)
            row = lax.broadcasted_iota(jnp.int32, scores.shape, 0) + t * tok_rows
            column = lax.broadcasted_iota(jnp.int32, scores.shape, 1)
            scores = jnp.where(row >= column, scores, masked_score)
            raised = jnp.exp(scores - jnp.max(scores, axis=-1, keepdims=True))
            probs = raised * (1.0 / jnp.sum(raised, axis=-1, keepdims=True))
            delta = jnp.sum(
                grad_mixed.astype(jnp.float32) * mixed_v[t, :, part(0)].astype(jnp.float32),
                axis=-1,
                keepdims=True,
            )
            grad_scores = (probs * (back_product(grad_mixed, values) - delta)).astype(jnp.bfloat16)
            rows = pl.ds(t * tok_rows, tok_rows)
            grad_query = product(grad_scores, keys)
            grad_query = turn_half(grad_query, cosine[rows], -sine[rows]) * HEAD_DIM ** (-0.5)
            grad_v[t, :, place_of(0)] = grad_query.astype(jnp.bfloat16)
            grad_key = gram_product(grad_scores, queries)
            grad_value = gram_product(probs.astype(jnp.bfloat16), grad_mixed)
            seen = count * tok_rows
            if t == ranks - 1:
                key_sum[...] = grad_key
                value_sum[...] = grad_value
            else:
                key_sum[:seen] += grad_key
                value_sum[:seen] += grad_value
        grad_key = turn_half(key_sum[...], cosine[...], -sine[...]).astype(jnp.bfloat16)
        grad_v[:, :, place_of(1)] = grad_key.reshape(ranks, tok_rows, HEAD_DIM)
        grad_value = value_sum[...].astype(jnp.bfloat16)
        grad_v[:, :, place_of(2)] = grad_value.reshape(ranks, tok_rows, HEAD_DIM)

        def qkv_tile(i, carry):
            rows = model_width // ranks
            left = attn_v[:, :, pl.ds(pl.multiple_of(i * rows, 128), rows)].reshape(-1, rows)
            right = grad_v[:, :, h * piece : (h + 1) * piece].reshape(-1, piece)
            value = gram_product(left, right)
            part_qkv[h, i] = value.astype(jnp.bfloat16).reshape(part_qkv.shape[2:])
            return carry

        if h == 0:
            load_attn.arrive()
        lax.fori_loop(0, ranks, qkv_tile, 0)
        return Beside(place, links, part_qkv.at[h], other_qkv.at[h])

    def along_head(h):
        return Along(
            place, links, lambda there: part_qkv.at[h, :, there, place.core], land_qkv.at[h]
        )

    beside_qkv = [head(0)]
    load_far.arrive()
    along_up.relay()
    beside_out.add()
    along_out = Along(place, links, lambda there: part_out.at[:, there, place.core], land_out)
    along_qkv = []
    for h in range(1, heads):
        beside_qkv.append(head(h))
        beside_qkv[h - 1].add()
        along_qkv.append(along_head(h - 1))
    along_out.relay()
    for copy in load_qkv:
        copy.arrive()
    load_tokens.arrive()
    scatter = PlaneScatter(place, links, partial, landing, passing)
    more_sums[...] = jnp.zeros_like(more_sums)

    def attn_back(t):
        def tile(i, carry):
            own = model_width // ranks
            value = back_product(grad_v[t], qkv_v[i].reshape(own, 3 * head_cols))
            partial[t, :, pl.ds(pl.multiple_of(i * own, 128), own)] = value.astype(jnp.bfloat16)
            return carry

        lax.fori_loop(0, ranks, tile, 0)

        def count(cut):
            value, unused = normed(tokens_v[t, cut].astype(jnp.float32))
            grad = partial[t, cut].astype(jnp.float32)
            more_sums[0:1] += jnp.sum(grad * value, axis=0, keepdims=True)
            more_sums[1:2] += jnp.sum(grad, axis=0, keepdims=True)

        return count

    count_across = attn_back(place.across)
    scatter.send_far()
    count_first = attn_back(place.first)
    scatter.send_near()
    beside_qkv[heads - 1].add()
    along_qkv.append(along_head(heads - 1))
    along_qkv[0].relay()
    count_second = attn_back(place.second)
    scatter.relay()
    for h in range(1, heads - 1):
        along_qkv[h].relay()
    count_own = attn_back(rank)
    for count in (count_across, count_first, count_second, count_own):
        in_rows(tok_rows, 64, count)

    def pieces(row):
        spread = (row * mask[...]).astype(jnp.float32)
        return lax.dot_general(
            spread,
            comb[...].astype(jnp.float32),
            (((1,), (1,)), ((), ())),
            precision=lax.Precision.HIGHEST,
            preferred_element_type=jnp.float32,
        )

    part_small[...] = jnp.zeros_like(part_small)
    rows = (more_sums[0:1], more_sums[1:2], sums[0:1], sums[1:2], sums[2:3])
    for k, row in enumerate(rows):
        part_small[:, :, :, k] = pieces(row).reshape(ranks, chips, 2, 128)
    part_small[rank, :, :, 5:9] = pieces(sums[3:4]).reshape(chips, 2, 4, 128)
    beside_small = Beside(place, links, part_small, other_small)
    along_qkv[heads - 1].relay()
    load_up.arrive()
    load_low.arrive()
    turn_up[:, :, first_cols:] = along_up.total(mine_up[...]).astype(jnp.bfloat16)
    deal_up = Deal(place, links, [(lambda r: turn_up.at[r], land_sum_up.at[rank])])
    beside_small.add()
    along_small = Along(place, links, lambda there: part_small.at[:, there, place.core], land_small)
    sum_out[...] = along_out.total(part_out[:, z, place.core])[0]
    along_small.relay()
    deal_qkv = []

    def settle_head(h):
        total = along_qkv[h].total(part_qkv[h, :, z, place.core])
        turn_qkv[h] = total.astype(jnp.bfloat16)
        deal_qkv.append(
            Deal(place, links, [(lambda r: turn_qkv.at[h, r], land_sum_qkv.at[h, rank])])
        )

    for h in range(heads - 1):
        settle_head(h)
    scatter.settle()

    def norm_back(cut):
        value, inverse = normed(tokens_v[rank, cut].astype(jnp.float32))
        grad = norm_backward(scatter.total(cut), value, inverse, gains[0:1])
        grad_tokens[cut] = (grad_hidden[cut] + grad).astype(jnp.bfloat16)

    in_rows(tok_rows, 64, norm_back)
    turn_small[...] = along_small.total(part_small[:, z, place.core])
    deal_small = Deal(place, links, [(lambda r: turn_small.at[r], land_sums.at[rank])])
    settle_head(heads - 1)
    for message in dealt:
        message.arrive()
    deal_up.arrive()
    deal_small.arrive()
    sum_small[...] = land_sums[0] + land_sums[1] + land_sums[2] + land_sums[3]
    for deal in deal_qkv:
        deal.arrive()
    links.drain()


def closing_kernel(*refs):
    own_term, ins, outs = refs[0], refs[1:10], refs[10:23]
    held, act_v, near, leaving = refs[23:32], refs[32], refs[33], refs[34]
    rank = lax.axis_index("dp")
    hidden, gains, term_in, extra_in, grad_in, out_in = held[:6]
    up_in, qkv_in, small_in = held[6:]
    activations, grad_tokens, sum_query, sum_key, sum_value, sum_out, sum_up = outs[:7]
    steps = near.shape[0] - 1
    rows = hidden.shape[0] // steps
    cuts = [pl.ds(k * rows, rows) for k in range(steps)]
    copies = []
    for k, cut in enumerate(cuts):
        batch = []
        for i in (0, 3, 4):
            copy = pltpu.make_async_copy(ins[i].at[cut], held[i].at[cut], near.at[k, i])
            copy.start()
            batch.append(copy)
        for r in range(term_in.shape[0]):
            here, sem = term_in.at[r, cut], near.at[k, 9 + r]
            there = pltpu.make_async_copy(ins[2].at[r, cut], here, sem)
            own = pltpu.make_async_copy(own_term.at[cut], here, sem)
            pl.when(rank != r)(there.start)
            pl.when(rank == r)(own.start)
            batch.append(there)
        copies.append(batch)
    rest = []
    for i in (1, 5, 6, 7, 8):
        rest.append(pltpu.make_async_copy(ins[i], held[i], near.at[steps, i]))
        rest[-1].start()
    rest[0].wait()
    left = []
    for k, cut in enumerate(cuts):
        for copy in copies[k]:
            copy.wait()
        total = hidden[cut] + gains[4:5] + term_in[0, cut].astype(jnp.float32)
        act_v[0, cut] = total.astype(jnp.bfloat16)
        total = total + extra_in[cut].astype(jnp.float32)
        act_v[1, cut] = total.astype(jnp.bfloat16)
        total = total + term_in[1, cut].astype(jnp.float32)
        act_v[2, cut] = total.astype(jnp.bfloat16)
        total = total + term_in[2, cut].astype(jnp.float32) + term_in[3, cut].astype(jnp.float32)
        act_v[3, cut] = total.astype(jnp.bfloat16)
        left.append(
            pltpu.make_async_copy(act_v.at[:, cut], activations.at[:, cut], leaving.at[k, 0])
        )
        left[-1].start()
        left.append(pltpu.make_async_copy(grad_in.at[cut], grad_tokens.at[cut], leaving.at[k, 1]))
        left[-1].start()
    for copy in rest[1:]:
        copy.wait()
    sum_out[...] = out_in[...]
    ranks, own, ff_cols = up_in.shape
    heads, head_cols = qkv_in.shape[0], qkv_in.shape[0] * HEAD_DIM
    for r in range(ranks):
        sum_up[:, r * ff_cols : (r + 1) * ff_cols] = up_in[r].astype(jnp.float32)
        for i, total in enumerate((sum_query, sum_key, sum_value)):
            for h in range(heads):
                start = r * head_cols + h * HEAD_DIM
                value = qkv_in[h, r, :, i * HEAD_DIM : (i + 1) * HEAD_DIM]
                total[:, start : start + HEAD_DIM] = value.astype(jnp.float32)
    small_sums = outs[7:]
    for i in range(5):
        small_sums[i][...] = small_in[i : i + 1, :own]
    small_sums[5][...] = jnp.concatenate([small_in[5 + q : 6 + q, :own] for q in range(4)], axis=1)
    for copy in left:
        copy.wait()


ANY = pl.BlockSpec(memory_space=pl.ANY)
ON_CORE = pl.BlockSpec(memory_space=pltpu.VMEM)


def connected(kernel, number, outs, out_specs, in_specs, scratch, operands):
    return pl.pallas_call(
        kernel,
        out_shape=outs,
        in_specs=in_specs,
        out_specs=out_specs,
        scratch_shapes=scratch + LINK_SCRATCH,
        compiler_params=pltpu.CompilerParams(
            collective_id=number, has_side_effects=True, vmem_limit_bytes=63 * 2**20
        ),
    )(*operands)


def array(shape, dtype=jnp.bfloat16):
    return jax.ShapeDtypeStruct(shape, dtype)


def turning(count):
    half_size = HEAD_DIM // 2
    inverse = np.exp(np.arange(half_size, dtype=np.float32) * np.float32(-math.log(10000.0) / half_size))
    angles = np.arange(count, dtype=np.float32)[:, None] * inverse.astype(np.float32)[None, :]
    cosine, sine = np.cos(angles), np.sin(angles)
    cosine = np.concatenate([cosine, cosine], axis=1)
    return jnp.asarray(cosine), jnp.asarray(np.concatenate([-sine, sine], axis=1))


def local_split(ranks, shards, *arguments):
    chips = shards // 2
    (
        tokens,
        cotangent,
        norm1_gain,
        norm1_bias,
        query_weight,
        key_weight,
        value_weight,
        out_weight,
        norm2_gain,
        norm2_bias,
        up_weight,
        up_bias,
        down_weight,
        down_bias,
    ) = arguments
    model_width = tokens.shape[2]
    tok_rows = tokens.shape[1]
    seq_len = tok_rows * ranks
    own = query_weight.shape[0]
    heads = HEADS // ranks
    head_cols = heads * HEAD_DIM
    ff_cols = FF // ranks
    scaling = HEAD_DIM ** (-0.5)
    rank = lax.axis_index("dp")

    column = np.arange(model_width)
    comb = jnp.asarray(column[None, :] % own == np.arange(128)[:, None], jnp.bfloat16)
    mask = jnp.asarray(column[None, :] // own == np.arange(ranks * shards)[:, None], jnp.float32)
    cosine, sine = turning(seq_len)
    own_tokens = tokens.reshape(tok_rows, model_width)
    blocks_low = array((ranks, tok_rows, model_width))
    down_rows = down_weight.shape[0]
    first_cols = ff_cols * 5 // 12
    vmem = pltpu.VMEM
    low = jnp.bfloat16
    f32 = jnp.float32
    (
        all_tokens,
        attn_in,
        qkv_rot,
        mixed_low,
        hidden,
        ffn_in,
        gains,
        incoming,
        cotangent_sum,
        next_sum,
        w_qkv,
        w_out,
        w_up,
        w_down,
    ) = connected(
        functools.partial(forward_kernel, chips),
        1,
        (
            blocks_low,
            blocks_low,
            array((ranks, tok_rows, 3 * head_cols)),
            array((ranks, tok_rows, head_cols)),
            array((tok_rows, model_width), jnp.float32),
            blocks_low,
            array((8, model_width), jnp.float32),
            blocks_low,
            array((tok_rows, model_width), f32),
            array((tok_rows, model_width)),
            array((ranks, shards, own, 3 * head_cols)),
            array((shards, own, model_width)),
            array((ranks, shards, own, ff_cols)),
            array((shards, down_rows, model_width // 2)),
        ),
        [ANY] * 6 + [ON_CORE] + [ANY] * 7,
        [ANY] * 2 + [ON_CORE] * 16,
        [
            vmem((tok_rows, model_width), f32),
            vmem((tok_rows, model_width), f32),
            vmem((GRAN, tok_rows, model_width), low),
            vmem((GRAN, tok_rows, model_width), low),
            vmem((16, 128), low),
            vmem((ranks, tok_rows, model_width), jnp.bfloat16),
            vmem((ranks, tok_rows, model_width), jnp.bfloat16),
            vmem((ranks, tok_rows, 3 * head_cols), jnp.bfloat16),
            vmem((ranks, tok_rows, head_cols), jnp.bfloat16),
            vmem((ranks, shards, own, 3 * head_cols), jnp.bfloat16),
            vmem((shards, own, model_width), jnp.bfloat16),
            vmem((ranks, tok_rows, model_width), jnp.bfloat16),
            vmem((3, tok_rows, model_width), jnp.bfloat16),
            vmem((tok_rows, model_width), jnp.bfloat16),
            vmem((tok_rows, model_width), jnp.bfloat16),
            vmem((ranks, shards, 16, 128), jnp.bfloat16),
        ],
        (
            own_tokens,
            cotangent.reshape(GRAN, tok_rows, model_width),
            norm1_gain.reshape(1, own),
            norm1_bias.reshape(1, own),
            norm2_gain.reshape(1, own),
            norm2_bias.reshape(1, own),
            down_bias.reshape(1, own),
            up_bias.reshape(1, -1),
            query_weight,
            key_weight,
            value_weight,
            out_weight,
            up_weight,
            down_weight,
            comb,
            mask,
            cosine,
            sine,
        ),
    )
    (
        grad_hidden,
        sums,
        sum_down,
        sum_up_low,
        share_up,
        all_branch,
        terms,
        own_term,
        extra_in,
    ) = connected(
        functools.partial(middle_kernel, chips),
        2,
        (
            array((tok_rows, model_width), f32),
            array((8, model_width), f32),
            array((down_rows, model_width), f32),
            array((ranks, own, first_cols)),
            array((ranks, chips, own, ff_cols - first_cols)),
            blocks_low,
            blocks_low,
            array((tok_rows, model_width)),
            array((tok_rows, model_width)),
        ),
        [ANY, ON_CORE, ANY, ON_CORE] + [ANY] * 5,
        [ANY] * 6 + [ON_CORE] * 3,
        [
            vmem((ranks, tok_rows, model_width), low),
            vmem((2, ranks, tok_rows, model_width), low),
            vmem((ranks, chips, 2, own, ff_cols), low),
            vmem((shards, down_rows, model_width), low),
            vmem((ranks, tok_rows, ff_cols), low),
            vmem((ranks, tok_rows, ff_cols), low),
            vmem((2, chips, 2, down_rows, model_width // 2), low),
            vmem((2, chips, down_rows, model_width // 2), low),
            vmem((2, 4, 1, down_rows, model_width // 2), low),
            vmem((ranks, chips, own, ff_cols), low),
            vmem((4, ranks, own, first_cols), low),
            vmem((2, ranks, tok_rows, model_width), low),
            vmem((tok_rows, model_width), low),
            vmem((tok_rows, model_width), low),
            vmem((tok_rows, model_width), low),
            vmem((tok_rows, model_width), f32),
            vmem((down_rows, model_width), f32),
            vmem((ranks, tok_rows, model_width), low),
            vmem((3, tok_rows, model_width), low),
            vmem((tok_rows, model_width), low),
        ],
        (
            ffn_in,
            incoming,
            next_sum,
            w_up.reshape(ranks, chips, 2, own, ff_cols),
            w_down,
            down_weight,
            hidden,
            cotangent_sum,
            gains,
        ),
    )
    term_in, grad_inputs, sum_out, sum_up, sum_qkv, small_sums = connected(
        functools.partial(last_kernel, chips),
        3,
        (
            blocks_low,
            array((tok_rows, model_width)),
            array((own, model_width), f32),
            array((ranks, own, ff_cols)),
            array((heads, ranks, own, 3 * HEAD_DIM)),
            array((16, 128), f32),
        ),
        [ANY] + [ON_CORE] * 2 + [ANY] * 2 + [ON_CORE],
        [ANY] * 10 + [ON_CORE] * 7,
        [
            vmem((ranks, tok_rows, model_width), low),
            vmem((ranks, tok_rows, 3 * head_cols), low),
            vmem((ranks, tok_rows, head_cols), low),
            vmem((ranks, tok_rows, head_cols), low),
            vmem((shards, own, model_width), low),
            vmem((ranks, shards, own, 3 * head_cols), low),
            vmem((ranks, tok_rows, model_width), low),
            vmem((ranks, tok_rows, model_width), low),
            vmem((ranks, tok_rows, 3 * head_cols), low),
            vmem((seq_len, HEAD_DIM), f32),
            vmem((seq_len, HEAD_DIM), f32),
            vmem((ranks, tok_rows, model_width), low),
            vmem((3, tok_rows, model_width), low),
            vmem((tok_rows, model_width), low),
            vmem((ranks, own, ff_cols), low),
            vmem((ranks, own, ff_cols - first_cols), low),
            vmem((ranks, own, ff_cols - first_cols), low),
            vmem((4, ranks, own, ff_cols - first_cols), low),
            vmem((1, chips, 2, own, model_width), low),
            vmem((1, chips, own, model_width), low),
            vmem((4, 1, own, model_width), low),
            vmem((heads, ranks, chips, 2, own, 3 * HEAD_DIM), low),
            vmem((heads, ranks, chips, own, 3 * HEAD_DIM), low),
            vmem((heads, 4, ranks, own, 3 * HEAD_DIM), low),
            vmem((heads, ranks, own, 3 * HEAD_DIM), low),
            vmem((ranks, chips, 2, 16, 128), f32),
            vmem((ranks, chips, 16, 128), f32),
            vmem((4, ranks, 16, 128), f32),
            vmem((ranks, 16, 128), f32),
            vmem((ranks, 16, 128), f32),
            vmem((8, model_width), f32),
        ],
        (
            all_branch,
            sum_up_low,
            share_up,
            terms,
            qkv_rot,
            mixed_low,
            w_out,
            w_qkv,
            attn_in,
            all_tokens,
            grad_hidden,
            gains,
            sums,
            comb,
            mask,
            cosine,
            sine,
        ),
    )
    (
        activations,
        grad_tokens,
        sum_query,
        sum_key,
        sum_value,
        sum_out,
        sum_up,
        *gain_sums,
    ) = pl.pallas_call(
        closing_kernel,
        out_shape=(
            array((GRAN, tok_rows, model_width)),
            array((tok_rows, model_width)),
            *[array((own, model_width), f32) for i in range(4)],
            array((own, FF), f32),
            *[array((1, own), f32) for i in range(5)],
            array((1, down_rows), f32),
        ),
        in_specs=[ANY] * 10,
        out_specs=[ANY] * 2 + [ON_CORE] * 11,
        scratch_shapes=[
            vmem((tok_rows, model_width), f32),
            vmem((8, model_width), f32),
            vmem((ranks, tok_rows, model_width), low),
            vmem((tok_rows, model_width), low),
            vmem((tok_rows, model_width), low),
            vmem((own, model_width), f32),
            vmem((ranks, own, ff_cols), low),
            vmem((heads, ranks, own, 3 * HEAD_DIM), low),
            vmem((16, 128), f32),
            vmem((GRAN, tok_rows, model_width), low),
            pltpu.SemaphoreType.DMA((5, 13)),
            pltpu.SemaphoreType.DMA((4, 2)),
        ],
        compiler_params=pltpu.CompilerParams(vmem_limit_bytes=60 * 2**20),
    )(
        own_term,
        hidden,
        gains,
        term_in,
        extra_in,
        grad_inputs,
        sum_out,
        sum_up,
        sum_qkv,
        small_sums,
    )
    gain_sums = [v.reshape(-1) for v in gain_sums]
    return (
        activations.reshape(GRAN, 1, tok_rows, model_width),
        grad_tokens.reshape(1, tok_rows, model_width),
        gain_sums[0],
        gain_sums[1],
        sum_query,
        sum_key,
        sum_value,
        sum_out,
        gain_sums[2],
        gain_sums[3],
        sum_up,
        gain_sums[5],
        sum_down,
        gain_sums[4],
    )


def solution(mesh):
    placed = (
        P("fsdp", "dp", None),
        P(None, "fsdp", "dp", None),
        P(("dp", "fsdp")),
        P(("dp", "fsdp")),
        P(("dp", "fsdp"), None),
        P(("dp", "fsdp"), None),
        P(("dp", "fsdp"), None),
        P(("dp", "fsdp"), None),
        P(("dp", "fsdp")),
        P(("dp", "fsdp")),
        P(("dp", "fsdp"), None),
        P(("dp", "fsdp")),
        P(("dp", "fsdp"), None),
        P(("dp", "fsdp")),
    )
    ranks, shards = mesh.shape["dp"], mesh.shape["fsdp"]
    local = local_gathered
    if ranks == 4 and shards == 8:
        local = functools.partial(local_split, ranks, shards)
    return jax.shard_map(
        local,
        mesh=mesh,
        in_specs=placed,
        out_specs=(
            P(None, "fsdp", "dp", None),
            P("fsdp", "dp", None),
            P(("dp", "fsdp")),
            P(("dp", "fsdp")),
            P(("dp", "fsdp"), None),
            P(("dp", "fsdp"), None),
            P(("dp", "fsdp"), None),
            P(("dp", "fsdp"), None),
            P(("dp", "fsdp")),
            P(("dp", "fsdp")),
            P(("dp", "fsdp"), None),
            P(("dp", "fsdp")),
            P(("dp", "fsdp"), None),
            P(("dp", "fsdp")),
        ),
        check_vma=False,
    )
```

```python
import functools
import math

import jax
import jax.numpy as jnp
import numpy as np
from jax import lax
from jax.experimental import pallas as pl
from jax.experimental.pallas import tpu as pltpu
from jax.sharding import PartitionSpec as P

HEADS = 12
HEAD_DIM = 128
FF = 6144
GRAN = 4


epsilon = 1e-05
masked_score = -1e30


def product(left, right):
    return jnp.dot(left, right, preferred_element_type=jnp.float32)


def gram_product(left, right):
    return lax.dot_general(
        left, right, (((0,), (0,)), ((), ())), preferred_element_type=jnp.float32
    )


def back_product(left, right):
    return lax.dot_general(
        left, right, (((1,), (1,)), ((), ())), preferred_element_type=jnp.float32
    )


def norm_parts(values):
    centred = values - jnp.mean(values, axis=-1, keepdims=True)
    inverse = lax.rsqrt(jnp.mean(centred * centred, axis=-1, keepdims=True) + epsilon)
    return (centred * inverse, inverse)


def norm_backward(grad_normed, normed, inverse, gain):
    scaled = grad_normed * gain
    return inverse * (
        scaled
        - jnp.mean(scaled, axis=-1, keepdims=True)
        - normed * jnp.mean(scaled * normed, axis=-1, keepdims=True)
    )


def gelu_value(values):
    return (
        0.5
        * values
        * (1.0 + jnp.tanh(0.7978845608028654 * (values + 0.044715 * values * values * values)))
    )


def gelu_grad(values):
    tangent = jnp.tanh(0.7978845608028654 * (values + 0.044715 * values * values * values))
    return 0.5 * (1.0 + tangent) + 0.5 * values * (1.0 - tangent * tangent) * 0.7978845608028654 * (
        1.0 + 3.0 * 0.044715 * values * values
    )


def rotary_tables(positions, half_size):
    ladder = jnp.arange(half_size).astype(jnp.float32)
    inverse = jnp.exp(ladder * (-math.log(10000.0) / half_size))
    angles = positions[:, None] * inverse[None, :]
    return (jnp.cos(angles)[:, None, :], jnp.sin(angles)[:, None, :])


def rotate(values, cosine, sine):
    half_size = values.shape[-1] // 2
    first = values[..., :half_size]
    second = values[..., half_size:]
    return jnp.concatenate(
        [first * cosine - second * sine, second * cosine + first * sine], axis=-1
    )


def block_scores(queries, positions, key_block, start_row):
    block_rows = key_block.shape[0]
    scores = jnp.einsum("qhd,khd->hqk", queries, key_block, preferred_element_type=jnp.float32)
    key_positions = start_row + jnp.arange(block_rows, dtype=jnp.int32)
    visible = positions[None, :, None] >= key_positions[None, None, :]
    return (jnp.where(visible, scores, masked_score), visible)


def key_blocking(keys_all, values_all, key_offset):
    seq_len = keys_all.shape[0]
    block_rows = min(512, seq_len)
    block_count = seq_len // block_rows
    key_blocks = keys_all.reshape(block_count, block_rows, HEADS, HEAD_DIM)
    value_blocks = values_all.reshape(block_count, block_rows, HEADS, HEAD_DIM)
    starts = key_offset + jnp.arange(block_count, dtype=jnp.int32) * block_rows
    return (key_blocks, value_blocks, starts)


def attend(queries, keys_all, values_all, positions):
    tok_rows = queries.shape[0]
    key_blocks, value_blocks, starts = key_blocking(keys_all, values_all, jnp.int32(0))

    def measure(state_pair, block_pair):
        top_score, total = state_pair
        key_block, start_row = block_pair
        scores, visible = block_scores(queries, positions, key_block, start_row)
        new_top = jnp.maximum(top_score, jnp.max(scores, axis=-1))
        raised = jnp.where(visible, jnp.exp(scores - new_top[..., None]), 0.0)
        total = total * jnp.exp(top_score - new_top) + jnp.sum(raised, axis=-1)
        return ((new_top, total), None)

    initial = (
        jnp.full((HEADS, tok_rows), masked_score, jnp.float32),
        jnp.zeros((HEADS, tok_rows), jnp.float32),
    )
    (top_score, total), unused = lax.scan(measure, initial, (key_blocks, starts))
    log_total = top_score + jnp.log(total)

    def accumulate(mixed, block_triple):
        key_block, value_block, start_row = block_triple
        scores, visible = block_scores(queries, positions, key_block, start_row)
        probs = jnp.where(visible, jnp.exp(scores - log_total[..., None]), 0.0).astype(jnp.bfloat16)
        return (
            mixed
            + jnp.einsum("hqk,khd->qhd", probs, value_block, preferred_element_type=jnp.float32),
            None,
        )

    mixed, unused = lax.scan(
        accumulate,
        jnp.zeros((tok_rows, HEADS, HEAD_DIM), jnp.float32),
        (key_blocks, value_blocks, starts),
    )
    return (mixed, log_total)


def attend_back(
    queries, positions, keys_all, values_all, key_offset, grad_mixed, log_total, row_delta
):
    tok_rows = queries.shape[0]
    key_blocks, value_blocks, starts = key_blocking(keys_all, values_all, key_offset)

    def backward_block(grad_queries, block_triple):
        key_block, value_block, start_row = block_triple
        scores, visible = block_scores(queries, positions, key_block, start_row)
        probs = jnp.where(visible, jnp.exp(scores - log_total[..., None]), 0.0)
        grad_probs = jnp.einsum(
            "qhd,khd->hqk", grad_mixed, value_block, preferred_element_type=jnp.float32
        )
        grad_scores = (probs * (grad_probs - row_delta[..., None])).astype(jnp.bfloat16)
        grad_queries = grad_queries + jnp.einsum(
            "hqk,khd->qhd", grad_scores, key_block, preferred_element_type=jnp.float32
        )
        grad_key_block = jnp.einsum(
            "hqk,qhd->khd", grad_scores, queries, preferred_element_type=jnp.float32
        )
        grad_value_block = jnp.einsum(
            "hqk,qhd->khd",
            probs.astype(jnp.bfloat16),
            grad_mixed,
            preferred_element_type=jnp.float32,
        )
        return (grad_queries, (grad_key_block, grad_value_block))

    grad_queries, (grad_keys, grad_values) = lax.scan(
        backward_block,
        jnp.zeros((tok_rows, HEADS, HEAD_DIM), jnp.float32),
        (key_blocks, value_blocks, starts),
    )
    key_len = keys_all.shape[0]
    return (
        grad_queries,
        grad_keys.reshape(key_len, HEADS * HEAD_DIM),
        grad_values.reshape(key_len, HEADS * HEAD_DIM),
    )


def local_gathered(
    tokens,
    cotangent,
    norm1_gain,
    norm1_bias,
    query_weight,
    key_weight,
    value_weight,
    out_weight,
    norm2_gain,
    norm2_bias,
    up_weight,
    up_bias,
    down_weight,
    down_bias,
):
    (
        gain_one,
        bias_one,
        w_query,
        w_key,
        w_value,
        w_out,
        gain_two,
        bias_two,
        w_up,
        b_up,
        w_down,
        b_down,
    ) = (
        lax.all_gather(norm1_gain, ("dp", "fsdp"), axis=0, tiled=True),
        lax.all_gather(norm1_bias, ("dp", "fsdp"), axis=0, tiled=True),
        lax.all_gather(query_weight, ("dp", "fsdp"), axis=0, tiled=True),
        lax.all_gather(key_weight, ("dp", "fsdp"), axis=0, tiled=True),
        lax.all_gather(value_weight, ("dp", "fsdp"), axis=0, tiled=True),
        lax.all_gather(out_weight, ("dp", "fsdp"), axis=0, tiled=True),
        lax.all_gather(norm2_gain, ("dp", "fsdp"), axis=0, tiled=True),
        lax.all_gather(norm2_bias, ("dp", "fsdp"), axis=0, tiled=True),
        lax.all_gather(up_weight, ("dp", "fsdp"), axis=0, tiled=True),
        lax.all_gather(up_bias, ("dp", "fsdp"), axis=0, tiled=True),
        lax.all_gather(down_weight, ("dp", "fsdp"), axis=0, tiled=True),
        lax.all_gather(down_bias, ("dp", "fsdp"), axis=0, tiled=True),
    )
    seq_count = tokens.shape[0]
    tok_rows = tokens.shape[1]
    model_width = tokens.shape[2]
    all_rows = seq_count * tok_rows
    scaling = HEAD_DIM ** (-0.5)
    inputs = tokens.reshape(all_rows, model_width).astype(jnp.float32)
    normed_one, inverse_one = norm_parts(inputs)
    attn_in = (normed_one * gain_one.astype(jnp.float32) + bias_one.astype(jnp.float32)).astype(
        jnp.bfloat16
    )
    queries = product(attn_in, w_query).reshape(seq_count, tok_rows, HEADS, HEAD_DIM)
    key_raw = product(attn_in, w_key).reshape(seq_count, tok_rows, HEADS, HEAD_DIM)
    value_low = (
        product(attn_in, w_value).astype(jnp.bfloat16).reshape(seq_count, tok_rows, model_width)
    )
    key_offset = lax.axis_index("dp") * tok_rows
    positions = key_offset + jnp.arange(tok_rows, dtype=jnp.int32)
    cosine, sine = rotary_tables(positions.astype(jnp.float32), HEAD_DIM // 2)
    q_rot = (rotate(queries, cosine, sine) * scaling).astype(jnp.bfloat16)
    k_flat = (
        rotate(key_raw, cosine, sine).astype(jnp.bfloat16).reshape(seq_count, tok_rows, model_width)
    )
    keys_all, values_all = (
        lax.all_gather(k_flat, "dp", axis=1, tiled=True),
        lax.all_gather(value_low, "dp", axis=1, tiled=True),
    )
    seq_len = keys_all.shape[1]
    mixed, log_total = jax.vmap(attend, in_axes=(0, 0, 0, None))(
        q_rot,
        keys_all.reshape(seq_count, seq_len, HEADS, HEAD_DIM),
        values_all.reshape(seq_count, seq_len, HEADS, HEAD_DIM),
        positions,
    )
    mixed_low = mixed.reshape(all_rows, model_width).astype(jnp.bfloat16)
    hidden = inputs + product(mixed_low, w_out)
    normed_two, inverse_two = norm_parts(hidden)
    ffn_in = (normed_two * gain_two.astype(jnp.float32) + bias_two.astype(jnp.float32)).astype(
        jnp.bfloat16
    )
    preact = product(ffn_in, w_up) + b_up.astype(jnp.float32)
    edges = [0] + [FF // 2 ** (GRAN - 1 - level_idx) for level_idx in range(GRAN)]
    gated_list = []
    result_list = []
    for level_idx in range(GRAN):
        level_width = edges[level_idx + 1]
        gated = gelu_value(preact[:, :level_width]).astype(jnp.bfloat16)
        gated_list.append(gated)
        result = hidden + product(gated, w_down[:level_width]) + b_down.astype(jnp.float32)
        result_list.append(result.astype(jnp.bfloat16))
    activations = jnp.stack(result_list).reshape(GRAN, seq_count, tok_rows, model_width)
    back_gain_one, back_query, back_key, back_value, back_out, back_gain_two, back_up, back_down = (
        lax.all_gather(norm1_gain, ("dp", "fsdp"), axis=0, tiled=True),
        lax.all_gather(query_weight, ("dp", "fsdp"), axis=0, tiled=True),
        lax.all_gather(key_weight, ("dp", "fsdp"), axis=0, tiled=True),
        lax.all_gather(value_weight, ("dp", "fsdp"), axis=0, tiled=True),
        lax.all_gather(out_weight, ("dp", "fsdp"), axis=0, tiled=True),
        lax.all_gather(norm2_gain, ("dp", "fsdp"), axis=0, tiled=True),
        lax.all_gather(up_weight, ("dp", "fsdp"), axis=0, tiled=True),
        lax.all_gather(down_weight, ("dp", "fsdp"), axis=0, tiled=True),
    )
    grads_out = cotangent.reshape(GRAN, all_rows, model_width)
    grad_hidden = jnp.sum(grads_out.astype(jnp.float32), axis=0)
    grad_down_bias = jnp.sum(grad_hidden, axis=0)
    grad_ffn_in = jnp.zeros((all_rows, model_width), jnp.float32)
    pre_grads = []
    for level_idx in range(GRAN):
        level_width = edges[level_idx + 1]
        grad_gated = back_product(grads_out[level_idx], back_down[:level_width])
        grad_pre = (grad_gated * gelu_grad(preact[:, :level_width])).astype(jnp.bfloat16)
        pre_grads.append(grad_pre)
        grad_ffn_in = grad_ffn_in + back_product(grad_pre, back_up[:, :level_width])
    up_blocks = []
    bias_blocks = []
    down_blocks = []
    for block_idx in range(GRAN):
        start_col = edges[block_idx]
        stop_col = edges[block_idx + 1]
        stacked_grad = jnp.concatenate(
            [pre_grads[level_idx][:, start_col:stop_col] for level_idx in range(block_idx, GRAN)],
            axis=0,
        )
        stacked_in = jnp.concatenate([ffn_in] * (GRAN - block_idx), axis=0)
        up_blocks.append(gram_product(stacked_in, stacked_grad))
        bias_blocks.append(jnp.sum(stacked_grad.astype(jnp.float32), axis=0))
        stacked_gated = jnp.concatenate(
            [gated_list[level_idx][:, start_col:stop_col] for level_idx in range(block_idx, GRAN)],
            axis=0,
        )
        stacked_out = jnp.concatenate(
            [grads_out[level_idx] for level_idx in range(block_idx, GRAN)], axis=0
        )
        down_blocks.append(gram_product(stacked_gated, stacked_out))
    grad_up_weight = jnp.concatenate(up_blocks, axis=1)
    grad_up_bias = jnp.concatenate(bias_blocks, axis=0)
    grad_down_weight = jnp.concatenate(down_blocks, axis=0)
    grad_gain_two = jnp.sum(grad_ffn_in * normed_two, axis=0)
    grad_bias_two = jnp.sum(grad_ffn_in, axis=0)
    grad_hidden = grad_hidden + norm_backward(
        grad_ffn_in, normed_two, inverse_two, back_gain_two.astype(jnp.float32)
    )
    grad_branch = grad_hidden.astype(jnp.bfloat16)
    grad_out_weight = gram_product(mixed_low, grad_branch)
    grad_mixed = (
        back_product(grad_branch, back_out)
        .astype(jnp.bfloat16)
        .reshape(seq_count, tok_rows, HEADS, HEAD_DIM)
    )
    row_delta = jnp.einsum("sqhd,sqhd->shq", grad_mixed.astype(jnp.float32), mixed)
    keys_again, values_again = (
        lax.all_gather(k_flat, "dp", axis=1, tiled=True),
        lax.all_gather(value_low, "dp", axis=1, tiled=True),
    )
    back_all = jax.vmap(attend_back, in_axes=(0, None, 0, 0, None, 0, 0, 0))
    grad_q_rot, grad_keys_all, grad_values_all = back_all(
        q_rot,
        positions,
        keys_again.reshape(seq_count, seq_len, HEADS, HEAD_DIM),
        values_again.reshape(seq_count, seq_len, HEADS, HEAD_DIM),
        jnp.int32(0),
        grad_mixed,
        log_total,
        row_delta,
    )
    every_query, every_grad = (
        lax.all_gather(q_rot, "dp", axis=1, tiled=True),
        lax.all_gather(grad_mixed, "dp", axis=1, tiled=True),
    )
    every_total, every_delta = (
        lax.all_gather(jnp.transpose(log_total, (0, 2, 1)), "dp", axis=1, tiled=True),
        lax.all_gather(jnp.transpose(row_delta, (0, 2, 1)), "dp", axis=1, tiled=True),
    )
    every_position = jnp.arange(seq_len, dtype=jnp.int32)
    unused_rows, grad_key_mine, grad_value_mine = back_all(
        every_query,
        every_position,
        k_flat.reshape(seq_count, tok_rows, HEADS, HEAD_DIM),
        value_low.reshape(seq_count, tok_rows, HEADS, HEAD_DIM),
        key_offset,
        every_grad,
        jnp.transpose(every_total, (0, 2, 1)),
        jnp.transpose(every_delta, (0, 2, 1)),
    )
    grad_query = (
        rotate(grad_q_rot * scaling, cosine, -sine)
        .reshape(all_rows, model_width)
        .astype(jnp.bfloat16)
    )
    grad_key = (
        rotate(grad_key_mine.reshape(seq_count, tok_rows, HEADS, HEAD_DIM), cosine, -sine)
        .reshape(all_rows, model_width)
        .astype(jnp.bfloat16)
    )
    grad_val = grad_value_mine.reshape(all_rows, model_width).astype(jnp.bfloat16)
    grad_query_weight = gram_product(attn_in, grad_query)
    grad_key_weight = gram_product(attn_in, grad_key)
    grad_value_weight = gram_product(attn_in, grad_val)
    grad_attn_in = (
        back_product(grad_query, back_query)
        + back_product(grad_key, back_key)
        + back_product(grad_val, back_value)
    )
    grad_gain_one = jnp.sum(grad_attn_in * normed_one, axis=0)
    grad_bias_one = jnp.sum(grad_attn_in, axis=0)
    grad_inputs = grad_hidden + norm_backward(
        grad_attn_in, normed_one, inverse_one, back_gain_one.astype(jnp.float32)
    )
    (
        sum_gain_one,
        sum_bias_one,
        sum_query,
        sum_key,
        sum_value,
        sum_out,
        sum_gain_two,
        sum_bias_two,
        sum_up,
        sum_up_bias,
        sum_down,
        sum_down_bias,
    ) = (
        lax.psum_scatter(grad_gain_one, ("dp", "fsdp"), scatter_dimension=0, tiled=True),
        lax.psum_scatter(grad_bias_one, ("dp", "fsdp"), scatter_dimension=0, tiled=True),
        lax.psum_scatter(grad_query_weight, ("dp", "fsdp"), scatter_dimension=0, tiled=True),
        lax.psum_scatter(grad_key_weight, ("dp", "fsdp"), scatter_dimension=0, tiled=True),
        lax.psum_scatter(grad_value_weight, ("dp", "fsdp"), scatter_dimension=0, tiled=True),
        lax.psum_scatter(grad_out_weight, ("dp", "fsdp"), scatter_dimension=0, tiled=True),
        lax.psum_scatter(grad_gain_two, ("dp", "fsdp"), scatter_dimension=0, tiled=True),
        lax.psum_scatter(grad_bias_two, ("dp", "fsdp"), scatter_dimension=0, tiled=True),
        lax.psum_scatter(grad_up_weight, ("dp", "fsdp"), scatter_dimension=0, tiled=True),
        lax.psum_scatter(grad_up_bias, ("dp", "fsdp"), scatter_dimension=0, tiled=True),
        lax.psum_scatter(grad_down_weight, ("dp", "fsdp"), scatter_dimension=0, tiled=True),
        lax.psum_scatter(grad_down_bias, ("dp", "fsdp"), scatter_dimension=0, tiled=True),
    )
    return (
        activations,
        grad_inputs.astype(jnp.bfloat16).reshape(seq_count, tok_rows, model_width),
        sum_gain_one,
        sum_bias_one,
        sum_query,
        sum_key,
        sum_value,
        sum_out,
        sum_gain_two,
        sum_bias_two,
        sum_up,
        sum_up_bias,
        sum_down,
        sum_down_bias,
    )


MESH = pl.DeviceIdType.MESH


class Place:
    def __init__(self, chips):
        self.chips = chips
        self.rank = lax.axis_index("dp")
        self.shard = lax.axis_index("fsdp")
        self.z = lax.div(self.shard, 2)
        self.core = lax.rem(self.shard, 2)
        along_x = self.rank + 1 - 2 * lax.rem(self.rank, 2)
        along_y = self.rank + 2 - 4 * lax.div(self.rank, 2)
        self.first = jnp.where(self.core == 0, along_x, along_y)
        self.second = jnp.where(self.core == 0, along_y, along_x)
        self.across = 3 - self.rank
        self.sibling = self.shard + 1 - 2 * self.core
        self.above = lax.rem(self.shard + 2, 2 * chips)
        self.below = lax.rem(self.shard + 2 * chips - 2, 2 * chips)

    def at(self, rank=None, shard=None):
        return (self.rank if rank is None else rank, self.shard if shard is None else shard)

    def others(self):
        return [lax.rem(self.shard + k, 2 * self.chips) for k in range(1, 2 * self.chips)]

    def greet(self, plane=True, sibling=False, ring=False, group=False):
        barrier = pltpu.get_barrier_semaphore()
        count = 0
        targets = []
        if plane:
            targets += [self.at(rank=r) for r in (self.first, self.second, self.across)]
        if sibling:
            targets.append(self.at(shard=self.sibling))
        if ring:
            targets += [self.at(shard=self.hop(k)) for k in range(1, self.chips)]
        if group:
            targets += [self.at(shard=f) for f in self.others()]
        for target in targets:
            pl.semaphore_signal(barrier, inc=1, device_id=target, device_id_type=MESH)
            count += 1
        pl.semaphore_wait(barrier, count)

    def hop(self, k):
        return 2 * lax.rem(self.z + k, self.chips) + self.core


def under(condition, action):
    if condition is None:
        action()
    else:
        pl.when(condition)(action)


class Message:
    def __init__(self, links, src, dst, target, sent=None, comes=None):
        index = links.take()
        self.copy = pltpu.make_async_remote_copy(
            src_ref=src,
            dst_ref=dst,
            send_sem=links.send.at[index],
            recv_sem=links.recv.at[index],
            device_id=target,
            device_id_type=MESH,
        )
        self.sent, self.comes = sent, comes
        self.left = False
        links.open.append(self)
        under(sent, self.copy.start)

    def arrive(self):
        under(self.comes, self.copy.wait_recv)

    def leave(self):
        if not self.left:
            under(self.sent, self.copy.wait_send)
        self.left = True


class Near:
    def __init__(self, links, src, dst, where):
        self.copy = pltpu.make_async_copy(src, dst, links.near.at[links.used_near])
        links.used_near += 1
        self.where = where
        self.waits = True
        under(where, self.copy.start)

    def arrive(self):
        if self.waits:
            under(self.where, self.copy.wait)
        self.waits = False


class Links:
    def __init__(self, send, recv, near):
        self.send, self.recv, self.near = send, recv, near
        self.used = 0
        self.used_near = 0
        self.open = []
        self.open_near = []

    def take(self):
        self.used += 1
        return self.used - 1

    def keep(self, src, dst, where=None):
        copy = Near(self, src, dst, where)
        self.open_near.append(copy)
        return copy

    def drain(self):
        for copy in self.open_near:
            copy.arrive()
        for message in self.open:
            message.leave()


LINK_SCRATCH = [
    pltpu.SemaphoreType.DMA((128,)),
    pltpu.SemaphoreType.DMA((128,)),
    pltpu.SemaphoreType.DMA((32,)),
]


def normed(values):
    centred = values - jnp.mean(values, axis=-1, keepdims=True)
    inverse = lax.rsqrt(jnp.mean(centred * centred, axis=-1, keepdims=True) + epsilon)
    return centred * inverse, inverse


def in_rows(count, step, body):
    def one(i, carry):
        body(pl.ds(pl.multiple_of(i * step, step), step))
        return carry

    lax.fori_loop(0, count // step, one, 0)


def turn_half(values, cosine, sine):
    return values * cosine + pltpu.roll(values, HEAD_DIM // 2, 1) * sine


class PlaneGather:
    def __init__(self, place, links, src, dst, parts):
        self.place, self.links, self.dst = place, links, dst
        rows = src.shape[0] // parts
        self.cuts = [pl.ds(k * rows, rows) for k in range(parts)]
        self.own = links.keep(src, dst.at[place.rank])
        self.first, self.second = [], []
        for cut in self.cuts:
            for side, target in ((self.first, place.first), (self.second, place.second)):
                block = dst.at[place.rank, cut]
                side.append(Message(links, src.at[cut], block, place.at(rank=target)))
        self.passed = []

    def relay(self, k):
        self.first[k].arrive()
        block = self.dst.at[self.place.first, self.cuts[k]]
        target = self.place.at(rank=self.place.second)
        self.passed.append(Message(self.links, block, block, target))

    def finish(self):
        for message in self.second + self.passed:
            message.arrive()


class PlaneScatter:
    def __init__(self, place, links, partial, landing, turn):
        self.place, self.links, self.partial, self.landing, self.turn = (
            place,
            links,
            partial,
            landing,
            turn,
        )
        self.target = place.at(rank=place.first)

    def send_far(self):
        self.far = Message(
            self.links, self.partial.at[self.place.across], self.landing.at[0], self.target
        )

    def send_near(self):
        self.near = Message(
            self.links, self.partial.at[self.place.first], self.landing.at[1], self.target
        )

    def relay(self):
        self.far.arrive()

        def add(cut):
            mine = self.partial[self.place.second, cut].astype(jnp.float32)
            mine = mine + self.landing[0, cut].astype(jnp.float32)
            self.turn[cut] = mine.astype(jnp.bfloat16)

        in_rows(self.turn.shape[0], 64, add)
        self.last = Message(
            self.links, self.turn, self.landing.at[2], self.place.at(rank=self.place.second)
        )

    def settle(self):
        self.near.arrive()
        self.last.arrive()

    def total(self, cut):
        total = self.partial[self.place.rank, cut].astype(jnp.float32)
        total = total + self.landing[1, cut].astype(jnp.float32)
        return total + self.landing[2, cut].astype(jnp.float32)


class Chain:
    def __init__(self, place, links, src, slot):
        self.place, self.links, self.slot = place, links, slot
        z, last = place.z, place.chips - 1
        own = slot(place.shard)
        self.up = Message(links, src, own, place.at(shard=place.above), z < last, z > 0)
        self.down = Message(links, src, own, place.at(shard=place.below), z > 0, z < last)
        self.beside = [Message(links, src, own, place.at(shard=place.sibling))]

    def step(self, s):
        place, links = self.place, self.links
        z, last = place.z, place.chips - 1
        below = self.slot(jnp.maximum(place.shard - 2 * s, place.core))
        above = self.slot(jnp.minimum(place.shard + 2 * s, 2 * last + place.core))
        self.up.arrive()
        has_below, has_above = z >= s, z <= last - s
        up = down = None
        if s < last:
            target = place.at(shard=place.above)
            up = Message(links, below, below, target, has_below & (z < last), z >= s + 1)
        self.beside.append(
            Message(links, below, below, place.at(shard=place.sibling), has_below, has_below)
        )
        self.down.arrive()
        if s < last:
            target = place.at(shard=place.below)
            down = Message(links, above, above, target, has_above & (z > 0), z <= last - s - 1)
        self.beside.append(
            Message(links, above, above, place.at(shard=place.sibling), has_above, has_above)
        )
        self.up, self.down = up, down

    def finish(self):
        for message in self.beside:
            message.arrive()


class Beside:
    def __init__(self, place, links, part, other):
        self.place, self.part, self.other = place, part, other
        self.message = Message(
            links, part.at[:, :, 1 - place.core], other, place.at(shard=place.sibling)
        )

    def add(self):
        self.message.arrive()
        core = self.place.core

        def one(k, carry):
            total = self.part[:, k, core].astype(jnp.float32) + self.other[:, k].astype(jnp.float32)
            self.part[:, k, core] = total.astype(self.part.dtype)
            return carry

        lax.fori_loop(0, self.place.chips, one, 0)


class Along:
    def __init__(self, place, links, share, landing, far=None):
        self.place, self.links, self.landing = place, links, landing
        z = place.z
        self.middle = (z == 1) | (z == 2)
        end = jnp.logical_not(self.middle)
        partner = z + 1 - 2 * lax.rem(z, 2)
        over = jnp.where(z < 2, 2, 1)
        self.other_end = jnp.where(z < 2, 3, 0)
        self.far = share(self.other_end) if far is None else far

        def to(chip):
            return place.at(shard=2 * chip + place.core)

        self.to = to

        @pl.when(end)
        def nothing_comes():
            landing[2] = jnp.zeros_like(landing[2])

        self.merge = Message(
            links, share(self.other_end), landing.at[3], to(partner), end, self.middle
        )
        self.messages = [
            Message(links, share(partner), landing.at[0], to(partner)),
            Message(links, share(over), landing.at[1], to(over), end, self.middle),
            Message(links, share(over), landing.at[2], to(over), self.middle, self.middle),
        ]

    def relay(self):
        self.merge.arrive()
        landing = self.landing

        @pl.when(self.middle)
        def add():
            total = landing[3].astype(jnp.float32) + self.far[...].astype(jnp.float32)
            landing[3] = total.astype(landing.dtype)

        end = jnp.logical_not(self.middle)
        self.messages.append(
            Message(
                self.links, landing.at[3], landing.at[1], self.to(self.other_end), self.middle, end
            )
        )

    def total(self, mine):
        total = mine.astype(jnp.float32)
        for message in self.messages:
            message.arrive()
        for k in range(3):
            total = total + self.landing[k].astype(jnp.float32)
        return total


class Detour:
    def __init__(self, place, links, src, dst, stop, source, turn, goal):
        self.place, self.links, self.dst, self.stop = place, links, dst, stop
        straight = place.core == 0
        around = place.core == 1
        across = place.at(rank=place.across)
        self.goal = around & (place.rank == goal)
        self.turn = around & (place.rank == turn)
        here = place.rank == source
        self.straight = Message(
            links, src, dst, across, straight & here, straight & (place.rank == goal)
        )
        self.leg = Message(
            links, src, stop, place.at(rank=place.first), around & here, self.turn
        )

    def relay(self):
        self.leg.arrive()
        target = self.place.at(rank=self.place.second)
        self.last = Message(self.links, self.stop, self.dst, target, self.turn, self.goal)

    def arrive(self):
        self.straight.arrive()
        self.last.arrive()


class Deal:
    def __init__(self, place, links, pairs):
        self.messages = []
        for part, dst in pairs:
            self.messages.append(links.keep(part(place.rank), dst))
            for rank in (place.first, place.second, place.across):
                self.messages.append(Message(links, part(rank), dst, place.at(rank=rank)))

    def arrive(self):
        for message in self.messages:
            message.arrive()


def block_of(r):
    return jnp.where(r == 0, 0, jnp.minimum(r + 1, GRAN - 1))


def forward_kernel(
    chips,
    tokens,
    cotangent,
    gain_one,
    bias_one,
    gain_two,
    bias_two,
    b_down,
    b_up,
    w_query,
    w_key,
    w_value,
    w_out,
    w_up,
    w_down,
    comb,
    mask,
    cosine,
    sine,
    all_tokens,
    attn_in,
    qkv_rot,
    mixed_low,
    hidden,
    all_ffn_in,
    gains,
    incoming,
    cotangent_sum,
    next_sum,
    all_qkv,
    all_out,
    all_up,
    all_down,
    hidden_v,
    sum_v,
    cotangent_v,
    suffix,
    small,
    tokens_v,
    attn_v,
    rot_v,
    mixed_v,
    qkv_v,
    out_v,
    partial,
    landing,
    passing,
    ffn_v,
    all_small,
    send,
    recv,
    near,
):
    place = Place(chips)
    links = Links(send, recv, near)
    load_cotangent = links.keep(cotangent, cotangent_v)
    own = gain_one.shape[1]
    packed = [v[...].astype(jnp.float32) for v in (gain_one, bias_one, gain_two, bias_two, b_down)]
    wide_bias = b_up[...].astype(jnp.float32)
    packed += [wide_bias[:, q * own : (q + 1) * own] for q in range(4)]
    packed = jnp.concatenate(packed + [jnp.zeros((7, own), jnp.float32)], axis=0)
    packed = jnp.concatenate([packed, jnp.zeros((16, 128 - own), jnp.float32)], axis=1)
    small[...] = packed.astype(jnp.bfloat16)
    place.greet(plane=True, group=True)
    rank, shard = place.rank, place.shard
    ranks, tok_rows, model_width = tokens_v.shape
    head_cols = w_query.shape[1] // ranks
    heads = head_cols // HEAD_DIM

    def columns(weight, width):
        return lambda r: weight.at[:, pl.ds(pl.multiple_of(r * width, 128), width)]

    own_qkv = all_qkv.at[rank, shard]
    deal_small = Deal(place, links, [(lambda r: small, all_small.at[rank, shard])])
    pairs = []
    for i, weight in enumerate((w_query, w_key, w_value)):
        pairs.append(
            (columns(weight, head_cols), own_qkv.at[:, pl.ds(i * head_cols, head_cols)])
        )
    deal_qkv = Deal(place, links, pairs)
    gather = PlaneGather(place, links, tokens, tokens_v, 2)
    deal_up = Deal(place, links, [(columns(w_up, w_up.shape[1] // ranks), all_up.at[rank, shard])])
    links.keep(w_out, all_out.at[shard])
    low_half = pl.ds(0, model_width // 2)
    links.keep(w_down.at[:, low_half], all_down.at[shard])
    out_slot = lambda f: all_out.at[f]
    down_slot = lambda f: all_down.at[f]
    small_slot = lambda f: all_small.at[:, f]
    qkv_slot = lambda f: all_qkv.at[:, f]
    up_slot = lambda f: all_up.at[:, f]
    chain_out = Chain(place, links, w_out, out_slot)
    deal_small.arrive()
    own_small = small_slot(shard)
    told = [Message(links, own_small, own_small, place.at(shard=f)) for f in place.others()]
    deal_qkv.arrive()
    chain_qkv = Chain(place, links, qkv_slot(shard), qkv_slot)
    load_cotangent.arrive()

    def add_cotangents(cut):
        total = jnp.zeros((64, model_width), jnp.float32)
        for g in range(GRAN - 1, -1, -1):
            total = total + cotangent_v[g, cut].astype(jnp.float32)
            suffix[g, cut] = total.astype(jnp.bfloat16)
        sum_v[cut] = total

    in_rows(tok_rows, 64, add_cotangents)
    links.keep(sum_v, cotangent_sum)
    links.keep(suffix.at[1], next_sum)
    for message in told:
        message.arrive()
    chain_qkv.step(1)
    gather.relay(0)
    gather.relay(1)

    def wide(rows):
        spread = jnp.dot(rows, comb[...], preferred_element_type=jnp.float32)
        return jnp.sum(spread * mask[...], axis=0, keepdims=True)

    devices = ranks * 2 * chips
    for i in range(5):
        gains[i : i + 1] = wide(all_small[:, :, i].reshape(devices, 128))
    up_rows = all_small[rank, :, 5:9].astype(jnp.float32).reshape(devices, 128)
    gains[5:6] = wide(up_rows.astype(jnp.bfloat16))
    gains[6:8] = jnp.zeros((2, model_width), jnp.float32)

    def norm_block(r):
        def rows_of(cut):
            value, unused = normed(tokens_v[r, cut].astype(jnp.float32))
            attn_v[r, cut] = (value * gains[0:1] + gains[1:2]).astype(jnp.bfloat16)

        in_rows(tok_rows, 64, rows_of)

    for copy in links.open_near:
        copy.arrive()
    norm_block(rank)
    norm_block(place.first)
    chain_qkv.step(2)
    gather.finish()
    links.keep(suffix.at[block_of(rank)], incoming.at[rank])
    dealt = []
    for r in (place.first, place.second, place.across):
        dealt.append(Message(links, suffix.at[block_of(r)], incoming.at[rank], place.at(rank=r)))
    norm_block(place.second)
    norm_block(place.across)
    links.keep(tokens_v, all_tokens)
    links.keep(attn_v, attn_in)
    deal_up.arrive()
    chain_qkv.up.leave()
    chain_qkv.down.leave()
    chain_out.step(1)
    chain_up = Chain(place, links, up_slot(shard), up_slot)
    chain_qkv.step(3)
    chain_out.step(2)
    chain_down = Chain(place, links, w_down.at[:, low_half], down_slot)
    chain_qkv.finish()
    load_qkv = links.keep(all_qkv, qkv_v)
    load_qkv.arrive()

    def project(r, carry):
        rows = pl.ds(pl.multiple_of(r * tok_rows, tok_rows), tok_rows)
        for part in range(3):
            cut = slice(part * head_cols, (part + 1) * head_cols)
            weight = qkv_v[:, :, :, cut].reshape(model_width, head_cols)
            value = jnp.dot(attn_v[r], weight, preferred_element_type=jnp.float32)
            if part < 2:
                turned = []
                for h in range(heads):
                    head = value[:, h * HEAD_DIM : (h + 1) * HEAD_DIM]
                    turned.append(turn_half(head, cosine[rows], sine[rows]))
                value = jnp.concatenate(turned, axis=1)
                if part == 0:
                    value = value * HEAD_DIM ** (-0.5)
            rot_v[r, :, cut] = value.astype(jnp.bfloat16)
        return carry

    lax.fori_loop(0, ranks, project, 0)
    links.keep(rot_v, qkv_rot)
    chain_out.step(3)
    chain_up.step(1)
    chain_out.finish()
    load_out = links.keep(all_out, out_v)

    def attend_block(r):
        def head(h, carry):
            def part(i):
                return pl.ds(pl.multiple_of(i * head_cols + h * HEAD_DIM, HEAD_DIM), HEAD_DIM)

            for t in range(ranks):

                @pl.when(r == t)
                def with_keys(seen=t + 1):
                    keys = rot_v[:seen, :, part(1)].reshape(-1, HEAD_DIM)
                    scores = back_product(rot_v[r, :, part(0)], keys)
                    row = lax.broadcasted_iota(jnp.int32, scores.shape, 0) + r * tok_rows
                    column = lax.broadcasted_iota(jnp.int32, scores.shape, 1)
                    scores = jnp.where(row >= column, scores, masked_score)
                    raised = jnp.exp(scores - jnp.max(scores, axis=-1, keepdims=True))
                    scale = 1.0 / jnp.sum(raised, axis=-1, keepdims=True)
                    probs = (raised * scale).astype(jnp.bfloat16)
                    mixed = product(probs, rot_v[:seen, :, part(2)].reshape(-1, HEAD_DIM))
                    mixed_v[r, :, part(0)] = mixed.astype(jnp.bfloat16)

            return carry

        lax.fori_loop(0, heads, head, 0)

    def project_block(r):
        weight = out_v[...].reshape(head_cols, model_width)
        partial[r] = product(mixed_v[r], weight).astype(jnp.bfloat16)

    scatter = PlaneScatter(place, links, partial, landing, passing)
    attend_block(place.across)
    load_out.arrive()
    project_block(place.across)
    scatter.send_far()
    attend_block(place.first)
    project_block(place.first)
    scatter.send_near()
    chain_down.step(1)
    attend_block(place.second)
    project_block(place.second)
    scatter.relay()
    chain_up.step(2)
    attend_block(rank)
    project_block(rank)
    chain_down.step(2)
    links.keep(mixed_v, mixed_low)
    scatter.settle()

    def second_norm(cut):
        value = scatter.total(cut) + tokens_v[rank, cut].astype(jnp.float32)
        hidden_v[cut] = value
        value, unused = normed(value)
        ffn_v[cut] = (value * gains[2:3] + gains[3:4]).astype(jnp.bfloat16)

    in_rows(tok_rows, 64, second_norm)
    gather = PlaneGather(place, links, ffn_v, all_ffn_in, 4)
    links.keep(hidden_v, hidden)
    chain_up.step(3)
    gather.relay(0)
    gather.relay(1)
    chain_down.step(3)
    gather.relay(2)
    gather.relay(3)
    chain_up.finish()
    gather.finish()
    chain_down.finish()
    for message in dealt:
        message.arrive()
    links.drain()


def middle_kernel(
    chips,
    all_ffn_in,
    incoming,
    next_sum,
    w_up,
    down_low,
    w_down,
    hidden,
    cotangent_sum,
    gains,
    grad_hidden,
    sums,
    sum_down,
    sum_up_low,
    share_up,
    all_branch,
    terms,
    own_term,
    extra_in,
    ffn_v,
    csum_v,
    up_v,
    down_v,
    gated_v,
    grad_v,
    part_down,
    other_down,
    land_down,
    other_up,
    land_up,
    terms_v,
    stop,
    stop_more,
    branch,
    grad_hidden_v,
    sum_down_v,
    partial,
    landing,
    passing,
    send,
    recv,
    near,
):
    place = Place(chips)
    links = Links(send, recv, near)
    rank = place.rank
    ranks, tok_rows, model_width = ffn_v.shape
    ff_cols = up_v.shape[-1]
    half = ff_cols // 2
    load_up = links.keep(w_up, up_v)
    order = (place.across, place.first, place.second, rank)
    load_ffn = [links.keep(all_ffn_in.at[t], ffn_v.at[t]) for t in order]
    wide = model_width // 2
    columns = (pl.ds(0, wide), pl.ds(wide, wide))
    own_down = w_down.at[:, columns[1]]
    load_own = links.keep(own_down, down_v.at[place.shard, :, columns[1]])
    load_more = links.keep(next_sum, csum_v.at[1, rank], rank == 0)
    place.greet(plane=True, sibling=True, ring=True)
    chain_down = Chain(place, links, own_down, lambda f: down_v.at[f, :, columns[1]])
    detour = Detour(place, links, next_sum, csum_v.at[1, 3], stop, 3, 1, 0)
    dealt = []
    for r in (place.first, place.second):
        dealt.append(
            Message(links, next_sum, csum_v.at[1, rank], place.at(rank=r), r == 0, rank == 0)
        )
    slots = (0, jnp.where(rank == 0, 1, 0))
    sums[...] = jnp.zeros_like(sums)
    load_up.arrive()
    for copy in load_ffn:
        copy.arrive()
    load_down = links.keep(down_low, down_v.at[:, :, columns[0]])
    load_csum = links.keep(incoming, csum_v.at[0])
    scatter = PlaneScatter(place, links, partial, landing, passing)

    def widen(i):
        def one(t, carry):
            cut = slice(i * half, (i + 1) * half)
            weight = up_v[:, :, :, :, cut].reshape(model_width, half)
            pre = product(ffn_v[t], weight) + gains[5:6, cut]
            square = pre * pre
            tangent = jnp.tanh(0.7978845608028654 * pre * (1.0 + 0.044715 * square))
            gated_v[t, :, cut] = (0.5 * pre * (1.0 + tangent)).astype(jnp.bfloat16)
            slope = 0.5 * (1.0 + tangent) + 0.5 * pre * (1.0 - tangent * tangent) * (
                0.7978845608028654 * (1.0 + 3.0 * 0.044715 * square)
            )
            grad_v[t, :, cut] = slope.astype(jnp.bfloat16)
            return carry

        return one

    def high_tile(h):
        right = slice(h * wide, (h + 1) * wide)

        def one(t, carry):
            weight = down_v[4:, :, right].reshape(half, wide)
            value = product(gated_v[t, :, half:], weight)
            terms_v[1, t, :, right] = value.astype(jnp.bfloat16)
            return carry

        lax.fori_loop(0, ranks, one, 0)
        cut = columns[h]
        links.keep(terms_v.at[1, rank, :, cut], extra_in.at[:, cut], rank == 0)
        detour = Detour(
            place,
            links,
            terms_v.at[1, place.across, :, cut],
            extra_in.at[:, cut],
            stop_more.at[:, cut],
            0,
            2,
            3,
        )
        for r in (place.first, place.second):
            dealt_more.append(
                Message(
                    links,
                    terms_v.at[1, r, :, cut],
                    extra_in.at[:, cut],
                    place.at(rank=r),
                    rank == 0,
                    r == 0,
                )
            )
        return detour

    def low_tile(t, carry):
        low_term = product(gated_v[t, :, :half], down_v[:4].reshape(half, model_width))
        high_term = terms_v[1, t].astype(jnp.float32) * jnp.where(rank == 0, 0.0, 1.0)
        terms_v[0, t] = (low_term + high_term).astype(jnp.bfloat16)
        return carry

    def block(k):
        t = order[k]
        for i in range(2):
            cut = slice(i * half, (i + 1) * half)
            weight = down_v[4 * i : 4 * i + 4].reshape(half, model_width)
            grad = back_product(csum_v[slots[i], t], weight) * grad_v[t, :, cut].astype(jnp.float32)
            grad_v[t, :, cut] = grad.astype(jnp.bfloat16)
            sums[3:4, cut] += jnp.sum(grad, axis=0, keepdims=True)

        def back(i, carry):
            own = model_width // ranks
            value = back_product(grad_v[t], up_v[i].reshape(own, ff_cols))
            partial[t, :, pl.ds(pl.multiple_of(i * own, 128), own)] = value.astype(jnp.bfloat16)
            return carry

        lax.fori_loop(0, ranks, back, 0)

    dealt_more = []
    lax.fori_loop(0, ranks, widen(1), 0)
    detour.relay()
    chain_down.step(1)
    load_down.arrive()
    detour_low = high_tile(0)
    chain_down.step(2)
    lax.fori_loop(0, ranks // 2, widen(0), 0)
    chain_down.step(3)
    lax.fori_loop(ranks // 2, ranks, widen(0), 0)
    chain_down.finish()
    load_own.arrive()
    detour_high = high_tile(1)
    detour_low.relay()
    load_csum.arrive()
    load_more.arrive()
    for message in dealt + [detour]:
        message.arrive()

    def down_tiles(h):
        width = model_width // 2
        right = slice(h * width, (h + 1) * width)

        def down_tile(i, carry):
            rows = ff_cols // ranks
            left = gated_v[:, :, pl.ds(pl.multiple_of(i * rows, 128), rows)].reshape(-1, rows)
            slot = jnp.where(i < 2, slots[0], slots[1])
            value = gram_product(left, csum_v[slot, :, :, right].reshape(-1, width))
            part_down[h, i] = value.astype(jnp.bfloat16).reshape(part_down.shape[2:])
            return carry

        lax.fori_loop(0, ranks, down_tile, 0)
        here = pl.ds(h, 1)
        return Beside(place, links, part_down.at[here], other_down.at[here])

    def along_half(beside, h):
        beside.add()
        share = part_down.at[pl.ds(h, 1)]
        return Along(
            place, links, lambda there: share.at[:, there, place.core], land_down.at[h]
        )

    beside_low = down_tiles(0)
    block(0)
    scatter.send_far()
    along_low = along_half(beside_low, 0)
    block(1)
    scatter.send_near()
    beside_high = down_tiles(1)
    block(2)
    scatter.relay()
    along_high = along_half(beside_high, 1)
    detour_high.relay()
    along_low.relay()
    block(3)

    def up_tile(i, carry):
        rows = model_width // ranks
        left = ffn_v[:, :, pl.ds(pl.multiple_of(i * rows, 128), rows)].reshape(-1, rows)
        value = gram_product(left, grad_v[...].reshape(-1, ff_cols))
        up_v[i] = value.astype(jnp.bfloat16).reshape(up_v.shape[1:])
        return carry

    lax.fori_loop(0, ranks, up_tile, 0)
    beside_up = Beside(place, links, up_v, other_up)
    along_high.relay()

    beside_up.add()
    first_cols = sum_up_low.shape[2]
    share_low = up_v.at[:, :, :, :, pl.ds(0, first_cols)]
    along_up = Along(place, links, lambda there: share_low.at[:, there, place.core], land_up)
    rest = pl.ds(first_cols, ff_cols - first_cols)
    links.keep(up_v.at[:, :, place.core, :, rest], share_up)
    scatter.settle()

    def norm_back(cut):
        value, inverse = normed(hidden[cut])
        grad = scatter.total(cut)
        sums[0:1] += jnp.sum(grad * value, axis=0, keepdims=True)
        sums[1:2] += jnp.sum(grad, axis=0, keepdims=True)
        sums[2:3] += jnp.sum(cotangent_sum[cut], axis=0, keepdims=True)
        total = cotangent_sum[cut] + norm_backward(grad, value, inverse, gains[2:3])
        grad_hidden_v[cut] = total
        branch[cut] = total.astype(jnp.bfloat16)

    in_rows(tok_rows, 64, norm_back)
    gather = PlaneGather(place, links, branch, all_branch, 4)
    links.keep(grad_hidden_v, grad_hidden)
    lax.fori_loop(0, ranks, low_tile, 0)
    links.keep(terms_v.at[0], terms)
    links.keep(terms_v.at[0, rank], own_term)
    gather.relay(0)
    gather.relay(1)
    along_up.relay()
    gather.relay(2)
    gather.relay(3)
    for h, along in enumerate((along_low, along_high)):
        mine = part_down[h : h + 1, place.z, place.core]
        sum_down_v[:, h * wide : (h + 1) * wide] = along.total(mine)[0]
    links.keep(sum_down_v, sum_down)
    mine = up_v[:, place.z, place.core, :, :first_cols]
    sum_up_low[...] = along_up.total(mine).astype(jnp.bfloat16)
    gather.finish()
    for message in dealt_more + [detour_low, detour_high]:
        message.arrive()
    links.drain()


def last_kernel(
    chips,
    all_branch,
    sum_up_low,
    share_up,
    terms,
    qkv_rot,
    mixed_low,
    w_out,
    w_qkv,
    attn_in,
    all_tokens,
    grad_hidden,
    gains,
    sums,
    comb,
    mask,
    cosine,
    sine,
    term_in,
    grad_tokens,
    sum_out,
    land_sum_up,
    land_sum_qkv,
    sum_small,
    branch_v,
    rot_v,
    mixed_v,
    grad_mixed_v,
    out_v,
    qkv_v,
    attn_v,
    tokens_v,
    grad_v,
    key_sum,
    value_sum,
    partial,
    landing,
    passing,
    turn_up,
    mine_up,
    far_up,
    land_up,
    part_out,
    other_out,
    land_out,
    part_qkv,
    other_qkv,
    land_qkv,
    turn_qkv,
    part_small,
    other_small,
    land_small,
    turn_small,
    land_sums,
    more_sums,
    send,
    recv,
    near,
):
    place = Place(chips)
    links = Links(send, recv, near)
    rank, z = place.rank, place.z
    ranks, tok_rows, model_width = branch_v.shape
    head_cols = mixed_v.shape[2]
    heads = head_cols // HEAD_DIM
    load_branch = links.keep(all_branch, branch_v)
    load_out = links.keep(w_out, out_v)
    load_mixed = links.keep(mixed_low, mixed_v)
    load_rot = links.keep(qkv_rot, rot_v)
    other_end = jnp.where(z < 2, chips - 1, 0)
    piece = 3 * HEAD_DIM
    load_far = links.keep(share_up.at[:, other_end], far_up)
    first_cols = sum_up_low.shape[2]
    load_low = links.keep(sum_up_low, turn_up.at[:, :, pl.ds(0, first_cols)])
    place.greet(plane=True, sibling=True, ring=True)
    along_up = Along(place, links, lambda there: share_up.at[:, there], land_up, far_up)
    dealt = []
    for r in (place.first, place.second, place.across):
        dealt.append(Message(links, terms.at[r], term_in.at[rank], place.at(rank=r)))
    load_out.arrive()

    def mix_back(t):
        weight = out_v[...].reshape(head_cols, model_width)
        grad_mixed_v[t] = back_product(branch_v[t], weight).astype(jnp.bfloat16)

    load_branch.arrive()
    load_attn = links.keep(attn_in, attn_v)
    load_qkv = [
        links.keep(
            w_qkv.at[:, :, :, pl.ds(i * head_cols + h * HEAD_DIM, HEAD_DIM)],
            qkv_v.at[:, :, :, pl.ds(h * piece + i * HEAD_DIM, HEAD_DIM)],
        )
        for h in range(heads)
        for i in range(3)
    ]
    load_tokens = links.keep(all_tokens, tokens_v)
    load_up = links.keep(share_up.at[:, z], mine_up)
    for r in range(ranks):
        mix_back(r)
    load_mixed.arrive()
    value = gram_product(
        mixed_v[...].reshape(-1, head_cols), branch_v[...].reshape(-1, model_width)
    )
    part_out[0] = value.astype(jnp.bfloat16).reshape(part_out.shape[1:])
    beside_out = Beside(place, links, part_out, other_out)
    load_rot.arrive()

    def head(h):
        def part(i):
            return slice(i * head_cols + h * HEAD_DIM, i * head_cols + (h + 1) * HEAD_DIM)

        def place_of(i):
            return slice(h * piece + i * HEAD_DIM, h * piece + (i + 1) * HEAD_DIM)

        for t in range(ranks - 1, -1, -1):
            count = t + 1
            keys = rot_v[:count, :, part(1)].reshape(-1, HEAD_DIM)
            values = rot_v[:count, :, part(2)].reshape(-1, HEAD_DIM)
            queries = rot_v[t, :, part(0)]
            grad_mixed = grad_mixed_v[t, :, part(0)]
            scores = back_product(queries, keys)
            row = lax.broadcasted_iota(jnp.int32, scores.shape, 0) + t * tok_rows
            column = lax.broadcasted_iota(jnp.int32, scores.shape, 1)
            scores = jnp.where(row >= column, scores, masked_score)
            raised = jnp.exp(scores - jnp.max(scores, axis=-1, keepdims=True))
            probs = raised * (1.0 / jnp.sum(raised, axis=-1, keepdims=True))
            delta = jnp.sum(
                grad_mixed.astype(jnp.float32) * mixed_v[t, :, part(0)].astype(jnp.float32),
                axis=-1,
                keepdims=True,
            )
            grad_scores = (probs * (back_product(grad_mixed, values) - delta)).astype(jnp.bfloat16)
            rows = pl.ds(t * tok_rows, tok_rows)
            grad_query = product(grad_scores, keys)
            grad_query = turn_half(grad_query, cosine[rows], -sine[rows]) * HEAD_DIM ** (-0.5)
            grad_v[t, :, place_of(0)] = grad_query.astype(jnp.bfloat16)
            grad_key = gram_product(grad_scores, queries)
            grad_value = gram_product(probs.astype(jnp.bfloat16), grad_mixed)
            seen = count * tok_rows
            if t == ranks - 1:
                key_sum[...] = grad_key
                value_sum[...] = grad_value
            else:
                key_sum[:seen] += grad_key
                value_sum[:seen] += grad_value
        grad_key = turn_half(key_sum[...], cosine[...], -sine[...]).astype(jnp.bfloat16)
        grad_v[:, :, place_of(1)] = grad_key.reshape(ranks, tok_rows, HEAD_DIM)
        grad_value = value_sum[...].astype(jnp.bfloat16)
        grad_v[:, :, place_of(2)] = grad_value.reshape(ranks, tok_rows, HEAD_DIM)

        def qkv_tile(i, carry):
            rows = model_width // ranks
            left = attn_v[:, :, pl.ds(pl.multiple_of(i * rows, 128), rows)].reshape(-1, rows)
            right = grad_v[:, :, h * piece : (h + 1) * piece].reshape(-1, piece)
            value = gram_product(left, right)
            part_qkv[h, i] = value.astype(jnp.bfloat16).reshape(part_qkv.shape[2:])
            return carry

        if h == 0:
            load_attn.arrive()
        lax.fori_loop(0, ranks, qkv_tile, 0)
        return Beside(place, links, part_qkv.at[h], other_qkv.at[h])

    def along_head(h):
        return Along(
            place, links, lambda there: part_qkv.at[h, :, there, place.core], land_qkv.at[h]
        )

    beside_qkv = [head(0)]
    load_far.arrive()
    along_up.relay()
    beside_out.add()
    along_out = Along(place, links, lambda there: part_out.at[:, there, place.core], land_out)
    along_qkv = []
    for h in range(1, heads):
        beside_qkv.append(head(h))
        beside_qkv[h - 1].add()
        along_qkv.append(along_head(h - 1))
    along_out.relay()
    for copy in load_qkv:
        copy.arrive()
    load_tokens.arrive()
    scatter = PlaneScatter(place, links, partial, landing, passing)
    more_sums[...] = jnp.zeros_like(more_sums)

    def attn_back(t):
        def tile(i, carry):
            own = model_width // ranks
            value = back_product(grad_v[t], qkv_v[i].reshape(own, 3 * head_cols))
            partial[t, :, pl.ds(pl.multiple_of(i * own, 128), own)] = value.astype(jnp.bfloat16)
            return carry

        lax.fori_loop(0, ranks, tile, 0)

        def count(cut):
            value, unused = normed(tokens_v[t, cut].astype(jnp.float32))
            grad = partial[t, cut].astype(jnp.float32)
            more_sums[0:1] += jnp.sum(grad * value, axis=0, keepdims=True)
            more_sums[1:2] += jnp.sum(grad, axis=0, keepdims=True)

        return count

    count_across = attn_back(place.across)
    scatter.send_far()
    count_first = attn_back(place.first)
    scatter.send_near()
    beside_qkv[heads - 1].add()
    along_qkv.append(along_head(heads - 1))
    along_qkv[0].relay()
    count_second = attn_back(place.second)
    scatter.relay()
    for h in range(1, heads - 1):
        along_qkv[h].relay()
    count_own = attn_back(rank)
    for count in (count_across, count_first, count_second, count_own):
        in_rows(tok_rows, 64, count)

    def pieces(row):
        spread = (row * mask[...]).astype(jnp.float32)
        return lax.dot_general(
            spread,
            comb[...].astype(jnp.float32),
            (((1,), (1,)), ((), ())),
            precision=lax.Precision.HIGHEST,
            preferred_element_type=jnp.float32,
        )

    part_small[...] = jnp.zeros_like(part_small)
    rows = (more_sums[0:1], more_sums[1:2], sums[0:1], sums[1:2], sums[2:3])
    for k, row in enumerate(rows):
        part_small[:, :, :, k] = pieces(row).reshape(ranks, chips, 2, 128)
    part_small[rank, :, :, 5:9] = pieces(sums[3:4]).reshape(chips, 2, 4, 128)
    beside_small = Beside(place, links, part_small, other_small)
    along_qkv[heads - 1].relay()
    load_up.arrive()
    load_low.arrive()
    turn_up[:, :, first_cols:] = along_up.total(mine_up[...]).astype(jnp.bfloat16)
    deal_up = Deal(place, links, [(lambda r: turn_up.at[r], land_sum_up.at[rank])])
    beside_small.add()
    along_small = Along(place, links, lambda there: part_small.at[:, there, place.core], land_small)
    sum_out[...] = along_out.total(part_out[:, z, place.core])[0]
    along_small.relay()
    deal_qkv = []

    def settle_head(h):
        total = along_qkv[h].total(part_qkv[h, :, z, place.core])
        turn_qkv[h] = total.astype(jnp.bfloat16)
        deal_qkv.append(
            Deal(place, links, [(lambda r: turn_qkv.at[h, r], land_sum_qkv.at[h, rank])])
        )

    for h in range(heads - 1):
        settle_head(h)
    scatter.settle()

    def norm_back(cut):
        value, inverse = normed(tokens_v[rank, cut].astype(jnp.float32))
        grad = norm_backward(scatter.total(cut), value, inverse, gains[0:1])
        grad_tokens[cut] = (grad_hidden[cut] + grad).astype(jnp.bfloat16)

    in_rows(tok_rows, 64, norm_back)
    turn_small[...] = along_small.total(part_small[:, z, place.core])
    deal_small = Deal(place, links, [(lambda r: turn_small.at[r], land_sums.at[rank])])
    settle_head(heads - 1)
    for message in dealt:
        message.arrive()
    deal_up.arrive()
    deal_small.arrive()
    sum_small[...] = land_sums[0] + land_sums[1] + land_sums[2] + land_sums[3]
    for deal in deal_qkv:
        deal.arrive()
    links.drain()


def closing_kernel(*refs):
    own_term, ins, outs = refs[0], refs[1:10], refs[10:23]
    held, act_v, near, leaving = refs[23:32], refs[32], refs[33], refs[34]
    rank = lax.axis_index("dp")
    hidden, gains, term_in, extra_in, grad_in, out_in = held[:6]
    up_in, qkv_in, small_in = held[6:]
    activations, grad_tokens, sum_query, sum_key, sum_value, sum_out, sum_up = outs[:7]
    steps = near.shape[0] - 1
    rows = hidden.shape[0] // steps
    cuts = [pl.ds(k * rows, rows) for k in range(steps)]
    copies = []
    for k, cut in enumerate(cuts):
        batch = []
        for i in (0, 3, 4):
            copy = pltpu.make_async_copy(ins[i].at[cut], held[i].at[cut], near.at[k, i])
            copy.start()
            batch.append(copy)
        for r in range(term_in.shape[0]):
            here, sem = term_in.at[r, cut], near.at[k, 9 + r]
            there = pltpu.make_async_copy(ins[2].at[r, cut], here, sem)
            own = pltpu.make_async_copy(own_term.at[cut], here, sem)
            pl.when(rank != r)(there.start)
            pl.when(rank == r)(own.start)
            batch.append(there)
        copies.append(batch)
    rest = []
    for i in (1, 5, 6, 7, 8):
        rest.append(pltpu.make_async_copy(ins[i], held[i], near.at[steps, i]))
        rest[-1].start()
    rest[0].wait()
    left = []
    for k, cut in enumerate(cuts):
        for copy in copies[k]:
            copy.wait()
        total = hidden[cut] + gains[4:5] + term_in[0, cut].astype(jnp.float32)
        act_v[0, cut] = total.astype(jnp.bfloat16)
        total = total + extra_in[cut].astype(jnp.float32)
        act_v[1, cut] = total.astype(jnp.bfloat16)
        total = total + term_in[1, cut].astype(jnp.float32)
        act_v[2, cut] = total.astype(jnp.bfloat16)
        total = total + term_in[2, cut].astype(jnp.float32) + term_in[3, cut].astype(jnp.float32)
        act_v[3, cut] = total.astype(jnp.bfloat16)
        left.append(
            pltpu.make_async_copy(act_v.at[:, cut], activations.at[:, cut], leaving.at[k, 0])
        )
        left[-1].start()
        left.append(pltpu.make_async_copy(grad_in.at[cut], grad_tokens.at[cut], leaving.at[k, 1]))
        left[-1].start()
    for copy in rest[1:]:
        copy.wait()
    sum_out[...] = out_in[...]
    ranks, own, ff_cols = up_in.shape
    heads, head_cols = qkv_in.shape[0], qkv_in.shape[0] * HEAD_DIM
    for r in range(ranks):
        sum_up[:, r * ff_cols : (r + 1) * ff_cols] = up_in[r].astype(jnp.float32)
        for i, total in enumerate((sum_query, sum_key, sum_value)):
            for h in range(heads):
                start = r * head_cols + h * HEAD_DIM
                value = qkv_in[h, r, :, i * HEAD_DIM : (i + 1) * HEAD_DIM]
                total[:, start : start + HEAD_DIM] = value.astype(jnp.float32)
    small_sums = outs[7:]
    for i in range(5):
        small_sums[i][...] = small_in[i : i + 1, :own]
    small_sums[5][...] = jnp.concatenate([small_in[5 + q : 6 + q, :own] for q in range(4)], axis=1)
    for copy in left:
        copy.wait()


ANY = pl.BlockSpec(memory_space=pl.ANY)
ON_CORE = pl.BlockSpec(memory_space=pltpu.VMEM)


def connected(kernel, number, outs, out_specs, in_specs, scratch, operands):
    return pl.pallas_call(
        kernel,
        out_shape=outs,
        in_specs=in_specs,
        out_specs=out_specs,
        scratch_shapes=scratch + LINK_SCRATCH,
        compiler_params=pltpu.CompilerParams(
            collective_id=number, has_side_effects=True, vmem_limit_bytes=63 * 2**20
        ),
    )(*operands)


def array(shape, dtype=jnp.bfloat16):
    return jax.ShapeDtypeStruct(shape, dtype)


def turning(count):
    half_size = HEAD_DIM // 2
    inverse = np.exp(np.arange(half_size, dtype=np.float32) * np.float32(-math.log(10000.0) / half_size))
    angles = np.arange(count, dtype=np.float32)[:, None] * inverse.astype(np.float32)[None, :]
    cosine, sine = np.cos(angles), np.sin(angles)
    cosine = np.concatenate([cosine, cosine], axis=1)
    return jnp.asarray(cosine), jnp.asarray(np.concatenate([-sine, sine], axis=1))


def local_split(ranks, shards, *arguments):
    chips = shards // 2
    (
        tokens,
        cotangent,
        norm1_gain,
        norm1_bias,
        query_weight,
        key_weight,
        value_weight,
        out_weight,
        norm2_gain,
        norm2_bias,
        up_weight,
        up_bias,
        down_weight,
        down_bias,
    ) = arguments
    model_width = tokens.shape[2]
    tok_rows = tokens.shape[1]
    seq_len = tok_rows * ranks
    own = query_weight.shape[0]
    heads = HEADS // ranks
    head_cols = heads * HEAD_DIM
    ff_cols = FF // ranks
    scaling = HEAD_DIM ** (-0.5)
    rank = lax.axis_index("dp")

    column = np.arange(model_width)
    comb = jnp.asarray(column[None, :] % own == np.arange(128)[:, None], jnp.bfloat16)
    mask = jnp.asarray(column[None, :] // own == np.arange(ranks * shards)[:, None], jnp.float32)
    cosine, sine = turning(seq_len)
    own_tokens = tokens.reshape(tok_rows, model_width)
    blocks_low = array((ranks, tok_rows, model_width))
    down_rows = down_weight.shape[0]
    first_cols = ff_cols * 5 // 12
    vmem = pltpu.VMEM
    low = jnp.bfloat16
    f32 = jnp.float32
    (
        all_tokens,
        attn_in,
        qkv_rot,
        mixed_low,
        hidden,
        ffn_in,
        gains,
        incoming,
        cotangent_sum,
        next_sum,
        w_qkv,
        w_out,
        w_up,
        w_down,
    ) = connected(
        functools.partial(forward_kernel, chips),
        1,
        (
            blocks_low,
            blocks_low,
            array((ranks, tok_rows, 3 * head_cols)),
            array((ranks, tok_rows, head_cols)),
            array((tok_rows, model_width), jnp.float32),
            blocks_low,
            array((8, model_width), jnp.float32),
            blocks_low,
            array((tok_rows, model_width), f32),
            array((tok_rows, model_width)),
            array((ranks, shards, own, 3 * head_cols)),
            array((shards, own, model_width)),
            array((ranks, shards, own, ff_cols)),
            array((shards, down_rows, model_width // 2)),
        ),
        [ANY] * 6 + [ON_CORE] + [ANY] * 7,
        [ANY] * 2 + [ON_CORE] * 16,
        [
            vmem((tok_rows, model_width), f32),
            vmem((tok_rows, model_width), f32),
            vmem((GRAN, tok_rows, model_width), low),
            vmem((GRAN, tok_rows, model_width), low),
            vmem((16, 128), low),
            vmem((ranks, tok_rows, model_width), jnp.bfloat16),
            vmem((ranks, tok_rows, model_width), jnp.bfloat16),
            vmem((ranks, tok_rows, 3 * head_cols), jnp.bfloat16),
            vmem((ranks, tok_rows, head_cols), jnp.bfloat16),
            vmem((ranks, shards, own, 3 * head_cols), jnp.bfloat16),
            vmem((shards, own, model_width), jnp.bfloat16),
            vmem((ranks, tok_rows, model_width), jnp.bfloat16),
            vmem((3, tok_rows, model_width), jnp.bfloat16),
            vmem((tok_rows, model_width), jnp.bfloat16),
            vmem((tok_rows, model_width), jnp.bfloat16),
            vmem((ranks, shards, 16, 128), jnp.bfloat16),
        ],
        (
            own_tokens,
            cotangent.reshape(GRAN, tok_rows, model_width),
            norm1_gain.reshape(1, own),
            norm1_bias.reshape(1, own),
            norm2_gain.reshape(1, own),
            norm2_bias.reshape(1, own),
            down_bias.reshape(1, own),
            up_bias.reshape(1, -1),
            query_weight,
            key_weight,
            value_weight,
            out_weight,
            up_weight,
            down_weight,
            comb,
            mask,
            cosine,
            sine,
        ),
    )
    (
        grad_hidden,
        sums,
        sum_down,
        sum_up_low,
        share_up,
        all_branch,
        terms,
        own_term,
        extra_in,
    ) = connected(
        functools.partial(middle_kernel, chips),
        2,
        (
            array((tok_rows, model_width), f32),
            array((8, model_width), f32),
            array((down_rows, model_width), f32),
            array((ranks, own, first_cols)),
            array((ranks, chips, own, ff_cols - first_cols)),
            blocks_low,
            blocks_low,
            array((tok_rows, model_width)),
            array((tok_rows, model_width)),
        ),
        [ANY, ON_CORE, ANY, ON_CORE] + [ANY] * 5,
        [ANY] * 6 + [ON_CORE] * 3,
        [
            vmem((ranks, tok_rows, model_width), low),
            vmem((2, ranks, tok_rows, model_width), low),
            vmem((ranks, chips, 2, own, ff_cols), low),
            vmem((shards, down_rows, model_width), low),
            vmem((ranks, tok_rows, ff_cols), low),
            vmem((ranks, tok_rows, ff_cols), low),
            vmem((2, chips, 2, down_rows, model_width // 2), low),
            vmem((2, chips, down_rows, model_width // 2), low),
            vmem((2, 4, 1, down_rows, model_width // 2), low),
            vmem((ranks, chips, own, ff_cols), low),
            vmem((4, ranks, own, first_cols), low),
            vmem((2, ranks, tok_rows, model_width), low),
            vmem((tok_rows, model_width), low),
            vmem((tok_rows, model_width), low),
            vmem((tok_rows, model_width), low),
            vmem((tok_rows, model_width), f32),
            vmem((down_rows, model_width), f32),
            vmem((ranks, tok_rows, model_width), low),
            vmem((3, tok_rows, model_width), low),
            vmem((tok_rows, model_width), low),
        ],
        (
            ffn_in,
            incoming,
            next_sum,
            w_up.reshape(ranks, chips, 2, own, ff_cols),
            w_down,
            down_weight,
            hidden,
            cotangent_sum,
            gains,
        ),
    )
    term_in, grad_inputs, sum_out, sum_up, sum_qkv, small_sums = connected(
        functools.partial(last_kernel, chips),
        3,
        (
            blocks_low,
            array((tok_rows, model_width)),
            array((own, model_width), f32),
            array((ranks, own, ff_cols)),
            array((heads, ranks, own, 3 * HEAD_DIM)),
            array((16, 128), f32),
        ),
        [ANY] + [ON_CORE] * 2 + [ANY] * 2 + [ON_CORE],
        [ANY] * 10 + [ON_CORE] * 7,
        [
            vmem((ranks, tok_rows, model_width), low),
            vmem((ranks, tok_rows, 3 * head_cols), low),
            vmem((ranks, tok_rows, head_cols), low),
            vmem((ranks, tok_rows, head_cols), low),
            vmem((shards, own, model_width), low),
            vmem((ranks, shards, own, 3 * head_cols), low),
            vmem((ranks, tok_rows, model_width), low),
            vmem((ranks, tok_rows, model_width), low),
            vmem((ranks, tok_rows, 3 * head_cols), low),
            vmem((seq_len, HEAD_DIM), f32),
            vmem((seq_len, HEAD_DIM), f32),
            vmem((ranks, tok_rows, model_width), low),
            vmem((3, tok_rows, model_width), low),
            vmem((tok_rows, model_width), low),
            vmem((ranks, own, ff_cols), low),
            vmem((ranks, own, ff_cols - first_cols), low),
            vmem((ranks, own, ff_cols - first_cols), low),
            vmem((4, ranks, own, ff_cols - first_cols), low),
            vmem((1, chips, 2, own, model_width), low),
            vmem((1, chips, own, model_width), low),
            vmem((4, 1, own, model_width), low),
            vmem((heads, ranks, chips, 2, own, 3 * HEAD_DIM), low),
            vmem((heads, ranks, chips, own, 3 * HEAD_DIM), low),
            vmem((heads, 4, ranks, own, 3 * HEAD_DIM), low),
            vmem((heads, ranks, own, 3 * HEAD_DIM), low),
            vmem((ranks, chips, 2, 16, 128), f32),
            vmem((ranks, chips, 16, 128), f32),
            vmem((4, ranks, 16, 128), f32),
            vmem((ranks, 16, 128), f32),
            vmem((ranks, 16, 128), f32),
            vmem((8, model_width), f32),
        ],
        (
            all_branch,
            sum_up_low,
            share_up,
            terms,
            qkv_rot,
            mixed_low,
            w_out,
            w_qkv,
            attn_in,
            all_tokens,
            grad_hidden,
            gains,
            sums,
            comb,
            mask,
            cosine,
            sine,
        ),
    )
    (
        activations,
        grad_tokens,
        sum_query,
        sum_key,
        sum_value,
        sum_out,
        sum_up,
        *gain_sums,
    ) = pl.pallas_call(
        closing_kernel,
        out_shape=(
            array((GRAN, tok_rows, model_width)),
            array((tok_rows, model_width)),
            *[array((own, model_width), f32) for i in range(4)],
            array((own, FF), f32),
            *[array((1, own), f32) for i in range(5)],
            array((1, down_rows), f32),
        ),
        in_specs=[ANY] * 10,
        out_specs=[ANY] * 2 + [ON_CORE] * 11,
        scratch_shapes=[
            vmem((tok_rows, model_width), f32),
            vmem((8, model_width), f32),
            vmem((ranks, tok_rows, model_width), low),
            vmem((tok_rows, model_width), low),
            vmem((tok_rows, model_width), low),
            vmem((own, model_width), f32),
            vmem((ranks, own, ff_cols), low),
            vmem((heads, ranks, own, 3 * HEAD_DIM), low),
            vmem((16, 128), f32),
            vmem((GRAN, tok_rows, model_width), low),
            pltpu.SemaphoreType.DMA((5, 13)),
            pltpu.SemaphoreType.DMA((4, 2)),
        ],
        compiler_params=pltpu.CompilerParams(vmem_limit_bytes=60 * 2**20),
    )(
        own_term,
        hidden,
        gains,
        term_in,
        extra_in,
        grad_inputs,
        sum_out,
        sum_up,
        sum_qkv,
        small_sums,
    )
    gain_sums = [v.reshape(-1) for v in gain_sums]
    return (
        activations.reshape(GRAN, 1, tok_rows, model_width),
        grad_tokens.reshape(1, tok_rows, model_width),
        gain_sums[0],
        gain_sums[1],
        sum_query,
        sum_key,
        sum_value,
        sum_out,
        gain_sums[2],
        gain_sums[3],
        sum_up,
        gain_sums[5],
        sum_down,
        gain_sums[4],
    )


def solution(mesh):
    placed = (
        P("fsdp", "dp", None),
        P(None, "fsdp", "dp", None),
        P(("dp", "fsdp")),
        P(("dp", "fsdp")),
        P(("dp", "fsdp"), None),
        P(("dp", "fsdp"), None),
        P(("dp", "fsdp"), None),
        P(("dp", "fsdp"), None),
        P(("dp", "fsdp")),
        P(("dp", "fsdp")),
        P(("dp", "fsdp"), None),
        P(("dp", "fsdp")),
        P(("dp", "fsdp"), None),
        P(("dp", "fsdp")),
    )
    ranks, shards = mesh.shape["dp"], mesh.shape["fsdp"]
    local = local_gathered
    if ranks == 4 and shards == 8:
        local = functools.partial(local_split, ranks, shards)
    return jax.shard_map(
        local,
        mesh=mesh,
        in_specs=placed,
        out_specs=(
            P(None, "fsdp", "dp", None),
            P("fsdp", "dp", None),
            P(("dp", "fsdp")),
            P(("dp", "fsdp")),
            P(("dp", "fsdp"), None),
            P(("dp", "fsdp"), None),
            P(("dp", "fsdp"), None),
            P(("dp", "fsdp"), None),
            P(("dp", "fsdp")),
            P(("dp", "fsdp")),
            P(("dp", "fsdp"), None),
            P(("dp", "fsdp")),
            P(("dp", "fsdp"), None),
            P(("dp", "fsdp")),
        ),
        check_vma=False,
    )
```

```python
import functools
import math

import jax
import jax.numpy as jnp
import numpy as np
from jax import lax
from jax.experimental import pallas as pl
from jax.experimental.pallas import tpu as pltpu
from jax.sharding import PartitionSpec as P

HEADS = 12
HEAD_DIM = 128
FF = 6144
GRAN = 4


epsilon = 1e-05
masked_score = -1e30


def product(left, right):
    return jnp.dot(left, right, preferred_element_type=jnp.float32)


def gram_product(left, right):
    return lax.dot_general(
        left, right, (((0,), (0,)), ((), ())), preferred_element_type=jnp.float32
    )


def back_product(left, right):
    return lax.dot_general(
        left, right, (((1,), (1,)), ((), ())), preferred_element_type=jnp.float32
    )


def norm_parts(values):
    centred = values - jnp.mean(values, axis=-1, keepdims=True)
    inverse = lax.rsqrt(jnp.mean(centred * centred, axis=-1, keepdims=True) + epsilon)
    return (centred * inverse, inverse)


def norm_backward(grad_normed, normed, inverse, gain):
    scaled = grad_normed * gain
    return inverse * (
        scaled
        - jnp.mean(scaled, axis=-1, keepdims=True)
        - normed * jnp.mean(scaled * normed, axis=-1, keepdims=True)
    )


def gelu_value(values):
    return (
        0.5
        * values
        * (1.0 + jnp.tanh(0.7978845608028654 * (values + 0.044715 * values * values * values)))
    )


def gelu_grad(values):
    tangent = jnp.tanh(0.7978845608028654 * (values + 0.044715 * values * values * values))
    return 0.5 * (1.0 + tangent) + 0.5 * values * (1.0 - tangent * tangent) * 0.7978845608028654 * (
        1.0 + 3.0 * 0.044715 * values * values
    )


def rotary_tables(positions, half_size):
    ladder = jnp.arange(half_size).astype(jnp.float32)
    inverse = jnp.exp(ladder * (-math.log(10000.0) / half_size))
    angles = positions[:, None] * inverse[None, :]
    return (jnp.cos(angles)[:, None, :], jnp.sin(angles)[:, None, :])


def rotate(values, cosine, sine):
    half_size = values.shape[-1] // 2
    first = values[..., :half_size]
    second = values[..., half_size:]
    return jnp.concatenate(
        [first * cosine - second * sine, second * cosine + first * sine], axis=-1
    )


def block_scores(queries, positions, key_block, start_row):
    block_rows = key_block.shape[0]
    scores = jnp.einsum("qhd,khd->hqk", queries, key_block, preferred_element_type=jnp.float32)
    key_positions = start_row + jnp.arange(block_rows, dtype=jnp.int32)
    visible = positions[None, :, None] >= key_positions[None, None, :]
    return (jnp.where(visible, scores, masked_score), visible)


def key_blocking(keys_all, values_all, key_offset):
    seq_len = keys_all.shape[0]
    block_rows = min(512, seq_len)
    block_count = seq_len // block_rows
    key_blocks = keys_all.reshape(block_count, block_rows, HEADS, HEAD_DIM)
    value_blocks = values_all.reshape(block_count, block_rows, HEADS, HEAD_DIM)
    starts = key_offset + jnp.arange(block_count, dtype=jnp.int32) * block_rows
    return (key_blocks, value_blocks, starts)


def attend(queries, keys_all, values_all, positions):
    tok_rows = queries.shape[0]
    key_blocks, value_blocks, starts = key_blocking(keys_all, values_all, jnp.int32(0))

    def measure(state_pair, block_pair):
        top_score, total = state_pair
        key_block, start_row = block_pair
        scores, visible = block_scores(queries, positions, key_block, start_row)
        new_top = jnp.maximum(top_score, jnp.max(scores, axis=-1))
        raised = jnp.where(visible, jnp.exp(scores - new_top[..., None]), 0.0)
        total = total * jnp.exp(top_score - new_top) + jnp.sum(raised, axis=-1)
        return ((new_top, total), None)

    initial = (
        jnp.full((HEADS, tok_rows), masked_score, jnp.float32),
        jnp.zeros((HEADS, tok_rows), jnp.float32),
    )
    (top_score, total), unused = lax.scan(measure, initial, (key_blocks, starts))
    log_total = top_score + jnp.log(total)

    def accumulate(mixed, block_triple):
        key_block, value_block, start_row = block_triple
        scores, visible = block_scores(queries, positions, key_block, start_row)
        probs = jnp.where(visible, jnp.exp(scores - log_total[..., None]), 0.0).astype(jnp.bfloat16)
        return (
            mixed
            + jnp.einsum("hqk,khd->qhd", probs, value_block, preferred_element_type=jnp.float32),
            None,
        )

    mixed, unused = lax.scan(
        accumulate,
        jnp.zeros((tok_rows, HEADS, HEAD_DIM), jnp.float32),
        (key_blocks, value_blocks, starts),
    )
    return (mixed, log_total)


def attend_back(
    queries, positions, keys_all, values_all, key_offset, grad_mixed, log_total, row_delta
):
    tok_rows = queries.shape[0]
    key_blocks, value_blocks, starts = key_blocking(keys_all, values_all, key_offset)

    def backward_block(grad_queries, block_triple):
        key_block, value_block, start_row = block_triple
        scores, visible = block_scores(queries, positions, key_block, start_row)
        probs = jnp.where(visible, jnp.exp(scores - log_total[..., None]), 0.0)
        grad_probs = jnp.einsum(
            "qhd,khd->hqk", grad_mixed, value_block, preferred_element_type=jnp.float32
        )
        grad_scores = (probs * (grad_probs - row_delta[..., None])).astype(jnp.bfloat16)
        grad_queries = grad_queries + jnp.einsum(
            "hqk,khd->qhd", grad_scores, key_block, preferred_element_type=jnp.float32
        )
        grad_key_block = jnp.einsum(
            "hqk,qhd->khd", grad_scores, queries, preferred_element_type=jnp.float32
        )
        grad_value_block = jnp.einsum(
            "hqk,qhd->khd",
            probs.astype(jnp.bfloat16),
            grad_mixed,
            preferred_element_type=jnp.float32,
        )
        return (grad_queries, (grad_key_block, grad_value_block))

    grad_queries, (grad_keys, grad_values) = lax.scan(
        backward_block,
        jnp.zeros((tok_rows, HEADS, HEAD_DIM), jnp.float32),
        (key_blocks, value_blocks, starts),
    )
    key_len = keys_all.shape[0]
    return (
        grad_queries,
        grad_keys.reshape(key_len, HEADS * HEAD_DIM),
        grad_values.reshape(key_len, HEADS * HEAD_DIM),
    )


def local_gathered(
    tokens,
    cotangent,
    norm1_gain,
    norm1_bias,
    query_weight,
    key_weight,
    value_weight,
    out_weight,
    norm2_gain,
    norm2_bias,
    up_weight,
    up_bias,
    down_weight,
    down_bias,
):
    (
        gain_one,
        bias_one,
        w_query,
        w_key,
        w_value,
        w_out,
        gain_two,
        bias_two,
        w_up,
        b_up,
        w_down,
        b_down,
    ) = (
        lax.all_gather(norm1_gain, ("dp", "fsdp"), axis=0, tiled=True),
        lax.all_gather(norm1_bias, ("dp", "fsdp"), axis=0, tiled=True),
        lax.all_gather(query_weight, ("dp", "fsdp"), axis=0, tiled=True),
        lax.all_gather(key_weight, ("dp", "fsdp"), axis=0, tiled=True),
        lax.all_gather(value_weight, ("dp", "fsdp"), axis=0, tiled=True),
        lax.all_gather(out_weight, ("dp", "fsdp"), axis=0, tiled=True),
        lax.all_gather(norm2_gain, ("dp", "fsdp"), axis=0, tiled=True),
        lax.all_gather(norm2_bias, ("dp", "fsdp"), axis=0, tiled=True),
        lax.all_gather(up_weight, ("dp", "fsdp"), axis=0, tiled=True),
        lax.all_gather(up_bias, ("dp", "fsdp"), axis=0, tiled=True),
        lax.all_gather(down_weight, ("dp", "fsdp"), axis=0, tiled=True),
        lax.all_gather(down_bias, ("dp", "fsdp"), axis=0, tiled=True),
    )
    seq_count = tokens.shape[0]
    tok_rows = tokens.shape[1]
    model_width = tokens.shape[2]
    all_rows = seq_count * tok_rows
    scaling = HEAD_DIM ** (-0.5)
    inputs = tokens.reshape(all_rows, model_width).astype(jnp.float32)
    normed_one, inverse_one = norm_parts(inputs)
    attn_in = (normed_one * gain_one.astype(jnp.float32) + bias_one.astype(jnp.float32)).astype(
        jnp.bfloat16
    )
    queries = product(attn_in, w_query).reshape(seq_count, tok_rows, HEADS, HEAD_DIM)
    key_raw = product(attn_in, w_key).reshape(seq_count, tok_rows, HEADS, HEAD_DIM)
    value_low = (
        product(attn_in, w_value).astype(jnp.bfloat16).reshape(seq_count, tok_rows, model_width)
    )
    key_offset = lax.axis_index("dp") * tok_rows
    positions = key_offset + jnp.arange(tok_rows, dtype=jnp.int32)
    cosine, sine = rotary_tables(positions.astype(jnp.float32), HEAD_DIM // 2)
    q_rot = (rotate(queries, cosine, sine) * scaling).astype(jnp.bfloat16)
    k_flat = (
        rotate(key_raw, cosine, sine).astype(jnp.bfloat16).reshape(seq_count, tok_rows, model_width)
    )
    keys_all, values_all = (
        lax.all_gather(k_flat, "dp", axis=1, tiled=True),
        lax.all_gather(value_low, "dp", axis=1, tiled=True),
    )
    seq_len = keys_all.shape[1]
    mixed, log_total = jax.vmap(attend, in_axes=(0, 0, 0, None))(
        q_rot,
        keys_all.reshape(seq_count, seq_len, HEADS, HEAD_DIM),
        values_all.reshape(seq_count, seq_len, HEADS, HEAD_DIM),
        positions,
    )
    mixed_low = mixed.reshape(all_rows, model_width).astype(jnp.bfloat16)
    hidden = inputs + product(mixed_low, w_out)
    normed_two, inverse_two = norm_parts(hidden)
    ffn_in = (normed_two * gain_two.astype(jnp.float32) + bias_two.astype(jnp.float32)).astype(
        jnp.bfloat16
    )
    preact = product(ffn_in, w_up) + b_up.astype(jnp.float32)
    edges = [0] + [FF // 2 ** (GRAN - 1 - level_idx) for level_idx in range(GRAN)]
    gated_list = []
    result_list = []
    for level_idx in range(GRAN):
        level_width = edges[level_idx + 1]
        gated = gelu_value(preact[:, :level_width]).astype(jnp.bfloat16)
        gated_list.append(gated)
        result = hidden + product(gated, w_down[:level_width]) + b_down.astype(jnp.float32)
        result_list.append(result.astype(jnp.bfloat16))
    activations = jnp.stack(result_list).reshape(GRAN, seq_count, tok_rows, model_width)
    back_gain_one, back_query, back_key, back_value, back_out, back_gain_two, back_up, back_down = (
        lax.all_gather(norm1_gain, ("dp", "fsdp"), axis=0, tiled=True),
        lax.all_gather(query_weight, ("dp", "fsdp"), axis=0, tiled=True),
        lax.all_gather(key_weight, ("dp", "fsdp"), axis=0, tiled=True),
        lax.all_gather(value_weight, ("dp", "fsdp"), axis=0, tiled=True),
        lax.all_gather(out_weight, ("dp", "fsdp"), axis=0, tiled=True),
        lax.all_gather(norm2_gain, ("dp", "fsdp"), axis=0, tiled=True),
        lax.all_gather(up_weight, ("dp", "fsdp"), axis=0, tiled=True),
        lax.all_gather(down_weight, ("dp", "fsdp"), axis=0, tiled=True),
    )
    grads_out = cotangent.reshape(GRAN, all_rows, model_width)
    grad_hidden = jnp.sum(grads_out.astype(jnp.float32), axis=0)
    grad_down_bias = jnp.sum(grad_hidden, axis=0)
    grad_ffn_in = jnp.zeros((all_rows, model_width), jnp.float32)
    pre_grads = []
    for level_idx in range(GRAN):
        level_width = edges[level_idx + 1]
        grad_gated = back_product(grads_out[level_idx], back_down[:level_width])
        grad_pre = (grad_gated * gelu_grad(preact[:, :level_width])).astype(jnp.bfloat16)
        pre_grads.append(grad_pre)
        grad_ffn_in = grad_ffn_in + back_product(grad_pre, back_up[:, :level_width])
    up_blocks = []
    bias_blocks = []
    down_blocks = []
    for block_idx in range(GRAN):
        start_col = edges[block_idx]
        stop_col = edges[block_idx + 1]
        stacked_grad = jnp.concatenate(
            [pre_grads[level_idx][:, start_col:stop_col] for level_idx in range(block_idx, GRAN)],
            axis=0,
        )
        stacked_in = jnp.concatenate([ffn_in] * (GRAN - block_idx), axis=0)
        up_blocks.append(gram_product(stacked_in, stacked_grad))
        bias_blocks.append(jnp.sum(stacked_grad.astype(jnp.float32), axis=0))
        stacked_gated = jnp.concatenate(
            [gated_list[level_idx][:, start_col:stop_col] for level_idx in range(block_idx, GRAN)],
            axis=0,
        )
        stacked_out = jnp.concatenate(
            [grads_out[level_idx] for level_idx in range(block_idx, GRAN)], axis=0
        )
        down_blocks.append(gram_product(stacked_gated, stacked_out))
    grad_up_weight = jnp.concatenate(up_blocks, axis=1)
    grad_up_bias = jnp.concatenate(bias_blocks, axis=0)
    grad_down_weight = jnp.concatenate(down_blocks, axis=0)
    grad_gain_two = jnp.sum(grad_ffn_in * normed_two, axis=0)
    grad_bias_two = jnp.sum(grad_ffn_in, axis=0)
    grad_hidden = grad_hidden + norm_backward(
        grad_ffn_in, normed_two, inverse_two, back_gain_two.astype(jnp.float32)
    )
    grad_branch = grad_hidden.astype(jnp.bfloat16)
    grad_out_weight = gram_product(mixed_low, grad_branch)
    grad_mixed = (
        back_product(grad_branch, back_out)
        .astype(jnp.bfloat16)
        .reshape(seq_count, tok_rows, HEADS, HEAD_DIM)
    )
    row_delta = jnp.einsum("sqhd,sqhd->shq", grad_mixed.astype(jnp.float32), mixed)
    keys_again, values_again = (
        lax.all_gather(k_flat, "dp", axis=1, tiled=True),
        lax.all_gather(value_low, "dp", axis=1, tiled=True),
    )
    back_all = jax.vmap(attend_back, in_axes=(0, None, 0, 0, None, 0, 0, 0))
    grad_q_rot, grad_keys_all, grad_values_all = back_all(
        q_rot,
        positions,
        keys_again.reshape(seq_count, seq_len, HEADS, HEAD_DIM),
        values_again.reshape(seq_count, seq_len, HEADS, HEAD_DIM),
        jnp.int32(0),
        grad_mixed,
        log_total,
        row_delta,
    )
    every_query, every_grad = (
        lax.all_gather(q_rot, "dp", axis=1, tiled=True),
        lax.all_gather(grad_mixed, "dp", axis=1, tiled=True),
    )
    every_total, every_delta = (
        lax.all_gather(jnp.transpose(log_total, (0, 2, 1)), "dp", axis=1, tiled=True),
        lax.all_gather(jnp.transpose(row_delta, (0, 2, 1)), "dp", axis=1, tiled=True),
    )
    every_position = jnp.arange(seq_len, dtype=jnp.int32)
    unused_rows, grad_key_mine, grad_value_mine = back_all(
        every_query,
        every_position,
        k_flat.reshape(seq_count, tok_rows, HEADS, HEAD_DIM),
        value_low.reshape(seq_count, tok_rows, HEADS, HEAD_DIM),
        key_offset,
        every_grad,
        jnp.transpose(every_total, (0, 2, 1)),
        jnp.transpose(every_delta, (0, 2, 1)),
    )
    grad_query = (
        rotate(grad_q_rot * scaling, cosine, -sine)
        .reshape(all_rows, model_width)
        .astype(jnp.bfloat16)
    )
    grad_key = (
        rotate(grad_key_mine.reshape(seq_count, tok_rows, HEADS, HEAD_DIM), cosine, -sine)
        .reshape(all_rows, model_width)
        .astype(jnp.bfloat16)
    )
    grad_val = grad_value_mine.reshape(all_rows, model_width).astype(jnp.bfloat16)
    grad_query_weight = gram_product(attn_in, grad_query)
    grad_key_weight = gram_product(attn_in, grad_key)
    grad_value_weight = gram_product(attn_in, grad_val)
    grad_attn_in = (
        back_product(grad_query, back_query)
        + back_product(grad_key, back_key)
        + back_product(grad_val, back_value)
    )
    grad_gain_one = jnp.sum(grad_attn_in * normed_one, axis=0)
    grad_bias_one = jnp.sum(grad_attn_in, axis=0)
    grad_inputs = grad_hidden + norm_backward(
        grad_attn_in, normed_one, inverse_one, back_gain_one.astype(jnp.float32)
    )
    (
        sum_gain_one,
        sum_bias_one,
        sum_query,
        sum_key,
        sum_value,
        sum_out,
        sum_gain_two,
        sum_bias_two,
        sum_up,
        sum_up_bias,
        sum_down,
        sum_down_bias,
    ) = (
        lax.psum_scatter(grad_gain_one, ("dp", "fsdp"), scatter_dimension=0, tiled=True),
        lax.psum_scatter(grad_bias_one, ("dp", "fsdp"), scatter_dimension=0, tiled=True),
        lax.psum_scatter(grad_query_weight, ("dp", "fsdp"), scatter_dimension=0, tiled=True),
        lax.psum_scatter(grad_key_weight, ("dp", "fsdp"), scatter_dimension=0, tiled=True),
        lax.psum_scatter(grad_value_weight, ("dp", "fsdp"), scatter_dimension=0, tiled=True),
        lax.psum_scatter(grad_out_weight, ("dp", "fsdp"), scatter_dimension=0, tiled=True),
        lax.psum_scatter(grad_gain_two, ("dp", "fsdp"), scatter_dimension=0, tiled=True),
        lax.psum_scatter(grad_bias_two, ("dp", "fsdp"), scatter_dimension=0, tiled=True),
        lax.psum_scatter(grad_up_weight, ("dp", "fsdp"), scatter_dimension=0, tiled=True),
        lax.psum_scatter(grad_up_bias, ("dp", "fsdp"), scatter_dimension=0, tiled=True),
        lax.psum_scatter(grad_down_weight, ("dp", "fsdp"), scatter_dimension=0, tiled=True),
        lax.psum_scatter(grad_down_bias, ("dp", "fsdp"), scatter_dimension=0, tiled=True),
    )
    return (
        activations,
        grad_inputs.astype(jnp.bfloat16).reshape(seq_count, tok_rows, model_width),
        sum_gain_one,
        sum_bias_one,
        sum_query,
        sum_key,
        sum_value,
        sum_out,
        sum_gain_two,
        sum_bias_two,
        sum_up,
        sum_up_bias,
        sum_down,
        sum_down_bias,
    )


MESH = pl.DeviceIdType.MESH


class Place:
    def __init__(self, chips):
        self.chips = chips
        self.rank = lax.axis_index("dp")
        self.shard = lax.axis_index("fsdp")
        self.z = lax.div(self.shard, 2)
        self.core = lax.rem(self.shard, 2)
        along_x = self.rank + 1 - 2 * lax.rem(self.rank, 2)
        along_y = self.rank + 2 - 4 * lax.div(self.rank, 2)
        self.first = jnp.where(self.core == 0, along_x, along_y)
        self.second = jnp.where(self.core == 0, along_y, along_x)
        self.across = 3 - self.rank
        self.sibling = self.shard + 1 - 2 * self.core
        self.above = lax.rem(self.shard + 2, 2 * chips)
        self.below = lax.rem(self.shard + 2 * chips - 2, 2 * chips)

    def at(self, rank=None, shard=None):
        return (self.rank if rank is None else rank, self.shard if shard is None else shard)

    def others(self):
        return [lax.rem(self.shard + k, 2 * self.chips) for k in range(1, 2 * self.chips)]

    def greet(self, plane=True, sibling=False, ring=False, group=False):
        barrier = pltpu.get_barrier_semaphore()
        count = 0
        targets = []
        if plane:
            targets += [self.at(rank=r) for r in (self.first, self.second, self.across)]
        if sibling:
            targets.append(self.at(shard=self.sibling))
        if ring:
            targets += [self.at(shard=self.hop(k)) for k in range(1, self.chips)]
        if group:
            targets += [self.at(shard=f) for f in self.others()]
        for target in targets:
            pl.semaphore_signal(barrier, inc=1, device_id=target, device_id_type=MESH)
            count += 1
        pl.semaphore_wait(barrier, count)

    def hop(self, k):
        return 2 * lax.rem(self.z + k, self.chips) + self.core


def under(condition, action):
    if condition is None:
        action()
    else:
        pl.when(condition)(action)


class Message:
    def __init__(self, links, src, dst, target, sent=None, comes=None):
        index = links.take()
        self.copy = pltpu.make_async_remote_copy(
            src_ref=src,
            dst_ref=dst,
            send_sem=links.send.at[index],
            recv_sem=links.recv.at[index],
            device_id=target,
            device_id_type=MESH,
        )
        self.sent, self.comes = sent, comes
        self.left = False
        links.open.append(self)
        under(sent, self.copy.start)

    def arrive(self):
        under(self.comes, self.copy.wait_recv)

    def leave(self):
        if not self.left:
            under(self.sent, self.copy.wait_send)
        self.left = True


class Near:
    def __init__(self, links, src, dst, where):
        self.copy = pltpu.make_async_copy(src, dst, links.near.at[links.used_near])
        links.used_near += 1
        self.where = where
        self.waits = True
        under(where, self.copy.start)

    def arrive(self):
        if self.waits:
            under(self.where, self.copy.wait)
        self.waits = False


class Links:
    def __init__(self, send, recv, near):
        self.send, self.recv, self.near = send, recv, near
        self.used = 0
        self.used_near = 0
        self.open = []
        self.open_near = []

    def take(self):
        self.used += 1
        return self.used - 1

    def keep(self, src, dst, where=None):
        copy = Near(self, src, dst, where)
        self.open_near.append(copy)
        return copy

    def drain(self):
        for copy in self.open_near:
            copy.arrive()
        for message in self.open:
            message.leave()


LINK_SCRATCH = [
    pltpu.SemaphoreType.DMA((128,)),
    pltpu.SemaphoreType.DMA((128,)),
    pltpu.SemaphoreType.DMA((32,)),
]


def normed(values):
    centred = values - jnp.mean(values, axis=-1, keepdims=True)
    inverse = lax.rsqrt(jnp.mean(centred * centred, axis=-1, keepdims=True) + epsilon)
    return centred * inverse, inverse


def in_rows(count, step, body):
    def one(i, carry):
        body(pl.ds(pl.multiple_of(i * step, step), step))
        return carry

    lax.fori_loop(0, count // step, one, 0)


def turn_half(values, cosine, sine):
    return values * cosine + pltpu.roll(values, HEAD_DIM // 2, 1) * sine


class PlaneGather:
    def __init__(self, place, links, src, dst, parts):
        self.place, self.links, self.dst = place, links, dst
        rows = src.shape[0] // parts
        self.cuts = [pl.ds(k * rows, rows) for k in range(parts)]
        self.own = links.keep(src, dst.at[place.rank])
        self.first, self.second = [], []
        for cut in self.cuts:
            for side, target in ((self.first, place.first), (self.second, place.second)):
                block = dst.at[place.rank, cut]
                side.append(Message(links, src.at[cut], block, place.at(rank=target)))
        self.passed = []

    def relay(self, k):
        self.first[k].arrive()
        block = self.dst.at[self.place.first, self.cuts[k]]
        target = self.place.at(rank=self.place.second)
        self.passed.append(Message(self.links, block, block, target))

    def finish(self):
        for message in self.second + self.passed:
            message.arrive()


class PlaneScatter:
    def __init__(self, place, links, partial, landing, turn):
        self.place, self.links, self.partial, self.landing, self.turn = (
            place,
            links,
            partial,
            landing,
            turn,
        )
        self.target = place.at(rank=place.first)

    def send_far(self):
        self.far = Message(
            self.links, self.partial.at[self.place.across], self.landing.at[0], self.target
        )

    def send_near(self):
        self.near = Message(
            self.links, self.partial.at[self.place.first], self.landing.at[1], self.target
        )

    def relay(self):
        self.far.arrive()

        def add(cut):
            mine = self.partial[self.place.second, cut].astype(jnp.float32)
            mine = mine + self.landing[0, cut].astype(jnp.float32)
            self.turn[cut] = mine.astype(jnp.bfloat16)

        in_rows(self.turn.shape[0], 64, add)
        self.last = Message(
            self.links, self.turn, self.landing.at[2], self.place.at(rank=self.place.second)
        )

    def settle(self):
        self.near.arrive()
        self.last.arrive()

    def total(self, cut):
        total = self.partial[self.place.rank, cut].astype(jnp.float32)
        total = total + self.landing[1, cut].astype(jnp.float32)
        return total + self.landing[2, cut].astype(jnp.float32)


class Chain:
    def __init__(self, place, links, src, slot):
        self.place, self.links, self.slot = place, links, slot
        z, last = place.z, place.chips - 1
        own = slot(place.shard)
        self.up = Message(links, src, own, place.at(shard=place.above), z < last, z > 0)
        self.down = Message(links, src, own, place.at(shard=place.below), z > 0, z < last)
        self.beside = [Message(links, src, own, place.at(shard=place.sibling))]

    def step(self, s):
        place, links = self.place, self.links
        z, last = place.z, place.chips - 1
        below = self.slot(jnp.maximum(place.shard - 2 * s, place.core))
        above = self.slot(jnp.minimum(place.shard + 2 * s, 2 * last + place.core))
        self.up.arrive()
        has_below, has_above = z >= s, z <= last - s
        up = down = None
        if s < last:
            target = place.at(shard=place.above)
            up = Message(links, below, below, target, has_below & (z < last), z >= s + 1)
        self.beside.append(
            Message(links, below, below, place.at(shard=place.sibling), has_below, has_below)
        )
        self.down.arrive()
        if s < last:
            target = place.at(shard=place.below)
            down = Message(links, above, above, target, has_above & (z > 0), z <= last - s - 1)
        self.beside.append(
            Message(links, above, above, place.at(shard=place.sibling), has_above, has_above)
        )
        self.up, self.down = up, down

    def finish(self):
        for message in self.beside:
            message.arrive()


class Beside:
    def __init__(self, place, links, part, other):
        self.place, self.part, self.other = place, part, other
        self.message = Message(
            links, part.at[:, :, 1 - place.core], other, place.at(shard=place.sibling)
        )

    def add(self):
        self.message.arrive()
        core = self.place.core

        def one(k, carry):
            total = self.part[:, k, core].astype(jnp.float32) + self.other[:, k].astype(jnp.float32)
            self.part[:, k, core] = total.astype(self.part.dtype)
            return carry

        lax.fori_loop(0, self.place.chips, one, 0)


class Along:
    def __init__(self, place, links, share, landing, far=None):
        self.place, self.links, self.landing = place, links, landing
        z = place.z
        self.middle = (z == 1) | (z == 2)
        end = jnp.logical_not(self.middle)
        partner = z + 1 - 2 * lax.rem(z, 2)
        over = jnp.where(z < 2, 2, 1)
        self.other_end = jnp.where(z < 2, 3, 0)
        self.far = share(self.other_end) if far is None else far

        def to(chip):
            return place.at(shard=2 * chip + place.core)

        self.to = to

        @pl.when(end)
        def nothing_comes():
            landing[2] = jnp.zeros_like(landing[2])

        self.merge = Message(
            links, share(self.other_end), landing.at[3], to(partner), end, self.middle
        )
        self.messages = [
            Message(links, share(partner), landing.at[0], to(partner)),
            Message(links, share(over), landing.at[1], to(over), end, self.middle),
            Message(links, share(over), landing.at[2], to(over), self.middle, self.middle),
        ]

    def relay(self):
        self.merge.arrive()
        landing = self.landing

        @pl.when(self.middle)
        def add():
            total = landing[3].astype(jnp.float32) + self.far[...].astype(jnp.float32)
            landing[3] = total.astype(landing.dtype)

        end = jnp.logical_not(self.middle)
        self.messages.append(
            Message(
                self.links, landing.at[3], landing.at[1], self.to(self.other_end), self.middle, end
            )
        )

    def total(self, mine):
        total = mine.astype(jnp.float32)
        for message in self.messages:
            message.arrive()
        for k in range(3):
            total = total + self.landing[k].astype(jnp.float32)
        return total


class Detour:
    def __init__(self, place, links, src, dst, stop, source, turn, goal):
        self.place, self.links, self.dst, self.stop = place, links, dst, stop
        straight = place.core == 0
        around = place.core == 1
        across = place.at(rank=place.across)
        self.goal = around & (place.rank == goal)
        self.turn = around & (place.rank == turn)
        here = place.rank == source
        self.straight = Message(
            links, src, dst, across, straight & here, straight & (place.rank == goal)
        )
        self.leg = Message(
            links, src, stop, place.at(rank=place.first), around & here, self.turn
        )

    def relay(self):
        self.leg.arrive()
        target = self.place.at(rank=self.place.second)
        self.last = Message(self.links, self.stop, self.dst, target, self.turn, self.goal)

    def arrive(self):
        self.straight.arrive()
        self.last.arrive()


class Deal:
    def __init__(self, place, links, pairs):
        self.messages = []
        for part, dst in pairs:
            self.messages.append(links.keep(part(place.rank), dst))
            for rank in (place.first, place.second, place.across):
                self.messages.append(Message(links, part(rank), dst, place.at(rank=rank)))

    def arrive(self):
        for message in self.messages:
            message.arrive()


def block_of(r):
    return jnp.where(r == 0, 0, jnp.minimum(r + 1, GRAN - 1))


def forward_kernel(
    chips,
    tokens,
    cotangent,
    gain_one,
    bias_one,
    gain_two,
    bias_two,
    b_down,
    b_up,
    w_query,
    w_key,
    w_value,
    w_out,
    w_up,
    w_down,
    comb,
    mask,
    cosine,
    sine,
    all_tokens,
    attn_in,
    qkv_rot,
    mixed_low,
    hidden,
    all_ffn_in,
    gains,
    incoming,
    cotangent_sum,
    next_sum,
    all_qkv,
    all_out,
    all_up,
    all_down,
    hidden_v,
    sum_v,
    cotangent_v,
    suffix,
    small,
    tokens_v,
    attn_v,
    rot_v,
    mixed_v,
    qkv_v,
    out_v,
    partial,
    landing,
    passing,
    ffn_v,
    all_small,
    send,
    recv,
    near,
):
    place = Place(chips)
    links = Links(send, recv, near)
    load_cotangent = links.keep(cotangent, cotangent_v)
    own = gain_one.shape[1]
    packed = [v[...].astype(jnp.float32) for v in (gain_one, bias_one, gain_two, bias_two, b_down)]
    wide_bias = b_up[...].astype(jnp.float32)
    packed += [wide_bias[:, q * own : (q + 1) * own] for q in range(4)]
    packed = jnp.concatenate(packed + [jnp.zeros((7, own), jnp.float32)], axis=0)
    packed = jnp.concatenate([packed, jnp.zeros((16, 128 - own), jnp.float32)], axis=1)
    small[...] = packed.astype(jnp.bfloat16)
    place.greet(plane=True, group=True)
    rank, shard = place.rank, place.shard
    ranks, tok_rows, model_width = tokens_v.shape
    head_cols = w_query.shape[1] // ranks
    heads = head_cols // HEAD_DIM

    def columns(weight, width):
        return lambda r: weight.at[:, pl.ds(pl.multiple_of(r * width, 128), width)]

    own_qkv = all_qkv.at[rank, shard]
    deal_small = Deal(place, links, [(lambda r: small, all_small.at[rank, shard])])
    pairs = []
    for i, weight in enumerate((w_query, w_key, w_value)):
        pairs.append(
            (columns(weight, head_cols), own_qkv.at[:, pl.ds(i * head_cols, head_cols)])
        )
    deal_qkv = Deal(place, links, pairs)
    gather = PlaneGather(place, links, tokens, tokens_v, 2)
    deal_up = Deal(place, links, [(columns(w_up, w_up.shape[1] // ranks), all_up.at[rank, shard])])
    links.keep(w_out, all_out.at[shard])
    low_half = pl.ds(0, model_width // 2)
    links.keep(w_down.at[:, low_half], all_down.at[shard])
    out_slot = lambda f: all_out.at[f]
    down_slot = lambda f: all_down.at[f]
    small_slot = lambda f: all_small.at[:, f]
    qkv_slot = lambda f: all_qkv.at[:, f]
    up_slot = lambda f: all_up.at[:, f]
    chain_out = Chain(place, links, w_out, out_slot)
    deal_small.arrive()
    own_small = small_slot(shard)
    told = [Message(links, own_small, own_small, place.at(shard=f)) for f in place.others()]
    deal_qkv.arrive()
    chain_qkv = Chain(place, links, qkv_slot(shard), qkv_slot)
    load_cotangent.arrive()

    def add_cotangents(cut):
        total = jnp.zeros((64, model_width), jnp.float32)
        for g in range(GRAN - 1, -1, -1):
            total = total + cotangent_v[g, cut].astype(jnp.float32)
            suffix[g, cut] = total.astype(jnp.bfloat16)
        sum_v[cut] = total

    in_rows(tok_rows, 64, add_cotangents)
    links.keep(sum_v, cotangent_sum)
    links.keep(suffix.at[1], next_sum)
    for message in told:
        message.arrive()
    chain_qkv.step(1)
    gather.relay(0)
    gather.relay(1)

    def wide(rows):
        spread = jnp.dot(rows, comb[...], preferred_element_type=jnp.float32)
        return jnp.sum(spread * mask[...], axis=0, keepdims=True)

    devices = ranks * 2 * chips
    for i in range(5):
        gains[i : i + 1] = wide(all_small[:, :, i].reshape(devices, 128))
    up_rows = all_small[rank, :, 5:9].astype(jnp.float32).reshape(devices, 128)
    gains[5:6] = wide(up_rows.astype(jnp.bfloat16))
    gains[6:8] = jnp.zeros((2, model_width), jnp.float32)

    def norm_block(r):
        def rows_of(cut):
            value, unused = normed(tokens_v[r, cut].astype(jnp.float32))
            attn_v[r, cut] = (value * gains[0:1] + gains[1:2]).astype(jnp.bfloat16)

        in_rows(tok_rows, 64, rows_of)

    for copy in links.open_near:
        copy.arrive()
    norm_block(rank)
    norm_block(place.first)
    chain_qkv.step(2)
    gather.finish()
    links.keep(suffix.at[block_of(rank)], incoming.at[rank])
    dealt = []
    for r in (place.first, place.second, place.across):
        dealt.append(Message(links, suffix.at[block_of(r)], incoming.at[rank], place.at(rank=r)))
    norm_block(place.second)
    norm_block(place.across)
    links.keep(tokens_v, all_tokens)
    links.keep(attn_v, attn_in)
    deal_up.arrive()
    chain_qkv.up.leave()
    chain_qkv.down.leave()
    chain_out.step(1)
    chain_up = Chain(place, links, up_slot(shard), up_slot)
    chain_qkv.step(3)
    chain_out.step(2)
    chain_down = Chain(place, links, w_down.at[:, low_half], down_slot)
    chain_qkv.finish()
    load_qkv = links.keep(all_qkv, qkv_v)
    load_qkv.arrive()

    def project(r, carry):
        rows = pl.ds(pl.multiple_of(r * tok_rows, tok_rows), tok_rows)
        for part in range(3):
            cut = slice(part * head_cols, (part + 1) * head_cols)
            weight = qkv_v[:, :, :, cut].reshape(model_width, head_cols)
            value = jnp.dot(attn_v[r], weight, preferred_element_type=jnp.float32)
            if part < 2:
                turned = []
                for h in range(heads):
                    head = value[:, h * HEAD_DIM : (h + 1) * HEAD_DIM]
                    turned.append(turn_half(head, cosine[rows], sine[rows]))
                value = jnp.concatenate(turned, axis=1)
                if part == 0:
                    value = value * HEAD_DIM ** (-0.5)
            rot_v[r, :, cut] = value.astype(jnp.bfloat16)
        return carry

    lax.fori_loop(0, ranks, project, 0)
    links.keep(rot_v, qkv_rot)
    chain_out.step(3)
    chain_up.step(1)
    chain_out.finish()
    load_out = links.keep(all_out, out_v)

    def attend_block(r):
        def head(h, carry):
            def part(i):
                return pl.ds(pl.multiple_of(i * head_cols + h * HEAD_DIM, HEAD_DIM), HEAD_DIM)

            for t in range(ranks):

                @pl.when(r == t)
                def with_keys(seen=t + 1):
                    keys = rot_v[:seen, :, part(1)].reshape(-1, HEAD_DIM)
                    scores = back_product(rot_v[r, :, part(0)], keys)
                    row = lax.broadcasted_iota(jnp.int32, scores.shape, 0) + r * tok_rows
                    column = lax.broadcasted_iota(jnp.int32, scores.shape, 1)
                    scores = jnp.where(row >= column, scores, masked_score)
                    raised = jnp.exp(scores - jnp.max(scores, axis=-1, keepdims=True))
                    scale = 1.0 / jnp.sum(raised, axis=-1, keepdims=True)
                    probs = (raised * scale).astype(jnp.bfloat16)
                    mixed = product(probs, rot_v[:seen, :, part(2)].reshape(-1, HEAD_DIM))
                    mixed_v[r, :, part(0)] = mixed.astype(jnp.bfloat16)

            return carry

        lax.fori_loop(0, heads, head, 0)

    def project_block(r):
        weight = out_v[...].reshape(head_cols, model_width)
        partial[r] = product(mixed_v[r], weight).astype(jnp.bfloat16)

    scatter = PlaneScatter(place, links, partial, landing, passing)
    attend_block(place.across)
    load_out.arrive()
    project_block(place.across)
    scatter.send_far()
    attend_block(place.first)
    project_block(place.first)
    scatter.send_near()
    chain_down.step(1)
    attend_block(place.second)
    project_block(place.second)
    scatter.relay()
    chain_up.step(2)
    attend_block(rank)
    project_block(rank)
    chain_down.step(2)
    links.keep(mixed_v, mixed_low)
    scatter.settle()

    def second_norm(cut):
        value = scatter.total(cut) + tokens_v[rank, cut].astype(jnp.float32)
        hidden_v[cut] = value
        value, unused = normed(value)
        ffn_v[cut] = (value * gains[2:3] + gains[3:4]).astype(jnp.bfloat16)

    in_rows(tok_rows, 64, second_norm)
    gather = PlaneGather(place, links, ffn_v, all_ffn_in, 4)
    links.keep(hidden_v, hidden)
    chain_up.step(3)
    gather.relay(0)
    gather.relay(1)
    chain_down.step(3)
    gather.relay(2)
    gather.relay(3)
    chain_up.finish()
    gather.finish()
    chain_down.finish()
    for message in dealt:
        message.arrive()
    links.drain()


def middle_kernel(
    chips,
    all_ffn_in,
    incoming,
    next_sum,
    w_up,
    down_low,
    w_down,
    hidden,
    cotangent_sum,
    gains,
    grad_hidden,
    sums,
    sum_down,
    sum_up_low,
    share_up,
    all_branch,
    terms,
    own_term,
    extra_in,
    ffn_v,
    csum_v,
    up_v,
    down_v,
    gated_v,
    grad_v,
    part_down,
    other_down,
    land_down,
    other_up,
    land_up,
    terms_v,
    stop,
    stop_more,
    branch,
    grad_hidden_v,
    sum_down_v,
    partial,
    landing,
    passing,
    send,
    recv,
    near,
):
    place = Place(chips)
    links = Links(send, recv, near)
    rank = place.rank
    ranks, tok_rows, model_width = ffn_v.shape
    ff_cols = up_v.shape[-1]
    half = ff_cols // 2
    load_up = links.keep(w_up, up_v)
    order = (place.across, place.first, place.second, rank)
    load_ffn = [links.keep(all_ffn_in.at[t], ffn_v.at[t]) for t in order]
    wide = model_width // 2
    columns = (pl.ds(0, wide), pl.ds(wide, wide))
    own_down = w_down.at[:, columns[1]]
    load_own = links.keep(own_down, down_v.at[place.shard, :, columns[1]])
    load_more = links.keep(next_sum, csum_v.at[1, rank], rank == 0)
    place.greet(plane=True, sibling=True, ring=True)
    chain_down = Chain(place, links, own_down, lambda f: down_v.at[f, :, columns[1]])
    detour = Detour(place, links, next_sum, csum_v.at[1, 3], stop, 3, 1, 0)
    dealt = []
    for r in (place.first, place.second):
        dealt.append(
            Message(links, next_sum, csum_v.at[1, rank], place.at(rank=r), r == 0, rank == 0)
        )
    slots = (0, jnp.where(rank == 0, 1, 0))
    sums[...] = jnp.zeros_like(sums)
    load_up.arrive()
    for copy in load_ffn:
        copy.arrive()
    load_down = links.keep(down_low, down_v.at[:, :, columns[0]])
    load_csum = links.keep(incoming, csum_v.at[0])
    scatter = PlaneScatter(place, links, partial, landing, passing)

    def widen(i):
        def one(t, carry):
            cut = slice(i * half, (i + 1) * half)
            weight = up_v[:, :, :, :, cut].reshape(model_width, half)
            pre = product(ffn_v[t], weight) + gains[5:6, cut]
            square = pre * pre
            tangent = jnp.tanh(0.7978845608028654 * pre * (1.0 + 0.044715 * square))
            gated_v[t, :, cut] = (0.5 * pre * (1.0 + tangent)).astype(jnp.bfloat16)
            slope = 0.5 * (1.0 + tangent) + 0.5 * pre * (1.0 - tangent * tangent) * (
                0.7978845608028654 * (1.0 + 3.0 * 0.044715 * square)
            )
            grad_v[t, :, cut] = slope.astype(jnp.bfloat16)
            return carry

        return one

    def high_tile(h):
        right = slice(h * wide, (h + 1) * wide)

        def one(t, carry):
            weight = down_v[4:, :, right].reshape(half, wide)
            value = product(gated_v[t, :, half:], weight)
            terms_v[1, t, :, right] = value.astype(jnp.bfloat16)
            return carry

        lax.fori_loop(0, ranks, one, 0)
        cut = columns[h]
        links.keep(terms_v.at[1, rank, :, cut], extra_in.at[:, cut], rank == 0)
        detour = Detour(
            place,
            links,
            terms_v.at[1, place.across, :, cut],
            extra_in.at[:, cut],
            stop_more.at[:, cut],
            0,
            2,
            3,
        )
        for r in (place.first, place.second):
            dealt_more.append(
                Message(
                    links,
                    terms_v.at[1, r, :, cut],
                    extra_in.at[:, cut],
                    place.at(rank=r),
                    rank == 0,
                    r == 0,
                )
            )
        return detour

    def low_tile(t, carry):
        low_term = product(gated_v[t, :, :half], down_v[:4].reshape(half, model_width))
        high_term = terms_v[1, t].astype(jnp.float32) * jnp.where(rank == 0, 0.0, 1.0)
        terms_v[0, t] = (low_term + high_term).astype(jnp.bfloat16)
        return carry

    def block(k):
        t = order[k]
        for i in range(2):
            cut = slice(i * half, (i + 1) * half)
            weight = down_v[4 * i : 4 * i + 4].reshape(half, model_width)
            grad = back_product(csum_v[slots[i], t], weight) * grad_v[t, :, cut].astype(jnp.float32)
            grad_v[t, :, cut] = grad.astype(jnp.bfloat16)
            sums[3:4, cut] += jnp.sum(grad, axis=0, keepdims=True)

        def back(i, carry):
            own = model_width // ranks
            value = back_product(grad_v[t], up_v[i].reshape(own, ff_cols))
            partial[t, :, pl.ds(pl.multiple_of(i * own, 128), own)] = value.astype(jnp.bfloat16)
            return carry

        lax.fori_loop(0, ranks, back, 0)

    dealt_more = []
    lax.fori_loop(0, ranks, widen(1), 0)
    detour.relay()
    chain_down.step(1)
    load_down.arrive()
    detour_low = high_tile(0)
    chain_down.step(2)
    lax.fori_loop(0, ranks // 2, widen(0), 0)
    chain_down.step(3)
    lax.fori_loop(ranks // 2, ranks, widen(0), 0)
    chain_down.finish()
    load_own.arrive()
    detour_high = high_tile(1)
    detour_low.relay()
    load_csum.arrive()
    load_more.arrive()
    for message in dealt + [detour]:
        message.arrive()

    def down_tiles(h):
        width = model_width // 2
        right = slice(h * width, (h + 1) * width)

        def down_tile(i, carry):
            rows = ff_cols // ranks
            left = gated_v[:, :, pl.ds(pl.multiple_of(i * rows, 128), rows)].reshape(-1, rows)
            slot = jnp.where(i < 2, slots[0], slots[1])
            value = gram_product(left, csum_v[slot, :, :, right].reshape(-1, width))
            part_down[h, i] = value.astype(jnp.bfloat16).reshape(part_down.shape[2:])
            return carry

        lax.fori_loop(0, ranks, down_tile, 0)
        here = pl.ds(h, 1)
        return Beside(place, links, part_down.at[here], other_down.at[here])

    def along_half(beside, h):
        beside.add()
        share = part_down.at[pl.ds(h, 1)]
        return Along(
            place, links, lambda there: share.at[:, there, place.core], land_down.at[h]
        )

    beside_low = down_tiles(0)
    block(0)
    scatter.send_far()
    along_low = along_half(beside_low, 0)
    block(1)
    scatter.send_near()
    beside_high = down_tiles(1)
    block(2)
    scatter.relay()
    along_high = along_half(beside_high, 1)
    detour_high.relay()
    along_low.relay()
    block(3)

    def up_tile(i, carry):
        rows = model_width // ranks
        left = ffn_v[:, :, pl.ds(pl.multiple_of(i * rows, 128), rows)].reshape(-1, rows)
        value = gram_product(left, grad_v[...].reshape(-1, ff_cols))
        up_v[i] = value.astype(jnp.bfloat16).reshape(up_v.shape[1:])
        return carry

    lax.fori_loop(0, ranks, up_tile, 0)
    beside_up = Beside(place, links, up_v, other_up)
    along_high.relay()

    beside_up.add()
    first_cols = sum_up_low.shape[2]
    share_low = up_v.at[:, :, :, :, pl.ds(0, first_cols)]
    along_up = Along(place, links, lambda there: share_low.at[:, there, place.core], land_up)
    rest = pl.ds(first_cols, ff_cols - first_cols)
    links.keep(up_v.at[:, :, place.core, :, rest], share_up)
    scatter.settle()

    def norm_back(cut):
        value, inverse = normed(hidden[cut])
        grad = scatter.total(cut)
        sums[0:1] += jnp.sum(grad * value, axis=0, keepdims=True)
        sums[1:2] += jnp.sum(grad, axis=0, keepdims=True)
        sums[2:3] += jnp.sum(cotangent_sum[cut], axis=0, keepdims=True)
        total = cotangent_sum[cut] + norm_backward(grad, value, inverse, gains[2:3])
        grad_hidden_v[cut] = total
        branch[cut] = total.astype(jnp.bfloat16)

    in_rows(tok_rows, 64, norm_back)
    gather = PlaneGather(place, links, branch, all_branch, 4)
    links.keep(grad_hidden_v, grad_hidden)
    lax.fori_loop(0, ranks, low_tile, 0)
    links.keep(terms_v.at[0], terms)
    links.keep(terms_v.at[0, rank], own_term)
    gather.relay(0)
    gather.relay(1)
    along_up.relay()
    gather.relay(2)
    gather.relay(3)
    for h, along in enumerate((along_low, along_high)):
        mine = part_down[h : h + 1, place.z, place.core]
        sum_down_v[:, h * wide : (h + 1) * wide] = along.total(mine)[0]
    links.keep(sum_down_v, sum_down)
    mine = up_v[:, place.z, place.core, :, :first_cols]
    sum_up_low[...] = along_up.total(mine).astype(jnp.bfloat16)
    gather.finish()
    for message in dealt_more + [detour_low, detour_high]:
        message.arrive()
    links.drain()


def last_kernel(
    chips,
    all_branch,
    sum_up_low,
    share_up,
    terms,
    qkv_rot,
    mixed_low,
    w_out,
    w_qkv,
    attn_in,
    all_tokens,
    grad_hidden,
    gains,
    sums,
    comb,
    mask,
    cosine,
    sine,
    term_in,
    grad_tokens,
    sum_out,
    land_sum_up,
    land_sum_qkv,
    sum_small,
    branch_v,
    rot_v,
    mixed_v,
    grad_mixed_v,
    out_v,
    qkv_v,
    attn_v,
    tokens_v,
    grad_v,
    key_sum,
    value_sum,
    partial,
    landing,
    passing,
    turn_up,
    mine_up,
    far_up,
    land_up,
    part_out,
    other_out,
    land_out,
    part_qkv,
    other_qkv,
    land_qkv,
    turn_qkv,
    part_small,
    other_small,
    land_small,
    turn_small,
    land_sums,
    more_sums,
    send,
    recv,
    near,
):
    place = Place(chips)
    links = Links(send, recv, near)
    rank, z = place.rank, place.z
    ranks, tok_rows, model_width = branch_v.shape
    head_cols = mixed_v.shape[2]
    heads = head_cols // HEAD_DIM
    load_branch = links.keep(all_branch, branch_v)
    load_out = links.keep(w_out, out_v)
    load_mixed = links.keep(mixed_low, mixed_v)
    load_rot = links.keep(qkv_rot, rot_v)
    other_end = jnp.where(z < 2, chips - 1, 0)
    piece = 3 * HEAD_DIM
    load_far = links.keep(share_up.at[:, other_end], far_up)
    first_cols = sum_up_low.shape[2]
    load_low = links.keep(sum_up_low, turn_up.at[:, :, pl.ds(0, first_cols)])
    place.greet(plane=True, sibling=True, ring=True)
    along_up = Along(place, links, lambda there: share_up.at[:, there], land_up, far_up)
    dealt = []
    for r in (place.first, place.second, place.across):
        dealt.append(Message(links, terms.at[r], term_in.at[rank], place.at(rank=r)))
    load_out.arrive()

    def mix_back(t):
        weight = out_v[...].reshape(head_cols, model_width)
        grad_mixed_v[t] = back_product(branch_v[t], weight).astype(jnp.bfloat16)

    load_branch.arrive()
    load_attn = links.keep(attn_in, attn_v)
    load_qkv = [
        links.keep(
            w_qkv.at[:, :, :, pl.ds(i * head_cols + h * HEAD_DIM, HEAD_DIM)],
            qkv_v.at[:, :, :, pl.ds(h * piece + i * HEAD_DIM, HEAD_DIM)],
        )
        for h in range(heads)
        for i in range(3)
    ]
    load_tokens = links.keep(all_tokens, tokens_v)
    load_up = links.keep(share_up.at[:, z], mine_up)
    for r in range(ranks):
        mix_back(r)
    load_mixed.arrive()
    value = gram_product(
        mixed_v[...].reshape(-1, head_cols), branch_v[...].reshape(-1, model_width)
    )
    part_out[0] = value.astype(jnp.bfloat16).reshape(part_out.shape[1:])
    beside_out = Beside(place, links, part_out, other_out)
    load_rot.arrive()

    def head(h):
        def part(i):
            return slice(i * head_cols + h * HEAD_DIM, i * head_cols + (h + 1) * HEAD_DIM)

        def place_of(i):
            return slice(h * piece + i * HEAD_DIM, h * piece + (i + 1) * HEAD_DIM)

        for t in range(ranks - 1, -1, -1):
            count = t + 1
            keys = rot_v[:count, :, part(1)].reshape(-1, HEAD_DIM)
            values = rot_v[:count, :, part(2)].reshape(-1, HEAD_DIM)
            queries = rot_v[t, :, part(0)]
            grad_mixed = grad_mixed_v[t, :, part(0)]
            scores = back_product(queries, keys)
            row = lax.broadcasted_iota(jnp.int32, scores.shape, 0) + t * tok_rows
            column = lax.broadcasted_iota(jnp.int32, scores.shape, 1)
            scores = jnp.where(row >= column, scores, masked_score)
            raised = jnp.exp(scores - jnp.max(scores, axis=-1, keepdims=True))
            probs = raised * (1.0 / jnp.sum(raised, axis=-1, keepdims=True))
            delta = jnp.sum(
                grad_mixed.astype(jnp.float32) * mixed_v[t, :, part(0)].astype(jnp.float32),
                axis=-1,
                keepdims=True,
            )
            grad_scores = (probs * (back_product(grad_mixed, values) - delta)).astype(jnp.bfloat16)
            rows = pl.ds(t * tok_rows, tok_rows)
            grad_query = product(grad_scores, keys)
            grad_query = turn_half(grad_query, cosine[rows], -sine[rows]) * HEAD_DIM ** (-0.5)
            grad_v[t, :, place_of(0)] = grad_query.astype(jnp.bfloat16)
            grad_key = gram_product(grad_scores, queries)
            grad_value = gram_product(probs.astype(jnp.bfloat16), grad_mixed)
            seen = count * tok_rows
            if t == ranks - 1:
                key_sum[...] = grad_key
                value_sum[...] = grad_value
            else:
                key_sum[:seen] += grad_key
                value_sum[:seen] += grad_value
        grad_key = turn_half(key_sum[...], cosine[...], -sine[...]).astype(jnp.bfloat16)
        grad_v[:, :, place_of(1)] = grad_key.reshape(ranks, tok_rows, HEAD_DIM)
        grad_value = value_sum[...].astype(jnp.bfloat16)
        grad_v[:, :, place_of(2)] = grad_value.reshape(ranks, tok_rows, HEAD_DIM)

        def qkv_tile(i, carry):
            rows = model_width // ranks
            left = attn_v[:, :, pl.ds(pl.multiple_of(i * rows, 128), rows)].reshape(-1, rows)
            right = grad_v[:, :, h * piece : (h + 1) * piece].reshape(-1, piece)
            value = gram_product(left, right)
            part_qkv[h, i] = value.astype(jnp.bfloat16).reshape(part_qkv.shape[2:])
            return carry

        if h == 0:
            load_attn.arrive()
        lax.fori_loop(0, ranks, qkv_tile, 0)
        return Beside(place, links, part_qkv.at[h], other_qkv.at[h])

    def along_head(h):
        return Along(
            place, links, lambda there: part_qkv.at[h, :, there, place.core], land_qkv.at[h]
        )

    beside_qkv = [head(0)]
    load_far.arrive()
    along_up.relay()
    beside_out.add()
    along_out = Along(place, links, lambda there: part_out.at[:, there, place.core], land_out)
    along_qkv = []
    for h in range(1, heads):
        beside_qkv.append(head(h))
        beside_qkv[h - 1].add()
        along_qkv.append(along_head(h - 1))
    along_out.relay()
    for copy in load_qkv:
        copy.arrive()
    load_tokens.arrive()
    scatter = PlaneScatter(place, links, partial, landing, passing)
    more_sums[...] = jnp.zeros_like(more_sums)

    def attn_back(t):
        def tile(i, carry):
            own = model_width // ranks
            value = back_product(grad_v[t], qkv_v[i].reshape(own, 3 * head_cols))
            partial[t, :, pl.ds(pl.multiple_of(i * own, 128), own)] = value.astype(jnp.bfloat16)
            return carry

        lax.fori_loop(0, ranks, tile, 0)

        def count(cut):
            value, unused = normed(tokens_v[t, cut].astype(jnp.float32))
            grad = partial[t, cut].astype(jnp.float32)
            more_sums[0:1] += jnp.sum(grad * value, axis=0, keepdims=True)
            more_sums[1:2] += jnp.sum(grad, axis=0, keepdims=True)

        return count

    count_across = attn_back(place.across)
    scatter.send_far()
    count_first = attn_back(place.first)
    scatter.send_near()
    beside_qkv[heads - 1].add()
    along_qkv.append(along_head(heads - 1))
    along_qkv[0].relay()
    count_second = attn_back(place.second)
    scatter.relay()
    for h in range(1, heads - 1):
        along_qkv[h].relay()
    count_own = attn_back(rank)
    for count in (count_across, count_first, count_second, count_own):
        in_rows(tok_rows, 64, count)

    def pieces(row):
        spread = (row * mask[...]).astype(jnp.float32)
        return lax.dot_general(
            spread,
            comb[...].astype(jnp.float32),
            (((1,), (1,)), ((), ())),
            precision=lax.Precision.HIGHEST,
            preferred_element_type=jnp.float32,
        )

    part_small[...] = jnp.zeros_like(part_small)
    rows = (more_sums[0:1], more_sums[1:2], sums[0:1], sums[1:2], sums[2:3])
    for k, row in enumerate(rows):
        part_small[:, :, :, k] = pieces(row).reshape(ranks, chips, 2, 128)
    part_small[rank, :, :, 5:9] = pieces(sums[3:4]).reshape(chips, 2, 4, 128)
    beside_small = Beside(place, links, part_small, other_small)
    along_qkv[heads - 1].relay()
    load_up.arrive()
    load_low.arrive()
    turn_up[:, :, first_cols:] = along_up.total(mine_up[...]).astype(jnp.bfloat16)
    deal_up = Deal(place, links, [(lambda r: turn_up.at[r], land_sum_up.at[rank])])
    beside_small.add()
    along_small = Along(place, links, lambda there: part_small.at[:, there, place.core], land_small)
    sum_out[...] = along_out.total(part_out[:, z, place.core])[0]
    along_small.relay()
    deal_qkv = []

    def settle_head(h):
        total = along_qkv[h].total(part_qkv[h, :, z, place.core])
        turn_qkv[h] = total.astype(jnp.bfloat16)
        deal_qkv.append(
            Deal(place, links, [(lambda r: turn_qkv.at[h, r], land_sum_qkv.at[h, rank])])
        )

    for h in range(heads - 1):
        settle_head(h)
    scatter.settle()

    def norm_back(cut):
        value, inverse = normed(tokens_v[rank, cut].astype(jnp.float32))
        grad = norm_backward(scatter.total(cut), value, inverse, gains[0:1])
        grad_tokens[cut] = (grad_hidden[cut] + grad).astype(jnp.bfloat16)

    in_rows(tok_rows, 64, norm_back)
    turn_small[...] = along_small.total(part_small[:, z, place.core])
    deal_small = Deal(place, links, [(lambda r: turn_small.at[r], land_sums.at[rank])])
    settle_head(heads - 1)
    for message in dealt:
        message.arrive()
    deal_up.arrive()
    deal_small.arrive()
    sum_small[...] = land_sums[0] + land_sums[1] + land_sums[2] + land_sums[3]
    for deal in deal_qkv:
        deal.arrive()
    links.drain()


def closing_kernel(*refs):
    own_term, ins, outs = refs[0], refs[1:10], refs[10:23]
    held, act_v, near, leaving = refs[23:32], refs[32], refs[33], refs[34]
    sums_v, leaving_sums = refs[35:39], refs[39]
    rank = lax.axis_index("dp")
    hidden, gains, term_in, extra_in, grad_in, out_in = held[:6]
    up_in, qkv_in, small_in = held[6:]
    activations, grad_tokens, sum_out = outs[0], outs[1], outs[5]
    sum_query, sum_key, sum_value, sum_up = sums_v
    steps = near.shape[0] - 1
    rows = hidden.shape[0] // steps
    cuts = [pl.ds(k * rows, rows) for k in range(steps)]
    rest = []
    for i in (1, 5, 6, 7, 8):
        rest.append(pltpu.make_async_copy(ins[i], held[i], near.at[steps, i]))
        rest[-1].start()
    copies = []
    for k, cut in enumerate(cuts):
        batch = []
        for i in (0, 3, 4):
            copy = pltpu.make_async_copy(ins[i].at[cut], held[i].at[cut], near.at[k, i])
            copy.start()
            batch.append(copy)
        for r in range(term_in.shape[0]):
            here, sem = term_in.at[r, cut], near.at[k, 9 + r]
            there = pltpu.make_async_copy(ins[2].at[r, cut], here, sem)
            own = pltpu.make_async_copy(own_term.at[cut], here, sem)
            pl.when(rank != r)(there.start)
            pl.when(rank == r)(own.start)
            batch.append(there)
        copies.append(batch)
    rest[0].wait()
    for copy in rest[1:]:
        copy.wait()
    ranks, own, ff_cols = up_in.shape
    heads, head_cols = qkv_in.shape[0], qkv_in.shape[0] * HEAD_DIM
    for r in range(ranks):
        sum_up[:, r * ff_cols : (r + 1) * ff_cols] = up_in[r].astype(jnp.float32)
        for i, total in enumerate((sum_query, sum_key, sum_value)):
            for h in range(heads):
                start = r * head_cols + h * HEAD_DIM
                value = qkv_in[h, r, :, i * HEAD_DIM : (i + 1) * HEAD_DIM]
                total[:, start : start + HEAD_DIM] = value.astype(jnp.float32)
    small_sums = outs[7:]
    for i in range(5):
        small_sums[i][...] = small_in[i : i + 1, :own]
    small_sums[5][...] = jnp.concatenate([small_in[5 + q : 6 + q, :own] for q in range(4)], axis=1)
    left = [pltpu.make_async_copy(out_in, sum_out, leaving_sums.at[4])]
    for k, (total, out) in enumerate(zip(sums_v, outs[2:5] + outs[6:7])):
        left.append(pltpu.make_async_copy(total, out, leaving_sums.at[k]))
    for copy in left:
        copy.start()
    for k, cut in enumerate(cuts):
        for copy in copies[k]:
            copy.wait()
        total = hidden[cut] + gains[4:5] + term_in[0, cut].astype(jnp.float32)
        act_v[0, cut] = total.astype(jnp.bfloat16)
        total = total + extra_in[cut].astype(jnp.float32)
        act_v[1, cut] = total.astype(jnp.bfloat16)
        total = total + term_in[1, cut].astype(jnp.float32)
        act_v[2, cut] = total.astype(jnp.bfloat16)
        total = total + term_in[2, cut].astype(jnp.float32) + term_in[3, cut].astype(jnp.float32)
        act_v[3, cut] = total.astype(jnp.bfloat16)
        left.append(
            pltpu.make_async_copy(act_v.at[:, cut], activations.at[:, cut], leaving.at[k, 0])
        )
        left[-1].start()
        left.append(pltpu.make_async_copy(grad_in.at[cut], grad_tokens.at[cut], leaving.at[k, 1]))
        left[-1].start()
    for copy in left:
        copy.wait()


ANY = pl.BlockSpec(memory_space=pl.ANY)
ON_CORE = pl.BlockSpec(memory_space=pltpu.VMEM)


def connected(kernel, number, outs, out_specs, in_specs, scratch, operands):
    return pl.pallas_call(
        kernel,
        out_shape=outs,
        in_specs=in_specs,
        out_specs=out_specs,
        scratch_shapes=scratch + LINK_SCRATCH,
        compiler_params=pltpu.CompilerParams(
            collective_id=number, has_side_effects=True, vmem_limit_bytes=63 * 2**20
        ),
    )(*operands)


def array(shape, dtype=jnp.bfloat16):
    return jax.ShapeDtypeStruct(shape, dtype)


def turning(count):
    half_size = HEAD_DIM // 2
    inverse = np.exp(np.arange(half_size, dtype=np.float32) * np.float32(-math.log(10000.0) / half_size))
    angles = np.arange(count, dtype=np.float32)[:, None] * inverse.astype(np.float32)[None, :]
    cosine, sine = np.cos(angles), np.sin(angles)
    cosine = np.concatenate([cosine, cosine], axis=1)
    return jnp.asarray(cosine), jnp.asarray(np.concatenate([-sine, sine], axis=1))


def local_split(ranks, shards, *arguments):
    chips = shards // 2
    (
        tokens,
        cotangent,
        norm1_gain,
        norm1_bias,
        query_weight,
        key_weight,
        value_weight,
        out_weight,
        norm2_gain,
        norm2_bias,
        up_weight,
        up_bias,
        down_weight,
        down_bias,
    ) = arguments
    model_width = tokens.shape[2]
    tok_rows = tokens.shape[1]
    seq_len = tok_rows * ranks
    own = query_weight.shape[0]
    heads = HEADS // ranks
    head_cols = heads * HEAD_DIM
    ff_cols = FF // ranks
    scaling = HEAD_DIM ** (-0.5)
    rank = lax.axis_index("dp")

    column = np.arange(model_width)
    comb = jnp.asarray(column[None, :] % own == np.arange(128)[:, None], jnp.bfloat16)
    mask = jnp.asarray(column[None, :] // own == np.arange(ranks * shards)[:, None], jnp.float32)
    cosine, sine = turning(seq_len)
    own_tokens = tokens.reshape(tok_rows, model_width)
    blocks_low = array((ranks, tok_rows, model_width))
    down_rows = down_weight.shape[0]
    first_cols = ff_cols * 5 // 12
    vmem = pltpu.VMEM
    low = jnp.bfloat16
    f32 = jnp.float32
    (
        all_tokens,
        attn_in,
        qkv_rot,
        mixed_low,
        hidden,
        ffn_in,
        gains,
        incoming,
        cotangent_sum,
        next_sum,
        w_qkv,
        w_out,
        w_up,
        w_down,
    ) = connected(
        functools.partial(forward_kernel, chips),
        1,
        (
            blocks_low,
            blocks_low,
            array((ranks, tok_rows, 3 * head_cols)),
            array((ranks, tok_rows, head_cols)),
            array((tok_rows, model_width), jnp.float32),
            blocks_low,
            array((8, model_width), jnp.float32),
            blocks_low,
            array((tok_rows, model_width), f32),
            array((tok_rows, model_width)),
            array((ranks, shards, own, 3 * head_cols)),
            array((shards, own, model_width)),
            array((ranks, shards, own, ff_cols)),
            array((shards, down_rows, model_width // 2)),
        ),
        [ANY] * 6 + [ON_CORE] + [ANY] * 7,
        [ANY] * 2 + [ON_CORE] * 16,
        [
            vmem((tok_rows, model_width), f32),
            vmem((tok_rows, model_width), f32),
            vmem((GRAN, tok_rows, model_width), low),
            vmem((GRAN, tok_rows, model_width), low),
            vmem((16, 128), low),
            vmem((ranks, tok_rows, model_width), jnp.bfloat16),
            vmem((ranks, tok_rows, model_width), jnp.bfloat16),
            vmem((ranks, tok_rows, 3 * head_cols), jnp.bfloat16),
            vmem((ranks, tok_rows, head_cols), jnp.bfloat16),
            vmem((ranks, shards, own, 3 * head_cols), jnp.bfloat16),
            vmem((shards, own, model_width), jnp.bfloat16),
            vmem((ranks, tok_rows, model_width), jnp.bfloat16),
            vmem((3, tok_rows, model_width), jnp.bfloat16),
            vmem((tok_rows, model_width), jnp.bfloat16),
            vmem((tok_rows, model_width), jnp.bfloat16),
            vmem((ranks, shards, 16, 128), jnp.bfloat16),
        ],
        (
            own_tokens,
            cotangent.reshape(GRAN, tok_rows, model_width),
            norm1_gain.reshape(1, own),
            norm1_bias.reshape(1, own),
            norm2_gain.reshape(1, own),
            norm2_bias.reshape(1, own),
            down_bias.reshape(1, own),
            up_bias.reshape(1, -1),
            query_weight,
            key_weight,
            value_weight,
            out_weight,
            up_weight,
            down_weight,
            comb,
            mask,
            cosine,
            sine,
        ),
    )
    (
        grad_hidden,
        sums,
        sum_down,
        sum_up_low,
        share_up,
        all_branch,
        terms,
        own_term,
        extra_in,
    ) = connected(
        functools.partial(middle_kernel, chips),
        2,
        (
            array((tok_rows, model_width), f32),
            array((8, model_width), f32),
            array((down_rows, model_width), f32),
            array((ranks, own, first_cols)),
            array((ranks, chips, own, ff_cols - first_cols)),
            blocks_low,
            blocks_low,
            array((tok_rows, model_width)),
            array((tok_rows, model_width)),
        ),
        [ANY, ON_CORE, ANY, ON_CORE] + [ANY] * 5,
        [ANY] * 6 + [ON_CORE] * 3,
        [
            vmem((ranks, tok_rows, model_width), low),
            vmem((2, ranks, tok_rows, model_width), low),
            vmem((ranks, chips, 2, own, ff_cols), low),
            vmem((shards, down_rows, model_width), low),
            vmem((ranks, tok_rows, ff_cols), low),
            vmem((ranks, tok_rows, ff_cols), low),
            vmem((2, chips, 2, down_rows, model_width // 2), low),
            vmem((2, chips, down_rows, model_width // 2), low),
            vmem((2, 4, 1, down_rows, model_width // 2), low),
            vmem((ranks, chips, own, ff_cols), low),
            vmem((4, ranks, own, first_cols), low),
            vmem((2, ranks, tok_rows, model_width), low),
            vmem((tok_rows, model_width), low),
            vmem((tok_rows, model_width), low),
            vmem((tok_rows, model_width), low),
            vmem((tok_rows, model_width), f32),
            vmem((down_rows, model_width), f32),
            vmem((ranks, tok_rows, model_width), low),
            vmem((3, tok_rows, model_width), low),
            vmem((tok_rows, model_width), low),
        ],
        (
            ffn_in,
            incoming,
            next_sum,
            w_up.reshape(ranks, chips, 2, own, ff_cols),
            w_down,
            down_weight,
            hidden,
            cotangent_sum,
            gains,
        ),
    )
    term_in, grad_inputs, sum_out, sum_up, sum_qkv, small_sums = connected(
        functools.partial(last_kernel, chips),
        3,
        (
            blocks_low,
            array((tok_rows, model_width)),
            array((own, model_width), f32),
            array((ranks, own, ff_cols)),
            array((heads, ranks, own, 3 * HEAD_DIM)),
            array((16, 128), f32),
        ),
        [ANY] + [ON_CORE] * 2 + [ANY] * 2 + [ON_CORE],
        [ANY] * 10 + [ON_CORE] * 7,
        [
            vmem((ranks, tok_rows, model_width), low),
            vmem((ranks, tok_rows, 3 * head_cols), low),
            vmem((ranks, tok_rows, head_cols), low),
            vmem((ranks, tok_rows, head_cols), low),
            vmem((shards, own, model_width), low),
            vmem((ranks, shards, own, 3 * head_cols), low),
            vmem((ranks, tok_rows, model_width), low),
            vmem((ranks, tok_rows, model_width), low),
            vmem((ranks, tok_rows, 3 * head_cols), low),
            vmem((seq_len, HEAD_DIM), f32),
            vmem((seq_len, HEAD_DIM), f32),
            vmem((ranks, tok_rows, model_width), low),
            vmem((3, tok_rows, model_width), low),
            vmem((tok_rows, model_width), low),
            vmem((ranks, own, ff_cols), low),
            vmem((ranks, own, ff_cols - first_cols), low),
            vmem((ranks, own, ff_cols - first_cols), low),
            vmem((4, ranks, own, ff_cols - first_cols), low),
            vmem((1, chips, 2, own, model_width), low),
            vmem((1, chips, own, model_width), low),
            vmem((4, 1, own, model_width), low),
            vmem((heads, ranks, chips, 2, own, 3 * HEAD_DIM), low),
            vmem((heads, ranks, chips, own, 3 * HEAD_DIM), low),
            vmem((heads, 4, ranks, own, 3 * HEAD_DIM), low),
            vmem((heads, ranks, own, 3 * HEAD_DIM), low),
            vmem((ranks, chips, 2, 16, 128), f32),
            vmem((ranks, chips, 16, 128), f32),
            vmem((4, ranks, 16, 128), f32),
            vmem((ranks, 16, 128), f32),
            vmem((ranks, 16, 128), f32),
            vmem((8, model_width), f32),
        ],
        (
            all_branch,
            sum_up_low,
            share_up,
            terms,
            qkv_rot,
            mixed_low,
            w_out,
            w_qkv,
            attn_in,
            all_tokens,
            grad_hidden,
            gains,
            sums,
            comb,
            mask,
            cosine,
            sine,
        ),
    )
    (
        activations,
        grad_tokens,
        sum_query,
        sum_key,
        sum_value,
        sum_out,
        sum_up,
        *gain_sums,
    ) = pl.pallas_call(
        closing_kernel,
        out_shape=(
            array((GRAN, tok_rows, model_width)),
            array((tok_rows, model_width)),
            *[array((own, model_width), f32) for i in range(4)],
            array((own, FF), f32),
            *[array((1, own), f32) for i in range(5)],
            array((1, down_rows), f32),
        ),
        in_specs=[ANY] * 10,
        out_specs=[ANY] * 7 + [ON_CORE] * 6,
        scratch_shapes=[
            vmem((tok_rows, model_width), f32),
            vmem((8, model_width), f32),
            vmem((ranks, tok_rows, model_width), low),
            vmem((tok_rows, model_width), low),
            vmem((tok_rows, model_width), low),
            vmem((own, model_width), f32),
            vmem((ranks, own, ff_cols), low),
            vmem((heads, ranks, own, 3 * HEAD_DIM), low),
            vmem((16, 128), f32),
            vmem((GRAN, tok_rows, model_width), low),
            pltpu.SemaphoreType.DMA((5, 13)),
            pltpu.SemaphoreType.DMA((4, 2)),
            *[vmem((own, model_width), f32) for i in range(3)],
            vmem((own, FF), f32),
            pltpu.SemaphoreType.DMA((5,)),
        ],
        compiler_params=pltpu.CompilerParams(vmem_limit_bytes=60 * 2**20),
    )(
        own_term,
        hidden,
        gains,
        term_in,
        extra_in,
        grad_inputs,
        sum_out,
        sum_up,
        sum_qkv,
        small_sums,
    )
    gain_sums = [v.reshape(-1) for v in gain_sums]
    return (
        activations.reshape(GRAN, 1, tok_rows, model_width),
        grad_tokens.reshape(1, tok_rows, model_width),
        gain_sums[0],
        gain_sums[1],
        sum_query,
        sum_key,
        sum_value,
        sum_out,
        gain_sums[2],
        gain_sums[3],
        sum_up,
        gain_sums[5],
        sum_down,
        gain_sums[4],
    )


def solution(mesh):
    placed = (
        P("fsdp", "dp", None),
        P(None, "fsdp", "dp", None),
        P(("dp", "fsdp")),
        P(("dp", "fsdp")),
        P(("dp", "fsdp"), None),
        P(("dp", "fsdp"), None),
        P(("dp", "fsdp"), None),
        P(("dp", "fsdp"), None),
        P(("dp", "fsdp")),
        P(("dp", "fsdp")),
        P(("dp", "fsdp"), None),
        P(("dp", "fsdp")),
        P(("dp", "fsdp"), None),
        P(("dp", "fsdp")),
    )
    ranks, shards = mesh.shape["dp"], mesh.shape["fsdp"]
    local = local_gathered
    if ranks == 4 and shards == 8:
        local = functools.partial(local_split, ranks, shards)
    return jax.shard_map(
        local,
        mesh=mesh,
        in_specs=placed,
        out_specs=(
            P(None, "fsdp", "dp", None),
            P("fsdp", "dp", None),
            P(("dp", "fsdp")),
            P(("dp", "fsdp")),
            P(("dp", "fsdp"), None),
            P(("dp", "fsdp"), None),
            P(("dp", "fsdp"), None),
            P(("dp", "fsdp"), None),
            P(("dp", "fsdp")),
            P(("dp", "fsdp")),
            P(("dp", "fsdp"), None),
            P(("dp", "fsdp")),
            P(("dp", "fsdp"), None),
            P(("dp", "fsdp")),
        ),
        check_vma=False,
    )
```
